32 devices in a mesh: parts: 2 (over y), expert: 8 (over z, x), replica: 2 (over core).
Axes of the slice: x: 2, y: 2, z: 4, core: 2. Of those that a mesh axis runs over, the one named last changes fastest.
Arguments:
- tokens: bfloat16 [4096, 1024], P(('parts', 'expert', 'replica')), parts along dimension 0, may hold values from -6 to 6
- cotangent: bfloat16 [4096, 1024], P(('parts', 'expert', 'replica')), parts along dimension 0, may hold values from -2 to 2
- expert_ids: int32 [4096, 8], P(('parts', 'expert', 'replica')), parts along dimension 0, may hold values from 0 to 7, as said below
- gate_values: bfloat16 [4096, 8], P(('parts', 'expert', 'replica')), parts along dimension 0, may hold values from 0.049804688 to 0.5
- replica_pick: int32 [4096, 8], P(('parts', 'expert', 'replica')), parts along dimension 0, may hold values from 0 to 2
- replica_plan: int32 [16], P('parts'), parts along dimension 0, may hold values from 0 to 7, as said below
- gate_proj: bfloat16 [8, 1024, 384], P('expert'), may hold values from -0.1875 to 0.1875
- up_proj: bfloat16 [8, 1024, 384], P('expert'), may hold values from -0.1875 to 0.1875
- down_proj: bfloat16 [8, 1024, 384], P('expert'), may hold values from -0.3125 to 0.3125
Outputs:
- token_grad: bfloat16 [4096, 1024], P(('parts', 'expert', 'replica')), parts along dimension 0
- gate_grad: bfloat16 [4096, 8], P(('parts', 'expert', 'replica')), parts along dimension 0
- grad_gate_proj: bfloat16 [16, 1024, 384], P(('parts', 'expert'), 'replica'), parts along dimension 0
- grad_up_proj: bfloat16 [16, 1024, 384], P(('parts', 'expert'), 'replica'), parts along dimension 0
- grad_down_proj: bfloat16 [16, 1024, 384], P(('parts', 'expert'), 'replica'), parts along dimension 0
The draws below stay inside these ranges and needn't reach their ends.
There are 2 independent parts, one for each index of `parts`. The reference program is written for one: setup_inputs(seed, part) draws one part's arguments, and reference() takes and returns one part's arrays. A program takes and returns all parts, laid end to end along the dimension named above; an argument that names none is the same for every part. Nothing has to cross between parts.
Inputs may be any that keep to these rules, and one draw needn't show every extreme that they name: `expert_ids`: each row names 8 different experts. `replica_plan`: 4 different experts appear, each exactly 2 times.
All inputs are finite; a program needn't handle non-finite values.
Results may differ from the reference program's by a relative error of at most 0.0095.
Values may be sent and summed in bfloat16 or wider, within the bound.
No kernel may reach another device: no remote copies, remote signals or barrier semaphores. Data moves between devices by JAX's collectives and lax.ppermute only.
A program may use at most 128 MiB of HBM per device.

```python
import jax
import jax.numpy as jnp
from jax import lax

D = 1024
H = 384
TOPK = 8
TOK_DEV = 128
REPS = 2
EXPERTS = 8
HOT = 4
CAP = 6
TOKENS = 2048
N_REPLICA = 2


def hot_order(key):
    return jax.random.permutation(jax.random.fold_in(key, 11), EXPERTS).astype(jnp.int32)


def draw_expert_ids(key, part):
    ordering = hot_order(key)
    key = jax.random.fold_in(key, 1)
    expert_lane = jnp.arange(EXPERTS, dtype=jnp.int32)
    hot_mask = jnp.any(ordering[:HOT][:, None] == expert_lane[None, :], axis=0).astype(jnp.int32)
    raw_scores = jax.random.randint(key, (TOKENS, EXPERTS), 0, 65536, dtype=jnp.int32)
    scores = (raw_scores + hot_mask[None, :] * 13107) * 128 + expert_lane[None, :]
    chosen = lax.top_k(scores, TOPK)[1]
    return chosen.astype(jnp.int32)


def draw_replica_plan(key, part):
    ordering = hot_order(key)
    key = jax.random.fold_in(key, 2)
    holders = jax.random.permutation(key, EXPERTS).astype(jnp.int32)
    return ordering[holders // REPS].astype(jnp.int32)


def set_ends(result, own_key, least, largest):
    longest = result.shape.index(max(result.shape))
    spots = []
    for shift in (0, 1):
        where = [jax.random.randint(jax.random.fold_in(own_key, axis), (), 0, length) for axis, length in enumerate(result.shape)]
        where[longest] = (where[longest] + shift) % result.shape[longest]
        spots.append(tuple(where))
    return result.at[spots[0]].set(least).at[spots[1]].set(largest)


def block_levels(own_key, dims, pieces, low, high):
    def one(dim, blocks):
        draws = jax.random.uniform(jax.random.fold_in(jax.random.fold_in(own_key, 6), dim), (blocks,), jnp.float32, low / len(pieces), high / len(pieces))
        return jnp.repeat(jnp.exp(draws), dims[dim] // blocks).reshape((-1,) + (1,) * (len(dims) - dim - 1))

    loudness = one(*pieces[0])
    for cut in pieces[1:]:
        loudness = loudness * one(*cut)
    return loudness


def noise(rng, extent, width, bound, split=(), kind=jnp.bfloat16):
    gain = block_levels(rng, extent, split, -0.22, 0.18) if split else 1.0
    values = jax.random.normal(rng, extent, jnp.float32) * width * gain
    return jnp.minimum(jnp.maximum(values, -bound), bound).astype(kind)


def setup_inputs(seed: int = 0, part: int = 0) -> dict:
    splits = jax.random.split(jax.random.key(seed), 10)
    own_keys = jax.random.split(jax.random.fold_in(splits[9], part), 10)
    return {
        "tokens": noise(own_keys[0], (TOKENS, D), 1.0, 6.0, ((0, 16),)),
        "cotangent": noise(own_keys[1], (TOKENS, D), 0.3, 2.0, ((0, 16),)),
        "expert_ids": draw_expert_ids(jax.random.fold_in(jax.random.fold_in(splits[9], part), 71), part),
        "gate_values": jnp.clip(0.049804688 + 0.4501953 * jax.random.uniform(own_keys[3], (TOKENS, TOPK), jnp.float32) ** block_levels(own_keys[3], (TOKENS, TOPK), ((0, 16),), -0.2, 0.2), 0.049804688, 0.5).astype(jnp.bfloat16),
        "replica_pick": set_ends(jax.random.randint(own_keys[4], (TOKENS, TOPK), 0, REPS + 1), jax.random.fold_in(own_keys[4], 1), 0, REPS).astype(jnp.int32),
        "replica_plan": draw_replica_plan(jax.random.fold_in(jax.random.fold_in(splits[9], part), 71), part),
        "gate_proj": noise(splits[6], (EXPERTS, D, H), D ** -0.5, 0.1875, ((0, 8),)),
        "up_proj": noise(splits[7], (EXPERTS, D, H), D ** -0.5, 0.1875, ((0, 8),)),
        "down_proj": noise(splits[8], (EXPERTS, D, H), H ** -0.5, 0.3125, ((0, 8),)),
    }


def route_assignments(flat_ids, flat_pick, replica_plan, capacity):
    experts = replica_plan.shape[0]
    lane_ids = jnp.arange(experts, dtype=jnp.int32)
    same_plan = replica_plan[:, None] == replica_plan[None, :]
    earlier = lane_ids[None, :] < lane_ids[:, None]
    position = jnp.sum(jnp.logical_and(same_plan, earlier), axis=1).astype(jnp.int32)
    hot_mask = jnp.any(replica_plan[None, :] == lane_ids[:, None], axis=1)
    is_hot = jnp.any(jnp.logical_and(flat_ids[:, None] == lane_ids[None, :], hot_mask[None, :]), axis=1)
    use_copy = jnp.logical_and(is_hot, flat_pick >= 1)
    matches = jnp.logical_and(replica_plan[None, :] == flat_ids[:, None], position[None, :] == flat_pick[:, None] - 1)
    holder = jnp.sum(jnp.where(matches, lane_ids[None, :], 0), axis=1).astype(jnp.int32)
    target = jnp.where(use_copy, holder, flat_ids).astype(jnp.int32)
    copy_role = use_copy.astype(jnp.int32)
    bucket = target * 2 + copy_role
    sequence = jnp.arange(bucket.shape[0], dtype=jnp.int32)
    arrival = jnp.sum(jnp.logical_and(bucket[None, :] == bucket[:, None], sequence[None, :] < sequence[:, None]), axis=1).astype(jnp.int32)
    kept_mask = arrival < capacity
    slot_index = (target * (2 * capacity) + copy_role * capacity + jnp.minimum(arrival, capacity - 1)).astype(jnp.int32)
    return slot_index, kept_mask


def fill_slots(slot_index, kept_mask, slot_count):
    slot_ids = jnp.arange(slot_count, dtype=jnp.int32)
    matches = jnp.logical_and(slot_index[None, :] == slot_ids[:, None], kept_mask[None, :])
    sequence = jnp.arange(slot_index.shape[0], dtype=jnp.int32)
    source = jnp.sum(jnp.where(matches, sequence[None, :], 0), axis=1).astype(jnp.int32)
    filled = jnp.any(matches, axis=1)
    return source, filled


def expert_backward(row_block, upstream, weight, gate_w, up_w, down_w):
    contract_cols = (((1,), (1,)), ((), ()))
    contract_rows = (((0,), (0,)), ((), ()))
    gate_pre = jnp.dot(row_block, gate_w, preferred_element_type=jnp.float32)
    up_pre = jnp.dot(row_block, up_w, preferred_element_type=jnp.float32)
    sigmoid_gate = jax.nn.sigmoid(gate_pre)
    activated = gate_pre * sigmoid_gate
    hidden = (activated * up_pre).astype(jnp.bfloat16)
    output_rows = lax.dot_general(hidden, down_w, contract_cols, preferred_element_type=jnp.float32)
    weight_col = weight.astype(jnp.float32)[:, None]
    upstream_f = upstream.astype(jnp.float32)
    gate_rows = jnp.sum(upstream_f * output_rows, axis=1)
    hidden_grad = weight_col * jnp.dot(upstream, down_w, preferred_element_type=jnp.float32)
    slope = sigmoid_gate * (1.0 + gate_pre * (1.0 - sigmoid_gate))
    gate_delta = (hidden_grad * up_pre * slope).astype(jnp.bfloat16)
    up_delta = (hidden_grad * activated).astype(jnp.bfloat16)
    input_grad = (lax.dot_general(gate_delta, gate_w, contract_cols, preferred_element_type=jnp.float32)
                  + lax.dot_general(up_delta, up_w, contract_cols, preferred_element_type=jnp.float32)).astype(jnp.bfloat16)
    scaled = (weight_col * upstream_f).astype(jnp.bfloat16)
    grad_set = (lax.dot_general(row_block, gate_delta, contract_rows, preferred_element_type=jnp.float32),
                lax.dot_general(row_block, up_delta, contract_rows, preferred_element_type=jnp.float32),
                lax.dot_general(scaled, hidden, contract_rows, preferred_element_type=jnp.float32))
    return input_grad, gate_rows, grad_set


def reference(tokens, cotangent, expert_ids, gate_values, replica_pick, replica_plan, gate_proj, up_proj, down_proj):
    experts = EXPERTS
    groups = N_REPLICA
    blocks = experts * groups
    capacity = CAP
    slot_total = 2 * capacity
    per_block = TOK_DEV * TOPK
    ids_blocks = expert_ids.reshape(blocks, per_block)
    pick_blocks = replica_pick.reshape(blocks, per_block)

    def block_routes(inputs_pair):
        slot_index, kept_mask = route_assignments(inputs_pair[0], inputs_pair[1], replica_plan, capacity)
        return fill_slots(slot_index, kept_mask, experts * slot_total)

    sources, fills = lax.map(block_routes, (ids_blocks, pick_blocks))
    source_grid = sources.reshape(experts, groups, experts, slot_total)
    fill_grid = fills.reshape(experts, groups, experts, slot_total)
    sender = jnp.arange(experts, dtype=jnp.int32)
    gate_flat = gate_values.reshape(-1)
    hot_mask = jnp.any(replica_plan[None, :] == sender[:, None], axis=1)
    hot_rank = (jnp.cumsum(hot_mask.astype(jnp.int32)) - 1).astype(jnp.int32)

    def serve_slots(accums, target, member, copy_role, weights):
        token_acc, gate_acc = accums
        slot_src = source_grid[:, member, target, copy_role * capacity:(copy_role + 1) * capacity]
        present = fill_grid[:, member, target, copy_role * capacity:(copy_role + 1) * capacity].reshape(-1)
        assign = ((sender[:, None] * groups + member) * per_block + slot_src).reshape(-1).astype(jnp.int32)
        token_index = (assign // TOPK).astype(jnp.int32)
        row_block = jnp.where(present[:, None], tokens[token_index], jnp.zeros((), jnp.bfloat16))
        upstream = jnp.where(present[:, None], cotangent[token_index], jnp.zeros((), jnp.bfloat16))
        weight = jnp.where(present, gate_flat[assign], jnp.zeros((), jnp.bfloat16))
        input_grad, gate_rows, grad_set = expert_backward(row_block, upstream, weight, weights[0], weights[1], weights[2])
        input_f = lax.optimization_barrier(input_grad).astype(jnp.float32)
        gate_f = lax.optimization_barrier(gate_rows.astype(jnp.bfloat16)).astype(jnp.float32)
        token_acc = token_acc.at[token_index].add(jnp.where(present[:, None], input_f, jnp.float32(0.0)))
        gate_acc = gate_acc.at[assign].add(jnp.where(present, gate_f, jnp.float32(0.0)))
        return (token_acc, gate_acc), grad_set

    accums = (jnp.zeros((TOKENS, D), jnp.float32), jnp.zeros((TOKENS * TOPK,), jnp.float32))
    copies = jnp.zeros((groups, HOT, 3, D, H), jnp.float32)

    def copy_step(carried, target):
        state, sums = carried
        source_expert = replica_plan[target]
        weights = (gate_proj[source_expert], up_proj[source_expert], down_proj[source_expert])
        for member in range(groups):
            state, grad_set = serve_slots(state, target, member, 1, weights)
            stacked = lax.optimization_barrier(jnp.stack(grad_set).astype(jnp.bfloat16)).astype(jnp.float32)
            sums = sums.at[member, hot_rank[source_expert]].add(stacked)
        return (state, sums), None

    (accums, copies), unused = lax.scan(copy_step, (accums, copies), sender)
    copies_round = lax.optimization_barrier(copies.astype(jnp.bfloat16)).astype(jnp.float32)

    def own_step(state, target):
        weights = (gate_proj[target], up_proj[target], down_proj[target])
        total_sum = jnp.zeros((3, D, H), jnp.float32)
        for member in range(groups):
            state, grad_set = serve_slots(state, target, member, 0, weights)
            extra = jnp.where(hot_mask[target], copies_round[member, jnp.maximum(hot_rank[target], 0)], jnp.float32(0.0))
            total = jnp.stack(grad_set) + extra
            total_sum = total_sum + lax.optimization_barrier(total.astype(jnp.bfloat16)).astype(jnp.float32)
        return state, total_sum.astype(jnp.bfloat16)

    accums, grads_out = lax.scan(own_step, accums, sender)
    token_grad = accums[0].astype(jnp.bfloat16)
    gate_grad = accums[1].reshape(TOKENS, TOPK).astype(jnp.bfloat16)
    return token_grad, gate_grad, grads_out[:, 0], grads_out[:, 1], grads_out[:, 2]
```

```python
import jax
import jax.numpy as jnp
from jax import lax
from jax.experimental import pallas as pl
from jax.experimental.pallas import tpu as pltpu
from jax.sharding import PartitionSpec as P

CAP = 6


def route_assignments(flat_ids, flat_pick, replica_plan, capacity):
    experts = replica_plan.shape[0]
    lane_ids = jnp.arange(experts, dtype=jnp.int32)
    same_plan = replica_plan[:, None] == replica_plan[None, :]
    earlier = lane_ids[None, :] < lane_ids[:, None]
    position = jnp.sum(jnp.logical_and(same_plan, earlier), axis=1)
    hot_mask = jnp.any(replica_plan[None, :] == lane_ids[:, None], axis=1)
    is_hot = jnp.any(
        jnp.logical_and(flat_ids[:, None] == lane_ids[None, :], hot_mask[None, :]), axis=1
    )
    use_copy = jnp.logical_and(is_hot, flat_pick >= 1)
    matches = jnp.logical_and(
        replica_plan[None, :] == flat_ids[:, None], position[None, :] == flat_pick[:, None] - 1
    )
    holder = jnp.sum(jnp.where(matches, lane_ids[None, :], 0), axis=1)
    target = jnp.where(use_copy, holder, flat_ids)
    copy_role = use_copy.astype(jnp.int32)
    bucket = target * 2 + copy_role
    sequence = jnp.arange(bucket.shape[0], dtype=jnp.int32)
    arrival = jnp.sum(
        jnp.logical_and(bucket[None, :] == bucket[:, None], sequence[None, :] < sequence[:, None]),
        axis=1,
    )
    kept_mask = arrival < capacity
    slot_index = target * (2 * capacity) + copy_role * capacity + jnp.minimum(arrival, capacity - 1)
    return (slot_index, kept_mask)


def fill_slots(slot_index, kept_mask, slot_count):
    slot_ids = jnp.arange(slot_count, dtype=jnp.int32)
    matches = jnp.logical_and(slot_index[None, :] == slot_ids[:, None], kept_mask[None, :])
    sequence = jnp.arange(slot_index.shape[0], dtype=jnp.int32)
    source = jnp.sum(jnp.where(matches, sequence[None, :], 0), axis=1)
    filled = jnp.any(matches, axis=1)
    return (source, filled)


def expert_backward(row_block, upstream, weight, gate_w, up_w, down_w):
    contract_cols = (((1,), (1,)), ((), ()))
    contract_rows = (((0,), (0,)), ((), ()))
    gate_pre = jnp.dot(row_block, gate_w, preferred_element_type=jnp.float32)
    up_pre = jnp.dot(row_block, up_w, preferred_element_type=jnp.float32)
    sigmoid_gate = jax.nn.sigmoid(gate_pre)
    activated = gate_pre * sigmoid_gate
    hidden = (activated * up_pre).astype(jnp.bfloat16)
    output_rows = lax.dot_general(hidden, down_w, contract_cols, preferred_element_type=jnp.float32)
    weight_col = weight.astype(jnp.float32)[:, None]
    upstream_f = upstream.astype(jnp.float32)
    gate_rows = jnp.sum(upstream_f * output_rows, axis=1)
    hidden_grad = weight_col * jnp.dot(upstream, down_w, preferred_element_type=jnp.float32)
    slope = sigmoid_gate * (1.0 + gate_pre * (1.0 - sigmoid_gate))
    gate_delta = (hidden_grad * up_pre * slope).astype(jnp.bfloat16)
    up_delta = (hidden_grad * activated).astype(jnp.bfloat16)
    input_grad = (
        lax.dot_general(gate_delta, gate_w, contract_cols, preferred_element_type=jnp.float32)
        + lax.dot_general(up_delta, up_w, contract_cols, preferred_element_type=jnp.float32)
    ).astype(jnp.bfloat16)
    scaled = (weight_col * upstream_f).astype(jnp.bfloat16)
    grad_set = (
        lax.dot_general(row_block, gate_delta, contract_rows, preferred_element_type=jnp.float32),
        lax.dot_general(row_block, up_delta, contract_rows, preferred_element_type=jnp.float32),
        lax.dot_general(scaled, hidden, contract_rows, preferred_element_type=jnp.float32),
    )
    return (input_grad, gate_rows, grad_set)


def per_device_moving_weights(
    tokens,
    cotangent,
    expert_ids,
    gate_values,
    replica_pick,
    replica_plan,
    gate_proj,
    up_proj,
    down_proj,
):
    experts = lax.axis_size("expert")
    capacity = CAP
    slot_total = 2 * capacity
    model_width = tokens.shape[1]
    topk = expert_ids.shape[1]
    token_count = tokens.shape[0]
    slot_index, kept_mask = route_assignments(
        expert_ids.reshape(-1), replica_pick.reshape(-1), replica_plan, capacity
    )
    source, filled = fill_slots(slot_index, kept_mask, experts * slot_total)
    token_of = source // topk
    zero_half = jnp.zeros((), jnp.bfloat16)
    send_rows = jnp.where(filled[:, None], jnp.take(tokens, token_of, axis=0), zero_half).reshape(
        experts, slot_total, model_width
    )
    send_upstream = jnp.where(
        filled[:, None], jnp.take(cotangent, token_of, axis=0), zero_half
    ).reshape(experts, slot_total, model_width)
    send_weight = jnp.where(filled, gate_values.reshape(-1)[source], zero_half).reshape(
        experts, slot_total
    )
    arrived = lax.all_to_all(send_rows, "expert", split_axis=0, concat_axis=0, tiled=True)
    own_gate = gate_proj[0]
    own_up = up_proj[0]
    own_down = down_proj[0]
    hidden_width = own_gate.shape[1]
    spread = (
        lax.all_to_all(
            own_gate.reshape(experts, -1), "expert", split_axis=0, concat_axis=0, tiled=True
        ),
        lax.all_to_all(
            own_up.reshape(experts, -1), "expert", split_axis=0, concat_axis=0, tiled=True
        ),
        lax.all_to_all(
            own_down.reshape(experts, -1), "expert", split_axis=0, concat_axis=0, tiled=True
        ),
    )
    chosen_gate = jnp.take(spread[0], replica_plan, axis=0)
    chosen_up = jnp.take(spread[1], replica_plan, axis=0)
    chosen_down = jnp.take(spread[2], replica_plan, axis=0)
    collected = (
        lax.all_to_all(chosen_gate, "expert", split_axis=0, concat_axis=0, tiled=True),
        lax.all_to_all(chosen_up, "expert", split_axis=0, concat_axis=0, tiled=True),
        lax.all_to_all(chosen_down, "expert", split_axis=0, concat_axis=0, tiled=True),
    )
    copy_gate = collected[0].reshape(model_width, hidden_width)
    copy_up = collected[1].reshape(model_width, hidden_width)
    copy_down = collected[2].reshape(model_width, hidden_width)
    arrived_up, arrived_weight = (
        lax.all_to_all(send_upstream, "expert", split_axis=0, concat_axis=0, tiled=True),
        lax.all_to_all(send_weight, "expert", split_axis=0, concat_axis=0, tiled=True),
    )
    owned_dx, owned_gate_rows, owned_grads = expert_backward(
        arrived[:, :capacity].reshape(-1, model_width),
        arrived_up[:, :capacity].reshape(-1, model_width),
        arrived_weight[:, :capacity].reshape(-1),
        own_gate,
        own_up,
        own_down,
    )
    copied_dx, copied_gate_rows, copied_grads = expert_backward(
        arrived[:, capacity:].reshape(-1, model_width),
        arrived_up[:, capacity:].reshape(-1, model_width),
        arrived_weight[:, capacity:].reshape(-1),
        copy_gate,
        copy_up,
        copy_down,
    )
    back_rows = jnp.concatenate(
        [
            owned_dx.reshape(experts, capacity, model_width),
            copied_dx.reshape(experts, capacity, model_width),
        ],
        axis=1,
    )
    back_gate = jnp.concatenate(
        [owned_gate_rows.reshape(experts, capacity), copied_gate_rows.reshape(experts, capacity)],
        axis=1,
    ).astype(jnp.bfloat16)
    returned, returned_gate = (
        lax.all_to_all(back_rows, "expert", split_axis=0, concat_axis=0, tiled=True),
        lax.all_to_all(back_gate, "expert", split_axis=0, concat_axis=0, tiled=True),
    )
    copy_pieces = (
        copied_grads[0].astype(jnp.bfloat16).reshape(experts, -1),
        copied_grads[1].astype(jnp.bfloat16).reshape(experts, -1),
        copied_grads[2].astype(jnp.bfloat16).reshape(experts, -1),
    )
    grad_spread = (
        lax.all_to_all(copy_pieces[0], "expert", split_axis=0, concat_axis=0, tiled=True),
        lax.all_to_all(copy_pieces[1], "expert", split_axis=0, concat_axis=0, tiled=True),
        lax.all_to_all(copy_pieces[2], "expert", split_axis=0, concat_axis=0, tiled=True),
    )
    lane_ids = jnp.arange(experts, dtype=jnp.int32)
    owner_map = (replica_plan[None, :] == lane_ids[:, None]).astype(jnp.bfloat16)
    summed_gate = jnp.dot(owner_map, grad_spread[0], preferred_element_type=jnp.float32).astype(
        jnp.bfloat16
    )
    summed_up = jnp.dot(owner_map, grad_spread[1], preferred_element_type=jnp.float32).astype(
        jnp.bfloat16
    )
    summed_down = jnp.dot(owner_map, grad_spread[2], preferred_element_type=jnp.float32).astype(
        jnp.bfloat16
    )
    grad_back = (
        lax.all_to_all(summed_gate, "expert", split_axis=0, concat_axis=0, tiled=True),
        lax.all_to_all(summed_up, "expert", split_axis=0, concat_axis=0, tiled=True),
        lax.all_to_all(summed_down, "expert", split_axis=0, concat_axis=0, tiled=True),
    )
    total_gate = owned_grads[0] + grad_back[0].reshape(model_width, hidden_width).astype(
        jnp.float32
    )
    total_up = owned_grads[1] + grad_back[1].reshape(model_width, hidden_width).astype(jnp.float32)
    total_down = owned_grads[2] + grad_back[2].reshape(model_width, hidden_width).astype(
        jnp.float32
    )
    shares = (
        lax.psum_scatter(
            total_gate.astype(jnp.bfloat16), "replica", scatter_dimension=0, tiled=True
        ).astype(jnp.float32),
        lax.psum_scatter(
            total_up.astype(jnp.bfloat16), "replica", scatter_dimension=0, tiled=True
        ).astype(jnp.float32),
        lax.psum_scatter(
            total_down.astype(jnp.bfloat16), "replica", scatter_dimension=0, tiled=True
        ).astype(jnp.float32),
    )
    flat_back = returned.reshape(experts * slot_total, model_width)
    picked_rows = jnp.take(flat_back, slot_index, axis=0)
    picked_rows = jnp.where(kept_mask[:, None], picked_rows, zero_half).astype(jnp.float32)
    token_grad = jnp.sum(picked_rows.reshape(token_count, topk, model_width), axis=1).astype(
        jnp.bfloat16
    )
    gate_grad = jnp.where(kept_mask, returned_gate.reshape(-1)[slot_index], zero_half).reshape(
        token_count, topk
    )
    return (
        token_grad,
        gate_grad,
        shares[0].astype(jnp.bfloat16)[None],
        shares[1].astype(jnp.bfloat16)[None],
        shares[2].astype(jnp.bfloat16)[None],
    )


BF = jnp.bfloat16
F32 = jnp.float32
CONTRACT_ROWS = (((0,), (0,)), ((), ()))
CONTRACT_COLS = (((1,), (1,)), ((), ()))
VMEM_LIMIT = 40 * 1024 * 1024

MAIN = 16
QUARTERS = 4
SEND_ROWS = 2 * QUARTERS * MAIN + 16
BACK_ROWS = QUARTERS * MAIN + 16


def copies_of(experts):
    return 2 if experts <= 8 else 8


def iota(shape, axis):
    return lax.broadcasted_iota(jnp.int32, shape, axis)


def flip(values, eye):
    return lax.dot_general(values.astype(BF), eye, CONTRACT_ROWS, preferred_element_type=F32)


def repeat_rows(table, times):
    width = table.shape[1]
    return jnp.concatenate(
        [jnp.broadcast_to(table[e : e + 1], (times, width)) for e in range(table.shape[0])], axis=0
    )


def route_kernel(plan_ref, ids_ref, pick_ref, gate_ref, tok_ref, cot_ref, send_ref, slot_ref, gates_ref):
    tokens, topk = ids_ref.shape
    experts = send_ref.shape[0]
    width = tok_ref.shape[1] // QUARTERS
    copies = copies_of(experts)
    eye = (iota((tokens, tokens), 0) == iota((tokens, tokens), 1)).astype(BF)
    before = (iota((tokens, tokens), 0) < iota((tokens, tokens), 1)).astype(BF)
    ids = flip(ids_ref[...].astype(F32), eye).astype(jnp.int32)
    pick = flip(pick_ref[...].astype(F32), eye).astype(jnp.int32)
    gate = flip(gate_ref[...], eye)
    expert_row = iota((experts, tokens), 0)
    named = jnp.zeros((experts, tokens), jnp.int32)
    gates = jnp.zeros((experts, tokens), F32)
    for k in range(topk):
        hit = ids[k : k + 1] == expert_row
        named = jnp.where(hit, pick[k : k + 1] + 1, named)
        gates = jnp.where(hit, gate[k : k + 1], gates)
    hot = jnp.zeros((experts, tokens), jnp.int32)
    for j in range(experts):
        hot = jnp.where(expert_row == plan_ref[j], 1, hot)
    chosen = jnp.where(named == 0, -1, jnp.where(hot > 0, named - 1, 0))
    masks = jnp.concatenate([(chosen == c).astype(F32) for c in range(copies + 1)], axis=0)
    rank = jnp.dot(masks.astype(BF), before, preferred_element_type=F32).astype(jnp.int32)
    slot = jnp.full((experts, tokens), -1, jnp.int32)
    for c in range(copies + 1):
        rank_c = rank[c * experts : (c + 1) * experts]
        keep = jnp.logical_and(chosen == c, rank_c < CAP)
        slot = jnp.where(keep, c * CAP + rank_c, slot)
    slot_ref[...] = slot
    gates_ref[...] = gates
    slot16 = repeat_rows(slot, MAIN)
    gate16 = repeat_rows(gates, MAIN)
    lane_row = jnp.bitwise_and(iota(slot16.shape, 0), MAIN - 1)
    onehot = (slot16 == lane_row).astype(F32)
    rows = jnp.dot(onehot.astype(BF), tok_ref[...], preferred_element_type=F32).astype(BF)
    scaled = jnp.dot(
        (onehot * gate16).astype(BF), cot_ref[...], preferred_element_type=F32
    ).astype(BF)
    for e in range(experts):
        for q in range(QUARTERS):
            here = slice(e * MAIN, (e + 1) * MAIN)
            cols = slice(q * width, (q + 1) * width)
            send_ref[e, q * MAIN : (q + 1) * MAIN, :] = rows[here, cols]
            send_ref[e, (QUARTERS + q) * MAIN : (QUARTERS + q + 1) * MAIN, :] = scaled[here, cols]
    wanted = MAIN + jnp.bitwise_and(jnp.right_shift(lane_row, 2), 1)
    is_scaled = lane_row >= 8
    last = (slot16 == wanted).astype(F32)
    last_rows = jnp.where(is_scaled, 0.0, last)
    last_scaled = jnp.where(is_scaled, last * gate16, 0.0)
    tail = jnp.zeros((experts * MAIN, width), F32)
    for q in range(QUARTERS):
        mine = jnp.bitwise_and(lane_row, 3) == q
        cols = slice(q * width, (q + 1) * width)
        tail += jnp.dot(
            jnp.where(mine, last_rows, 0.0).astype(BF), tok_ref[:, cols], preferred_element_type=F32
        )
        tail += jnp.dot(
            jnp.where(mine, last_scaled, 0.0).astype(BF),
            cot_ref[:, cols],
            preferred_element_type=F32,
        )
    tail = tail.astype(BF)
    for e in range(experts):
        send_ref[e, 2 * QUARTERS * MAIN :, :] = tail[e * MAIN : (e + 1) * MAIN]


def expert_kernel(
    recv_ref, gate_ref, up_ref, down_ref, back_ref, x_ref, s_ref, dg_ref, du_ref, hid_ref
):
    experts, unused, width = recv_ref.shape
    main_rows = experts * MAIN
    tail = jnp.concatenate([recv_ref[i, 2 * QUARTERS * MAIN :, :] for i in range(experts)], axis=0)
    row = iota((4 * experts, main_rows), 0)
    col = iota((4 * experts, main_rows), 1)
    kind = (row >= 2 * experts).astype(jnp.int32)
    sender = jnp.right_shift(row - kind * 2 * experts, 1)
    base = sender * MAIN + kind * 8 + jnp.bitwise_and(row, 1) * 4
    for q in range(QUARTERS):
        cols = slice(q * width, (q + 1) * width)
        picked = jnp.dot(
            (col == base + q).astype(F32).astype(BF), tail, preferred_element_type=F32
        ).astype(BF)
        x_ref[main_rows:, cols] = picked[: 2 * experts]
        s_ref[main_rows:, cols] = picked[2 * experts :]
        for i in range(experts):
            here = slice(i * MAIN, (i + 1) * MAIN)
            x_ref[here, cols] = recv_ref[i, q * MAIN : (q + 1) * MAIN, :]
            s_ref[here, cols] = recv_ref[i, (QUARTERS + q) * MAIN : (QUARTERS + q + 1) * MAIN, :]
    rows = x_ref[...]
    gate_pre = jnp.dot(rows, gate_ref[...], preferred_element_type=F32)
    up_pre = jnp.dot(rows, up_ref[...], preferred_element_type=F32)
    hidden_grad = jnp.dot(s_ref[...], down_ref[...], preferred_element_type=F32)
    sig = jax.nn.sigmoid(gate_pre)
    activated = gate_pre * sig
    hidden = (activated * up_pre).astype(BF)
    slope = sig * (1.0 + gate_pre * (1.0 - sig))
    gate_delta = (hidden_grad * up_pre * slope).astype(BF)
    up_delta = (hidden_grad * activated).astype(BF)
    hid_ref[...] = hidden
    dg_ref[...] = gate_delta
    du_ref[...] = up_delta
    grad = (
        lax.dot_general(gate_delta, gate_ref[...], CONTRACT_COLS, preferred_element_type=F32)
        + lax.dot_general(up_delta, up_ref[...], CONTRACT_COLS, preferred_element_type=F32)
    ).astype(BF)
    product = hidden.astype(F32) * hidden_grad
    product = jnp.concatenate(
        [product, jnp.zeros((width - product.shape[0], product.shape[1]), F32)], axis=0
    )
    gate_lanes = lax.dot_general(
        jnp.ones((8, product.shape[1]), F32),
        product,
        CONTRACT_COLS,
        preferred_element_type=F32,
        precision=lax.Precision.HIGHEST,
    )
    trow = iota((main_rows, 2 * experts), 0)
    tcol = iota((main_rows, 2 * experts), 1)
    inner = jnp.bitwise_and(trow, MAIN - 1)
    source = jnp.right_shift(trow, 4) * 2 + jnp.right_shift(inner, 2)
    spread = jnp.zeros((main_rows, width), F32)
    for q in range(QUARTERS):
        cols = slice(q * width, (q + 1) * width)
        mine = jnp.logical_and(jnp.bitwise_and(inner, 3) == q, inner < 8)
        place = jnp.logical_and(mine, tcol == source).astype(F32).astype(BF)
        spread += jnp.dot(place, grad[main_rows:, cols], preferred_element_type=F32)
        for i in range(experts):
            back_ref[i, q * MAIN : (q + 1) * MAIN, :] = grad[i * MAIN : (i + 1) * MAIN, cols]
    for i in range(experts):
        back_ref[i, QUARTERS * MAIN :, :] = jnp.concatenate(
            [spread[i * MAIN : i * MAIN + 8], gate_lanes], axis=0
        ).astype(BF)


def grads_of(half, x_ref, s_ref, dg_ref, du_ref, hid_ref):
    rows = x_ref.shape[1] // 2
    cols = pl.ds(pl.multiple_of(half * rows, rows), rows)
    x_half = x_ref[:, cols]
    s_half = s_ref[:, cols]
    return (
        lax.dot_general(x_half, dg_ref[...], CONTRACT_ROWS, preferred_element_type=F32),
        lax.dot_general(x_half, du_ref[...], CONTRACT_ROWS, preferred_element_type=F32),
        lax.dot_general(s_half, hid_ref[...], CONTRACT_ROWS, preferred_element_type=F32),
    )


def other_half_kernel(member_ref, x_ref, s_ref, dg_ref, du_ref, hid_ref, out_ref):
    parts = grads_of(1 - member_ref[0], x_ref, s_ref, dg_ref, du_ref, hid_ref)
    rows = parts[0].shape[0]
    for n in range(3):
        out_ref[n * rows : (n + 1) * rows, :] = parts[n].astype(BF)


def own_half_kernel(
    member_ref, x_ref, s_ref, dg_ref, du_ref, hid_ref, came_ref, gate_ref, up_ref, down_ref
):
    parts = grads_of(member_ref[0], x_ref, s_ref, dg_ref, du_ref, hid_ref)
    rows = parts[0].shape[0]
    for n, out_ref in enumerate((gate_ref, up_ref, down_ref)):
        came = came_ref[n * rows : (n + 1) * rows, :].astype(F32)
        out_ref[...] = (parts[n].astype(BF).astype(F32) + came).astype(BF)


def combine_kernel(me_ref, ids_ref, slot_ref, gates_ref, ret_ref, token_ref, grad_ref):
    tokens, topk = ids_ref.shape
    experts, unused, width = ret_ref.shape
    eye = (iota((tokens, tokens), 0) == iota((tokens, tokens), 1)).astype(BF)
    ids = flip(ids_ref[...].astype(F32), eye).astype(jnp.int32)
    slot = slot_ref[...]
    slot16 = repeat_rows(slot, MAIN)
    lane_row = jnp.bitwise_and(iota(slot16.shape, 0), MAIN - 1)
    onehot = (slot16 == lane_row).astype(F32).astype(BF)
    wanted = MAIN + jnp.right_shift(lane_row, 2)
    last = jnp.where(jnp.logical_and(slot16 == wanted, lane_row < 8), 1.0, 0.0)
    tail = jnp.concatenate([ret_ref[e, QUARTERS * MAIN :, :] for e in range(experts)], axis=0)
    for q in range(QUARTERS):
        cols = slice(q * width, (q + 1) * width)
        main = jnp.concatenate(
            [ret_ref[e, q * MAIN : (q + 1) * MAIN, :] for e in range(experts)], axis=0
        )
        mine = jnp.bitwise_and(lane_row, 3) == q
        place = jnp.where(mine, last, 0.0).astype(BF)
        total = lax.dot_general(onehot, main, CONTRACT_ROWS, preferred_element_type=F32)
        total += lax.dot_general(place, tail, CONTRACT_ROWS, preferred_element_type=F32)
        token_ref[:, cols] = total.astype(BF)
    me = me_ref[0]
    lane = jnp.where(slot < MAIN, me * MAIN + slot, experts * MAIN + 2 * me + slot - MAIN)
    lane = jnp.where(slot < 0, -1, lane)
    lane_index = iota((width, tokens), 0)
    found = []
    for e in range(experts):
        pick = (lane_index == lane[e : e + 1]).astype(F32).astype(BF)
        mine = jnp.dot(ret_ref[e, QUARTERS * MAIN :, :], pick, preferred_element_type=F32)
        found.append(mine[8:9])
    found = jnp.concatenate(found, axis=0)
    kept = slot >= 0
    grads = jnp.where(kept, found / jnp.where(kept, gates_ref[...], 1.0), 0.0)
    expert_row = iota((experts, tokens), 0)
    by_choice = [
        jnp.sum(jnp.where(expert_row == ids[k : k + 1], grads, 0.0), axis=0, keepdims=True)
        for k in range(topk)
    ]
    by_choice = jnp.concatenate(by_choice, axis=0).astype(BF)
    grad_ref[...] = lax.dot_general(
        eye, by_choice, CONTRACT_COLS, preferred_element_type=F32
    ).astype(BF)


def local_call(kernel, outs, scalars, arrays, name, flops, moved):
    smem = pl.BlockSpec(memory_space=pltpu.SMEM)
    vmem = pl.BlockSpec(memory_space=pltpu.VMEM)
    return pl.pallas_call(
        kernel,
        out_shape=[jax.ShapeDtypeStruct(shape, kind) for shape, kind in outs],
        in_specs=[smem] * len(scalars) + [vmem] * len(arrays),
        out_specs=[vmem] * len(outs),
        compiler_params=pltpu.CompilerParams(vmem_limit_bytes=VMEM_LIMIT),
        cost_estimate=pl.CostEstimate(flops=flops, bytes_accessed=moved, transcendentals=0),
        name=name,
    )(*scalars, *arrays)


def per_device_moving_rows(
    tokens,
    cotangent,
    expert_ids,
    gate_values,
    replica_pick,
    replica_plan,
    gate_proj,
    up_proj,
    down_proj,
):
    experts = lax.axis_size("expert")
    token_count, model_width = tokens.shape
    topk = expert_ids.shape[1]
    hidden_width = gate_proj.shape[2]
    width = model_width // QUARTERS
    served = experts * (MAIN + 2)
    me = lax.axis_index("expert").reshape(1).astype(jnp.int32)
    member = lax.axis_index("replica").reshape(1).astype(jnp.int32)
    send, slot, gates = local_call(
        route_kernel,
        [
            ((experts, SEND_ROWS, width), BF),
            ((experts, token_count), jnp.int32),
            ((experts, token_count), F32),
        ],
        [replica_plan],
        [expert_ids, replica_pick, gate_values, tokens, cotangent],
        "route",
        2 * 2 * served * token_count * model_width,
        2 * 2 * (token_count + served) * model_width,
    )
    recv = lax.all_to_all(send, "expert", split_axis=0, concat_axis=0, tiled=True)
    matmul = 2 * served * model_width * hidden_width
    back, x_rows, s_rows, gate_delta, up_delta, hidden = local_call(
        expert_kernel,
        [
            ((experts, BACK_ROWS, width), BF),
            ((served, model_width), BF),
            ((served, model_width), BF),
            ((served, hidden_width), BF),
            ((served, hidden_width), BF),
            ((served, hidden_width), BF),
        ],
        [],
        [recv, gate_proj[0], up_proj[0], down_proj[0]],
        "expert_rows",
        5 * matmul,
        2 * 3 * model_width * hidden_width,
    )
    returned = lax.all_to_all(back, "expert", split_axis=0, concat_axis=0, tiled=True)
    half = model_width // 2
    (leaving,) = local_call(
        other_half_kernel,
        [((3 * half, hidden_width), BF)],
        [member],
        [x_rows, s_rows, gate_delta, up_delta, hidden],
        "other_half",
        3 * matmul // 2,
        2 * 3 * half * hidden_width,
    )
    came = lax.ppermute(leaving, "replica", [(0, 1), (1, 0)])
    shares = local_call(
        own_half_kernel,
        [((half, hidden_width), BF)] * 3,
        [member],
        [x_rows, s_rows, gate_delta, up_delta, hidden, came],
        "own_half",
        3 * matmul // 2,
        2 * 2 * 3 * half * hidden_width,
    )
    token_grad, gate_grad = local_call(
        combine_kernel,
        [((token_count, model_width), BF), ((token_count, topk), BF)],
        [me],
        [expert_ids, slot, gates, returned],
        "combine",
        2 * served * token_count * model_width,
        2 * 2 * token_count * model_width,
    )
    return (token_grad, gate_grad, shares[0][None], shares[1][None], shares[2][None])


def per_device(tokens, cotangent, expert_ids, gate_values, replica_pick, replica_plan, *matrices):
    experts = lax.axis_size("expert")
    slots = (copies_of(experts) + 1) * CAP
    row_bytes = 3 * 2 * tokens.shape[1] * experts
    matrix_bytes = 4 * sum(2 * m[0].size for m in matrices)
    fits = slots == MAIN + 2 and experts == 8 and lax.axis_size("replica") == 2
    rows_cheaper = slots * row_bytes < 2 * CAP * row_bytes + matrix_bytes
    plan = per_device_moving_rows if fits and rows_cheaper else per_device_moving_weights
    return plan(
        tokens, cotangent, expert_ids, gate_values, replica_pick, replica_plan, *matrices
    )


def solution(mesh):
    placed = (
        P(("parts", "expert", "replica"), None),
        P(("parts", "expert", "replica"), None),
        P(("parts", "expert", "replica"), None),
        P(("parts", "expert", "replica"), None),
        P(("parts", "expert", "replica"), None),
        P("parts"),
        P("expert", None, None),
        P("expert", None, None),
        P("expert", None, None),
    )
    return jax.shard_map(
        per_device,
        mesh=mesh,
        in_specs=placed,
        out_specs=(
            P(("parts", "expert", "replica"), None),
            P(("parts", "expert", "replica"), None),
            P(("parts", "expert"), "replica", None),
            P(("parts", "expert"), "replica", None),
            P(("parts", "expert"), "replica", None),
        ),
        check_vma=False,
    )
```

```python
import jax
import jax.numpy as jnp
from jax import lax
from jax.experimental import pallas as pl
from jax.experimental.pallas import tpu as pltpu
from jax.sharding import PartitionSpec as P

CAP = 6


def route_assignments(flat_ids, flat_pick, replica_plan, capacity):
    experts = replica_plan.shape[0]
    lane_ids = jnp.arange(experts, dtype=jnp.int32)
    same_plan = replica_plan[:, None] == replica_plan[None, :]
    earlier = lane_ids[None, :] < lane_ids[:, None]
    position = jnp.sum(jnp.logical_and(same_plan, earlier), axis=1)
    hot_mask = jnp.any(replica_plan[None, :] == lane_ids[:, None], axis=1)
    is_hot = jnp.any(
        jnp.logical_and(flat_ids[:, None] == lane_ids[None, :], hot_mask[None, :]), axis=1
    )
    use_copy = jnp.logical_and(is_hot, flat_pick >= 1)
    matches = jnp.logical_and(
        replica_plan[None, :] == flat_ids[:, None], position[None, :] == flat_pick[:, None] - 1
    )
    holder = jnp.sum(jnp.where(matches, lane_ids[None, :], 0), axis=1)
    target = jnp.where(use_copy, holder, flat_ids)
    copy_role = use_copy.astype(jnp.int32)
    bucket = target * 2 + copy_role
    sequence = jnp.arange(bucket.shape[0], dtype=jnp.int32)
    arrival = jnp.sum(
        jnp.logical_and(bucket[None, :] == bucket[:, None], sequence[None, :] < sequence[:, None]),
        axis=1,
    )
    kept_mask = arrival < capacity
    slot_index = target * (2 * capacity) + copy_role * capacity + jnp.minimum(arrival, capacity - 1)
    return (slot_index, kept_mask)


def fill_slots(slot_index, kept_mask, slot_count):
    slot_ids = jnp.arange(slot_count, dtype=jnp.int32)
    matches = jnp.logical_and(slot_index[None, :] == slot_ids[:, None], kept_mask[None, :])
    sequence = jnp.arange(slot_index.shape[0], dtype=jnp.int32)
    source = jnp.sum(jnp.where(matches, sequence[None, :], 0), axis=1)
    filled = jnp.any(matches, axis=1)
    return (source, filled)


def expert_backward(row_block, upstream, weight, gate_w, up_w, down_w):
    contract_cols = (((1,), (1,)), ((), ()))
    contract_rows = (((0,), (0,)), ((), ()))
    gate_pre = jnp.dot(row_block, gate_w, preferred_element_type=jnp.float32)
    up_pre = jnp.dot(row_block, up_w, preferred_element_type=jnp.float32)
    sigmoid_gate = jax.nn.sigmoid(gate_pre)
    activated = gate_pre * sigmoid_gate
    hidden = (activated * up_pre).astype(jnp.bfloat16)
    output_rows = lax.dot_general(hidden, down_w, contract_cols, preferred_element_type=jnp.float32)
    weight_col = weight.astype(jnp.float32)[:, None]
    upstream_f = upstream.astype(jnp.float32)
    gate_rows = jnp.sum(upstream_f * output_rows, axis=1)
    hidden_grad = weight_col * jnp.dot(upstream, down_w, preferred_element_type=jnp.float32)
    slope = sigmoid_gate * (1.0 + gate_pre * (1.0 - sigmoid_gate))
    gate_delta = (hidden_grad * up_pre * slope).astype(jnp.bfloat16)
    up_delta = (hidden_grad * activated).astype(jnp.bfloat16)
    input_grad = (
        lax.dot_general(gate_delta, gate_w, contract_cols, preferred_element_type=jnp.float32)
        + lax.dot_general(up_delta, up_w, contract_cols, preferred_element_type=jnp.float32)
    ).astype(jnp.bfloat16)
    scaled = (weight_col * upstream_f).astype(jnp.bfloat16)
    grad_set = (
        lax.dot_general(row_block, gate_delta, contract_rows, preferred_element_type=jnp.float32),
        lax.dot_general(row_block, up_delta, contract_rows, preferred_element_type=jnp.float32),
        lax.dot_general(scaled, hidden, contract_rows, preferred_element_type=jnp.float32),
    )
    return (input_grad, gate_rows, grad_set)


def per_device_moving_weights(
    tokens,
    cotangent,
    expert_ids,
    gate_values,
    replica_pick,
    replica_plan,
    gate_proj,
    up_proj,
    down_proj,
):
    experts = lax.axis_size("expert")
    capacity = CAP
    slot_total = 2 * capacity
    model_width = tokens.shape[1]
    topk = expert_ids.shape[1]
    token_count = tokens.shape[0]
    slot_index, kept_mask = route_assignments(
        expert_ids.reshape(-1), replica_pick.reshape(-1), replica_plan, capacity
    )
    source, filled = fill_slots(slot_index, kept_mask, experts * slot_total)
    token_of = source // topk
    zero_half = jnp.zeros((), jnp.bfloat16)
    send_rows = jnp.where(filled[:, None], jnp.take(tokens, token_of, axis=0), zero_half).reshape(
        experts, slot_total, model_width
    )
    send_upstream = jnp.where(
        filled[:, None], jnp.take(cotangent, token_of, axis=0), zero_half
    ).reshape(experts, slot_total, model_width)
    send_weight = jnp.where(filled, gate_values.reshape(-1)[source], zero_half).reshape(
        experts, slot_total
    )
    arrived = lax.all_to_all(send_rows, "expert", split_axis=0, concat_axis=0, tiled=True)
    own_gate = gate_proj[0]
    own_up = up_proj[0]
    own_down = down_proj[0]
    hidden_width = own_gate.shape[1]
    spread = (
        lax.all_to_all(
            own_gate.reshape(experts, -1), "expert", split_axis=0, concat_axis=0, tiled=True
        ),
        lax.all_to_all(
            own_up.reshape(experts, -1), "expert", split_axis=0, concat_axis=0, tiled=True
        ),
        lax.all_to_all(
            own_down.reshape(experts, -1), "expert", split_axis=0, concat_axis=0, tiled=True
        ),
    )
    chosen_gate = jnp.take(spread[0], replica_plan, axis=0)
    chosen_up = jnp.take(spread[1], replica_plan, axis=0)
    chosen_down = jnp.take(spread[2], replica_plan, axis=0)
    collected = (
        lax.all_to_all(chosen_gate, "expert", split_axis=0, concat_axis=0, tiled=True),
        lax.all_to_all(chosen_up, "expert", split_axis=0, concat_axis=0, tiled=True),
        lax.all_to_all(chosen_down, "expert", split_axis=0, concat_axis=0, tiled=True),
    )
    copy_gate = collected[0].reshape(model_width, hidden_width)
    copy_up = collected[1].reshape(model_width, hidden_width)
    copy_down = collected[2].reshape(model_width, hidden_width)
    arrived_up, arrived_weight = (
        lax.all_to_all(send_upstream, "expert", split_axis=0, concat_axis=0, tiled=True),
        lax.all_to_all(send_weight, "expert", split_axis=0, concat_axis=0, tiled=True),
    )
    owned_dx, owned_gate_rows, owned_grads = expert_backward(
        arrived[:, :capacity].reshape(-1, model_width),
        arrived_up[:, :capacity].reshape(-1, model_width),
        arrived_weight[:, :capacity].reshape(-1),
        own_gate,
        own_up,
        own_down,
    )
    copied_dx, copied_gate_rows, copied_grads = expert_backward(
        arrived[:, capacity:].reshape(-1, model_width),
        arrived_up[:, capacity:].reshape(-1, model_width),
        arrived_weight[:, capacity:].reshape(-1),
        copy_gate,
        copy_up,
        copy_down,
    )
    back_rows = jnp.concatenate(
        [
            owned_dx.reshape(experts, capacity, model_width),
            copied_dx.reshape(experts, capacity, model_width),
        ],
        axis=1,
    )
    back_gate = jnp.concatenate(
        [owned_gate_rows.reshape(experts, capacity), copied_gate_rows.reshape(experts, capacity)],
        axis=1,
    ).astype(jnp.bfloat16)
    returned, returned_gate = (
        lax.all_to_all(back_rows, "expert", split_axis=0, concat_axis=0, tiled=True),
        lax.all_to_all(back_gate, "expert", split_axis=0, concat_axis=0, tiled=True),
    )
    copy_pieces = (
        copied_grads[0].astype(jnp.bfloat16).reshape(experts, -1),
        copied_grads[1].astype(jnp.bfloat16).reshape(experts, -1),
        copied_grads[2].astype(jnp.bfloat16).reshape(experts, -1),
    )
    grad_spread = (
        lax.all_to_all(copy_pieces[0], "expert", split_axis=0, concat_axis=0, tiled=True),
        lax.all_to_all(copy_pieces[1], "expert", split_axis=0, concat_axis=0, tiled=True),
        lax.all_to_all(copy_pieces[2], "expert", split_axis=0, concat_axis=0, tiled=True),
    )
    lane_ids = jnp.arange(experts, dtype=jnp.int32)
    owner_map = (replica_plan[None, :] == lane_ids[:, None]).astype(jnp.bfloat16)
    summed_gate = jnp.dot(owner_map, grad_spread[0], preferred_element_type=jnp.float32).astype(
        jnp.bfloat16
    )
    summed_up = jnp.dot(owner_map, grad_spread[1], preferred_element_type=jnp.float32).astype(
        jnp.bfloat16
    )
    summed_down = jnp.dot(owner_map, grad_spread[2], preferred_element_type=jnp.float32).astype(
        jnp.bfloat16
    )
    grad_back = (
        lax.all_to_all(summed_gate, "expert", split_axis=0, concat_axis=0, tiled=True),
        lax.all_to_all(summed_up, "expert", split_axis=0, concat_axis=0, tiled=True),
        lax.all_to_all(summed_down, "expert", split_axis=0, concat_axis=0, tiled=True),
    )
    total_gate = owned_grads[0] + grad_back[0].reshape(model_width, hidden_width).astype(
        jnp.float32
    )
    total_up = owned_grads[1] + grad_back[1].reshape(model_width, hidden_width).astype(jnp.float32)
    total_down = owned_grads[2] + grad_back[2].reshape(model_width, hidden_width).astype(
        jnp.float32
    )
    shares = (
        lax.psum_scatter(
            total_gate.astype(jnp.bfloat16), "replica", scatter_dimension=0, tiled=True
        ).astype(jnp.float32),
        lax.psum_scatter(
            total_up.astype(jnp.bfloat16), "replica", scatter_dimension=0, tiled=True
        ).astype(jnp.float32),
        lax.psum_scatter(
            total_down.astype(jnp.bfloat16), "replica", scatter_dimension=0, tiled=True
        ).astype(jnp.float32),
    )
    flat_back = returned.reshape(experts * slot_total, model_width)
    picked_rows = jnp.take(flat_back, slot_index, axis=0)
    picked_rows = jnp.where(kept_mask[:, None], picked_rows, zero_half).astype(jnp.float32)
    token_grad = jnp.sum(picked_rows.reshape(token_count, topk, model_width), axis=1).astype(
        jnp.bfloat16
    )
    gate_grad = jnp.where(kept_mask, returned_gate.reshape(-1)[slot_index], zero_half).reshape(
        token_count, topk
    )
    return (
        token_grad,
        gate_grad,
        shares[0].astype(jnp.bfloat16)[None],
        shares[1].astype(jnp.bfloat16)[None],
        shares[2].astype(jnp.bfloat16)[None],
    )


BF = jnp.bfloat16
F32 = jnp.float32
CONTRACT_ROWS = (((0,), (0,)), ((), ()))
CONTRACT_COLS = (((1,), (1,)), ((), ()))
MIB = 1024 * 1024

MAIN = 16
QUARTERS = 4
SEND_ROWS = 2 * QUARTERS * MAIN + 16
BACK_ROWS = QUARTERS * MAIN + 16
FAR_FIRST = (4, 5, 6, 7, 1, 2, 3)


def copies_of(experts):
    return 2 if experts <= 8 else 8


def iota(shape, axis):
    return lax.broadcasted_iota(jnp.int32, shape, axis)


def mask(condition):
    return condition.astype(F32).astype(BF)


def repeat_rows(table, times):
    width = table.shape[1]
    return jnp.concatenate(
        [jnp.broadcast_to(table[e : e + 1], (times, width)) for e in range(table.shape[0])], axis=0
    )


def route_kernel(plan_hbm, ids_hbm, pick_hbm, gate_hbm, tok_hbm, cot_hbm, *refs):
    sems = refs[-1]
    plan_ref, ids_ref, pick_ref, gate_ref, tok_ref, cot_ref = refs[-7:-1]
    slot_ref, gates_ref = refs[-9:-7]
    send_refs = refs[:-9]
    topk, tokens = ids_ref.shape
    experts = len(send_refs)
    width = tok_ref.shape[1] // QUARTERS
    copies = copies_of(experts)
    loads = [
        pltpu.make_async_copy(source, place, sems.at[n])
        for n, (source, place) in enumerate(
            (
                (plan_hbm, plan_ref),
                (ids_hbm, ids_ref),
                (pick_hbm, pick_ref),
                (gate_hbm, gate_ref),
                (tok_hbm, tok_ref),
                (cot_hbm, cot_ref),
            )
        )
    ]
    for load in loads:
        load.start()
    before = mask(iota((tokens, tokens), 0) < iota((tokens, tokens), 1))
    me = lax.axis_index("expert")
    expert_row = jnp.bitwise_xor(iota((experts, tokens), 0), me)
    for load in loads[:4]:
        load.wait()
    ids = ids_ref[...]
    pick = pick_ref[...]
    gate = gate_ref[...].astype(F32)
    named = jnp.zeros((experts, tokens), jnp.int32)
    gates = jnp.zeros((experts, tokens), F32)
    for k in range(topk):
        hit = ids[k : k + 1] == expert_row
        named = jnp.where(hit, pick[k : k + 1] + 1, named)
        gates = jnp.where(hit, gate[k : k + 1], gates)
    hot = jnp.zeros((experts, tokens), jnp.int32)
    for j in range(experts):
        hot = jnp.where(expert_row == plan_ref[j], 1, hot)
    chosen = jnp.where(named == 0, -1, jnp.where(hot > 0, named - 1, 0))
    masks = jnp.concatenate([(chosen == c).astype(F32) for c in range(copies + 1)], axis=0)
    rank = jnp.dot(masks.astype(BF), before, preferred_element_type=F32).astype(jnp.int32)
    slot = jnp.full((experts, tokens), -1, jnp.int32)
    for c in range(copies + 1):
        rank_c = rank[c * experts : (c + 1) * experts]
        keep = jnp.logical_and(chosen == c, rank_c < CAP)
        slot = jnp.where(keep, c * CAP + rank_c, slot)
    slot_ref[...] = slot
    gates_ref[...] = gates
    slot16 = repeat_rows(slot, MAIN)
    gate16 = repeat_rows(gates, MAIN)
    inner = jnp.bitwise_and(iota(slot16.shape, 0), MAIN - 1)
    onehot = (slot16 == inner).astype(F32)
    wanted = MAIN + jnp.bitwise_and(jnp.right_shift(inner, 2), 1)
    last = (slot16 == wanted).astype(F32)
    last_rows = jnp.where(inner >= 8, 0.0, last)
    last_scaled = jnp.where(inner >= 8, last * gate16, 0.0)
    quarter = jnp.bitwise_and(inner, 3)
    for load in loads[4:]:
        load.wait()
    rows = jnp.dot(onehot.astype(BF), tok_ref[...], preferred_element_type=F32).astype(BF)
    scaled = jnp.dot(
        (onehot * gate16).astype(BF), cot_ref[...], preferred_element_type=F32
    ).astype(BF)
    tail = jnp.zeros((experts * MAIN, width), F32)
    for q in range(QUARTERS):
        cols = slice(q * width, (q + 1) * width)
        mine = quarter == q
        tail += jnp.dot(
            jnp.where(mine, last_rows, 0.0).astype(BF), tok_ref[:, cols], preferred_element_type=F32
        )
        tail += jnp.dot(
            jnp.where(mine, last_scaled, 0.0).astype(BF),
            cot_ref[:, cols],
            preferred_element_type=F32,
        )
    tail = tail.astype(BF)
    for k in range(experts):
        here = slice(k * MAIN, (k + 1) * MAIN)
        for q in range(QUARTERS):
            cols = slice(q * width, (q + 1) * width)
            send_refs[k][q * MAIN : (q + 1) * MAIN, :] = rows[here, cols]
            send_refs[k][(QUARTERS + q) * MAIN : (QUARTERS + q + 1) * MAIN, :] = scaled[here, cols]
        send_refs[k][2 * QUARTERS * MAIN :, :] = tail[here]


def expert_kernel(*refs):
    back_count = len(refs) - 8
    experts = back_count // 2
    recv_refs = refs[:experts]
    gate_ref, up_ref, down_ref = refs[experts : experts + 3]
    back_refs = refs[experts + 3 : 2 * experts + 3]
    x_ref, s_ref, dg_ref, du_ref, hid_ref = refs[2 * experts + 3 :]
    width = recv_refs[0].shape[1]
    main_rows = experts * MAIN
    tail = jnp.concatenate([ref[2 * QUARTERS * MAIN :, :] for ref in recv_refs], axis=0)
    row = iota((4 * experts, main_rows), 0)
    col = iota((4 * experts, main_rows), 1)
    kind = (row >= 2 * experts).astype(jnp.int32)
    chunk = jnp.right_shift(row - kind * 2 * experts, 1)
    base = chunk * MAIN + kind * 8 + jnp.bitwise_and(row, 1) * 4
    for q in range(QUARTERS):
        cols = slice(q * width, (q + 1) * width)
        picked = jnp.dot(mask(col == base + q), tail, preferred_element_type=F32).astype(BF)
        x_ref[main_rows:, cols] = picked[: 2 * experts]
        s_ref[main_rows:, cols] = picked[2 * experts :]
        for i, ref in enumerate(recv_refs):
            here = slice(i * MAIN, (i + 1) * MAIN)
            x_ref[here, cols] = ref[q * MAIN : (q + 1) * MAIN, :]
            s_ref[here, cols] = ref[(QUARTERS + q) * MAIN : (QUARTERS + q + 1) * MAIN, :]
    rows = x_ref[...]
    gate_pre = jnp.dot(rows, gate_ref[...], preferred_element_type=F32)
    up_pre = jnp.dot(rows, up_ref[...], preferred_element_type=F32)
    hidden_grad = jnp.dot(s_ref[...], down_ref[...], preferred_element_type=F32)
    sig = jax.nn.sigmoid(gate_pre)
    activated = gate_pre * sig
    hidden = (activated * up_pre).astype(BF)
    slope = sig * (1.0 + gate_pre * (1.0 - sig))
    gate_delta = (hidden_grad * up_pre * slope).astype(BF)
    up_delta = (hidden_grad * activated).astype(BF)
    hid_ref[...] = hidden
    dg_ref[...] = gate_delta
    du_ref[...] = up_delta
    grad = (
        lax.dot_general(gate_delta, gate_ref[...], CONTRACT_COLS, preferred_element_type=F32)
        + lax.dot_general(up_delta, up_ref[...], CONTRACT_COLS, preferred_element_type=F32)
    ).astype(BF)
    product = hidden.astype(F32) * hidden_grad
    product = jnp.concatenate(
        [product, jnp.zeros((width - product.shape[0], product.shape[1]), F32)], axis=0
    )
    gate_lanes = lax.dot_general(
        jnp.ones((8, product.shape[1]), F32),
        product,
        CONTRACT_COLS,
        preferred_element_type=F32,
        precision=lax.Precision.HIGHEST,
    )
    trow = iota((main_rows, 2 * experts), 0)
    tcol = iota((main_rows, 2 * experts), 1)
    inner = jnp.bitwise_and(trow, MAIN - 1)
    source = jnp.right_shift(trow, 4) * 2 + jnp.right_shift(inner, 2)
    spread = jnp.zeros((main_rows, width), F32)
    for q in range(QUARTERS):
        cols = slice(q * width, (q + 1) * width)
        mine = jnp.logical_and(jnp.bitwise_and(inner, 3) == q, inner < 8)
        place = mask(jnp.logical_and(mine, tcol == source))
        spread += jnp.dot(place, grad[main_rows:, cols], preferred_element_type=F32)
        for i, ref in enumerate(back_refs):
            ref[q * MAIN : (q + 1) * MAIN, :] = grad[i * MAIN : (i + 1) * MAIN, cols]
    for i, ref in enumerate(back_refs):
        ref[QUARTERS * MAIN :, :] = jnp.concatenate(
            [spread[i * MAIN : i * MAIN + 8], gate_lanes], axis=0
        ).astype(BF)


def grads_of(half, x_ref, s_ref, dg_ref, du_ref, hid_ref):
    rows = x_ref.shape[1] // 2
    cols = pl.ds(pl.multiple_of(half * rows, rows), rows)
    x_half = x_ref[:, cols]
    s_half = s_ref[:, cols]
    return (
        lax.dot_general(x_half, dg_ref[...], CONTRACT_ROWS, preferred_element_type=F32),
        lax.dot_general(x_half, du_ref[...], CONTRACT_ROWS, preferred_element_type=F32),
        lax.dot_general(s_half, hid_ref[...], CONTRACT_ROWS, preferred_element_type=F32),
    )


def other_half_kernel(x_ref, s_ref, dg_ref, du_ref, hid_ref, out_ref):
    half = 1 - lax.axis_index("replica")
    parts = grads_of(half, x_ref, s_ref, dg_ref, du_ref, hid_ref)
    rows = parts[0].shape[0]
    for n in range(3):
        out_ref[n * rows : (n + 1) * rows, :] = parts[n].astype(BF)


def own_half_kernel(
    x_ref, s_ref, dg_ref, du_ref, hid_ref, came_ref, gate_ref, up_ref, down_ref
):
    parts = grads_of(lax.axis_index("replica"), x_ref, s_ref, dg_ref, du_ref, hid_ref)
    rows = parts[0].shape[0]
    for n, out_ref in enumerate((gate_ref, up_ref, down_ref)):
        came = came_ref[n * rows : (n + 1) * rows, :].astype(F32)
        out_ref[...] = (parts[n].astype(BF).astype(F32) + came).astype(BF)


def combine_kernel(ids_ref, slot_ref, gates_ref, *refs):
    token_ref, grad_ref = refs[-2:]
    ret_refs = refs[:-2]
    topk, tokens = ids_ref.shape
    experts = len(ret_refs)
    width = ret_refs[0].shape[1]
    ids = ids_ref[...]
    slot = slot_ref[...]
    slot16 = repeat_rows(slot, MAIN)
    inner = jnp.bitwise_and(iota(slot16.shape, 0), MAIN - 1)
    onehot = mask(slot16 == inner)
    wanted = MAIN + jnp.right_shift(inner, 2)
    last = jnp.where(jnp.logical_and(slot16 == wanted, inner < 8), 1.0, 0.0)
    quarter = jnp.bitwise_and(inner, 3)
    tail = jnp.concatenate([ref[QUARTERS * MAIN :, :] for ref in ret_refs], axis=0)
    for q in range(QUARTERS):
        main = jnp.concatenate([ref[q * MAIN : (q + 1) * MAIN, :] for ref in ret_refs], axis=0)
        place = jnp.where(quarter == q, last, 0.0).astype(BF)
        total = lax.dot_general(onehot, main, CONTRACT_ROWS, preferred_element_type=F32)
        total += lax.dot_general(place, tail, CONTRACT_ROWS, preferred_element_type=F32)
        token_ref[:, q * width : (q + 1) * width] = total.astype(BF)
    lane_index = iota((width, tokens), 0)
    found = []
    for k, ref in enumerate(ret_refs):
        mine = slot[k : k + 1]
        lane = jnp.where(mine < MAIN, k * MAIN + mine, experts * MAIN + 2 * k + mine - MAIN)
        lane = jnp.where(mine < 0, -1, lane)
        sums = jnp.dot(
            ref[QUARTERS * MAIN :, :], mask(lane_index == lane), preferred_element_type=F32
        )
        found.append(sums[8:9])
    found = jnp.concatenate(found, axis=0)
    kept = slot >= 0
    grads = jnp.where(kept, found / jnp.where(kept, gates_ref[...], 1.0), 0.0)
    expert_row = jnp.bitwise_xor(iota((experts, tokens), 0), lax.axis_index("expert"))
    by_choice = [
        jnp.sum(jnp.where(expert_row == ids[k : k + 1], grads, 0.0), axis=0, keepdims=True)
        for k in range(topk)
    ]
    grad_ref[...] = jnp.concatenate(by_choice, axis=0).astype(BF)


def local_call(kernel, outs, arrays, name, flops, moved, space=pltpu.VMEM, scratch=(), limit=16):
    vmem = pl.BlockSpec(memory_space=pltpu.VMEM)
    return pl.pallas_call(
        kernel,
        out_shape=[jax.ShapeDtypeStruct(shape, kind) for shape, kind in outs],
        in_specs=[pl.BlockSpec(memory_space=space)] * len(arrays),
        out_specs=[vmem] * len(outs),
        scratch_shapes=list(scratch),
        compiler_params=pltpu.CompilerParams(vmem_limit_bytes=limit * MIB),
        cost_estimate=pl.CostEstimate(flops=flops, bytes_accessed=moved, transcendentals=0),
        name=name,
    )(*arrays)


def exchange(chunks):
    count = len(chunks)
    came = list(chunks)
    for k in FAR_FIRST:
        came[k] = lax.ppermute(chunks[k], "expert", [(i, i ^ k) for i in range(count)])
    return came


def per_device_moving_rows(
    tokens,
    cotangent,
    expert_ids,
    gate_values,
    replica_pick,
    replica_plan,
    gate_proj,
    up_proj,
    down_proj,
):
    experts = lax.axis_size("expert")
    token_count, model_width = tokens.shape
    topk = expert_ids.shape[1]
    hidden_width = gate_proj.shape[2]
    width = model_width // QUARTERS
    served = experts * (MAIN + 2)
    small = (topk, token_count)
    routed = local_call(
        route_kernel,
        [((SEND_ROWS, width), BF)] * experts
        + [((experts, token_count), jnp.int32), ((experts, token_count), F32)],
        [replica_plan, expert_ids.T, replica_pick.T, gate_values.T, tokens, cotangent],
        "route",
        2 * 2 * served * token_count * model_width,
        2 * 2 * (token_count + served) * model_width,
        space=pltpu.HBM,
        limit=58,
        scratch=[
            pltpu.SMEM((experts,), jnp.int32),
            pltpu.VMEM(small, jnp.int32),
            pltpu.VMEM(small, jnp.int32),
            pltpu.VMEM(small, BF),
            pltpu.VMEM(tokens.shape, BF),
            pltpu.VMEM(tokens.shape, BF),
            pltpu.SemaphoreType.DMA((6,)),
        ],
    )
    slot, gates = routed[experts:]
    recv = exchange(routed[:experts])
    matmul = 2 * served * model_width * hidden_width
    outs = local_call(
        expert_kernel,
        [((BACK_ROWS, width), BF)] * experts
        + [((served, model_width), BF)] * 2
        + [((served, hidden_width), BF)] * 3,
        [*recv, gate_proj[0], up_proj[0], down_proj[0]],
        "expert_rows",
        5 * matmul,
        2 * 3 * model_width * hidden_width,
    )
    factors = outs[experts:]
    returned = exchange(outs[:experts])
    half = model_width // 2
    (leaving,) = local_call(
        other_half_kernel,
        [((3 * half, hidden_width), BF)],
        factors,
        "other_half",
        3 * matmul // 2,
        2 * 3 * half * hidden_width,
    )
    came = lax.ppermute(leaving, "replica", [(0, 1), (1, 0)])
    shares = local_call(
        own_half_kernel,
        [((half, hidden_width), BF)] * 3,
        [*factors, came],
        "own_half",
        3 * matmul // 2,
        2 * 2 * 3 * half * hidden_width,
    )
    returned, shares = lax.optimization_barrier((returned, shares))
    token_grad, gate_grad = local_call(
        combine_kernel,
        [((token_count, model_width), BF), ((topk, token_count), BF)],
        [expert_ids.T, slot, gates, *returned],
        "combine",
        2 * served * token_count * model_width,
        2 * 2 * token_count * model_width,
    )
    return (token_grad, gate_grad.T, shares[0][None], shares[1][None], shares[2][None])


def per_device(tokens, cotangent, expert_ids, gate_values, replica_pick, replica_plan, *matrices):
    experts = lax.axis_size("expert")
    slots = (copies_of(experts) + 1) * CAP
    row_bytes = 3 * 2 * tokens.shape[1] * experts
    matrix_bytes = 4 * sum(2 * m[0].size for m in matrices)
    fits = slots == MAIN + 2 and experts == 8 and lax.axis_size("replica") == 2
    rows_cheaper = slots * row_bytes < 2 * CAP * row_bytes + matrix_bytes
    plan = per_device_moving_rows if fits and rows_cheaper else per_device_moving_weights
    return plan(
        tokens, cotangent, expert_ids, gate_values, replica_pick, replica_plan, *matrices
    )


def solution(mesh):
    placed = (
        P(("parts", "expert", "replica"), None),
        P(("parts", "expert", "replica"), None),
        P(("parts", "expert", "replica"), None),
        P(("parts", "expert", "replica"), None),
        P(("parts", "expert", "replica"), None),
        P("parts"),
        P("expert", None, None),
        P("expert", None, None),
        P("expert", None, None),
    )
    return jax.shard_map(
        per_device,
        mesh=mesh,
        in_specs=placed,
        out_specs=(
            P(("parts", "expert", "replica"), None),
            P(("parts", "expert", "replica"), None),
            P(("parts", "expert"), "replica", None),
            P(("parts", "expert"), "replica", None),
            P(("parts", "expert"), "replica", None),
        ),
        check_vma=False,
    )
```

```python
import jax
import jax.numpy as jnp
from jax import lax
from jax.experimental import pallas as pl
from jax.experimental.pallas import tpu as pltpu
from jax.sharding import PartitionSpec as P

CAP = 6


def route_assignments(flat_ids, flat_pick, replica_plan, capacity):
    experts = replica_plan.shape[0]
    lane_ids = jnp.arange(experts, dtype=jnp.int32)
    same_plan = replica_plan[:, None] == replica_plan[None, :]
    earlier = lane_ids[None, :] < lane_ids[:, None]
    position = jnp.sum(jnp.logical_and(same_plan, earlier), axis=1)
    hot_mask = jnp.any(replica_plan[None, :] == lane_ids[:, None], axis=1)
    is_hot = jnp.any(
        jnp.logical_and(flat_ids[:, None] == lane_ids[None, :], hot_mask[None, :]), axis=1
    )
    use_copy = jnp.logical_and(is_hot, flat_pick >= 1)
    matches = jnp.logical_and(
        replica_plan[None, :] == flat_ids[:, None], position[None, :] == flat_pick[:, None] - 1
    )
    holder = jnp.sum(jnp.where(matches, lane_ids[None, :], 0), axis=1)
    target = jnp.where(use_copy, holder, flat_ids)
    copy_role = use_copy.astype(jnp.int32)
    bucket = target * 2 + copy_role
    sequence = jnp.arange(bucket.shape[0], dtype=jnp.int32)
    arrival = jnp.sum(
        jnp.logical_and(bucket[None, :] == bucket[:, None], sequence[None, :] < sequence[:, None]),
        axis=1,
    )
    kept_mask = arrival < capacity
    slot_index = target * (2 * capacity) + copy_role * capacity + jnp.minimum(arrival, capacity - 1)
    return (slot_index, kept_mask)


def fill_slots(slot_index, kept_mask, slot_count):
    slot_ids = jnp.arange(slot_count, dtype=jnp.int32)
    matches = jnp.logical_and(slot_index[None, :] == slot_ids[:, None], kept_mask[None, :])
    sequence = jnp.arange(slot_index.shape[0], dtype=jnp.int32)
    source = jnp.sum(jnp.where(matches, sequence[None, :], 0), axis=1)
    filled = jnp.any(matches, axis=1)
    return (source, filled)


def expert_backward(row_block, upstream, weight, gate_w, up_w, down_w):
    contract_cols = (((1,), (1,)), ((), ()))
    contract_rows = (((0,), (0,)), ((), ()))
    gate_pre = jnp.dot(row_block, gate_w, preferred_element_type=jnp.float32)
    up_pre = jnp.dot(row_block, up_w, preferred_element_type=jnp.float32)
    sigmoid_gate = jax.nn.sigmoid(gate_pre)
    activated = gate_pre * sigmoid_gate
    hidden = (activated * up_pre).astype(jnp.bfloat16)
    output_rows = lax.dot_general(hidden, down_w, contract_cols, preferred_element_type=jnp.float32)
    weight_col = weight.astype(jnp.float32)[:, None]
    upstream_f = upstream.astype(jnp.float32)
    gate_rows = jnp.sum(upstream_f * output_rows, axis=1)
    hidden_grad = weight_col * jnp.dot(upstream, down_w, preferred_element_type=jnp.float32)
    slope = sigmoid_gate * (1.0 + gate_pre * (1.0 - sigmoid_gate))
    gate_delta = (hidden_grad * up_pre * slope).astype(jnp.bfloat16)
    up_delta = (hidden_grad * activated).astype(jnp.bfloat16)
    input_grad = (
        lax.dot_general(gate_delta, gate_w, contract_cols, preferred_element_type=jnp.float32)
        + lax.dot_general(up_delta, up_w, contract_cols, preferred_element_type=jnp.float32)
    ).astype(jnp.bfloat16)
    scaled = (weight_col * upstream_f).astype(jnp.bfloat16)
    grad_set = (
        lax.dot_general(row_block, gate_delta, contract_rows, preferred_element_type=jnp.float32),
        lax.dot_general(row_block, up_delta, contract_rows, preferred_element_type=jnp.float32),
        lax.dot_general(scaled, hidden, contract_rows, preferred_element_type=jnp.float32),
    )
    return (input_grad, gate_rows, grad_set)


def per_device_moving_weights(
    tokens,
    cotangent,
    expert_ids,
    gate_values,
    replica_pick,
    replica_plan,
    gate_proj,
    up_proj,
    down_proj,
):
    experts = lax.axis_size("expert")
    capacity = CAP
    slot_total = 2 * capacity
    model_width = tokens.shape[1]
    topk = expert_ids.shape[1]
    token_count = tokens.shape[0]
    slot_index, kept_mask = route_assignments(
        expert_ids.reshape(-1), replica_pick.reshape(-1), replica_plan, capacity
    )
    source, filled = fill_slots(slot_index, kept_mask, experts * slot_total)
    token_of = source // topk
    zero_half = jnp.zeros((), jnp.bfloat16)
    send_rows = jnp.where(filled[:, None], jnp.take(tokens, token_of, axis=0), zero_half).reshape(
        experts, slot_total, model_width
    )
    send_upstream = jnp.where(
        filled[:, None], jnp.take(cotangent, token_of, axis=0), zero_half
    ).reshape(experts, slot_total, model_width)
    send_weight = jnp.where(filled, gate_values.reshape(-1)[source], zero_half).reshape(
        experts, slot_total
    )
    arrived = lax.all_to_all(send_rows, "expert", split_axis=0, concat_axis=0, tiled=True)
    own_gate = gate_proj[0]
    own_up = up_proj[0]
    own_down = down_proj[0]
    hidden_width = own_gate.shape[1]
    spread = (
        lax.all_to_all(
            own_gate.reshape(experts, -1), "expert", split_axis=0, concat_axis=0, tiled=True
        ),
        lax.all_to_all(
            own_up.reshape(experts, -1), "expert", split_axis=0, concat_axis=0, tiled=True
        ),
        lax.all_to_all(
            own_down.reshape(experts, -1), "expert", split_axis=0, concat_axis=0, tiled=True
        ),
    )
    chosen_gate = jnp.take(spread[0], replica_plan, axis=0)
    chosen_up = jnp.take(spread[1], replica_plan, axis=0)
    chosen_down = jnp.take(spread[2], replica_plan, axis=0)
    collected = (
        lax.all_to_all(chosen_gate, "expert", split_axis=0, concat_axis=0, tiled=True),
        lax.all_to_all(chosen_up, "expert", split_axis=0, concat_axis=0, tiled=True),
        lax.all_to_all(chosen_down, "expert", split_axis=0, concat_axis=0, tiled=True),
    )
    copy_gate = collected[0].reshape(model_width, hidden_width)
    copy_up = collected[1].reshape(model_width, hidden_width)
    copy_down = collected[2].reshape(model_width, hidden_width)
    arrived_up, arrived_weight = (
        lax.all_to_all(send_upstream, "expert", split_axis=0, concat_axis=0, tiled=True),
        lax.all_to_all(send_weight, "expert", split_axis=0, concat_axis=0, tiled=True),
    )
    owned_dx, owned_gate_rows, owned_grads = expert_backward(
        arrived[:, :capacity].reshape(-1, model_width),
        arrived_up[:, :capacity].reshape(-1, model_width),
        arrived_weight[:, :capacity].reshape(-1),
        own_gate,
        own_up,
        own_down,
    )
    copied_dx, copied_gate_rows, copied_grads = expert_backward(
        arrived[:, capacity:].reshape(-1, model_width),
        arrived_up[:, capacity:].reshape(-1, model_width),
        arrived_weight[:, capacity:].reshape(-1),
        copy_gate,
        copy_up,
        copy_down,
    )
    back_rows = jnp.concatenate(
        [
            owned_dx.reshape(experts, capacity, model_width),
            copied_dx.reshape(experts, capacity, model_width),
        ],
        axis=1,
    )
    back_gate = jnp.concatenate(
        [owned_gate_rows.reshape(experts, capacity), copied_gate_rows.reshape(experts, capacity)],
        axis=1,
    ).astype(jnp.bfloat16)
    returned, returned_gate = (
        lax.all_to_all(back_rows, "expert", split_axis=0, concat_axis=0, tiled=True),
        lax.all_to_all(back_gate, "expert", split_axis=0, concat_axis=0, tiled=True),
    )
    copy_pieces = (
        copied_grads[0].astype(jnp.bfloat16).reshape(experts, -1),
        copied_grads[1].astype(jnp.bfloat16).reshape(experts, -1),
        copied_grads[2].astype(jnp.bfloat16).reshape(experts, -1),
    )
    grad_spread = (
        lax.all_to_all(copy_pieces[0], "expert", split_axis=0, concat_axis=0, tiled=True),
        lax.all_to_all(copy_pieces[1], "expert", split_axis=0, concat_axis=0, tiled=True),
        lax.all_to_all(copy_pieces[2], "expert", split_axis=0, concat_axis=0, tiled=True),
    )
    lane_ids = jnp.arange(experts, dtype=jnp.int32)
    owner_map = (replica_plan[None, :] == lane_ids[:, None]).astype(jnp.bfloat16)
    summed_gate = jnp.dot(owner_map, grad_spread[0], preferred_element_type=jnp.float32).astype(
        jnp.bfloat16
    )
    summed_up = jnp.dot(owner_map, grad_spread[1], preferred_element_type=jnp.float32).astype(
        jnp.bfloat16
    )
    summed_down = jnp.dot(owner_map, grad_spread[2], preferred_element_type=jnp.float32).astype(
        jnp.bfloat16
    )
    grad_back = (
        lax.all_to_all(summed_gate, "expert", split_axis=0, concat_axis=0, tiled=True),
        lax.all_to_all(summed_up, "expert", split_axis=0, concat_axis=0, tiled=True),
        lax.all_to_all(summed_down, "expert", split_axis=0, concat_axis=0, tiled=True),
    )
    total_gate = owned_grads[0] + grad_back[0].reshape(model_width, hidden_width).astype(
        jnp.float32
    )
    total_up = owned_grads[1] + grad_back[1].reshape(model_width, hidden_width).astype(jnp.float32)
    total_down = owned_grads[2] + grad_back[2].reshape(model_width, hidden_width).astype(
        jnp.float32
    )
    shares = (
        lax.psum_scatter(
            total_gate.astype(jnp.bfloat16), "replica", scatter_dimension=0, tiled=True
        ).astype(jnp.float32),
        lax.psum_scatter(
            total_up.astype(jnp.bfloat16), "replica", scatter_dimension=0, tiled=True
        ).astype(jnp.float32),
        lax.psum_scatter(
            total_down.astype(jnp.bfloat16), "replica", scatter_dimension=0, tiled=True
        ).astype(jnp.float32),
    )
    flat_back = returned.reshape(experts * slot_total, model_width)
    picked_rows = jnp.take(flat_back, slot_index, axis=0)
    picked_rows = jnp.where(kept_mask[:, None], picked_rows, zero_half).astype(jnp.float32)
    token_grad = jnp.sum(picked_rows.reshape(token_count, topk, model_width), axis=1).astype(
        jnp.bfloat16
    )
    gate_grad = jnp.where(kept_mask, returned_gate.reshape(-1)[slot_index], zero_half).reshape(
        token_count, topk
    )
    return (
        token_grad,
        gate_grad,
        shares[0].astype(jnp.bfloat16)[None],
        shares[1].astype(jnp.bfloat16)[None],
        shares[2].astype(jnp.bfloat16)[None],
    )


BF = jnp.bfloat16
F32 = jnp.float32
CONTRACT_ROWS = (((0,), (0,)), ((), ()))
CONTRACT_COLS = (((1,), (1,)), ((), ()))
MIB = 1024 * 1024

MAIN = 16
QUARTERS = 4
SEND_ROWS = 2 * QUARTERS * MAIN + 16
BACK_ROWS = QUARTERS * MAIN + 16
STEPS = (0, 1, 4, 5, 6, 7, 2, 3)


def copies_of(experts):
    return 2 if experts <= 8 else 8


def iota(shape, axis):
    return lax.broadcasted_iota(jnp.int32, shape, axis)


def partners(experts, tokens):
    row = iota((experts, tokens), 0)
    step = jnp.zeros((experts, tokens), jnp.int32)
    for c in range(1, experts):
        step = jnp.where(row == c, STEPS[c], step)
    return jnp.bitwise_xor(step, lax.axis_index("expert"))


def mask(condition):
    return condition.astype(F32).astype(BF)


def repeat_rows(table, times):
    width = table.shape[1]
    return jnp.concatenate(
        [jnp.broadcast_to(table[e : e + 1], (times, width)) for e in range(table.shape[0])], axis=0
    )


def route_kernel(plan_hbm, ids_hbm, pick_hbm, gate_hbm, tok_hbm, cot_hbm, *refs):
    sems = refs[-1]
    plan_ref, ids_ref, pick_ref, gate_ref, tok_ref, cot_ref = refs[-7:-1]
    slot_ref, gates_ref = refs[-9:-7]
    send_refs = refs[:-9]
    topk, tokens = ids_ref.shape
    experts = len(send_refs)
    width = tok_ref.shape[1] // QUARTERS
    copies = copies_of(experts)
    loads = [
        pltpu.make_async_copy(source, place, sems.at[n])
        for n, (source, place) in enumerate(
            (
                (plan_hbm, plan_ref),
                (ids_hbm, ids_ref),
                (pick_hbm, pick_ref),
                (gate_hbm, gate_ref),
                (tok_hbm, tok_ref),
                (cot_hbm, cot_ref),
            )
        )
    ]
    for load in loads:
        load.start()
    before = mask(iota((tokens, tokens), 0) < iota((tokens, tokens), 1))
    expert_row = partners(experts, tokens)
    for load in loads[:4]:
        load.wait()
    ids = ids_ref[...]
    pick = pick_ref[...]
    gate = gate_ref[...].astype(F32)
    named = jnp.zeros((experts, tokens), jnp.int32)
    gates = jnp.zeros((experts, tokens), F32)
    for k in range(topk):
        hit = ids[k : k + 1] == expert_row
        named = jnp.where(hit, pick[k : k + 1] + 1, named)
        gates = jnp.where(hit, gate[k : k + 1], gates)
    hot = jnp.zeros((experts, tokens), jnp.int32)
    for j in range(experts):
        hot = jnp.where(expert_row == plan_ref[j], 1, hot)
    chosen = jnp.where(named == 0, -1, jnp.where(hot > 0, named - 1, 0))
    masks = jnp.concatenate([(chosen == c).astype(F32) for c in range(copies + 1)], axis=0)
    rank = jnp.dot(masks.astype(BF), before, preferred_element_type=F32).astype(jnp.int32)
    slot = jnp.full((experts, tokens), -1, jnp.int32)
    for c in range(copies + 1):
        rank_c = rank[c * experts : (c + 1) * experts]
        keep = jnp.logical_and(chosen == c, rank_c < CAP)
        slot = jnp.where(keep, c * CAP + rank_c, slot)
    slot_ref[...] = slot
    gates_ref[...] = gates
    slot16 = repeat_rows(slot, MAIN)
    gate16 = repeat_rows(gates, MAIN)
    inner = jnp.bitwise_and(iota(slot16.shape, 0), MAIN - 1)
    onehot = (slot16 == inner).astype(F32)
    wanted = MAIN + jnp.bitwise_and(jnp.right_shift(inner, 2), 1)
    last = (slot16 == wanted).astype(F32)
    last_rows = jnp.where(inner >= 8, 0.0, last)
    last_scaled = jnp.where(inner >= 8, last * gate16, 0.0)
    quarter = jnp.bitwise_and(inner, 3)
    for load in loads[4:]:
        load.wait()
    rows = jnp.dot(onehot.astype(BF), tok_ref[...], preferred_element_type=F32).astype(BF)
    scaled = jnp.dot(
        (onehot * gate16).astype(BF), cot_ref[...], preferred_element_type=F32
    ).astype(BF)
    tail = jnp.zeros((experts * MAIN, width), F32)
    for q in range(QUARTERS):
        cols = slice(q * width, (q + 1) * width)
        mine = quarter == q
        tail += jnp.dot(
            jnp.where(mine, last_rows, 0.0).astype(BF), tok_ref[:, cols], preferred_element_type=F32
        )
        tail += jnp.dot(
            jnp.where(mine, last_scaled, 0.0).astype(BF),
            cot_ref[:, cols],
            preferred_element_type=F32,
        )
    tail = tail.astype(BF)
    for k in range(experts):
        here = slice(k * MAIN, (k + 1) * MAIN)
        for q in range(QUARTERS):
            cols = slice(q * width, (q + 1) * width)
            send_refs[k][q * MAIN : (q + 1) * MAIN, :] = rows[here, cols]
            send_refs[k][(QUARTERS + q) * MAIN : (QUARTERS + q + 1) * MAIN, :] = scaled[here, cols]
        send_refs[k][2 * QUARTERS * MAIN :, :] = tail[here]


def expert_kernel(*refs):
    back_count = len(refs) - 8
    experts = back_count // 2
    recv_refs = refs[:experts]
    gate_ref, up_ref, down_ref = refs[experts : experts + 3]
    back_refs = refs[experts + 3 : 2 * experts + 3]
    x_ref, s_ref, dg_ref, du_ref, hid_ref = refs[2 * experts + 3 :]
    width = recv_refs[0].shape[1]
    main_rows = experts * MAIN
    tail = jnp.concatenate([ref[2 * QUARTERS * MAIN :, :] for ref in recv_refs], axis=0)
    row = iota((4 * experts, main_rows), 0)
    col = iota((4 * experts, main_rows), 1)
    kind = (row >= 2 * experts).astype(jnp.int32)
    chunk = jnp.right_shift(row - kind * 2 * experts, 1)
    base = chunk * MAIN + kind * 8 + jnp.bitwise_and(row, 1) * 4
    for q in range(QUARTERS):
        cols = slice(q * width, (q + 1) * width)
        picked = jnp.dot(mask(col == base + q), tail, preferred_element_type=F32).astype(BF)
        x_ref[main_rows:, cols] = picked[: 2 * experts]
        s_ref[main_rows:, cols] = picked[2 * experts :]
        for i, ref in enumerate(recv_refs):
            here = slice(i * MAIN, (i + 1) * MAIN)
            x_ref[here, cols] = ref[q * MAIN : (q + 1) * MAIN, :]
            s_ref[here, cols] = ref[(QUARTERS + q) * MAIN : (QUARTERS + q + 1) * MAIN, :]
    rows = x_ref[...]
    gate_pre = jnp.dot(rows, gate_ref[...], preferred_element_type=F32)
    up_pre = jnp.dot(rows, up_ref[...], preferred_element_type=F32)
    hidden_grad = jnp.dot(s_ref[...], down_ref[...], preferred_element_type=F32)
    sig = jax.nn.sigmoid(gate_pre)
    activated = gate_pre * sig
    hidden = (activated * up_pre).astype(BF)
    slope = sig * (1.0 + gate_pre * (1.0 - sig))
    gate_delta = (hidden_grad * up_pre * slope).astype(BF)
    up_delta = (hidden_grad * activated).astype(BF)
    hid_ref[...] = hidden
    dg_ref[...] = gate_delta
    du_ref[...] = up_delta
    grad = (
        lax.dot_general(gate_delta, gate_ref[...], CONTRACT_COLS, preferred_element_type=F32)
        + lax.dot_general(up_delta, up_ref[...], CONTRACT_COLS, preferred_element_type=F32)
    ).astype(BF)
    product = hidden.astype(F32) * hidden_grad
    product = jnp.concatenate(
        [product, jnp.zeros((width - product.shape[0], product.shape[1]), F32)], axis=0
    )
    gate_lanes = lax.dot_general(
        jnp.ones((8, product.shape[1]), F32),
        product,
        CONTRACT_COLS,
        preferred_element_type=F32,
        precision=lax.Precision.HIGHEST,
    )
    trow = iota((main_rows, 2 * experts), 0)
    tcol = iota((main_rows, 2 * experts), 1)
    inner = jnp.bitwise_and(trow, MAIN - 1)
    source = jnp.right_shift(trow, 4) * 2 + jnp.right_shift(inner, 2)
    spread = jnp.zeros((main_rows, width), F32)
    for q in range(QUARTERS):
        cols = slice(q * width, (q + 1) * width)
        mine = jnp.logical_and(jnp.bitwise_and(inner, 3) == q, inner < 8)
        place = mask(jnp.logical_and(mine, tcol == source))
        spread += jnp.dot(place, grad[main_rows:, cols], preferred_element_type=F32)
        for i, ref in enumerate(back_refs):
            ref[q * MAIN : (q + 1) * MAIN, :] = grad[i * MAIN : (i + 1) * MAIN, cols]
    for i, ref in enumerate(back_refs):
        ref[QUARTERS * MAIN :, :] = jnp.concatenate(
            [spread[i * MAIN : i * MAIN + 8], gate_lanes], axis=0
        ).astype(BF)


def grads_of(half, x_ref, s_ref, dg_ref, du_ref, hid_ref):
    rows = x_ref.shape[1] // 2
    cols = pl.ds(pl.multiple_of(half * rows, rows), rows)
    x_half = x_ref[:, cols]
    s_half = s_ref[:, cols]
    return (
        lax.dot_general(x_half, dg_ref[...], CONTRACT_ROWS, preferred_element_type=F32),
        lax.dot_general(x_half, du_ref[...], CONTRACT_ROWS, preferred_element_type=F32),
        lax.dot_general(s_half, hid_ref[...], CONTRACT_ROWS, preferred_element_type=F32),
    )


def other_half_kernel(x_ref, s_ref, dg_ref, du_ref, hid_ref, out_ref):
    half = 1 - lax.axis_index("replica")
    parts = grads_of(half, x_ref, s_ref, dg_ref, du_ref, hid_ref)
    rows = parts[0].shape[0]
    for n in range(3):
        out_ref[n * rows : (n + 1) * rows, :] = parts[n].astype(BF)


def own_half_kernel(
    x_ref, s_ref, dg_ref, du_ref, hid_ref, came_ref, gate_ref, up_ref, down_ref
):
    parts = grads_of(lax.axis_index("replica"), x_ref, s_ref, dg_ref, du_ref, hid_ref)
    rows = parts[0].shape[0]
    for n, out_ref in enumerate((gate_ref, up_ref, down_ref)):
        came = came_ref[n * rows : (n + 1) * rows, :].astype(F32)
        out_ref[...] = (parts[n].astype(BF).astype(F32) + came).astype(BF)


def combine_kernel(ids_ref, slot_ref, gates_ref, *refs):
    token_ref, grad_ref = refs[-2:]
    ret_refs = refs[:-2]
    topk, tokens = ids_ref.shape
    experts = len(ret_refs)
    width = ret_refs[0].shape[1]
    ids = ids_ref[...]
    slot = slot_ref[...]
    slot16 = repeat_rows(slot, MAIN)
    inner = jnp.bitwise_and(iota(slot16.shape, 0), MAIN - 1)
    onehot = mask(slot16 == inner)
    wanted = MAIN + jnp.right_shift(inner, 2)
    last = jnp.where(jnp.logical_and(slot16 == wanted, inner < 8), 1.0, 0.0)
    quarter = jnp.bitwise_and(inner, 3)
    tail = jnp.concatenate([ref[QUARTERS * MAIN :, :] for ref in ret_refs], axis=0)
    for q in range(QUARTERS):
        main = jnp.concatenate([ref[q * MAIN : (q + 1) * MAIN, :] for ref in ret_refs], axis=0)
        place = jnp.where(quarter == q, last, 0.0).astype(BF)
        total = lax.dot_general(onehot, main, CONTRACT_ROWS, preferred_element_type=F32)
        total += lax.dot_general(place, tail, CONTRACT_ROWS, preferred_element_type=F32)
        token_ref[:, q * width : (q + 1) * width] = total.astype(BF)
    lane_index = iota((width, tokens), 0)
    found = []
    for k, ref in enumerate(ret_refs):
        mine = slot[k : k + 1]
        lane = jnp.where(mine < MAIN, k * MAIN + mine, experts * MAIN + 2 * k + mine - MAIN)
        lane = jnp.where(mine < 0, -1, lane)
        sums = jnp.dot(
            ref[QUARTERS * MAIN :, :], mask(lane_index == lane), preferred_element_type=F32
        )
        found.append(sums[8:9])
    found = jnp.concatenate(found, axis=0)
    kept = slot >= 0
    grads = jnp.where(kept, found / jnp.where(kept, gates_ref[...], 1.0), 0.0)
    expert_row = partners(experts, tokens)
    by_choice = [
        jnp.sum(jnp.where(expert_row == ids[k : k + 1], grads, 0.0), axis=0, keepdims=True)
        for k in range(topk)
    ]
    grad_ref[...] = jnp.concatenate(by_choice, axis=0).astype(BF)


def local_call(kernel, outs, arrays, name, flops, moved, space=pltpu.VMEM, scratch=(), limit=16):
    vmem = pl.BlockSpec(memory_space=pltpu.VMEM)
    return pl.pallas_call(
        kernel,
        out_shape=[jax.ShapeDtypeStruct(shape, kind) for shape, kind in outs],
        in_specs=[pl.BlockSpec(memory_space=space)] * len(arrays),
        out_specs=[vmem] * len(outs),
        scratch_shapes=list(scratch),
        compiler_params=pltpu.CompilerParams(vmem_limit_bytes=limit * MIB),
        cost_estimate=pl.CostEstimate(flops=flops, bytes_accessed=moved, transcendentals=0),
        name=name,
    )(*arrays)


def exchange(chunks):
    count = len(chunks)
    moved = [
        lax.ppermute(chunk, "expert", [(i, i ^ step) for i in range(count)])
        for chunk, step in zip(chunks[1:], STEPS[1:])
    ]
    return [chunks[0], *moved]


def hold_kernel(*refs):
    count = len(refs) // 2
    for source, place in zip(refs[:count], refs[count:]):
        place[...] = source[...]


def per_device_moving_rows(
    tokens,
    cotangent,
    expert_ids,
    gate_values,
    replica_pick,
    replica_plan,
    gate_proj,
    up_proj,
    down_proj,
):
    experts = lax.axis_size("expert")
    token_count, model_width = tokens.shape
    topk = expert_ids.shape[1]
    hidden_width = gate_proj.shape[2]
    width = model_width // QUARTERS
    served = experts * (MAIN + 2)
    small = (topk, token_count)
    routed = local_call(
        route_kernel,
        [((SEND_ROWS, width), BF)] * experts
        + [((experts, token_count), jnp.int32), ((experts, token_count), F32)],
        [replica_plan, expert_ids.T, replica_pick.T, gate_values.T, tokens, cotangent],
        "route",
        2 * 2 * served * token_count * model_width,
        2 * 2 * (token_count + served) * model_width,
        space=pltpu.HBM,
        limit=58,
        scratch=[
            pltpu.SMEM((experts,), jnp.int32),
            pltpu.VMEM(small, jnp.int32),
            pltpu.VMEM(small, jnp.int32),
            pltpu.VMEM(small, BF),
            pltpu.VMEM(tokens.shape, BF),
            pltpu.VMEM(tokens.shape, BF),
            pltpu.SemaphoreType.DMA((6,)),
        ],
    )
    slot, gates = routed[experts:]
    recv = exchange(routed[:experts])
    held = [recv[0], gate_proj[0], up_proj[0], down_proj[0]]
    held = local_call(
        hold_kernel,
        [(array.shape, BF) for array in held],
        held,
        "hold",
        0,
        4 * 3 * model_width * hidden_width,
    )
    matmul = 2 * served * model_width * hidden_width
    outs = local_call(
        expert_kernel,
        [((BACK_ROWS, width), BF)] * experts
        + [((served, model_width), BF)] * 2
        + [((served, hidden_width), BF)] * 3,
        [held[0], *recv[1:], *held[1:]],
        "expert_rows",
        5 * matmul,
        2 * 3 * model_width * hidden_width,
    )
    factors = outs[experts:]
    returned = exchange(outs[:experts])
    returned[1], factors = lax.optimization_barrier((returned[1], factors))
    half = model_width // 2
    (leaving,) = local_call(
        other_half_kernel,
        [((3 * half, hidden_width), BF)],
        factors,
        "other_half",
        3 * matmul // 2,
        2 * 3 * half * hidden_width,
    )
    came = lax.ppermute(leaving, "replica", [(0, 1), (1, 0)])
    shares = local_call(
        own_half_kernel,
        [((half, hidden_width), BF)] * 3,
        [*factors, came],
        "own_half",
        3 * matmul // 2,
        2 * 2 * 3 * half * hidden_width,
    )
    returned, shares = lax.optimization_barrier((returned, shares))
    token_grad, gate_grad = local_call(
        combine_kernel,
        [((token_count, model_width), BF), ((topk, token_count), BF)],
        [expert_ids.T, slot, gates, *returned],
        "combine",
        2 * served * token_count * model_width,
        2 * 2 * token_count * model_width,
    )
    return (token_grad, gate_grad.T, shares[0][None], shares[1][None], shares[2][None])


def per_device(tokens, cotangent, expert_ids, gate_values, replica_pick, replica_plan, *matrices):
    experts = lax.axis_size("expert")
    slots = (copies_of(experts) + 1) * CAP
    row_bytes = 3 * 2 * tokens.shape[1] * experts
    matrix_bytes = 4 * sum(2 * m[0].size for m in matrices)
    fits = slots == MAIN + 2 and experts == 8 and lax.axis_size("replica") == 2
    rows_cheaper = slots * row_bytes < 2 * CAP * row_bytes + matrix_bytes
    plan = per_device_moving_rows if fits and rows_cheaper else per_device_moving_weights
    return plan(
        tokens, cotangent, expert_ids, gate_values, replica_pick, replica_plan, *matrices
    )


def solution(mesh):
    placed = (
        P(("parts", "expert", "replica"), None),
        P(("parts", "expert", "replica"), None),
        P(("parts", "expert", "replica"), None),
        P(("parts", "expert", "replica"), None),
        P(("parts", "expert", "replica"), None),
        P("parts"),
        P("expert", None, None),
        P("expert", None, None),
        P("expert", None, None),
    )
    return jax.shard_map(
        per_device,
        mesh=mesh,
        in_specs=placed,
        out_specs=(
            P(("parts", "expert", "replica"), None),
            P(("parts", "expert", "replica"), None),
            P(("parts", "expert"), "replica", None),
            P(("parts", "expert"), "replica", None),
            P(("parts", "expert"), "replica", None),
        ),
        check_vma=False,
    )
```

```python
import jax
import jax.numpy as jnp
from jax import lax
from jax.experimental import pallas as pl
from jax.experimental.pallas import tpu as pltpu
from jax.sharding import PartitionSpec as P

CAP = 6


def route_assignments(flat_ids, flat_pick, replica_plan, capacity):
    experts = replica_plan.shape[0]
    lane_ids = jnp.arange(experts, dtype=jnp.int32)
    same_plan = replica_plan[:, None] == replica_plan[None, :]
    earlier = lane_ids[None, :] < lane_ids[:, None]
    position = jnp.sum(jnp.logical_and(same_plan, earlier), axis=1)
    hot_mask = jnp.any(replica_plan[None, :] == lane_ids[:, None], axis=1)
    is_hot = jnp.any(
        jnp.logical_and(flat_ids[:, None] == lane_ids[None, :], hot_mask[None, :]), axis=1
    )
    use_copy = jnp.logical_and(is_hot, flat_pick >= 1)
    matches = jnp.logical_and(
        replica_plan[None, :] == flat_ids[:, None], position[None, :] == flat_pick[:, None] - 1
    )
    holder = jnp.sum(jnp.where(matches, lane_ids[None, :], 0), axis=1)
    target = jnp.where(use_copy, holder, flat_ids)
    copy_role = use_copy.astype(jnp.int32)
    bucket = target * 2 + copy_role
    sequence = jnp.arange(bucket.shape[0], dtype=jnp.int32)
    arrival = jnp.sum(
        jnp.logical_and(bucket[None, :] == bucket[:, None], sequence[None, :] < sequence[:, None]),
        axis=1,
    )
    kept_mask = arrival < capacity
    slot_index = target * (2 * capacity) + copy_role * capacity + jnp.minimum(arrival, capacity - 1)
    return (slot_index, kept_mask)


def fill_slots(slot_index, kept_mask, slot_count):
    slot_ids = jnp.arange(slot_count, dtype=jnp.int32)
    matches = jnp.logical_and(slot_index[None, :] == slot_ids[:, None], kept_mask[None, :])
    sequence = jnp.arange(slot_index.shape[0], dtype=jnp.int32)
    source = jnp.sum(jnp.where(matches, sequence[None, :], 0), axis=1)
    filled = jnp.any(matches, axis=1)
    return (source, filled)


def expert_backward(row_block, upstream, weight, gate_w, up_w, down_w):
    contract_cols = (((1,), (1,)), ((), ()))
    contract_rows = (((0,), (0,)), ((), ()))
    gate_pre = jnp.dot(row_block, gate_w, preferred_element_type=jnp.float32)
    up_pre = jnp.dot(row_block, up_w, preferred_element_type=jnp.float32)
    sigmoid_gate = jax.nn.sigmoid(gate_pre)
    activated = gate_pre * sigmoid_gate
    hidden = (activated * up_pre).astype(jnp.bfloat16)
    output_rows = lax.dot_general(hidden, down_w, contract_cols, preferred_element_type=jnp.float32)
    weight_col = weight.astype(jnp.float32)[:, None]
    upstream_f = upstream.astype(jnp.float32)
    gate_rows = jnp.sum(upstream_f * output_rows, axis=1)
    hidden_grad = weight_col * jnp.dot(upstream, down_w, preferred_element_type=jnp.float32)
    slope = sigmoid_gate * (1.0 + gate_pre * (1.0 - sigmoid_gate))
    gate_delta = (hidden_grad * up_pre * slope).astype(jnp.bfloat16)
    up_delta = (hidden_grad * activated).astype(jnp.bfloat16)
    input_grad = (
        lax.dot_general(gate_delta, gate_w, contract_cols, preferred_element_type=jnp.float32)
        + lax.dot_general(up_delta, up_w, contract_cols, preferred_element_type=jnp.float32)
    ).astype(jnp.bfloat16)
    scaled = (weight_col * upstream_f).astype(jnp.bfloat16)
    grad_set = (
        lax.dot_general(row_block, gate_delta, contract_rows, preferred_element_type=jnp.float32),
        lax.dot_general(row_block, up_delta, contract_rows, preferred_element_type=jnp.float32),
        lax.dot_general(scaled, hidden, contract_rows, preferred_element_type=jnp.float32),
    )
    return (input_grad, gate_rows, grad_set)


def per_device_moving_weights(
    tokens,
    cotangent,
    expert_ids,
    gate_values,
    replica_pick,
    replica_plan,
    gate_proj,
    up_proj,
    down_proj,
):
    experts = lax.axis_size("expert")
    capacity = CAP
    slot_total = 2 * capacity
    model_width = tokens.shape[1]
    topk = expert_ids.shape[1]
    token_count = tokens.shape[0]
    slot_index, kept_mask = route_assignments(
        expert_ids.reshape(-1), replica_pick.reshape(-1), replica_plan, capacity
    )
    source, filled = fill_slots(slot_index, kept_mask, experts * slot_total)
    token_of = source // topk
    zero_half = jnp.zeros((), jnp.bfloat16)
    send_rows = jnp.where(filled[:, None], jnp.take(tokens, token_of, axis=0), zero_half).reshape(
        experts, slot_total, model_width
    )
    send_upstream = jnp.where(
        filled[:, None], jnp.take(cotangent, token_of, axis=0), zero_half
    ).reshape(experts, slot_total, model_width)
    send_weight = jnp.where(filled, gate_values.reshape(-1)[source], zero_half).reshape(
        experts, slot_total
    )
    arrived = lax.all_to_all(send_rows, "expert", split_axis=0, concat_axis=0, tiled=True)
    own_gate = gate_proj[0]
    own_up = up_proj[0]
    own_down = down_proj[0]
    hidden_width = own_gate.shape[1]
    spread = (
        lax.all_to_all(
            own_gate.reshape(experts, -1), "expert", split_axis=0, concat_axis=0, tiled=True
        ),
        lax.all_to_all(
            own_up.reshape(experts, -1), "expert", split_axis=0, concat_axis=0, tiled=True
        ),
        lax.all_to_all(
            own_down.reshape(experts, -1), "expert", split_axis=0, concat_axis=0, tiled=True
        ),
    )
    chosen_gate = jnp.take(spread[0], replica_plan, axis=0)
    chosen_up = jnp.take(spread[1], replica_plan, axis=0)
    chosen_down = jnp.take(spread[2], replica_plan, axis=0)
    collected = (
        lax.all_to_all(chosen_gate, "expert", split_axis=0, concat_axis=0, tiled=True),
        lax.all_to_all(chosen_up, "expert", split_axis=0, concat_axis=0, tiled=True),
        lax.all_to_all(chosen_down, "expert", split_axis=0, concat_axis=0, tiled=True),
    )
    copy_gate = collected[0].reshape(model_width, hidden_width)
    copy_up = collected[1].reshape(model_width, hidden_width)
    copy_down = collected[2].reshape(model_width, hidden_width)
    arrived_up, arrived_weight = (
        lax.all_to_all(send_upstream, "expert", split_axis=0, concat_axis=0, tiled=True),
        lax.all_to_all(send_weight, "expert", split_axis=0, concat_axis=0, tiled=True),
    )
    owned_dx, owned_gate_rows, owned_grads = expert_backward(
        arrived[:, :capacity].reshape(-1, model_width),
        arrived_up[:, :capacity].reshape(-1, model_width),
        arrived_weight[:, :capacity].reshape(-1),
        own_gate,
        own_up,
        own_down,
    )
    copied_dx, copied_gate_rows, copied_grads = expert_backward(
        arrived[:, capacity:].reshape(-1, model_width),
        arrived_up[:, capacity:].reshape(-1, model_width),
        arrived_weight[:, capacity:].reshape(-1),
        copy_gate,
        copy_up,
        copy_down,
    )
    back_rows = jnp.concatenate(
        [
            owned_dx.reshape(experts, capacity, model_width),
            copied_dx.reshape(experts, capacity, model_width),
        ],
        axis=1,
    )
    back_gate = jnp.concatenate(
        [owned_gate_rows.reshape(experts, capacity), copied_gate_rows.reshape(experts, capacity)],
        axis=1,
    ).astype(jnp.bfloat16)
    returned, returned_gate = (
        lax.all_to_all(back_rows, "expert", split_axis=0, concat_axis=0, tiled=True),
        lax.all_to_all(back_gate, "expert", split_axis=0, concat_axis=0, tiled=True),
    )
    copy_pieces = (
        copied_grads[0].astype(jnp.bfloat16).reshape(experts, -1),
        copied_grads[1].astype(jnp.bfloat16).reshape(experts, -1),
        copied_grads[2].astype(jnp.bfloat16).reshape(experts, -1),
    )
    grad_spread = (
        lax.all_to_all(copy_pieces[0], "expert", split_axis=0, concat_axis=0, tiled=True),
        lax.all_to_all(copy_pieces[1], "expert", split_axis=0, concat_axis=0, tiled=True),
        lax.all_to_all(copy_pieces[2], "expert", split_axis=0, concat_axis=0, tiled=True),
    )
    lane_ids = jnp.arange(experts, dtype=jnp.int32)
    owner_map = (replica_plan[None, :] == lane_ids[:, None]).astype(jnp.bfloat16)
    summed_gate = jnp.dot(owner_map, grad_spread[0], preferred_element_type=jnp.float32).astype(
        jnp.bfloat16
    )
    summed_up = jnp.dot(owner_map, grad_spread[1], preferred_element_type=jnp.float32).astype(
        jnp.bfloat16
    )
    summed_down = jnp.dot(owner_map, grad_spread[2], preferred_element_type=jnp.float32).astype(
        jnp.bfloat16
    )
    grad_back = (
        lax.all_to_all(summed_gate, "expert", split_axis=0, concat_axis=0, tiled=True),
        lax.all_to_all(summed_up, "expert", split_axis=0, concat_axis=0, tiled=True),
        lax.all_to_all(summed_down, "expert", split_axis=0, concat_axis=0, tiled=True),
    )
    total_gate = owned_grads[0] + grad_back[0].reshape(model_width, hidden_width).astype(
        jnp.float32
    )
    total_up = owned_grads[1] + grad_back[1].reshape(model_width, hidden_width).astype(jnp.float32)
    total_down = owned_grads[2] + grad_back[2].reshape(model_width, hidden_width).astype(
        jnp.float32
    )
    shares = (
        lax.psum_scatter(
            total_gate.astype(jnp.bfloat16), "replica", scatter_dimension=0, tiled=True
        ).astype(jnp.float32),
        lax.psum_scatter(
            total_up.astype(jnp.bfloat16), "replica", scatter_dimension=0, tiled=True
        ).astype(jnp.float32),
        lax.psum_scatter(
            total_down.astype(jnp.bfloat16), "replica", scatter_dimension=0, tiled=True
        ).astype(jnp.float32),
    )
    flat_back = returned.reshape(experts * slot_total, model_width)
    picked_rows = jnp.take(flat_back, slot_index, axis=0)
    picked_rows = jnp.where(kept_mask[:, None], picked_rows, zero_half).astype(jnp.float32)
    token_grad = jnp.sum(picked_rows.reshape(token_count, topk, model_width), axis=1).astype(
        jnp.bfloat16
    )
    gate_grad = jnp.where(kept_mask, returned_gate.reshape(-1)[slot_index], zero_half).reshape(
        token_count, topk
    )
    return (
        token_grad,
        gate_grad,
        shares[0].astype(jnp.bfloat16)[None],
        shares[1].astype(jnp.bfloat16)[None],
        shares[2].astype(jnp.bfloat16)[None],
    )


BF = jnp.bfloat16
F32 = jnp.float32
CONTRACT_ROWS = (((0,), (0,)), ((), ()))
CONTRACT_COLS = (((1,), (1,)), ((), ()))
MIB = 1024 * 1024

MAIN = 16
QUARTERS = 4
SEND_ROWS = 2 * QUARTERS * MAIN + 16
BACK_ROWS = QUARTERS * MAIN + 16
STEPS = (4, 5, 6, 7, 0, 1, 2, 3)
GROUP = 4
GROUP_ROWS = GROUP * MAIN + 16


def copies_of(experts):
    return 2 if experts <= 8 else 8


def iota(shape, axis):
    return lax.broadcasted_iota(jnp.int32, shape, axis)


def partners(experts, tokens):
    row = iota((experts, tokens), 0)
    step = jnp.zeros((experts, tokens), jnp.int32)
    for c in range(experts):
        step = jnp.where(row == c, STEPS[c], step)
    return jnp.bitwise_xor(step, lax.axis_index("expert"))


def mask(condition):
    return condition.astype(F32).astype(BF)


def repeat_rows(table, times):
    width = table.shape[1]
    return jnp.concatenate(
        [jnp.broadcast_to(table[e : e + 1], (times, width)) for e in range(table.shape[0])], axis=0
    )


def route_kernel(plan_hbm, ids_hbm, pick_hbm, gate_hbm, tok_hbm, cot_hbm, *refs):
    sems = refs[-1]
    plan_ref, ids_ref, pick_ref, gate_ref, tok_ref, cot_ref = refs[-7:-1]
    slot_ref, gates_ref = refs[-9:-7]
    send_refs = refs[:-9]
    topk, tokens = ids_ref.shape
    experts = len(send_refs)
    width = tok_ref.shape[1] // QUARTERS
    copies = copies_of(experts)
    loads = [
        pltpu.make_async_copy(source, place, sems.at[n])
        for n, (source, place) in enumerate(
            (
                (plan_hbm, plan_ref),
                (ids_hbm, ids_ref),
                (pick_hbm, pick_ref),
                (gate_hbm, gate_ref),
                (tok_hbm, tok_ref),
                (cot_hbm, cot_ref),
            )
        )
    ]
    for load in loads:
        load.start()
    before = mask(iota((tokens, tokens), 0) < iota((tokens, tokens), 1))
    expert_row = partners(experts, tokens)
    for load in loads[:4]:
        load.wait()
    ids = ids_ref[...]
    pick = pick_ref[...]
    gate = gate_ref[...].astype(F32)
    named = jnp.zeros((experts, tokens), jnp.int32)
    gates = jnp.zeros((experts, tokens), F32)
    for k in range(topk):
        hit = ids[k : k + 1] == expert_row
        named = jnp.where(hit, pick[k : k + 1] + 1, named)
        gates = jnp.where(hit, gate[k : k + 1], gates)
    hot = jnp.zeros((experts, tokens), jnp.int32)
    for j in range(experts):
        hot = jnp.where(expert_row == plan_ref[j], 1, hot)
    chosen = jnp.where(named == 0, -1, jnp.where(hot > 0, named - 1, 0))
    masks = jnp.concatenate([(chosen == c).astype(F32) for c in range(copies + 1)], axis=0)
    rank = jnp.dot(masks.astype(BF), before, preferred_element_type=F32).astype(jnp.int32)
    slot = jnp.full((experts, tokens), -1, jnp.int32)
    for c in range(copies + 1):
        rank_c = rank[c * experts : (c + 1) * experts]
        keep = jnp.logical_and(chosen == c, rank_c < CAP)
        slot = jnp.where(keep, c * CAP + rank_c, slot)
    slot_ref[...] = slot
    gates_ref[...] = gates
    slot16 = repeat_rows(slot, MAIN)
    gate16 = repeat_rows(gates, MAIN)
    inner = jnp.bitwise_and(iota(slot16.shape, 0), MAIN - 1)
    onehot = (slot16 == inner).astype(F32)
    wanted = MAIN + jnp.bitwise_and(jnp.right_shift(inner, 2), 1)
    last = (slot16 == wanted).astype(F32)
    last_rows = jnp.where(inner >= 8, 0.0, last)
    last_scaled = jnp.where(inner >= 8, last * gate16, 0.0)
    quarter = jnp.bitwise_and(inner, 3)
    for load in loads[4:]:
        load.wait()
    rows = jnp.dot(onehot.astype(BF), tok_ref[...], preferred_element_type=F32).astype(BF)
    scaled = jnp.dot(
        (onehot * gate16).astype(BF), cot_ref[...], preferred_element_type=F32
    ).astype(BF)
    tail = jnp.zeros((experts * MAIN, width), F32)
    for q in range(QUARTERS):
        cols = slice(q * width, (q + 1) * width)
        mine = quarter == q
        tail += jnp.dot(
            jnp.where(mine, last_rows, 0.0).astype(BF), tok_ref[:, cols], preferred_element_type=F32
        )
        tail += jnp.dot(
            jnp.where(mine, last_scaled, 0.0).astype(BF),
            cot_ref[:, cols],
            preferred_element_type=F32,
        )
    tail = tail.astype(BF)
    for k in range(experts):
        here = slice(k * MAIN, (k + 1) * MAIN)
        for q in range(QUARTERS):
            cols = slice(q * width, (q + 1) * width)
            send_refs[k][q * MAIN : (q + 1) * MAIN, :] = rows[here, cols]
            send_refs[k][(QUARTERS + q) * MAIN : (QUARTERS + q + 1) * MAIN, :] = scaled[here, cols]
        send_refs[k][2 * QUARTERS * MAIN :, :] = tail[here]


def expert_kernel(*refs):
    recv_refs = refs[:GROUP]
    gate_ref, up_ref, down_ref = refs[GROUP : GROUP + 3]
    back_refs = refs[GROUP + 3 : 2 * GROUP + 3]
    x_ref, s_ref, dg_ref, du_ref, hid_ref = refs[2 * GROUP + 3 :]
    width = recv_refs[0].shape[1]
    main_rows = GROUP * MAIN
    tail = jnp.concatenate([ref[2 * QUARTERS * MAIN :, :] for ref in recv_refs], axis=0)
    row = iota((2 * MAIN, main_rows), 0)
    col = iota((2 * MAIN, main_rows), 1)
    inner = jnp.bitwise_and(row, MAIN - 1)
    base = jnp.right_shift(inner, 1) * MAIN + (row - inner) // 2 + jnp.bitwise_and(row, 1) * 4
    real = inner < 2 * GROUP
    for q in range(QUARTERS):
        cols = slice(q * width, (q + 1) * width)
        place = mask(jnp.logical_and(real, col == base + q))
        picked = jnp.dot(place, tail, preferred_element_type=F32).astype(BF)
        x_ref[main_rows:, cols] = picked[:MAIN]
        s_ref[main_rows:, cols] = picked[MAIN:]
        for i, ref in enumerate(recv_refs):
            here = slice(i * MAIN, (i + 1) * MAIN)
            x_ref[here, cols] = ref[q * MAIN : (q + 1) * MAIN, :]
            s_ref[here, cols] = ref[(QUARTERS + q) * MAIN : (QUARTERS + q + 1) * MAIN, :]
    rows = x_ref[...]
    gate_pre = jnp.dot(rows, gate_ref[...], preferred_element_type=F32)
    up_pre = jnp.dot(rows, up_ref[...], preferred_element_type=F32)
    hidden_grad = jnp.dot(s_ref[...], down_ref[...], preferred_element_type=F32)
    sig = jax.nn.sigmoid(gate_pre)
    activated = gate_pre * sig
    hidden = (activated * up_pre).astype(BF)
    slope = sig * (1.0 + gate_pre * (1.0 - sig))
    gate_delta = (hidden_grad * up_pre * slope).astype(BF)
    up_delta = (hidden_grad * activated).astype(BF)
    hid_ref[...] = hidden
    dg_ref[...] = gate_delta
    du_ref[...] = up_delta
    grad = (
        lax.dot_general(gate_delta, gate_ref[...], CONTRACT_COLS, preferred_element_type=F32)
        + lax.dot_general(up_delta, up_ref[...], CONTRACT_COLS, preferred_element_type=F32)
    ).astype(BF)
    product = hidden.astype(F32) * hidden_grad
    product = jnp.concatenate(
        [product, jnp.zeros((width - product.shape[0], product.shape[1]), F32)], axis=0
    )
    gate_lanes = lax.dot_general(
        jnp.ones((8, product.shape[1]), F32),
        product,
        CONTRACT_COLS,
        preferred_element_type=F32,
        precision=lax.Precision.HIGHEST,
    )
    trow = iota((main_rows, MAIN), 0)
    tcol = iota((main_rows, MAIN), 1)
    inner = jnp.bitwise_and(trow, MAIN - 1)
    source = jnp.right_shift(trow, 4) * 2 + jnp.right_shift(inner, 2)
    spread = jnp.zeros((main_rows, width), F32)
    for q in range(QUARTERS):
        cols = slice(q * width, (q + 1) * width)
        mine = jnp.logical_and(jnp.bitwise_and(inner, 3) == q, inner < 8)
        place = mask(jnp.logical_and(mine, tcol == source))
        spread += jnp.dot(place, grad[main_rows:, cols], preferred_element_type=F32)
        for i, ref in enumerate(back_refs):
            ref[q * MAIN : (q + 1) * MAIN, :] = grad[i * MAIN : (i + 1) * MAIN, cols]
    for i, ref in enumerate(back_refs):
        ref[QUARTERS * MAIN :, :] = jnp.concatenate(
            [spread[i * MAIN : i * MAIN + 8], gate_lanes], axis=0
        ).astype(BF)


def grads_of(half, refs):
    sums = [None] * 3
    for first in range(0, len(refs), 5):
        x_ref, s_ref, *right = refs[first : first + 5]
        rows = x_ref.shape[1] // 2
        cols = pl.ds(pl.multiple_of(half * rows, rows), rows)
        x_half = x_ref[:, cols]
        for n, left in enumerate((x_half, x_half, s_ref[:, cols])):
            part = lax.dot_general(left, right[n][...], CONTRACT_ROWS, preferred_element_type=F32)
            sums[n] = part if sums[n] is None else sums[n] + part
    return sums


def other_half_kernel(*refs):
    out_ref = refs[-1]
    parts = grads_of(1 - lax.axis_index("replica"), refs[:-1])
    rows = parts[0].shape[0]
    for n in range(3):
        out_ref[n * rows : (n + 1) * rows, :] = parts[n].astype(BF)


def own_half_kernel(*refs):
    came_ref = refs[-4]
    parts = grads_of(lax.axis_index("replica"), refs[:-4])
    rows = parts[0].shape[0]
    for n, out_ref in enumerate(refs[-3:]):
        came = came_ref[n * rows : (n + 1) * rows, :].astype(F32)
        out_ref[...] = (parts[n].astype(BF).astype(F32) + came).astype(BF)


def combine_kernel(ids_ref, slot_ref, gates_ref, *refs):
    token_ref, grad_ref = refs[-2:]
    ret_refs = refs[:-2]
    topk, tokens = ids_ref.shape
    experts = len(ret_refs)
    width = ret_refs[0].shape[1]
    ids = ids_ref[...]
    slot = slot_ref[...]
    slot16 = repeat_rows(slot, MAIN)
    inner = jnp.bitwise_and(iota(slot16.shape, 0), MAIN - 1)
    onehot = mask(slot16 == inner)
    wanted = MAIN + jnp.right_shift(inner, 2)
    last = jnp.where(jnp.logical_and(slot16 == wanted, inner < 8), 1.0, 0.0)
    quarter = jnp.bitwise_and(inner, 3)
    tail = jnp.concatenate([ref[QUARTERS * MAIN :, :] for ref in ret_refs], axis=0)
    for q in range(QUARTERS):
        main = jnp.concatenate([ref[q * MAIN : (q + 1) * MAIN, :] for ref in ret_refs], axis=0)
        place = jnp.where(quarter == q, last, 0.0).astype(BF)
        total = lax.dot_general(onehot, main, CONTRACT_ROWS, preferred_element_type=F32)
        total += lax.dot_general(place, tail, CONTRACT_ROWS, preferred_element_type=F32)
        token_ref[:, q * width : (q + 1) * width] = total.astype(BF)
    lane_index = iota((width, tokens), 0)
    found = []
    for c, ref in enumerate(ret_refs):
        mine = slot[c : c + 1]
        place = c % GROUP
        lane = jnp.where(mine < MAIN, place * MAIN + mine, GROUP * MAIN + 2 * place + mine - MAIN)
        lane = jnp.where(mine < 0, -1, lane)
        sums = jnp.dot(
            ref[QUARTERS * MAIN :, :], mask(lane_index == lane), preferred_element_type=F32
        )
        found.append(sums[8:9])
    found = jnp.concatenate(found, axis=0)
    kept = slot >= 0
    grads = jnp.where(kept, found / jnp.where(kept, gates_ref[...], 1.0), 0.0)
    expert_row = partners(experts, tokens)
    by_choice = [
        jnp.sum(jnp.where(expert_row == ids[k : k + 1], grads, 0.0), axis=0, keepdims=True)
        for k in range(topk)
    ]
    grad_ref[...] = jnp.concatenate(by_choice, axis=0).astype(BF)


def local_call(kernel, outs, arrays, name, flops, moved, space=pltpu.VMEM, scratch=(), limit=16):
    vmem = pl.BlockSpec(memory_space=pltpu.VMEM)
    return pl.pallas_call(
        kernel,
        out_shape=[jax.ShapeDtypeStruct(shape, kind) for shape, kind in outs],
        in_specs=[pl.BlockSpec(memory_space=space)] * len(arrays),
        out_specs=[vmem] * len(outs),
        scratch_shapes=list(scratch),
        compiler_params=pltpu.CompilerParams(vmem_limit_bytes=limit * MIB),
        cost_estimate=pl.CostEstimate(flops=flops, bytes_accessed=moved, transcendentals=0),
        name=name,
    )(*arrays)


def exchange(chunks, steps):
    experts = lax.axis_size("expert")
    return [
        lax.ppermute(chunk, "expert", [(i, i ^ step) for i in range(experts)]) if step else chunk
        for chunk, step in zip(chunks, steps)
    ]


def hold_kernel(*refs):
    count = len(refs) // 2
    for source, place in zip(refs[:count], refs[count:]):
        place[...] = source[...]


def per_device_moving_rows(
    tokens,
    cotangent,
    expert_ids,
    gate_values,
    replica_pick,
    replica_plan,
    gate_proj,
    up_proj,
    down_proj,
):
    experts = lax.axis_size("expert")
    token_count, model_width = tokens.shape
    topk = expert_ids.shape[1]
    hidden_width = gate_proj.shape[2]
    width = model_width // QUARTERS
    served = experts * (MAIN + 2)
    small = (topk, token_count)
    routed = local_call(
        route_kernel,
        [((SEND_ROWS, width), BF)] * experts
        + [((experts, token_count), jnp.int32), ((experts, token_count), F32)],
        [replica_plan, expert_ids.T, replica_pick.T, gate_values.T, tokens, cotangent],
        "route",
        2 * 2 * served * token_count * model_width,
        2 * 2 * (token_count + served) * model_width,
        space=pltpu.HBM,
        limit=58,
        scratch=[
            pltpu.SMEM((experts,), jnp.int32),
            pltpu.VMEM(small, jnp.int32),
            pltpu.VMEM(small, jnp.int32),
            pltpu.VMEM(small, BF),
            pltpu.VMEM(tokens.shape, BF),
            pltpu.VMEM(tokens.shape, BF),
            pltpu.SemaphoreType.DMA((6,)),
        ],
    )
    slot, gates = routed[experts:]
    recv = exchange(routed[:experts], STEPS)
    matrices = [gate_proj[0], up_proj[0], down_proj[0]]
    matrices = local_call(
        hold_kernel,
        [(array.shape, BF) for array in matrices],
        matrices,
        "hold",
        0,
        4 * 3 * model_width * hidden_width,
    )
    matmul = 2 * GROUP_ROWS * model_width * hidden_width
    returned, factors = [], []
    for first in range(0, experts, GROUP):
        outs = local_call(
            expert_kernel,
            [((BACK_ROWS, width), BF)] * GROUP
            + [((GROUP_ROWS, model_width), BF)] * 2
            + [((GROUP_ROWS, hidden_width), BF)] * 3,
            [*recv[first : first + GROUP], *matrices],
            "expert_rows",
            5 * matmul,
            2 * 3 * model_width * hidden_width,
        )
        returned += exchange(outs[:GROUP], STEPS[first : first + GROUP])
        factors += outs[GROUP:]
    returned[:GROUP], factors = lax.optimization_barrier((returned[:GROUP], factors))
    half = model_width // 2
    (leaving,) = local_call(
        other_half_kernel,
        [((3 * half, hidden_width), BF)],
        factors,
        "other_half",
        1,
        1,
    )
    came = lax.ppermute(leaving, "replica", [(0, 1), (1, 0)])
    shares = local_call(
        own_half_kernel,
        [((half, hidden_width), BF)] * 3,
        [*factors, came],
        "own_half",
        1,
        1,
    )
    returned, shares = lax.optimization_barrier((returned, shares))
    token_grad, gate_grad = local_call(
        combine_kernel,
        [((token_count, model_width), BF), ((topk, token_count), BF)],
        [expert_ids.T, slot, gates, *returned],
        "combine",
        2 * served * token_count * model_width,
        2 * 2 * token_count * model_width,
    )
    return (token_grad, gate_grad.T, shares[0][None], shares[1][None], shares[2][None])


def per_device(tokens, cotangent, expert_ids, gate_values, replica_pick, replica_plan, *matrices):
    experts = lax.axis_size("expert")
    slots = (copies_of(experts) + 1) * CAP
    row_bytes = 3 * 2 * tokens.shape[1] * experts
    matrix_bytes = 4 * sum(2 * m[0].size for m in matrices)
    fits = slots == MAIN + 2 and experts == 8 and lax.axis_size("replica") == 2
    rows_cheaper = slots * row_bytes < 2 * CAP * row_bytes + matrix_bytes
    plan = per_device_moving_rows if fits and rows_cheaper else per_device_moving_weights
    return plan(
        tokens, cotangent, expert_ids, gate_values, replica_pick, replica_plan, *matrices
    )


def solution(mesh):
    placed = (
        P(("parts", "expert", "replica"), None),
        P(("parts", "expert", "replica"), None),
        P(("parts", "expert", "replica"), None),
        P(("parts", "expert", "replica"), None),
        P(("parts", "expert", "replica"), None),
        P("parts"),
        P("expert", None, None),
        P("expert", None, None),
        P("expert", None, None),
    )
    return jax.shard_map(
        per_device,
        mesh=mesh,
        in_specs=placed,
        out_specs=(
            P(("parts", "expert", "replica"), None),
            P(("parts", "expert", "replica"), None),
            P(("parts", "expert"), "replica", None),
            P(("parts", "expert"), "replica", None),
            P(("parts", "expert"), "replica", None),
        ),
        check_vma=False,
    )
```

```python
import jax
import jax.numpy as jnp
from jax import lax
from jax.experimental import pallas as pl
from jax.experimental.pallas import tpu as pltpu
from jax.sharding import PartitionSpec as P

CAP = 6


def route_assignments(flat_ids, flat_pick, replica_plan, capacity):
    experts = replica_plan.shape[0]
    lane_ids = jnp.arange(experts, dtype=jnp.int32)
    same_plan = replica_plan[:, None] == replica_plan[None, :]
    earlier = lane_ids[None, :] < lane_ids[:, None]
    position = jnp.sum(jnp.logical_and(same_plan, earlier), axis=1)
    hot_mask = jnp.any(replica_plan[None, :] == lane_ids[:, None], axis=1)
    is_hot = jnp.any(
        jnp.logical_and(flat_ids[:, None] == lane_ids[None, :], hot_mask[None, :]), axis=1
    )
    use_copy = jnp.logical_and(is_hot, flat_pick >= 1)
    matches = jnp.logical_and(
        replica_plan[None, :] == flat_ids[:, None], position[None, :] == flat_pick[:, None] - 1
    )
    holder = jnp.sum(jnp.where(matches, lane_ids[None, :], 0), axis=1)
    target = jnp.where(use_copy, holder, flat_ids)
    copy_role = use_copy.astype(jnp.int32)
    bucket = target * 2 + copy_role
    sequence = jnp.arange(bucket.shape[0], dtype=jnp.int32)
    arrival = jnp.sum(
        jnp.logical_and(bucket[None, :] == bucket[:, None], sequence[None, :] < sequence[:, None]),
        axis=1,
    )
    kept_mask = arrival < capacity
    slot_index = target * (2 * capacity) + copy_role * capacity + jnp.minimum(arrival, capacity - 1)
    return (slot_index, kept_mask)


def fill_slots(slot_index, kept_mask, slot_count):
    slot_ids = jnp.arange(slot_count, dtype=jnp.int32)
    matches = jnp.logical_and(slot_index[None, :] == slot_ids[:, None], kept_mask[None, :])
    sequence = jnp.arange(slot_index.shape[0], dtype=jnp.int32)
    source = jnp.sum(jnp.where(matches, sequence[None, :], 0), axis=1)
    filled = jnp.any(matches, axis=1)
    return (source, filled)


def expert_backward(row_block, upstream, weight, gate_w, up_w, down_w):
    contract_cols = (((1,), (1,)), ((), ()))
    contract_rows = (((0,), (0,)), ((), ()))
    gate_pre = jnp.dot(row_block, gate_w, preferred_element_type=jnp.float32)
    up_pre = jnp.dot(row_block, up_w, preferred_element_type=jnp.float32)
    sigmoid_gate = jax.nn.sigmoid(gate_pre)
    activated = gate_pre * sigmoid_gate
    hidden = (activated * up_pre).astype(jnp.bfloat16)
    output_rows = lax.dot_general(hidden, down_w, contract_cols, preferred_element_type=jnp.float32)
    weight_col = weight.astype(jnp.float32)[:, None]
    upstream_f = upstream.astype(jnp.float32)
    gate_rows = jnp.sum(upstream_f * output_rows, axis=1)
    hidden_grad = weight_col * jnp.dot(upstream, down_w, preferred_element_type=jnp.float32)
    slope = sigmoid_gate * (1.0 + gate_pre * (1.0 - sigmoid_gate))
    gate_delta = (hidden_grad * up_pre * slope).astype(jnp.bfloat16)
    up_delta = (hidden_grad * activated).astype(jnp.bfloat16)
    input_grad = (
        lax.dot_general(gate_delta, gate_w, contract_cols, preferred_element_type=jnp.float32)
        + lax.dot_general(up_delta, up_w, contract_cols, preferred_element_type=jnp.float32)
    ).astype(jnp.bfloat16)
    scaled = (weight_col * upstream_f).astype(jnp.bfloat16)
    grad_set = (
        lax.dot_general(row_block, gate_delta, contract_rows, preferred_element_type=jnp.float32),
        lax.dot_general(row_block, up_delta, contract_rows, preferred_element_type=jnp.float32),
        lax.dot_general(scaled, hidden, contract_rows, preferred_element_type=jnp.float32),
    )
    return (input_grad, gate_rows, grad_set)


def per_device_moving_weights(
    tokens,
    cotangent,
    expert_ids,
    gate_values,
    replica_pick,
    replica_plan,
    gate_proj,
    up_proj,
    down_proj,
):
    experts = lax.axis_size("expert")
    capacity = CAP
    slot_total = 2 * capacity
    model_width = tokens.shape[1]
    topk = expert_ids.shape[1]
    token_count = tokens.shape[0]
    slot_index, kept_mask = route_assignments(
        expert_ids.reshape(-1), replica_pick.reshape(-1), replica_plan, capacity
    )
    source, filled = fill_slots(slot_index, kept_mask, experts * slot_total)
    token_of = source // topk
    zero_half = jnp.zeros((), jnp.bfloat16)
    send_rows = jnp.where(filled[:, None], jnp.take(tokens, token_of, axis=0), zero_half).reshape(
        experts, slot_total, model_width
    )
    send_upstream = jnp.where(
        filled[:, None], jnp.take(cotangent, token_of, axis=0), zero_half
    ).reshape(experts, slot_total, model_width)
    send_weight = jnp.where(filled, gate_values.reshape(-1)[source], zero_half).reshape(
        experts, slot_total
    )
    arrived = lax.all_to_all(send_rows, "expert", split_axis=0, concat_axis=0, tiled=True)
    own_gate = gate_proj[0]
    own_up = up_proj[0]
    own_down = down_proj[0]
    hidden_width = own_gate.shape[1]
    spread = (
        lax.all_to_all(
            own_gate.reshape(experts, -1), "expert", split_axis=0, concat_axis=0, tiled=True
        ),
        lax.all_to_all(
            own_up.reshape(experts, -1), "expert", split_axis=0, concat_axis=0, tiled=True
        ),
        lax.all_to_all(
            own_down.reshape(experts, -1), "expert", split_axis=0, concat_axis=0, tiled=True
        ),
    )
    chosen_gate = jnp.take(spread[0], replica_plan, axis=0)
    chosen_up = jnp.take(spread[1], replica_plan, axis=0)
    chosen_down = jnp.take(spread[2], replica_plan, axis=0)
    collected = (
        lax.all_to_all(chosen_gate, "expert", split_axis=0, concat_axis=0, tiled=True),
        lax.all_to_all(chosen_up, "expert", split_axis=0, concat_axis=0, tiled=True),
        lax.all_to_all(chosen_down, "expert", split_axis=0, concat_axis=0, tiled=True),
    )
    copy_gate = collected[0].reshape(model_width, hidden_width)
    copy_up = collected[1].reshape(model_width, hidden_width)
    copy_down = collected[2].reshape(model_width, hidden_width)
    arrived_up, arrived_weight = (
        lax.all_to_all(send_upstream, "expert", split_axis=0, concat_axis=0, tiled=True),
        lax.all_to_all(send_weight, "expert", split_axis=0, concat_axis=0, tiled=True),
    )
    owned_dx, owned_gate_rows, owned_grads = expert_backward(
        arrived[:, :capacity].reshape(-1, model_width),
        arrived_up[:, :capacity].reshape(-1, model_width),
        arrived_weight[:, :capacity].reshape(-1),
        own_gate,
        own_up,
        own_down,
    )
    copied_dx, copied_gate_rows, copied_grads = expert_backward(
        arrived[:, capacity:].reshape(-1, model_width),
        arrived_up[:, capacity:].reshape(-1, model_width),
        arrived_weight[:, capacity:].reshape(-1),
        copy_gate,
        copy_up,
        copy_down,
    )
    back_rows = jnp.concatenate(
        [
            owned_dx.reshape(experts, capacity, model_width),
            copied_dx.reshape(experts, capacity, model_width),
        ],
        axis=1,
    )
    back_gate = jnp.concatenate(
        [owned_gate_rows.reshape(experts, capacity), copied_gate_rows.reshape(experts, capacity)],
        axis=1,
    ).astype(jnp.bfloat16)
    returned, returned_gate = (
        lax.all_to_all(back_rows, "expert", split_axis=0, concat_axis=0, tiled=True),
        lax.all_to_all(back_gate, "expert", split_axis=0, concat_axis=0, tiled=True),
    )
    copy_pieces = (
        copied_grads[0].astype(jnp.bfloat16).reshape(experts, -1),
        copied_grads[1].astype(jnp.bfloat16).reshape(experts, -1),
        copied_grads[2].astype(jnp.bfloat16).reshape(experts, -1),
    )
    grad_spread = (
        lax.all_to_all(copy_pieces[0], "expert", split_axis=0, concat_axis=0, tiled=True),
        lax.all_to_all(copy_pieces[1], "expert", split_axis=0, concat_axis=0, tiled=True),
        lax.all_to_all(copy_pieces[2], "expert", split_axis=0, concat_axis=0, tiled=True),
    )
    lane_ids = jnp.arange(experts, dtype=jnp.int32)
    owner_map = (replica_plan[None, :] == lane_ids[:, None]).astype(jnp.bfloat16)
    summed_gate = jnp.dot(owner_map, grad_spread[0], preferred_element_type=jnp.float32).astype(
        jnp.bfloat16
    )
    summed_up = jnp.dot(owner_map, grad_spread[1], preferred_element_type=jnp.float32).astype(
        jnp.bfloat16
    )
    summed_down = jnp.dot(owner_map, grad_spread[2], preferred_element_type=jnp.float32).astype(
        jnp.bfloat16
    )
    grad_back = (
        lax.all_to_all(summed_gate, "expert", split_axis=0, concat_axis=0, tiled=True),
        lax.all_to_all(summed_up, "expert", split_axis=0, concat_axis=0, tiled=True),
        lax.all_to_all(summed_down, "expert", split_axis=0, concat_axis=0, tiled=True),
    )
    total_gate = owned_grads[0] + grad_back[0].reshape(model_width, hidden_width).astype(
        jnp.float32
    )
    total_up = owned_grads[1] + grad_back[1].reshape(model_width, hidden_width).astype(jnp.float32)
    total_down = owned_grads[2] + grad_back[2].reshape(model_width, hidden_width).astype(
        jnp.float32
    )
    shares = (
        lax.psum_scatter(
            total_gate.astype(jnp.bfloat16), "replica", scatter_dimension=0, tiled=True
        ).astype(jnp.float32),
        lax.psum_scatter(
            total_up.astype(jnp.bfloat16), "replica", scatter_dimension=0, tiled=True
        ).astype(jnp.float32),
        lax.psum_scatter(
            total_down.astype(jnp.bfloat16), "replica", scatter_dimension=0, tiled=True
        ).astype(jnp.float32),
    )
    flat_back = returned.reshape(experts * slot_total, model_width)
    picked_rows = jnp.take(flat_back, slot_index, axis=0)
    picked_rows = jnp.where(kept_mask[:, None], picked_rows, zero_half).astype(jnp.float32)
    token_grad = jnp.sum(picked_rows.reshape(token_count, topk, model_width), axis=1).astype(
        jnp.bfloat16
    )
    gate_grad = jnp.where(kept_mask, returned_gate.reshape(-1)[slot_index], zero_half).reshape(
        token_count, topk
    )
    return (
        token_grad,
        gate_grad,
        shares[0].astype(jnp.bfloat16)[None],
        shares[1].astype(jnp.bfloat16)[None],
        shares[2].astype(jnp.bfloat16)[None],
    )


BF = jnp.bfloat16
F32 = jnp.float32
CONTRACT_ROWS = (((0,), (0,)), ((), ()))
CONTRACT_COLS = (((1,), (1,)), ((), ()))
MIB = 1024 * 1024

BASES = (4, 6, 2)
MAIN = 16
QUARTERS = 4
SEND_ROWS = 2 * QUARTERS * MAIN + 16
BACK_ROWS = QUARTERS * MAIN + 16


def copies_of(experts):
    return 2 if experts <= 8 else 8


def iota(shape, axis):
    return lax.broadcasted_iota(jnp.int32, shape, axis)


def partners(experts, tokens):
    row = iota((experts, tokens), 0)
    step = jnp.bitwise_xor(jnp.bitwise_and(row, 1), lax.axis_index("replica"))
    for d, base in enumerate(BASES):
        step = jnp.where(jnp.right_shift(row, 1) == d + 1, step + base, step)
    step = jnp.where(row < 2, row, step)
    return jnp.bitwise_xor(step, lax.axis_index("expert"))


def chunk_views(refs, rows):
    return [(refs[0], 0), (refs[1], 0)] + [(ref, part * rows) for ref in refs[2:] for part in (0, 1)]


def mask(condition):
    return condition.astype(F32).astype(BF)


def repeat_rows(table, times):
    width = table.shape[1]
    return jnp.concatenate(
        [jnp.broadcast_to(table[e : e + 1], (times, width)) for e in range(table.shape[0])], axis=0
    )


def route_kernel(plan_hbm, ids_hbm, pick_hbm, gate_hbm, tok_hbm, cot_hbm, *refs):
    sems = refs[-1]
    plan_ref, ids_ref, pick_ref, gate_ref, tok_ref, cot_ref = refs[-7:-1]
    slot_ref, gates_ref = refs[-9:-7]
    self_ref, near_ref, keep_ref, give_ref = refs[:-9]
    topk, tokens = ids_ref.shape
    experts = slot_ref.shape[0]
    send_views = [(self_ref, 0), (near_ref, 0)] + [
        (ref, d * SEND_ROWS) for d in range(len(BASES)) for ref in (keep_ref, give_ref)
    ]
    width = tok_ref.shape[1] // QUARTERS
    copies = copies_of(experts)
    loads = [
        pltpu.make_async_copy(source, place, sems.at[n])
        for n, (source, place) in enumerate(
            (
                (plan_hbm, plan_ref),
                (ids_hbm, ids_ref),
                (pick_hbm, pick_ref),
                (gate_hbm, gate_ref),
                (tok_hbm, tok_ref),
                (cot_hbm, cot_ref),
            )
        )
    ]
    for load in loads:
        load.start()
    before = mask(iota((tokens, tokens), 0) < iota((tokens, tokens), 1))
    expert_row = partners(experts, tokens)
    for load in loads[:4]:
        load.wait()
    ids = ids_ref[...]
    pick = pick_ref[...]
    gate = gate_ref[...].astype(F32)
    named = jnp.zeros((experts, tokens), jnp.int32)
    gates = jnp.zeros((experts, tokens), F32)
    for k in range(topk):
        hit = ids[k : k + 1] == expert_row
        named = jnp.where(hit, pick[k : k + 1] + 1, named)
        gates = jnp.where(hit, gate[k : k + 1], gates)
    hot = jnp.zeros((experts, tokens), jnp.int32)
    for j in range(experts):
        hot = jnp.where(expert_row == plan_ref[j], 1, hot)
    chosen = jnp.where(named == 0, -1, jnp.where(hot > 0, named - 1, 0))
    masks = jnp.concatenate([(chosen == c).astype(F32) for c in range(copies + 1)], axis=0)
    rank = jnp.dot(masks.astype(BF), before, preferred_element_type=F32).astype(jnp.int32)
    slot = jnp.full((experts, tokens), -1, jnp.int32)
    for c in range(copies + 1):
        rank_c = rank[c * experts : (c + 1) * experts]
        keep = jnp.logical_and(chosen == c, rank_c < CAP)
        slot = jnp.where(keep, c * CAP + rank_c, slot)
    slot_ref[...] = slot
    gates_ref[...] = gates
    slot16 = repeat_rows(slot, MAIN)
    gate16 = repeat_rows(gates, MAIN)
    inner = jnp.bitwise_and(iota(slot16.shape, 0), MAIN - 1)
    onehot = (slot16 == inner).astype(F32)
    wanted = MAIN + jnp.bitwise_and(jnp.right_shift(inner, 2), 1)
    last = (slot16 == wanted).astype(F32)
    last_rows = jnp.where(inner >= 8, 0.0, last)
    last_scaled = jnp.where(inner >= 8, last * gate16, 0.0)
    quarter = jnp.bitwise_and(inner, 3)
    for load in loads[4:]:
        load.wait()
    rows = jnp.dot(onehot.astype(BF), tok_ref[...], preferred_element_type=F32).astype(BF)
    scaled = jnp.dot(
        (onehot * gate16).astype(BF), cot_ref[...], preferred_element_type=F32
    ).astype(BF)
    tail = jnp.zeros((experts * MAIN, width), F32)
    for q in range(QUARTERS):
        cols = slice(q * width, (q + 1) * width)
        mine = quarter == q
        tail += jnp.dot(
            jnp.where(mine, last_rows, 0.0).astype(BF), tok_ref[:, cols], preferred_element_type=F32
        )
        tail += jnp.dot(
            jnp.where(mine, last_scaled, 0.0).astype(BF),
            cot_ref[:, cols],
            preferred_element_type=F32,
        )
    tail = tail.astype(BF)
    for c, (ref, first) in enumerate(send_views):
        here = slice(c * MAIN, (c + 1) * MAIN)
        for q in range(QUARTERS):
            cols = slice(q * width, (q + 1) * width)
            ref[first + q * MAIN : first + (q + 1) * MAIN, :] = rows[here, cols]
            low = first + (QUARTERS + q) * MAIN
            ref[low : low + MAIN, :] = scaled[here, cols]
        low = first + 2 * QUARTERS * MAIN
        ref[low : low + 16, :] = tail[here]


def join_kernel(self_hbm, keep_ref, came_ref, self_ref, *double_refs):
    self_ref[...] = self_hbm[...]
    for d, ref in enumerate(double_refs):
        rows = slice(d * SEND_ROWS, (d + 1) * SEND_ROWS)
        ref[:SEND_ROWS, :] = keep_ref[rows, :]
        ref[SEND_ROWS:, :] = came_ref[rows, :]


def expert_kernel(*refs):
    count = 2 + len(BASES)
    recv_views = chunk_views(refs[:count], SEND_ROWS)
    gate_ref, up_ref, down_ref = refs[count : count + 3]
    back_views = chunk_views(refs[count + 3 : 2 * count + 3], BACK_ROWS)
    x_ref, s_ref, dg_ref, du_ref, hid_ref = refs[2 * count + 3 :]
    experts = len(recv_views)
    width = refs[0].shape[1]
    main_rows = experts * MAIN
    tail = jnp.concatenate(
        [ref[first + SEND_ROWS - 16 : first + SEND_ROWS, :] for ref, first in recv_views], axis=0
    )
    row = iota((4 * experts, main_rows), 0)
    col = iota((4 * experts, main_rows), 1)
    kind = (row >= 2 * experts).astype(jnp.int32)
    chunk = jnp.right_shift(row - kind * 2 * experts, 1)
    base = chunk * MAIN + kind * 8 + jnp.bitwise_and(row, 1) * 4
    for q in range(QUARTERS):
        cols = slice(q * width, (q + 1) * width)
        picked = jnp.dot(mask(col == base + q), tail, preferred_element_type=F32).astype(BF)
        x_ref[main_rows:, cols] = picked[: 2 * experts]
        s_ref[main_rows:, cols] = picked[2 * experts :]
        for i, (ref, first) in enumerate(recv_views):
            here = slice(i * MAIN, (i + 1) * MAIN)
            x_ref[here, cols] = ref[first + q * MAIN : first + (q + 1) * MAIN, :]
            low = first + (QUARTERS + q) * MAIN
            s_ref[here, cols] = ref[low : low + MAIN, :]
    rows = x_ref[...]
    gate_pre = jnp.dot(rows, gate_ref[...], preferred_element_type=F32)
    up_pre = jnp.dot(rows, up_ref[...], preferred_element_type=F32)
    hidden_grad = jnp.dot(s_ref[...], down_ref[...], preferred_element_type=F32)
    sig = jax.nn.sigmoid(gate_pre)
    activated = gate_pre * sig
    hidden = (activated * up_pre).astype(BF)
    slope = sig * (1.0 + gate_pre * (1.0 - sig))
    gate_delta = (hidden_grad * up_pre * slope).astype(BF)
    up_delta = (hidden_grad * activated).astype(BF)
    hid_ref[...] = hidden
    dg_ref[...] = gate_delta
    du_ref[...] = up_delta
    grad = (
        lax.dot_general(gate_delta, gate_ref[...], CONTRACT_COLS, preferred_element_type=F32)
        + lax.dot_general(up_delta, up_ref[...], CONTRACT_COLS, preferred_element_type=F32)
    ).astype(BF)
    product = hidden.astype(F32) * hidden_grad
    product = jnp.concatenate(
        [product, jnp.zeros((width - product.shape[0], product.shape[1]), F32)], axis=0
    )
    gate_lanes = lax.dot_general(
        jnp.ones((8, product.shape[1]), F32),
        product,
        CONTRACT_COLS,
        preferred_element_type=F32,
        precision=lax.Precision.HIGHEST,
    )
    trow = iota((main_rows, 2 * experts), 0)
    tcol = iota((main_rows, 2 * experts), 1)
    inner = jnp.bitwise_and(trow, MAIN - 1)
    source = jnp.right_shift(trow, 4) * 2 + jnp.right_shift(inner, 2)
    spread = jnp.zeros((main_rows, width), F32)
    for q in range(QUARTERS):
        cols = slice(q * width, (q + 1) * width)
        mine = jnp.logical_and(jnp.bitwise_and(inner, 3) == q, inner < 8)
        place = mask(jnp.logical_and(mine, tcol == source))
        spread += jnp.dot(place, grad[main_rows:, cols], preferred_element_type=F32)
        for i, (ref, first) in enumerate(back_views):
            low = first + q * MAIN
            ref[low : low + MAIN, :] = grad[i * MAIN : (i + 1) * MAIN, cols]
    for i, (ref, first) in enumerate(back_views):
        low = first + QUARTERS * MAIN
        ref[low : low + 16, :] = jnp.concatenate(
            [spread[i * MAIN : i * MAIN + 8], gate_lanes], axis=0
        ).astype(BF)


def grads_of(half, x_ref, s_ref, dg_ref, du_ref, hid_ref):
    rows = x_ref.shape[1] // 2
    cols = pl.ds(pl.multiple_of(half * rows, rows), rows)
    x_half = x_ref[:, cols]
    s_half = s_ref[:, cols]
    return (
        lax.dot_general(x_half, dg_ref[...], CONTRACT_ROWS, preferred_element_type=F32),
        lax.dot_general(x_half, du_ref[...], CONTRACT_ROWS, preferred_element_type=F32),
        lax.dot_general(s_half, hid_ref[...], CONTRACT_ROWS, preferred_element_type=F32),
    )


def other_half_kernel(x_ref, s_ref, dg_ref, du_ref, hid_ref, out_ref):
    half = 1 - lax.axis_index("replica")
    parts = grads_of(half, x_ref, s_ref, dg_ref, du_ref, hid_ref)
    rows = parts[0].shape[0]
    for n in range(3):
        out_ref[n * rows : (n + 1) * rows, :] = parts[n].astype(BF)


def own_half_kernel(
    x_ref, s_ref, dg_ref, du_ref, hid_ref, came_ref, gate_ref, up_ref, down_ref
):
    parts = grads_of(lax.axis_index("replica"), x_ref, s_ref, dg_ref, du_ref, hid_ref)
    rows = parts[0].shape[0]
    for n, out_ref in enumerate((gate_ref, up_ref, down_ref)):
        came = came_ref[n * rows : (n + 1) * rows, :].astype(F32)
        out_ref[...] = (parts[n].astype(BF).astype(F32) + came).astype(BF)


def combine_kernel(ids_ref, slot_ref, gates_ref, *refs):
    token_ref, grad_ref = refs[-2:]
    doubles = 2 + len(BASES)
    ret_views = [(refs[0], 0), (refs[1], 0)]
    for kept_ref, given_ref in zip(refs[2:doubles], refs[doubles:-2]):
        ret_views += [(kept_ref, 0), (given_ref, BACK_ROWS)]
    topk, tokens = ids_ref.shape
    experts = len(ret_views)
    width = refs[0].shape[1]
    ids = ids_ref[...]
    slot = slot_ref[...]
    slot16 = repeat_rows(slot, MAIN)
    inner = jnp.bitwise_and(iota(slot16.shape, 0), MAIN - 1)
    onehot = mask(slot16 == inner)
    wanted = MAIN + jnp.right_shift(inner, 2)
    last = jnp.where(jnp.logical_and(slot16 == wanted, inner < 8), 1.0, 0.0)
    quarter = jnp.bitwise_and(inner, 3)
    tails = [ref[first + BACK_ROWS - 16 : first + BACK_ROWS, :] for ref, first in ret_views]
    tail = jnp.concatenate(tails, axis=0)
    for q in range(QUARTERS):
        main = jnp.concatenate(
            [ref[first + q * MAIN : first + (q + 1) * MAIN, :] for ref, first in ret_views], axis=0
        )
        place = jnp.where(quarter == q, last, 0.0).astype(BF)
        total = lax.dot_general(onehot, main, CONTRACT_ROWS, preferred_element_type=F32)
        total += lax.dot_general(place, tail, CONTRACT_ROWS, preferred_element_type=F32)
        token_ref[:, q * width : (q + 1) * width] = total.astype(BF)
    lane_index = iota((width, tokens), 0)
    found = []
    for c in range(experts):
        mine = slot[c : c + 1]
        lane = jnp.where(mine < MAIN, c * MAIN + mine, experts * MAIN + 2 * c + mine - MAIN)
        lane = jnp.where(mine < 0, -1, lane)
        sums = jnp.dot(tails[c], mask(lane_index == lane), preferred_element_type=F32)
        found.append(sums[8:9])
    found = jnp.concatenate(found, axis=0)
    kept = slot >= 0
    grads = jnp.where(kept, found / jnp.where(kept, gates_ref[...], 1.0), 0.0)
    expert_row = partners(experts, tokens)
    by_choice = [
        jnp.sum(jnp.where(expert_row == ids[k : k + 1], grads, 0.0), axis=0, keepdims=True)
        for k in range(topk)
    ]
    grad_ref[...] = jnp.concatenate(by_choice, axis=0).astype(BF)


def local_call(kernel, outs, arrays, name, flops, moved, space=pltpu.VMEM, scratch=(), limit=16):
    vmem = pl.BlockSpec(memory_space=pltpu.VMEM)
    return pl.pallas_call(
        kernel,
        out_shape=[jax.ShapeDtypeStruct(shape, kind) for shape, kind in outs],
        in_specs=[pl.BlockSpec(memory_space=space)] * len(arrays),
        out_specs=[vmem] * len(outs),
        scratch_shapes=list(scratch),
        compiler_params=pltpu.CompilerParams(vmem_limit_bytes=limit * MIB),
        cost_estimate=pl.CostEstimate(flops=flops, bytes_accessed=moved, transcendentals=0),
        name=name,
    )(*arrays)


def to_step(chunk, base):
    experts = lax.axis_size("expert")
    if base == 1:
        return lax.ppermute(chunk, "expert", [(i, i ^ 1) for i in range(experts)])
    pairs = [(2 * i + r, 2 * (i ^ (base + r)) + r) for i in range(experts) for r in range(2)]
    return lax.ppermute(chunk, ("expert", "replica"), pairs)


def to_twin(chunk):
    return lax.ppermute(chunk, "replica", [(0, 1), (1, 0)])


def hold_kernel(*refs):
    count = len(refs) // 2
    for source, place in zip(refs[:count], refs[count:]):
        place[...] = source[...]


def per_device_moving_rows(
    tokens,
    cotangent,
    expert_ids,
    gate_values,
    replica_pick,
    replica_plan,
    gate_proj,
    up_proj,
    down_proj,
):
    experts = lax.axis_size("expert")
    token_count, model_width = tokens.shape
    topk = expert_ids.shape[1]
    hidden_width = gate_proj.shape[2]
    width = model_width // QUARTERS
    served = experts * (MAIN + 2)
    small = (topk, token_count)
    count = len(BASES)
    self_rows, near_rows, keep, give, slot, gates = local_call(
        route_kernel,
        [((SEND_ROWS, width), BF)] * 2
        + [((count * SEND_ROWS, width), BF)] * 2
        + [((experts, token_count), jnp.int32), ((experts, token_count), F32)],
        [replica_plan, expert_ids.T, replica_pick.T, gate_values.T, tokens, cotangent],
        "route",
        2 * 2 * served * token_count * model_width,
        2 * 2 * (token_count + served) * model_width,
        space=pltpu.HBM,
        limit=58,
        scratch=[
            pltpu.SMEM((experts,), jnp.int32),
            pltpu.VMEM(small, jnp.int32),
            pltpu.VMEM(small, jnp.int32),
            pltpu.VMEM(small, BF),
            pltpu.VMEM(tokens.shape, BF),
            pltpu.VMEM(tokens.shape, BF),
            pltpu.SemaphoreType.DMA((6,)),
        ],
    )
    came = to_twin(give)
    near_rows = to_step(near_rows, 1)
    self_rows, *doubles = local_call(
        join_kernel,
        [((SEND_ROWS, width), BF)] + [((2 * SEND_ROWS, width), BF)] * count,
        [self_rows, keep, came],
        "join",
        0,
        2 * 2 * 7 * SEND_ROWS * width,
    )
    recv = [self_rows, near_rows, *map(to_step, doubles, BASES)]
    matrices = [gate_proj[0], up_proj[0], down_proj[0]]
    matrices = local_call(
        hold_kernel,
        [(array.shape, BF) for array in matrices],
        matrices,
        "hold",
        0,
        4 * 3 * model_width * hidden_width,
    )
    matmul = 2 * served * model_width * hidden_width
    outs = local_call(
        expert_kernel,
        [((BACK_ROWS, width), BF)] * 2
        + [((2 * BACK_ROWS, width), BF)] * count
        + [((served, model_width), BF)] * 2
        + [((served, hidden_width), BF)] * 3,
        [*recv, *matrices],
        "expert_rows",
        5 * matmul,
        2 * 3 * model_width * hidden_width,
    )
    backs, factors = outs[: 2 + count], outs[2 + count :]
    kept = list(map(to_step, backs[2:], BASES))
    returned = [backs[0], to_step(backs[1], 1), *kept, *map(to_twin, kept)]
    half = model_width // 2
    (leaving,) = local_call(
        other_half_kernel,
        [((3 * half, hidden_width), BF)],
        factors,
        "other_half",
        1,
        1,
    )
    shares = local_call(
        own_half_kernel,
        [((half, hidden_width), BF)] * 3,
        [*factors, to_twin(leaving)],
        "own_half",
        1,
        1,
    )
    returned, shares = lax.optimization_barrier((returned, shares))
    token_grad, gate_grad = local_call(
        combine_kernel,
        [((token_count, model_width), BF), ((topk, token_count), BF)],
        [expert_ids.T, slot, gates, *returned],
        "combine",
        2 * served * token_count * model_width,
        2 * 2 * token_count * model_width,
    )
    return (token_grad, gate_grad.T, shares[0][None], shares[1][None], shares[2][None])


def per_device(tokens, cotangent, expert_ids, gate_values, replica_pick, replica_plan, *matrices):
    experts = lax.axis_size("expert")
    slots = (copies_of(experts) + 1) * CAP
    row_bytes = 3 * 2 * tokens.shape[1] * experts
    matrix_bytes = 4 * sum(2 * m[0].size for m in matrices)
    fits = slots == MAIN + 2 and experts == 8 and lax.axis_size("replica") == 2
    rows_cheaper = slots * row_bytes < 2 * CAP * row_bytes + matrix_bytes
    plan = per_device_moving_rows if fits and rows_cheaper else per_device_moving_weights
    return plan(
        tokens, cotangent, expert_ids, gate_values, replica_pick, replica_plan, *matrices
    )


def solution(mesh):
    placed = (
        P(("parts", "expert", "replica"), None),
        P(("parts", "expert", "replica"), None),
        P(("parts", "expert", "replica"), None),
        P(("parts", "expert", "replica"), None),
        P(("parts", "expert", "replica"), None),
        P("parts"),
        P("expert", None, None),
        P("expert", None, None),
        P("expert", None, None),
    )
    return jax.shard_map(
        per_device,
        mesh=mesh,
        in_specs=placed,
        out_specs=(
            P(("parts", "expert", "replica"), None),
            P(("parts", "expert", "replica"), None),
            P(("parts", "expert"), "replica", None),
            P(("parts", "expert"), "replica", None),
            P(("parts", "expert"), "replica", None),
        ),
        check_vma=False,
    )
```

```python
import jax
import jax.numpy as jnp
from jax import lax
from jax.experimental import pallas as pl
from jax.experimental.pallas import tpu as pltpu
from jax.sharding import PartitionSpec as P

CAP = 6


def route_assignments(flat_ids, flat_pick, replica_plan, capacity):
    experts = replica_plan.shape[0]
    lane_ids = jnp.arange(experts, dtype=jnp.int32)
    same_plan = replica_plan[:, None] == replica_plan[None, :]
    earlier = lane_ids[None, :] < lane_ids[:, None]
    position = jnp.sum(jnp.logical_and(same_plan, earlier), axis=1)
    hot_mask = jnp.any(replica_plan[None, :] == lane_ids[:, None], axis=1)
    is_hot = jnp.any(
        jnp.logical_and(flat_ids[:, None] == lane_ids[None, :], hot_mask[None, :]), axis=1
    )
    use_copy = jnp.logical_and(is_hot, flat_pick >= 1)
    matches = jnp.logical_and(
        replica_plan[None, :] == flat_ids[:, None], position[None, :] == flat_pick[:, None] - 1
    )
    holder = jnp.sum(jnp.where(matches, lane_ids[None, :], 0), axis=1)
    target = jnp.where(use_copy, holder, flat_ids)
    copy_role = use_copy.astype(jnp.int32)
    bucket = target * 2 + copy_role
    sequence = jnp.arange(bucket.shape[0], dtype=jnp.int32)
    arrival = jnp.sum(
        jnp.logical_and(bucket[None, :] == bucket[:, None], sequence[None, :] < sequence[:, None]),
        axis=1,
    )
    kept_mask = arrival < capacity
    slot_index = target * (2 * capacity) + copy_role * capacity + jnp.minimum(arrival, capacity - 1)
    return (slot_index, kept_mask)


def fill_slots(slot_index, kept_mask, slot_count):
    slot_ids = jnp.arange(slot_count, dtype=jnp.int32)
    matches = jnp.logical_and(slot_index[None, :] == slot_ids[:, None], kept_mask[None, :])
    sequence = jnp.arange(slot_index.shape[0], dtype=jnp.int32)
    source = jnp.sum(jnp.where(matches, sequence[None, :], 0), axis=1)
    filled = jnp.any(matches, axis=1)
    return (source, filled)


def expert_backward(row_block, upstream, weight, gate_w, up_w, down_w):
    contract_cols = (((1,), (1,)), ((), ()))
    contract_rows = (((0,), (0,)), ((), ()))
    gate_pre = jnp.dot(row_block, gate_w, preferred_element_type=jnp.float32)
    up_pre = jnp.dot(row_block, up_w, preferred_element_type=jnp.float32)
    sigmoid_gate = jax.nn.sigmoid(gate_pre)
    activated = gate_pre * sigmoid_gate
    hidden = (activated * up_pre).astype(jnp.bfloat16)
    output_rows = lax.dot_general(hidden, down_w, contract_cols, preferred_element_type=jnp.float32)
    weight_col = weight.astype(jnp.float32)[:, None]
    upstream_f = upstream.astype(jnp.float32)
    gate_rows = jnp.sum(upstream_f * output_rows, axis=1)
    hidden_grad = weight_col * jnp.dot(upstream, down_w, preferred_element_type=jnp.float32)
    slope = sigmoid_gate * (1.0 + gate_pre * (1.0 - sigmoid_gate))
    gate_delta = (hidden_grad * up_pre * slope).astype(jnp.bfloat16)
    up_delta = (hidden_grad * activated).astype(jnp.bfloat16)
    input_grad = (
        lax.dot_general(gate_delta, gate_w, contract_cols, preferred_element_type=jnp.float32)
        + lax.dot_general(up_delta, up_w, contract_cols, preferred_element_type=jnp.float32)
    ).astype(jnp.bfloat16)
    scaled = (weight_col * upstream_f).astype(jnp.bfloat16)
    grad_set = (
        lax.dot_general(row_block, gate_delta, contract_rows, preferred_element_type=jnp.float32),
        lax.dot_general(row_block, up_delta, contract_rows, preferred_element_type=jnp.float32),
        lax.dot_general(scaled, hidden, contract_rows, preferred_element_type=jnp.float32),
    )
    return (input_grad, gate_rows, grad_set)


def per_device_moving_weights(
    tokens,
    cotangent,
    expert_ids,
    gate_values,
    replica_pick,
    replica_plan,
    gate_proj,
    up_proj,
    down_proj,
):
    experts = lax.axis_size("expert")
    capacity = CAP
    slot_total = 2 * capacity
    model_width = tokens.shape[1]
    topk = expert_ids.shape[1]
    token_count = tokens.shape[0]
    slot_index, kept_mask = route_assignments(
        expert_ids.reshape(-1), replica_pick.reshape(-1), replica_plan, capacity
    )
    source, filled = fill_slots(slot_index, kept_mask, experts * slot_total)
    token_of = source // topk
    zero_half = jnp.zeros((), jnp.bfloat16)
    send_rows = jnp.where(filled[:, None], jnp.take(tokens, token_of, axis=0), zero_half).reshape(
        experts, slot_total, model_width
    )
    send_upstream = jnp.where(
        filled[:, None], jnp.take(cotangent, token_of, axis=0), zero_half
    ).reshape(experts, slot_total, model_width)
    send_weight = jnp.where(filled, gate_values.reshape(-1)[source], zero_half).reshape(
        experts, slot_total
    )
    arrived = lax.all_to_all(send_rows, "expert", split_axis=0, concat_axis=0, tiled=True)
    own_gate = gate_proj[0]
    own_up = up_proj[0]
    own_down = down_proj[0]
    hidden_width = own_gate.shape[1]
    spread = (
        lax.all_to_all(
            own_gate.reshape(experts, -1), "expert", split_axis=0, concat_axis=0, tiled=True
        ),
        lax.all_to_all(
            own_up.reshape(experts, -1), "expert", split_axis=0, concat_axis=0, tiled=True
        ),
        lax.all_to_all(
            own_down.reshape(experts, -1), "expert", split_axis=0, concat_axis=0, tiled=True
        ),
    )
    chosen_gate = jnp.take(spread[0], replica_plan, axis=0)
    chosen_up = jnp.take(spread[1], replica_plan, axis=0)
    chosen_down = jnp.take(spread[2], replica_plan, axis=0)
    collected = (
        lax.all_to_all(chosen_gate, "expert", split_axis=0, concat_axis=0, tiled=True),
        lax.all_to_all(chosen_up, "expert", split_axis=0, concat_axis=0, tiled=True),
        lax.all_to_all(chosen_down, "expert", split_axis=0, concat_axis=0, tiled=True),
    )
    copy_gate = collected[0].reshape(model_width, hidden_width)
    copy_up = collected[1].reshape(model_width, hidden_width)
    copy_down = collected[2].reshape(model_width, hidden_width)
    arrived_up, arrived_weight = (
        lax.all_to_all(send_upstream, "expert", split_axis=0, concat_axis=0, tiled=True),
        lax.all_to_all(send_weight, "expert", split_axis=0, concat_axis=0, tiled=True),
    )
    owned_dx, owned_gate_rows, owned_grads = expert_backward(
        arrived[:, :capacity].reshape(-1, model_width),
        arrived_up[:, :capacity].reshape(-1, model_width),
        arrived_weight[:, :capacity].reshape(-1),
        own_gate,
        own_up,
        own_down,
    )
    copied_dx, copied_gate_rows, copied_grads = expert_backward(
        arrived[:, capacity:].reshape(-1, model_width),
        arrived_up[:, capacity:].reshape(-1, model_width),
        arrived_weight[:, capacity:].reshape(-1),
        copy_gate,
        copy_up,
        copy_down,
    )
    back_rows = jnp.concatenate(
        [
            owned_dx.reshape(experts, capacity, model_width),
            copied_dx.reshape(experts, capacity, model_width),
        ],
        axis=1,
    )
    back_gate = jnp.concatenate(
        [owned_gate_rows.reshape(experts, capacity), copied_gate_rows.reshape(experts, capacity)],
        axis=1,
    ).astype(jnp.bfloat16)
    returned, returned_gate = (
        lax.all_to_all(back_rows, "expert", split_axis=0, concat_axis=0, tiled=True),
        lax.all_to_all(back_gate, "expert", split_axis=0, concat_axis=0, tiled=True),
    )
    copy_pieces = (
        copied_grads[0].astype(jnp.bfloat16).reshape(experts, -1),
        copied_grads[1].astype(jnp.bfloat16).reshape(experts, -1),
        copied_grads[2].astype(jnp.bfloat16).reshape(experts, -1),
    )
    grad_spread = (
        lax.all_to_all(copy_pieces[0], "expert", split_axis=0, concat_axis=0, tiled=True),
        lax.all_to_all(copy_pieces[1], "expert", split_axis=0, concat_axis=0, tiled=True),
        lax.all_to_all(copy_pieces[2], "expert", split_axis=0, concat_axis=0, tiled=True),
    )
    lane_ids = jnp.arange(experts, dtype=jnp.int32)
    owner_map = (replica_plan[None, :] == lane_ids[:, None]).astype(jnp.bfloat16)
    summed_gate = jnp.dot(owner_map, grad_spread[0], preferred_element_type=jnp.float32).astype(
        jnp.bfloat16
    )
    summed_up = jnp.dot(owner_map, grad_spread[1], preferred_element_type=jnp.float32).astype(
        jnp.bfloat16
    )
    summed_down = jnp.dot(owner_map, grad_spread[2], preferred_element_type=jnp.float32).astype(
        jnp.bfloat16
    )
    grad_back = (
        lax.all_to_all(summed_gate, "expert", split_axis=0, concat_axis=0, tiled=True),
        lax.all_to_all(summed_up, "expert", split_axis=0, concat_axis=0, tiled=True),
        lax.all_to_all(summed_down, "expert", split_axis=0, concat_axis=0, tiled=True),
    )
    total_gate = owned_grads[0] + grad_back[0].reshape(model_width, hidden_width).astype(
        jnp.float32
    )
    total_up = owned_grads[1] + grad_back[1].reshape(model_width, hidden_width).astype(jnp.float32)
    total_down = owned_grads[2] + grad_back[2].reshape(model_width, hidden_width).astype(
        jnp.float32
    )
    shares = (
        lax.psum_scatter(
            total_gate.astype(jnp.bfloat16), "replica", scatter_dimension=0, tiled=True
        ).astype(jnp.float32),
        lax.psum_scatter(
            total_up.astype(jnp.bfloat16), "replica", scatter_dimension=0, tiled=True
        ).astype(jnp.float32),
        lax.psum_scatter(
            total_down.astype(jnp.bfloat16), "replica", scatter_dimension=0, tiled=True
        ).astype(jnp.float32),
    )
    flat_back = returned.reshape(experts * slot_total, model_width)
    picked_rows = jnp.take(flat_back, slot_index, axis=0)
    picked_rows = jnp.where(kept_mask[:, None], picked_rows, zero_half).astype(jnp.float32)
    token_grad = jnp.sum(picked_rows.reshape(token_count, topk, model_width), axis=1).astype(
        jnp.bfloat16
    )
    gate_grad = jnp.where(kept_mask, returned_gate.reshape(-1)[slot_index], zero_half).reshape(
        token_count, topk
    )
    return (
        token_grad,
        gate_grad,
        shares[0].astype(jnp.bfloat16)[None],
        shares[1].astype(jnp.bfloat16)[None],
        shares[2].astype(jnp.bfloat16)[None],
    )


BF = jnp.bfloat16
F32 = jnp.float32
CONTRACT_ROWS = (((0,), (0,)), ((), ()))
CONTRACT_COLS = (((1,), (1,)), ((), ()))
MIB = 1024 * 1024

MAIN = 16
QUARTERS = 4
SEND_ROWS = 2 * QUARTERS * MAIN + 16
BACK_ROWS = QUARTERS * MAIN + 16
STEPS = (0, 1, 4, 5, 6, 7, 2, 3)


def copies_of(experts):
    return 2 if experts <= 8 else 8


def iota(shape, axis):
    return lax.broadcasted_iota(jnp.int32, shape, axis)


def partners(experts, tokens):
    row = iota((experts, tokens), 0)
    step = jnp.zeros((experts, tokens), jnp.int32)
    for c in range(1, experts):
        step = jnp.where(row == c, STEPS[c], step)
    return jnp.bitwise_xor(step, lax.axis_index("expert"))


def mask(condition):
    return condition.astype(F32).astype(BF)


def repeat_rows(table, times):
    width = table.shape[1]
    return jnp.concatenate(
        [jnp.broadcast_to(table[e : e + 1], (times, width)) for e in range(table.shape[0])], axis=0
    )


def route_kernel(plan_hbm, ids_hbm, pick_hbm, gate_hbm, tok_hbm, cot_hbm, *refs):
    sems = refs[-1]
    plan_ref, ids_ref, pick_ref, gate_ref, tok_ref, cot_ref = refs[-7:-1]
    slot_ref, gates_ref = refs[-9:-7]
    send_refs = refs[:-9]
    topk, tokens = ids_ref.shape
    experts = len(send_refs)
    width = tok_ref.shape[1] // QUARTERS
    copies = copies_of(experts)
    loads = [
        pltpu.make_async_copy(source, place, sems.at[n])
        for n, (source, place) in enumerate(
            (
                (plan_hbm, plan_ref),
                (ids_hbm, ids_ref),
                (pick_hbm, pick_ref),
                (gate_hbm, gate_ref),
                (tok_hbm, tok_ref),
                (cot_hbm, cot_ref),
            )
        )
    ]
    for load in loads:
        load.start()
    before = mask(iota((tokens, tokens), 0) < iota((tokens, tokens), 1))
    expert_row = partners(experts, tokens)
    for load in loads[:4]:
        load.wait()
    ids = ids_ref[...]
    pick = pick_ref[...]
    gate = gate_ref[...].astype(F32)
    named = jnp.zeros((experts, tokens), jnp.int32)
    gates = jnp.zeros((experts, tokens), F32)
    for k in range(topk):
        hit = ids[k : k + 1] == expert_row
        named = jnp.where(hit, pick[k : k + 1] + 1, named)
        gates = jnp.where(hit, gate[k : k + 1], gates)
    hot = jnp.zeros((experts, tokens), jnp.int32)
    for j in range(experts):
        hot = jnp.where(expert_row == plan_ref[j], 1, hot)
    chosen = jnp.where(named == 0, -1, jnp.where(hot > 0, named - 1, 0))
    masks = jnp.concatenate([(chosen == c).astype(F32) for c in range(copies + 1)], axis=0)
    rank = jnp.dot(masks.astype(BF), before, preferred_element_type=F32).astype(jnp.int32)
    slot = jnp.full((experts, tokens), -1, jnp.int32)
    for c in range(copies + 1):
        rank_c = rank[c * experts : (c + 1) * experts]
        keep = jnp.logical_and(chosen == c, rank_c < CAP)
        slot = jnp.where(keep, c * CAP + rank_c, slot)
    slot_ref[...] = slot
    gates_ref[...] = gates
    slot16 = repeat_rows(slot, MAIN)
    gate16 = repeat_rows(gates, MAIN)
    inner = jnp.bitwise_and(iota(slot16.shape, 0), MAIN - 1)
    onehot = (slot16 == inner).astype(F32)
    wanted = MAIN + jnp.bitwise_and(jnp.right_shift(inner, 2), 1)
    last = (slot16 == wanted).astype(F32)
    last_rows = jnp.where(inner >= 8, 0.0, last)
    last_scaled = jnp.where(inner >= 8, last * gate16, 0.0)
    quarter = jnp.bitwise_and(inner, 3)
    for load in loads[4:]:
        load.wait()
    rows = jnp.dot(onehot.astype(BF), tok_ref[...], preferred_element_type=F32).astype(BF)
    scaled = jnp.dot(
        (onehot * gate16).astype(BF), cot_ref[...], preferred_element_type=F32
    ).astype(BF)
    tail = jnp.zeros((experts * MAIN, width), F32)
    for q in range(QUARTERS):
        cols = slice(q * width, (q + 1) * width)
        mine = quarter == q
        tail += jnp.dot(
            jnp.where(mine, last_rows, 0.0).astype(BF), tok_ref[:, cols], preferred_element_type=F32
        )
        tail += jnp.dot(
            jnp.where(mine, last_scaled, 0.0).astype(BF),
            cot_ref[:, cols],
            preferred_element_type=F32,
        )
    tail = tail.astype(BF)
    for k in range(experts):
        here = slice(k * MAIN, (k + 1) * MAIN)
        for q in range(QUARTERS):
            cols = slice(q * width, (q + 1) * width)
            send_refs[k][q * MAIN : (q + 1) * MAIN, :] = rows[here, cols]
            send_refs[k][(QUARTERS + q) * MAIN : (QUARTERS + q + 1) * MAIN, :] = scaled[here, cols]
        send_refs[k][2 * QUARTERS * MAIN :, :] = tail[here]


def expert_kernel(*refs):
    experts = len(refs) - 9
    recv_refs = refs[:experts]
    gate_ref, up_ref, down_ref, back_ref = refs[experts : experts + 4]
    x_ref, s_ref, dg_ref, du_ref, hid_ref = refs[experts + 4 :]
    me = lax.axis_index("expert")
    width = recv_refs[0].shape[1]
    main_rows = experts * MAIN
    tail = jnp.concatenate([ref[2 * QUARTERS * MAIN :, :] for ref in recv_refs], axis=0)
    row = iota((4 * experts, main_rows), 0)
    col = iota((4 * experts, main_rows), 1)
    kind = (row >= 2 * experts).astype(jnp.int32)
    chunk = jnp.right_shift(row - kind * 2 * experts, 1)
    base = chunk * MAIN + kind * 8 + jnp.bitwise_and(row, 1) * 4
    for q in range(QUARTERS):
        cols = slice(q * width, (q + 1) * width)
        picked = jnp.dot(mask(col == base + q), tail, preferred_element_type=F32).astype(BF)
        x_ref[main_rows:, cols] = picked[: 2 * experts]
        s_ref[main_rows:, cols] = picked[2 * experts :]
        for i, ref in enumerate(recv_refs):
            here = slice(i * MAIN, (i + 1) * MAIN)
            x_ref[here, cols] = ref[q * MAIN : (q + 1) * MAIN, :]
            s_ref[here, cols] = ref[(QUARTERS + q) * MAIN : (QUARTERS + q + 1) * MAIN, :]
    rows = x_ref[...]
    gate_pre = jnp.dot(rows, gate_ref[...], preferred_element_type=F32)
    up_pre = jnp.dot(rows, up_ref[...], preferred_element_type=F32)
    hidden_grad = jnp.dot(s_ref[...], down_ref[...], preferred_element_type=F32)
    sig = jax.nn.sigmoid(gate_pre)
    activated = gate_pre * sig
    hidden = (activated * up_pre).astype(BF)
    slope = sig * (1.0 + gate_pre * (1.0 - sig))
    gate_delta = (hidden_grad * up_pre * slope).astype(BF)
    up_delta = (hidden_grad * activated).astype(BF)
    hid_ref[...] = hidden
    dg_ref[...] = gate_delta
    du_ref[...] = up_delta
    grad = (
        lax.dot_general(gate_delta, gate_ref[...], CONTRACT_COLS, preferred_element_type=F32)
        + lax.dot_general(up_delta, up_ref[...], CONTRACT_COLS, preferred_element_type=F32)
    ).astype(BF)
    product = hidden.astype(F32) * hidden_grad
    product = jnp.concatenate(
        [product, jnp.zeros((width - product.shape[0], product.shape[1]), F32)], axis=0
    )
    gate_lanes = lax.dot_general(
        jnp.ones((8, product.shape[1]), F32),
        product,
        CONTRACT_COLS,
        preferred_element_type=F32,
        precision=lax.Precision.HIGHEST,
    )
    trow = iota((main_rows, 2 * experts), 0)
    tcol = iota((main_rows, 2 * experts), 1)
    inner = jnp.bitwise_and(trow, MAIN - 1)
    source = jnp.right_shift(trow, 4) * 2 + jnp.right_shift(inner, 2)
    spread = jnp.zeros((main_rows, width), F32)
    for q in range(QUARTERS):
        cols = slice(q * width, (q + 1) * width)
        mine = jnp.logical_and(jnp.bitwise_and(inner, 3) == q, inner < 8)
        place = mask(jnp.logical_and(mine, tcol == source))
        spread += jnp.dot(place, grad[main_rows:, cols], preferred_element_type=F32)
        for i, step in enumerate(STEPS):
            back_ref[me ^ step, q * MAIN : (q + 1) * MAIN, :] = grad[i * MAIN : (i + 1) * MAIN, cols]
    for i, step in enumerate(STEPS):
        back_ref[me ^ step, QUARTERS * MAIN :, :] = jnp.concatenate(
            [spread[i * MAIN : i * MAIN + 8], gate_lanes], axis=0
        ).astype(BF)


def grads_of(half, x_ref, s_ref, dg_ref, du_ref, hid_ref):
    rows = x_ref.shape[1] // 2
    cols = pl.ds(pl.multiple_of(half * rows, rows), rows)
    x_half = x_ref[:, cols]
    s_half = s_ref[:, cols]
    return (
        lax.dot_general(x_half, dg_ref[...], CONTRACT_ROWS, preferred_element_type=F32),
        lax.dot_general(x_half, du_ref[...], CONTRACT_ROWS, preferred_element_type=F32),
        lax.dot_general(s_half, hid_ref[...], CONTRACT_ROWS, preferred_element_type=F32),
    )


def other_half_kernel(x_ref, s_ref, dg_ref, du_ref, hid_ref, out_ref):
    half = 1 - lax.axis_index("replica")
    parts = grads_of(half, x_ref, s_ref, dg_ref, du_ref, hid_ref)
    rows = parts[0].shape[0]
    for n in range(3):
        out_ref[n * rows : (n + 1) * rows, :] = parts[n].astype(BF)


def own_half_kernel(
    x_ref, s_ref, dg_ref, du_ref, hid_ref, came_ref, gate_ref, up_ref, down_ref
):
    parts = grads_of(lax.axis_index("replica"), x_ref, s_ref, dg_ref, du_ref, hid_ref)
    rows = parts[0].shape[0]
    for n, out_ref in enumerate((gate_ref, up_ref, down_ref)):
        came = came_ref[n * rows : (n + 1) * rows, :].astype(F32)
        out_ref[...] = (parts[n].astype(BF).astype(F32) + came).astype(BF)


def combine_kernel(ids_ref, slot_ref, gates_ref, ret_ref, token_ref, grad_ref):
    topk, tokens = ids_ref.shape
    experts, unused, width = ret_ref.shape
    me = lax.axis_index("expert")
    places = [me ^ step for step in STEPS]
    ids = ids_ref[...]
    slot = slot_ref[...]
    slot16 = repeat_rows(slot, MAIN)
    inner = jnp.bitwise_and(iota(slot16.shape, 0), MAIN - 1)
    onehot = mask(slot16 == inner)
    wanted = MAIN + jnp.right_shift(inner, 2)
    last = jnp.where(jnp.logical_and(slot16 == wanted, inner < 8), 1.0, 0.0)
    quarter = jnp.bitwise_and(inner, 3)
    tails = [ret_ref[place, QUARTERS * MAIN :, :] for place in places]
    tail = jnp.concatenate(tails, axis=0)
    for q in range(QUARTERS):
        main = jnp.concatenate(
            [ret_ref[place, q * MAIN : (q + 1) * MAIN, :] for place in places], axis=0
        )
        place = jnp.where(quarter == q, last, 0.0).astype(BF)
        total = lax.dot_general(onehot, main, CONTRACT_ROWS, preferred_element_type=F32)
        total += lax.dot_general(place, tail, CONTRACT_ROWS, preferred_element_type=F32)
        token_ref[:, q * width : (q + 1) * width] = total.astype(BF)
    lane_index = iota((width, tokens), 0)
    found = []
    for c in range(experts):
        mine = slot[c : c + 1]
        lane = jnp.where(mine < MAIN, c * MAIN + mine, experts * MAIN + 2 * c + mine - MAIN)
        lane = jnp.where(mine < 0, -1, lane)
        sums = jnp.dot(tails[c], mask(lane_index == lane), preferred_element_type=F32)
        found.append(sums[8:9])
    found = jnp.concatenate(found, axis=0)
    kept = slot >= 0
    grads = jnp.where(kept, found / jnp.where(kept, gates_ref[...], 1.0), 0.0)
    expert_row = partners(experts, tokens)
    by_choice = [
        jnp.sum(jnp.where(expert_row == ids[k : k + 1], grads, 0.0), axis=0, keepdims=True)
        for k in range(topk)
    ]
    grad_ref[...] = jnp.concatenate(by_choice, axis=0).astype(BF)


def local_call(kernel, outs, arrays, name, flops, moved, space=pltpu.VMEM, scratch=(), limit=16):
    vmem = pl.BlockSpec(memory_space=pltpu.VMEM)
    return pl.pallas_call(
        kernel,
        out_shape=[jax.ShapeDtypeStruct(shape, kind) for shape, kind in outs],
        in_specs=[pl.BlockSpec(memory_space=space)] * len(arrays),
        out_specs=[vmem] * len(outs),
        scratch_shapes=list(scratch),
        compiler_params=pltpu.CompilerParams(vmem_limit_bytes=limit * MIB),
        cost_estimate=pl.CostEstimate(flops=flops, bytes_accessed=moved, transcendentals=0),
        name=name,
    )(*arrays)


def exchange(chunks):
    count = len(chunks)
    moved = [
        lax.ppermute(chunk, "expert", [(i, i ^ step) for i in range(count)])
        for chunk, step in zip(chunks[1:], STEPS[1:])
    ]
    return [chunks[0], *moved]


def hold_kernel(*refs):
    count = len(refs) // 2
    for source, place in zip(refs[:count], refs[count:]):
        place[...] = source[...]


def per_device_moving_rows(
    tokens,
    cotangent,
    expert_ids,
    gate_values,
    replica_pick,
    replica_plan,
    gate_proj,
    up_proj,
    down_proj,
):
    experts = lax.axis_size("expert")
    token_count, model_width = tokens.shape
    topk = expert_ids.shape[1]
    hidden_width = gate_proj.shape[2]
    width = model_width // QUARTERS
    served = experts * (MAIN + 2)
    small = (topk, token_count)
    routed = local_call(
        route_kernel,
        [((SEND_ROWS, width), BF)] * experts
        + [((experts, token_count), jnp.int32), ((experts, token_count), F32)],
        [replica_plan, expert_ids.T, replica_pick.T, gate_values.T, tokens, cotangent],
        "route",
        2 * 2 * served * token_count * model_width,
        2 * 2 * (token_count + served) * model_width,
        space=pltpu.HBM,
        limit=58,
        scratch=[
            pltpu.SMEM((experts,), jnp.int32),
            pltpu.VMEM(small, jnp.int32),
            pltpu.VMEM(small, jnp.int32),
            pltpu.VMEM(small, BF),
            pltpu.VMEM(tokens.shape, BF),
            pltpu.VMEM(tokens.shape, BF),
            pltpu.SemaphoreType.DMA((6,)),
        ],
    )
    slot, gates = routed[experts:]
    recv = exchange(routed[:experts])
    held = [recv[0], gate_proj[0], up_proj[0], down_proj[0]]
    held = local_call(
        hold_kernel,
        [(array.shape, BF) for array in held],
        held,
        "hold",
        0,
        4 * 3 * model_width * hidden_width,
    )
    matmul = 2 * served * model_width * hidden_width
    back, *factors = local_call(
        expert_kernel,
        [((experts, BACK_ROWS, width), BF)]
        + [((served, model_width), BF)] * 2
        + [((served, hidden_width), BF)] * 3,
        [held[0], *recv[1:], *held[1:]],
        "expert_rows",
        5 * matmul,
        2 * 3 * model_width * hidden_width,
    )
    returned = lax.all_to_all(back, "expert", split_axis=0, concat_axis=0, tiled=True)
    half = model_width // 2
    (leaving,) = local_call(
        other_half_kernel,
        [((3 * half, hidden_width), BF)],
        factors,
        "other_half",
        1,
        1,
    )
    came = lax.ppermute(leaving, "replica", [(0, 1), (1, 0)])
    shares = local_call(
        own_half_kernel,
        [((half, hidden_width), BF)] * 3,
        [*factors, came],
        "own_half",
        1,
        1,
    )
    returned, shares = lax.optimization_barrier((returned, shares))
    token_grad, gate_grad = local_call(
        combine_kernel,
        [((token_count, model_width), BF), ((topk, token_count), BF)],
        [expert_ids.T, slot, gates, returned],
        "combine",
        2 * served * token_count * model_width,
        2 * 2 * token_count * model_width,
    )
    return (token_grad, gate_grad.T, shares[0][None], shares[1][None], shares[2][None])


def per_device(tokens, cotangent, expert_ids, gate_values, replica_pick, replica_plan, *matrices):
    experts = lax.axis_size("expert")
    slots = (copies_of(experts) + 1) * CAP
    row_bytes = 3 * 2 * tokens.shape[1] * experts
    matrix_bytes = 4 * sum(2 * m[0].size for m in matrices)
    fits = slots == MAIN + 2 and experts == 8 and lax.axis_size("replica") == 2
    rows_cheaper = slots * row_bytes < 2 * CAP * row_bytes + matrix_bytes
    plan = per_device_moving_rows if fits and rows_cheaper else per_device_moving_weights
    return plan(
        tokens, cotangent, expert_ids, gate_values, replica_pick, replica_plan, *matrices
    )


def solution(mesh):
    placed = (
        P(("parts", "expert", "replica"), None),
        P(("parts", "expert", "replica"), None),
        P(("parts", "expert", "replica"), None),
        P(("parts", "expert", "replica"), None),
        P(("parts", "expert", "replica"), None),
        P("parts"),
        P("expert", None, None),
        P("expert", None, None),
        P("expert", None, None),
    )
    return jax.shard_map(
        per_device,
        mesh=mesh,
        in_specs=placed,
        out_specs=(
            P(("parts", "expert", "replica"), None),
            P(("parts", "expert", "replica"), None),
            P(("parts", "expert"), "replica", None),
            P(("parts", "expert"), "replica", None),
            P(("parts", "expert"), "replica", None),
        ),
        check_vma=False,
    )
```

```python
import jax
import jax.numpy as jnp
from jax import lax
from jax.experimental import pallas as pl
from jax.experimental.pallas import tpu as pltpu
from jax.sharding import PartitionSpec as P

CAP = 6


def route_assignments(flat_ids, flat_pick, replica_plan, capacity):
    experts = replica_plan.shape[0]
    lane_ids = jnp.arange(experts, dtype=jnp.int32)
    same_plan = replica_plan[:, None] == replica_plan[None, :]
    earlier = lane_ids[None, :] < lane_ids[:, None]
    position = jnp.sum(jnp.logical_and(same_plan, earlier), axis=1)
    hot_mask = jnp.any(replica_plan[None, :] == lane_ids[:, None], axis=1)
    is_hot = jnp.any(
        jnp.logical_and(flat_ids[:, None] == lane_ids[None, :], hot_mask[None, :]), axis=1
    )
    use_copy = jnp.logical_and(is_hot, flat_pick >= 1)
    matches = jnp.logical_and(
        replica_plan[None, :] == flat_ids[:, None], position[None, :] == flat_pick[:, None] - 1
    )
    holder = jnp.sum(jnp.where(matches, lane_ids[None, :], 0), axis=1)
    target = jnp.where(use_copy, holder, flat_ids)
    copy_role = use_copy.astype(jnp.int32)
    bucket = target * 2 + copy_role
    sequence = jnp.arange(bucket.shape[0], dtype=jnp.int32)
    arrival = jnp.sum(
        jnp.logical_and(bucket[None, :] == bucket[:, None], sequence[None, :] < sequence[:, None]),
        axis=1,
    )
    kept_mask = arrival < capacity
    slot_index = target * (2 * capacity) + copy_role * capacity + jnp.minimum(arrival, capacity - 1)
    return (slot_index, kept_mask)


def fill_slots(slot_index, kept_mask, slot_count):
    slot_ids = jnp.arange(slot_count, dtype=jnp.int32)
    matches = jnp.logical_and(slot_index[None, :] == slot_ids[:, None], kept_mask[None, :])
    sequence = jnp.arange(slot_index.shape[0], dtype=jnp.int32)
    source = jnp.sum(jnp.where(matches, sequence[None, :], 0), axis=1)
    filled = jnp.any(matches, axis=1)
    return (source, filled)


def expert_backward(row_block, upstream, weight, gate_w, up_w, down_w):
    contract_cols = (((1,), (1,)), ((), ()))
    contract_rows = (((0,), (0,)), ((), ()))
    gate_pre = jnp.dot(row_block, gate_w, preferred_element_type=jnp.float32)
    up_pre = jnp.dot(row_block, up_w, preferred_element_type=jnp.float32)
    sigmoid_gate = jax.nn.sigmoid(gate_pre)
    activated = gate_pre * sigmoid_gate
    hidden = (activated * up_pre).astype(jnp.bfloat16)
    output_rows = lax.dot_general(hidden, down_w, contract_cols, preferred_element_type=jnp.float32)
    weight_col = weight.astype(jnp.float32)[:, None]
    upstream_f = upstream.astype(jnp.float32)
    gate_rows = jnp.sum(upstream_f * output_rows, axis=1)
    hidden_grad = weight_col * jnp.dot(upstream, down_w, preferred_element_type=jnp.float32)
    slope = sigmoid_gate * (1.0 + gate_pre * (1.0 - sigmoid_gate))
    gate_delta = (hidden_grad * up_pre * slope).astype(jnp.bfloat16)
    up_delta = (hidden_grad * activated).astype(jnp.bfloat16)
    input_grad = (
        lax.dot_general(gate_delta, gate_w, contract_cols, preferred_element_type=jnp.float32)
        + lax.dot_general(up_delta, up_w, contract_cols, preferred_element_type=jnp.float32)
    ).astype(jnp.bfloat16)
    scaled = (weight_col * upstream_f).astype(jnp.bfloat16)
    grad_set = (
        lax.dot_general(row_block, gate_delta, contract_rows, preferred_element_type=jnp.float32),
        lax.dot_general(row_block, up_delta, contract_rows, preferred_element_type=jnp.float32),
        lax.dot_general(scaled, hidden, contract_rows, preferred_element_type=jnp.float32),
    )
    return (input_grad, gate_rows, grad_set)


def per_device_moving_weights(
    tokens,
    cotangent,
    expert_ids,
    gate_values,
    replica_pick,
    replica_plan,
    gate_proj,
    up_proj,
    down_proj,
):
    experts = lax.axis_size("expert")
    capacity = CAP
    slot_total = 2 * capacity
    model_width = tokens.shape[1]
    topk = expert_ids.shape[1]
    token_count = tokens.shape[0]
    slot_index, kept_mask = route_assignments(
        expert_ids.reshape(-1), replica_pick.reshape(-1), replica_plan, capacity
    )
    source, filled = fill_slots(slot_index, kept_mask, experts * slot_total)
    token_of = source // topk
    zero_half = jnp.zeros((), jnp.bfloat16)
    send_rows = jnp.where(filled[:, None], jnp.take(tokens, token_of, axis=0), zero_half).reshape(
        experts, slot_total, model_width
    )
    send_upstream = jnp.where(
        filled[:, None], jnp.take(cotangent, token_of, axis=0), zero_half
    ).reshape(experts, slot_total, model_width)
    send_weight = jnp.where(filled, gate_values.reshape(-1)[source], zero_half).reshape(
        experts, slot_total
    )
    arrived = lax.all_to_all(send_rows, "expert", split_axis=0, concat_axis=0, tiled=True)
    own_gate = gate_proj[0]
    own_up = up_proj[0]
    own_down = down_proj[0]
    hidden_width = own_gate.shape[1]
    spread = (
        lax.all_to_all(
            own_gate.reshape(experts, -1), "expert", split_axis=0, concat_axis=0, tiled=True
        ),
        lax.all_to_all(
            own_up.reshape(experts, -1), "expert", split_axis=0, concat_axis=0, tiled=True
        ),
        lax.all_to_all(
            own_down.reshape(experts, -1), "expert", split_axis=0, concat_axis=0, tiled=True
        ),
    )
    chosen_gate = jnp.take(spread[0], replica_plan, axis=0)
    chosen_up = jnp.take(spread[1], replica_plan, axis=0)
    chosen_down = jnp.take(spread[2], replica_plan, axis=0)
    collected = (
        lax.all_to_all(chosen_gate, "expert", split_axis=0, concat_axis=0, tiled=True),
        lax.all_to_all(chosen_up, "expert", split_axis=0, concat_axis=0, tiled=True),
        lax.all_to_all(chosen_down, "expert", split_axis=0, concat_axis=0, tiled=True),
    )
    copy_gate = collected[0].reshape(model_width, hidden_width)
    copy_up = collected[1].reshape(model_width, hidden_width)
    copy_down = collected[2].reshape(model_width, hidden_width)
    arrived_up, arrived_weight = (
        lax.all_to_all(send_upstream, "expert", split_axis=0, concat_axis=0, tiled=True),
        lax.all_to_all(send_weight, "expert", split_axis=0, concat_axis=0, tiled=True),
    )
    owned_dx, owned_gate_rows, owned_grads = expert_backward(
        arrived[:, :capacity].reshape(-1, model_width),
        arrived_up[:, :capacity].reshape(-1, model_width),
        arrived_weight[:, :capacity].reshape(-1),
        own_gate,
        own_up,
        own_down,
    )
    copied_dx, copied_gate_rows, copied_grads = expert_backward(
        arrived[:, capacity:].reshape(-1, model_width),
        arrived_up[:, capacity:].reshape(-1, model_width),
        arrived_weight[:, capacity:].reshape(-1),
        copy_gate,
        copy_up,
        copy_down,
    )
    back_rows = jnp.concatenate(
        [
            owned_dx.reshape(experts, capacity, model_width),
            copied_dx.reshape(experts, capacity, model_width),
        ],
        axis=1,
    )
    back_gate = jnp.concatenate(
        [owned_gate_rows.reshape(experts, capacity), copied_gate_rows.reshape(experts, capacity)],
        axis=1,
    ).astype(jnp.bfloat16)
    returned, returned_gate = (
        lax.all_to_all(back_rows, "expert", split_axis=0, concat_axis=0, tiled=True),
        lax.all_to_all(back_gate, "expert", split_axis=0, concat_axis=0, tiled=True),
    )
    copy_pieces = (
        copied_grads[0].astype(jnp.bfloat16).reshape(experts, -1),
        copied_grads[1].astype(jnp.bfloat16).reshape(experts, -1),
        copied_grads[2].astype(jnp.bfloat16).reshape(experts, -1),
    )
    grad_spread = (
        lax.all_to_all(copy_pieces[0], "expert", split_axis=0, concat_axis=0, tiled=True),
        lax.all_to_all(copy_pieces[1], "expert", split_axis=0, concat_axis=0, tiled=True),
        lax.all_to_all(copy_pieces[2], "expert", split_axis=0, concat_axis=0, tiled=True),
    )
    lane_ids = jnp.arange(experts, dtype=jnp.int32)
    owner_map = (replica_plan[None, :] == lane_ids[:, None]).astype(jnp.bfloat16)
    summed_gate = jnp.dot(owner_map, grad_spread[0], preferred_element_type=jnp.float32).astype(
        jnp.bfloat16
    )
    summed_up = jnp.dot(owner_map, grad_spread[1], preferred_element_type=jnp.float32).astype(
        jnp.bfloat16
    )
    summed_down = jnp.dot(owner_map, grad_spread[2], preferred_element_type=jnp.float32).astype(
        jnp.bfloat16
    )
    grad_back = (
        lax.all_to_all(summed_gate, "expert", split_axis=0, concat_axis=0, tiled=True),
        lax.all_to_all(summed_up, "expert", split_axis=0, concat_axis=0, tiled=True),
        lax.all_to_all(summed_down, "expert", split_axis=0, concat_axis=0, tiled=True),
    )
    total_gate = owned_grads[0] + grad_back[0].reshape(model_width, hidden_width).astype(
        jnp.float32
    )
    total_up = owned_grads[1] + grad_back[1].reshape(model_width, hidden_width).astype(jnp.float32)
    total_down = owned_grads[2] + grad_back[2].reshape(model_width, hidden_width).astype(
        jnp.float32
    )
    shares = (
        lax.psum_scatter(
            total_gate.astype(jnp.bfloat16), "replica", scatter_dimension=0, tiled=True
        ).astype(jnp.float32),
        lax.psum_scatter(
            total_up.astype(jnp.bfloat16), "replica", scatter_dimension=0, tiled=True
        ).astype(jnp.float32),
        lax.psum_scatter(
            total_down.astype(jnp.bfloat16), "replica", scatter_dimension=0, tiled=True
        ).astype(jnp.float32),
    )
    flat_back = returned.reshape(experts * slot_total, model_width)
    picked_rows = jnp.take(flat_back, slot_index, axis=0)
    picked_rows = jnp.where(kept_mask[:, None], picked_rows, zero_half).astype(jnp.float32)
    token_grad = jnp.sum(picked_rows.reshape(token_count, topk, model_width), axis=1).astype(
        jnp.bfloat16
    )
    gate_grad = jnp.where(kept_mask, returned_gate.reshape(-1)[slot_index], zero_half).reshape(
        token_count, topk
    )
    return (
        token_grad,
        gate_grad,
        shares[0].astype(jnp.bfloat16)[None],
        shares[1].astype(jnp.bfloat16)[None],
        shares[2].astype(jnp.bfloat16)[None],
    )


BF = jnp.bfloat16
F32 = jnp.float32
CONTRACT_ROWS = (((0,), (0,)), ((), ()))
CONTRACT_COLS = (((1,), (1,)), ((), ()))
MIB = 1024 * 1024

MAIN = 16
QUARTERS = 4
SEND_ROWS = 2 * QUARTERS * MAIN + 16
BACK_ROWS = QUARTERS * MAIN + 16
STEPS = (0, 1, 4, 5, 6, 7, 2, 3)
GROUP = 4
GROUP_ROWS = GROUP * MAIN + 16


def copies_of(experts):
    return 2 if experts <= 8 else 8


def iota(shape, axis):
    return lax.broadcasted_iota(jnp.int32, shape, axis)


def partners(experts, tokens):
    row = iota((experts, tokens), 0)
    step = jnp.zeros((experts, tokens), jnp.int32)
    for c in range(experts):
        step = jnp.where(row == c, STEPS[c], step)
    return jnp.bitwise_xor(step, lax.axis_index("expert"))


def mask(condition):
    return condition.astype(F32).astype(BF)


def repeat_rows(table, times):
    width = table.shape[1]
    return jnp.concatenate(
        [jnp.broadcast_to(table[e : e + 1], (times, width)) for e in range(table.shape[0])], axis=0
    )


def route_kernel(plan_hbm, ids_hbm, pick_hbm, gate_hbm, tok_hbm, cot_hbm, *refs):
    sems = refs[-1]
    plan_ref, ids_ref, pick_ref, gate_ref, tok_ref, cot_ref = refs[-7:-1]
    slot_ref, gates_ref = refs[-9:-7]
    send_refs = refs[:-9]
    topk, tokens = ids_ref.shape
    experts = len(send_refs)
    width = tok_ref.shape[1] // QUARTERS
    copies = copies_of(experts)
    loads = [
        pltpu.make_async_copy(source, place, sems.at[n])
        for n, (source, place) in enumerate(
            (
                (plan_hbm, plan_ref),
                (ids_hbm, ids_ref),
                (pick_hbm, pick_ref),
                (gate_hbm, gate_ref),
                (tok_hbm, tok_ref),
                (cot_hbm, cot_ref),
            )
        )
    ]
    for load in loads:
        load.start()
    before = mask(iota((tokens, tokens), 0) < iota((tokens, tokens), 1))
    expert_row = partners(experts, tokens)
    for load in loads[:4]:
        load.wait()
    ids = ids_ref[...]
    pick = pick_ref[...]
    gate = gate_ref[...].astype(F32)
    named = jnp.zeros((experts, tokens), jnp.int32)
    gates = jnp.zeros((experts, tokens), F32)
    for k in range(topk):
        hit = ids[k : k + 1] == expert_row
        named = jnp.where(hit, pick[k : k + 1] + 1, named)
        gates = jnp.where(hit, gate[k : k + 1], gates)
    hot = jnp.zeros((experts, tokens), jnp.int32)
    for j in range(experts):
        hot = jnp.where(expert_row == plan_ref[j], 1, hot)
    chosen = jnp.where(named == 0, -1, jnp.where(hot > 0, named - 1, 0))
    masks = jnp.concatenate([(chosen == c).astype(F32) for c in range(copies + 1)], axis=0)
    rank = jnp.dot(masks.astype(BF), before, preferred_element_type=F32).astype(jnp.int32)
    slot = jnp.full((experts, tokens), -1, jnp.int32)
    for c in range(copies + 1):
        rank_c = rank[c * experts : (c + 1) * experts]
        keep = jnp.logical_and(chosen == c, rank_c < CAP)
        slot = jnp.where(keep, c * CAP + rank_c, slot)
    slot_ref[...] = slot
    gates_ref[...] = gates
    slot16 = repeat_rows(slot, MAIN)
    gate16 = repeat_rows(gates, MAIN)
    inner = jnp.bitwise_and(iota(slot16.shape, 0), MAIN - 1)
    onehot = (slot16 == inner).astype(F32)
    wanted = MAIN + jnp.bitwise_and(jnp.right_shift(inner, 2), 1)
    last = (slot16 == wanted).astype(F32)
    last_rows = jnp.where(inner >= 8, 0.0, last)
    last_scaled = jnp.where(inner >= 8, last * gate16, 0.0)
    quarter = jnp.bitwise_and(inner, 3)
    for load in loads[4:]:
        load.wait()
    rows = jnp.dot(onehot.astype(BF), tok_ref[...], preferred_element_type=F32).astype(BF)
    scaled = jnp.dot(
        (onehot * gate16).astype(BF), cot_ref[...], preferred_element_type=F32
    ).astype(BF)
    tail = jnp.zeros((experts * MAIN, width), F32)
    for q in range(QUARTERS):
        cols = slice(q * width, (q + 1) * width)
        mine = quarter == q
        tail += jnp.dot(
            jnp.where(mine, last_rows, 0.0).astype(BF), tok_ref[:, cols], preferred_element_type=F32
        )
        tail += jnp.dot(
            jnp.where(mine, last_scaled, 0.0).astype(BF),
            cot_ref[:, cols],
            preferred_element_type=F32,
        )
    tail = tail.astype(BF)
    for k in range(experts):
        here = slice(k * MAIN, (k + 1) * MAIN)
        for q in range(QUARTERS):
            cols = slice(q * width, (q + 1) * width)
            send_refs[k][q * MAIN : (q + 1) * MAIN, :] = rows[here, cols]
            send_refs[k][(QUARTERS + q) * MAIN : (QUARTERS + q + 1) * MAIN, :] = scaled[here, cols]
        send_refs[k][2 * QUARTERS * MAIN :, :] = tail[here]


def expert_kernel(*refs):
    recv_refs = refs[:GROUP]
    gate_ref, up_ref, down_ref = refs[GROUP : GROUP + 3]
    back_refs = refs[GROUP + 3 : 2 * GROUP + 3]
    x_ref, s_ref, dg_ref, du_ref, hid_ref = refs[2 * GROUP + 3 :]
    width = recv_refs[0].shape[1]
    main_rows = GROUP * MAIN
    tail = jnp.concatenate([ref[2 * QUARTERS * MAIN :, :] for ref in recv_refs], axis=0)
    row = iota((2 * MAIN, main_rows), 0)
    col = iota((2 * MAIN, main_rows), 1)
    inner = jnp.bitwise_and(row, MAIN - 1)
    base = jnp.right_shift(inner, 1) * MAIN + (row - inner) // 2 + jnp.bitwise_and(row, 1) * 4
    real = inner < 2 * GROUP
    for q in range(QUARTERS):
        cols = slice(q * width, (q + 1) * width)
        place = mask(jnp.logical_and(real, col == base + q))
        picked = jnp.dot(place, tail, preferred_element_type=F32).astype(BF)
        x_ref[main_rows:, cols] = picked[:MAIN]
        s_ref[main_rows:, cols] = picked[MAIN:]
        for i, ref in enumerate(recv_refs):
            here = slice(i * MAIN, (i + 1) * MAIN)
            x_ref[here, cols] = ref[q * MAIN : (q + 1) * MAIN, :]
            s_ref[here, cols] = ref[(QUARTERS + q) * MAIN : (QUARTERS + q + 1) * MAIN, :]
    rows = x_ref[...]
    gate_pre = jnp.dot(rows, gate_ref[...], preferred_element_type=F32)
    up_pre = jnp.dot(rows, up_ref[...], preferred_element_type=F32)
    hidden_grad = jnp.dot(s_ref[...], down_ref[...], preferred_element_type=F32)
    sig = jax.nn.sigmoid(gate_pre)
    activated = gate_pre * sig
    hidden = (activated * up_pre).astype(BF)
    slope = sig * (1.0 + gate_pre * (1.0 - sig))
    gate_delta = (hidden_grad * up_pre * slope).astype(BF)
    up_delta = (hidden_grad * activated).astype(BF)
    hid_ref[...] = hidden
    dg_ref[...] = gate_delta
    du_ref[...] = up_delta
    grad = (
        lax.dot_general(gate_delta, gate_ref[...], CONTRACT_COLS, preferred_element_type=F32)
        + lax.dot_general(up_delta, up_ref[...], CONTRACT_COLS, preferred_element_type=F32)
    ).astype(BF)
    product = hidden.astype(F32) * hidden_grad
    product = jnp.concatenate(
        [product, jnp.zeros((width - product.shape[0], product.shape[1]), F32)], axis=0
    )
    gate_lanes = lax.dot_general(
        jnp.ones((8, product.shape[1]), F32),
        product,
        CONTRACT_COLS,
        preferred_element_type=F32,
        precision=lax.Precision.HIGHEST,
    )
    trow = iota((main_rows, MAIN), 0)
    tcol = iota((main_rows, MAIN), 1)
    inner = jnp.bitwise_and(trow, MAIN - 1)
    source = jnp.right_shift(trow, 4) * 2 + jnp.right_shift(inner, 2)
    spread = jnp.zeros((main_rows, width), F32)
    for q in range(QUARTERS):
        cols = slice(q * width, (q + 1) * width)
        mine = jnp.logical_and(jnp.bitwise_and(inner, 3) == q, inner < 8)
        place = mask(jnp.logical_and(mine, tcol == source))
        spread += jnp.dot(place, grad[main_rows:, cols], preferred_element_type=F32)
        for i, ref in enumerate(back_refs):
            ref[q * MAIN : (q + 1) * MAIN, :] = grad[i * MAIN : (i + 1) * MAIN, cols]
    for i, ref in enumerate(back_refs):
        ref[QUARTERS * MAIN :, :] = jnp.concatenate(
            [spread[i * MAIN : i * MAIN + 8], gate_lanes], axis=0
        ).astype(BF)


def grads_of(half, refs):
    sums = [None] * 3
    for first in range(0, len(refs), 5):
        x_ref, s_ref, *right = refs[first : first + 5]
        rows = x_ref.shape[1] // 2
        cols = pl.ds(pl.multiple_of(half * rows, rows), rows)
        x_half = x_ref[:, cols]
        for n, left in enumerate((x_half, x_half, s_ref[:, cols])):
            part = lax.dot_general(left, right[n][...], CONTRACT_ROWS, preferred_element_type=F32)
            sums[n] = part if sums[n] is None else sums[n] + part
    return sums


def other_half_kernel(*refs):
    out_ref = refs[-1]
    parts = grads_of(1 - lax.axis_index("replica"), refs[:-1])
    rows = parts[0].shape[0]
    for n in range(3):
        out_ref[n * rows : (n + 1) * rows, :] = parts[n].astype(BF)


def own_half_kernel(*refs):
    came_ref = refs[-4]
    parts = grads_of(lax.axis_index("replica"), refs[:-4])
    rows = parts[0].shape[0]
    for n, out_ref in enumerate(refs[-3:]):
        came = came_ref[n * rows : (n + 1) * rows, :].astype(F32)
        out_ref[...] = (parts[n].astype(BF).astype(F32) + came).astype(BF)


def combine_kernel(ids_ref, slot_ref, gates_ref, *refs):
    token_ref, grad_ref = refs[-2:]
    ret_refs = refs[:-2]
    topk, tokens = ids_ref.shape
    experts = len(ret_refs)
    width = ret_refs[0].shape[1]
    ids = ids_ref[...]
    slot = slot_ref[...]
    slot16 = repeat_rows(slot, MAIN)
    inner = jnp.bitwise_and(iota(slot16.shape, 0), MAIN - 1)
    onehot = mask(slot16 == inner)
    wanted = MAIN + jnp.right_shift(inner, 2)
    last = jnp.where(jnp.logical_and(slot16 == wanted, inner < 8), 1.0, 0.0)
    quarter = jnp.bitwise_and(inner, 3)
    tail = jnp.concatenate([ref[QUARTERS * MAIN :, :] for ref in ret_refs], axis=0)
    for q in range(QUARTERS):
        main = jnp.concatenate([ref[q * MAIN : (q + 1) * MAIN, :] for ref in ret_refs], axis=0)
        place = jnp.where(quarter == q, last, 0.0).astype(BF)
        total = lax.dot_general(onehot, main, CONTRACT_ROWS, preferred_element_type=F32)
        total += lax.dot_general(place, tail, CONTRACT_ROWS, preferred_element_type=F32)
        token_ref[:, q * width : (q + 1) * width] = total.astype(BF)
    lane_index = iota((width, tokens), 0)
    found = []
    for c, ref in enumerate(ret_refs):
        mine = slot[c : c + 1]
        place = c % GROUP
        lane = jnp.where(mine < MAIN, place * MAIN + mine, GROUP * MAIN + 2 * place + mine - MAIN)
        lane = jnp.where(mine < 0, -1, lane)
        sums = jnp.dot(
            ref[QUARTERS * MAIN :, :], mask(lane_index == lane), preferred_element_type=F32
        )
        found.append(sums[8:9])
    found = jnp.concatenate(found, axis=0)
    kept = slot >= 0
    grads = jnp.where(kept, found / jnp.where(kept, gates_ref[...], 1.0), 0.0)
    expert_row = partners(experts, tokens)
    by_choice = [
        jnp.sum(jnp.where(expert_row == ids[k : k + 1], grads, 0.0), axis=0, keepdims=True)
        for k in range(topk)
    ]
    grad_ref[...] = jnp.concatenate(by_choice, axis=0).astype(BF)


def local_call(kernel, outs, arrays, name, flops, moved, space=pltpu.VMEM, scratch=(), limit=16):
    vmem = pl.BlockSpec(memory_space=pltpu.VMEM)
    return pl.pallas_call(
        kernel,
        out_shape=[jax.ShapeDtypeStruct(shape, kind) for shape, kind in outs],
        in_specs=[pl.BlockSpec(memory_space=space)] * len(arrays),
        out_specs=[vmem] * len(outs),
        scratch_shapes=list(scratch),
        compiler_params=pltpu.CompilerParams(vmem_limit_bytes=int(limit * MIB)),
        cost_estimate=pl.CostEstimate(flops=flops, bytes_accessed=moved, transcendentals=0),
        name=name,
    )(*arrays)


def exchange(chunks, steps):
    experts = lax.axis_size("expert")
    return [
        lax.ppermute(chunk, "expert", [(i, i ^ step) for i in range(experts)]) if step else chunk
        for chunk, step in zip(chunks, steps)
    ]


def hold_kernel(*refs):
    *refs, sems = refs
    count = len(refs) // 2
    loads = [
        pltpu.make_async_copy(source, place, sems.at[n])
        for n, (source, place) in enumerate(zip(refs[:count], refs[count:]))
    ]
    for load in loads:
        load.start()
    for load in loads:
        load.wait()


def per_device_moving_rows(
    tokens,
    cotangent,
    expert_ids,
    gate_values,
    replica_pick,
    replica_plan,
    gate_proj,
    up_proj,
    down_proj,
):
    experts = lax.axis_size("expert")
    token_count, model_width = tokens.shape
    topk = expert_ids.shape[1]
    hidden_width = gate_proj.shape[2]
    width = model_width // QUARTERS
    served = experts * (MAIN + 2)
    small = (topk, token_count)
    routed = local_call(
        route_kernel,
        [((SEND_ROWS, width), BF)] * experts
        + [((experts, token_count), jnp.int32), ((experts, token_count), F32)],
        [replica_plan, expert_ids.T, replica_pick.T, gate_values.T, tokens, cotangent],
        "route",
        2 * 2 * served * token_count * model_width,
        2 * 2 * (token_count + served) * model_width,
        space=pltpu.HBM,
        limit=58,
        scratch=[
            pltpu.SMEM((experts,), jnp.int32),
            pltpu.VMEM(small, jnp.int32),
            pltpu.VMEM(small, jnp.int32),
            pltpu.VMEM(small, BF),
            pltpu.VMEM(tokens.shape, BF),
            pltpu.VMEM(tokens.shape, BF),
            pltpu.SemaphoreType.DMA((6,)),
        ],
    )
    slot, gates = routed[experts:]
    recv = exchange(routed[:experts], STEPS)
    matrices = [gate_proj[0], up_proj[0], down_proj[0]]
    matrices = local_call(
        hold_kernel,
        [(array.shape, BF) for array in matrices],
        matrices,
        "hold",
        0,
        4 * 3 * model_width * hidden_width,
        space=pltpu.HBM,
        limit=51.25,
        scratch=[pltpu.SemaphoreType.DMA((len(matrices),))],
    )
    matmul = 2 * GROUP_ROWS * model_width * hidden_width
    returned, factors = [], []
    for first in range(0, experts, GROUP):
        outs = local_call(
            expert_kernel,
            [((BACK_ROWS, width), BF)] * GROUP
            + [((GROUP_ROWS, model_width), BF)] * 2
            + [((GROUP_ROWS, hidden_width), BF)] * 3,
            [*recv[first : first + GROUP], *matrices],
            "expert_rows",
            5 * matmul,
            2 * 3 * model_width * hidden_width,
        )
        returned += exchange(outs[:GROUP], STEPS[first : first + GROUP])
        factors += outs[GROUP:]
    returned[:GROUP], factors = lax.optimization_barrier((returned[:GROUP], factors))
    half = model_width // 2
    (leaving,) = local_call(
        other_half_kernel,
        [((3 * half, hidden_width), BF)],
        factors,
        "other_half",
        1,
        1,
    )
    came = lax.ppermute(leaving, "replica", [(0, 1), (1, 0)])
    shares = local_call(
        own_half_kernel,
        [((half, hidden_width), BF)] * 3,
        [*factors, came],
        "own_half",
        1,
        1,
    )
    returned, shares = lax.optimization_barrier((returned, shares))
    token_grad, gate_grad = local_call(
        combine_kernel,
        [((token_count, model_width), BF), ((topk, token_count), BF)],
        [expert_ids.T, slot, gates, *returned],
        "combine",
        2 * served * token_count * model_width,
        2 * 2 * token_count * model_width,
    )
    return (token_grad, gate_grad.T, shares[0][None], shares[1][None], shares[2][None])


def per_device(tokens, cotangent, expert_ids, gate_values, replica_pick, replica_plan, *matrices):
    experts = lax.axis_size("expert")
    slots = (copies_of(experts) + 1) * CAP
    row_bytes = 3 * 2 * tokens.shape[1] * experts
    matrix_bytes = 4 * sum(2 * m[0].size for m in matrices)
    fits = slots == MAIN + 2 and experts == 8 and lax.axis_size("replica") == 2
    rows_cheaper = slots * row_bytes < 2 * CAP * row_bytes + matrix_bytes
    plan = per_device_moving_rows if fits and rows_cheaper else per_device_moving_weights
    return plan(
        tokens, cotangent, expert_ids, gate_values, replica_pick, replica_plan, *matrices
    )


def solution(mesh):
    placed = (
        P(("parts", "expert", "replica"), None),
        P(("parts", "expert", "replica"), None),
        P(("parts", "expert", "replica"), None),
        P(("parts", "expert", "replica"), None),
        P(("parts", "expert", "replica"), None),
        P("parts"),
        P("expert", None, None),
        P("expert", None, None),
        P("expert", None, None),
    )
    return jax.shard_map(
        per_device,
        mesh=mesh,
        in_specs=placed,
        out_specs=(
            P(("parts", "expert", "replica"), None),
            P(("parts", "expert", "replica"), None),
            P(("parts", "expert"), "replica", None),
            P(("parts", "expert"), "replica", None),
            P(("parts", "expert"), "replica", None),
        ),
        check_vma=False,
    )
```

```python
import jax
import jax.numpy as jnp
from jax import lax
from jax.experimental import pallas as pl
from jax.experimental.pallas import tpu as pltpu
from jax.sharding import PartitionSpec as P

CAP = 6


def route_assignments(flat_ids, flat_pick, replica_plan, capacity):
    experts = replica_plan.shape[0]
    lane_ids = jnp.arange(experts, dtype=jnp.int32)
    same_plan = replica_plan[:, None] == replica_plan[None, :]
    earlier = lane_ids[None, :] < lane_ids[:, None]
    position = jnp.sum(jnp.logical_and(same_plan, earlier), axis=1)
    hot_mask = jnp.any(replica_plan[None, :] == lane_ids[:, None], axis=1)
    is_hot = jnp.any(
        jnp.logical_and(flat_ids[:, None] == lane_ids[None, :], hot_mask[None, :]), axis=1
    )
    use_copy = jnp.logical_and(is_hot, flat_pick >= 1)
    matches = jnp.logical_and(
        replica_plan[None, :] == flat_ids[:, None], position[None, :] == flat_pick[:, None] - 1
    )
    holder = jnp.sum(jnp.where(matches, lane_ids[None, :], 0), axis=1)
    target = jnp.where(use_copy, holder, flat_ids)
    copy_role = use_copy.astype(jnp.int32)
    bucket = target * 2 + copy_role
    sequence = jnp.arange(bucket.shape[0], dtype=jnp.int32)
    arrival = jnp.sum(
        jnp.logical_and(bucket[None, :] == bucket[:, None], sequence[None, :] < sequence[:, None]),
        axis=1,
    )
    kept_mask = arrival < capacity
    slot_index = target * (2 * capacity) + copy_role * capacity + jnp.minimum(arrival, capacity - 1)
    return (slot_index, kept_mask)


def fill_slots(slot_index, kept_mask, slot_count):
    slot_ids = jnp.arange(slot_count, dtype=jnp.int32)
    matches = jnp.logical_and(slot_index[None, :] == slot_ids[:, None], kept_mask[None, :])
    sequence = jnp.arange(slot_index.shape[0], dtype=jnp.int32)
    source = jnp.sum(jnp.where(matches, sequence[None, :], 0), axis=1)
    filled = jnp.any(matches, axis=1)
    return (source, filled)


def expert_backward(row_block, upstream, weight, gate_w, up_w, down_w):
    contract_cols = (((1,), (1,)), ((), ()))
    contract_rows = (((0,), (0,)), ((), ()))
    gate_pre = jnp.dot(row_block, gate_w, preferred_element_type=jnp.float32)
    up_pre = jnp.dot(row_block, up_w, preferred_element_type=jnp.float32)
    sigmoid_gate = jax.nn.sigmoid(gate_pre)
    activated = gate_pre * sigmoid_gate
    hidden = (activated * up_pre).astype(jnp.bfloat16)
    output_rows = lax.dot_general(hidden, down_w, contract_cols, preferred_element_type=jnp.float32)
    weight_col = weight.astype(jnp.float32)[:, None]
    upstream_f = upstream.astype(jnp.float32)
    gate_rows = jnp.sum(upstream_f * output_rows, axis=1)
    hidden_grad = weight_col * jnp.dot(upstream, down_w, preferred_element_type=jnp.float32)
    slope = sigmoid_gate * (1.0 + gate_pre * (1.0 - sigmoid_gate))
    gate_delta = (hidden_grad * up_pre * slope).astype(jnp.bfloat16)
    up_delta = (hidden_grad * activated).astype(jnp.bfloat16)
    input_grad = (
        lax.dot_general(gate_delta, gate_w, contract_cols, preferred_element_type=jnp.float32)
        + lax.dot_general(up_delta, up_w, contract_cols, preferred_element_type=jnp.float32)
    ).astype(jnp.bfloat16)
    scaled = (weight_col * upstream_f).astype(jnp.bfloat16)
    grad_set = (
        lax.dot_general(row_block, gate_delta, contract_rows, preferred_element_type=jnp.float32),
        lax.dot_general(row_block, up_delta, contract_rows, preferred_element_type=jnp.float32),
        lax.dot_general(scaled, hidden, contract_rows, preferred_element_type=jnp.float32),
    )
    return (input_grad, gate_rows, grad_set)


def per_device_moving_weights(
    tokens,
    cotangent,
    expert_ids,
    gate_values,
    replica_pick,
    replica_plan,
    gate_proj,
    up_proj,
    down_proj,
):
    experts = lax.axis_size("expert")
    capacity = CAP
    slot_total = 2 * capacity
    model_width = tokens.shape[1]
    topk = expert_ids.shape[1]
    token_count = tokens.shape[0]
    slot_index, kept_mask = route_assignments(
        expert_ids.reshape(-1), replica_pick.reshape(-1), replica_plan, capacity
    )
    source, filled = fill_slots(slot_index, kept_mask, experts * slot_total)
    token_of = source // topk
    zero_half = jnp.zeros((), jnp.bfloat16)
    send_rows = jnp.where(filled[:, None], jnp.take(tokens, token_of, axis=0), zero_half).reshape(
        experts, slot_total, model_width
    )
    send_upstream = jnp.where(
        filled[:, None], jnp.take(cotangent, token_of, axis=0), zero_half
    ).reshape(experts, slot_total, model_width)
    send_weight = jnp.where(filled, gate_values.reshape(-1)[source], zero_half).reshape(
        experts, slot_total
    )
    arrived = lax.all_to_all(send_rows, "expert", split_axis=0, concat_axis=0, tiled=True)
    own_gate = gate_proj[0]
    own_up = up_proj[0]
    own_down = down_proj[0]
    hidden_width = own_gate.shape[1]
    spread = (
        lax.all_to_all(
            own_gate.reshape(experts, -1), "expert", split_axis=0, concat_axis=0, tiled=True
        ),
        lax.all_to_all(
            own_up.reshape(experts, -1), "expert", split_axis=0, concat_axis=0, tiled=True
        ),
        lax.all_to_all(
            own_down.reshape(experts, -1), "expert", split_axis=0, concat_axis=0, tiled=True
        ),
    )
    chosen_gate = jnp.take(spread[0], replica_plan, axis=0)
    chosen_up = jnp.take(spread[1], replica_plan, axis=0)
    chosen_down = jnp.take(spread[2], replica_plan, axis=0)
    collected = (
        lax.all_to_all(chosen_gate, "expert", split_axis=0, concat_axis=0, tiled=True),
        lax.all_to_all(chosen_up, "expert", split_axis=0, concat_axis=0, tiled=True),
        lax.all_to_all(chosen_down, "expert", split_axis=0, concat_axis=0, tiled=True),
    )
    copy_gate = collected[0].reshape(model_width, hidden_width)
    copy_up = collected[1].reshape(model_width, hidden_width)
    copy_down = collected[2].reshape(model_width, hidden_width)
    arrived_up, arrived_weight = (
        lax.all_to_all(send_upstream, "expert", split_axis=0, concat_axis=0, tiled=True),
        lax.all_to_all(send_weight, "expert", split_axis=0, concat_axis=0, tiled=True),
    )
    owned_dx, owned_gate_rows, owned_grads = expert_backward(
        arrived[:, :capacity].reshape(-1, model_width),
        arrived_up[:, :capacity].reshape(-1, model_width),
        arrived_weight[:, :capacity].reshape(-1),
        own_gate,
        own_up,
        own_down,
    )
    copied_dx, copied_gate_rows, copied_grads = expert_backward(
        arrived[:, capacity:].reshape(-1, model_width),
        arrived_up[:, capacity:].reshape(-1, model_width),
        arrived_weight[:, capacity:].reshape(-1),
        copy_gate,
        copy_up,
        copy_down,
    )
    back_rows = jnp.concatenate(
        [
            owned_dx.reshape(experts, capacity, model_width),
            copied_dx.reshape(experts, capacity, model_width),
        ],
        axis=1,
    )
    back_gate = jnp.concatenate(
        [owned_gate_rows.reshape(experts, capacity), copied_gate_rows.reshape(experts, capacity)],
        axis=1,
    ).astype(jnp.bfloat16)
    returned, returned_gate = (
        lax.all_to_all(back_rows, "expert", split_axis=0, concat_axis=0, tiled=True),
        lax.all_to_all(back_gate, "expert", split_axis=0, concat_axis=0, tiled=True),
    )
    copy_pieces = (
        copied_grads[0].astype(jnp.bfloat16).reshape(experts, -1),
        copied_grads[1].astype(jnp.bfloat16).reshape(experts, -1),
        copied_grads[2].astype(jnp.bfloat16).reshape(experts, -1),
    )
    grad_spread = (
        lax.all_to_all(copy_pieces[0], "expert", split_axis=0, concat_axis=0, tiled=True),
        lax.all_to_all(copy_pieces[1], "expert", split_axis=0, concat_axis=0, tiled=True),
        lax.all_to_all(copy_pieces[2], "expert", split_axis=0, concat_axis=0, tiled=True),
    )
    lane_ids = jnp.arange(experts, dtype=jnp.int32)
    owner_map = (replica_plan[None, :] == lane_ids[:, None]).astype(jnp.bfloat16)
    summed_gate = jnp.dot(owner_map, grad_spread[0], preferred_element_type=jnp.float32).astype(
        jnp.bfloat16
    )
    summed_up = jnp.dot(owner_map, grad_spread[1], preferred_element_type=jnp.float32).astype(
        jnp.bfloat16
    )
    summed_down = jnp.dot(owner_map, grad_spread[2], preferred_element_type=jnp.float32).astype(
        jnp.bfloat16
    )
    grad_back = (
        lax.all_to_all(summed_gate, "expert", split_axis=0, concat_axis=0, tiled=True),
        lax.all_to_all(summed_up, "expert", split_axis=0, concat_axis=0, tiled=True),
        lax.all_to_all(summed_down, "expert", split_axis=0, concat_axis=0, tiled=True),
    )
    total_gate = owned_grads[0] + grad_back[0].reshape(model_width, hidden_width).astype(
        jnp.float32
    )
    total_up = owned_grads[1] + grad_back[1].reshape(model_width, hidden_width).astype(jnp.float32)
    total_down = owned_grads[2] + grad_back[2].reshape(model_width, hidden_width).astype(
        jnp.float32
    )
    shares = (
        lax.psum_scatter(
            total_gate.astype(jnp.bfloat16), "replica", scatter_dimension=0, tiled=True
        ).astype(jnp.float32),
        lax.psum_scatter(
            total_up.astype(jnp.bfloat16), "replica", scatter_dimension=0, tiled=True
        ).astype(jnp.float32),
        lax.psum_scatter(
            total_down.astype(jnp.bfloat16), "replica", scatter_dimension=0, tiled=True
        ).astype(jnp.float32),
    )
    flat_back = returned.reshape(experts * slot_total, model_width)
    picked_rows = jnp.take(flat_back, slot_index, axis=0)
    picked_rows = jnp.where(kept_mask[:, None], picked_rows, zero_half).astype(jnp.float32)
    token_grad = jnp.sum(picked_rows.reshape(token_count, topk, model_width), axis=1).astype(
        jnp.bfloat16
    )
    gate_grad = jnp.where(kept_mask, returned_gate.reshape(-1)[slot_index], zero_half).reshape(
        token_count, topk
    )
    return (
        token_grad,
        gate_grad,
        shares[0].astype(jnp.bfloat16)[None],
        shares[1].astype(jnp.bfloat16)[None],
        shares[2].astype(jnp.bfloat16)[None],
    )


BF = jnp.bfloat16
F32 = jnp.float32
CONTRACT_ROWS = (((0,), (0,)), ((), ()))
CONTRACT_COLS = (((1,), (1,)), ((), ()))
MIB = 1024 * 1024

MAIN = 16
QUARTERS = 4
SEND_ROWS = 2 * QUARTERS * MAIN + 16
BACK_ROWS = QUARTERS * MAIN + 16
STEPS = (0, 4, 1, 5, 6, 7, 2, 3)


def copies_of(experts):
    return 2 if experts <= 8 else 8


def iota(shape, axis):
    return lax.broadcasted_iota(jnp.int32, shape, axis)


def partners(experts, tokens):
    row = iota((experts, tokens), 0)
    step = jnp.zeros((experts, tokens), jnp.int32)
    for c in range(experts):
        step = jnp.where(row == c, STEPS[c], step)
    return jnp.bitwise_xor(step, lax.axis_index("expert"))


def mask(condition):
    return condition.astype(F32).astype(BF)


def repeat_rows(table, times):
    width = table.shape[1]
    return jnp.concatenate(
        [jnp.broadcast_to(table[e : e + 1], (times, width)) for e in range(table.shape[0])], axis=0
    )


def route_kernel(plan_hbm, ids_hbm, pick_hbm, gate_hbm, tok_hbm, cot_hbm, *refs):
    sems = refs[-1]
    plan_ref, ids_ref, pick_ref, gate_ref, tok_ref, cot_ref = refs[-7:-1]
    slot_ref, gates_ref = refs[-9:-7]
    send_refs = refs[:-9]
    topk, tokens = ids_ref.shape
    experts = len(send_refs)
    width = tok_ref.shape[1] // QUARTERS
    copies = copies_of(experts)
    loads = [
        pltpu.make_async_copy(source, place, sems.at[n])
        for n, (source, place) in enumerate(
            (
                (plan_hbm, plan_ref),
                (ids_hbm, ids_ref),
                (pick_hbm, pick_ref),
                (gate_hbm, gate_ref),
                (tok_hbm, tok_ref),
                (cot_hbm, cot_ref),
            )
        )
    ]
    for load in loads:
        load.start()
    before = mask(iota((tokens, tokens), 0) < iota((tokens, tokens), 1))
    expert_row = partners(experts, tokens)
    for load in loads[:4]:
        load.wait()
    ids = ids_ref[...]
    pick = pick_ref[...]
    gate = gate_ref[...].astype(F32)
    named = jnp.zeros((experts, tokens), jnp.int32)
    gates = jnp.zeros((experts, tokens), F32)
    for k in range(topk):
        hit = ids[k : k + 1] == expert_row
        named = jnp.where(hit, pick[k : k + 1] + 1, named)
        gates = jnp.where(hit, gate[k : k + 1], gates)
    hot = jnp.zeros((experts, tokens), jnp.int32)
    for j in range(experts):
        hot = jnp.where(expert_row == plan_ref[j], 1, hot)
    chosen = jnp.where(named == 0, -1, jnp.where(hot > 0, named - 1, 0))
    masks = jnp.concatenate([(chosen == c).astype(F32) for c in range(copies + 1)], axis=0)
    rank = jnp.dot(masks.astype(BF), before, preferred_element_type=F32).astype(jnp.int32)
    slot = jnp.full((experts, tokens), -1, jnp.int32)
    for c in range(copies + 1):
        rank_c = rank[c * experts : (c + 1) * experts]
        keep = jnp.logical_and(chosen == c, rank_c < CAP)
        slot = jnp.where(keep, c * CAP + rank_c, slot)
    slot_ref[...] = slot
    gates_ref[...] = gates
    slot16 = repeat_rows(slot, MAIN)
    gate16 = repeat_rows(gates, MAIN)
    inner = jnp.bitwise_and(iota(slot16.shape, 0), MAIN - 1)
    onehot = (slot16 == inner).astype(F32)
    wanted = MAIN + jnp.bitwise_and(jnp.right_shift(inner, 2), 1)
    last = (slot16 == wanted).astype(F32)
    last_rows = jnp.where(inner >= 8, 0.0, last)
    last_scaled = jnp.where(inner >= 8, last * gate16, 0.0)
    quarter = jnp.bitwise_and(inner, 3)
    for load in loads[4:]:
        load.wait()
    rows = jnp.dot(onehot.astype(BF), tok_ref[...], preferred_element_type=F32).astype(BF)
    scaled = jnp.dot(
        (onehot * gate16).astype(BF), cot_ref[...], preferred_element_type=F32
    ).astype(BF)
    tail = jnp.zeros((experts * MAIN, width), F32)
    for q in range(QUARTERS):
        cols = slice(q * width, (q + 1) * width)
        mine = quarter == q
        tail += jnp.dot(
            jnp.where(mine, last_rows, 0.0).astype(BF), tok_ref[:, cols], preferred_element_type=F32
        )
        tail += jnp.dot(
            jnp.where(mine, last_scaled, 0.0).astype(BF),
            cot_ref[:, cols],
            preferred_element_type=F32,
        )
    tail = tail.astype(BF)
    for k in range(experts):
        here = slice(k * MAIN, (k + 1) * MAIN)
        for q in range(QUARTERS):
            cols = slice(q * width, (q + 1) * width)
            send_refs[k][q * MAIN : (q + 1) * MAIN, :] = rows[here, cols]
            send_refs[k][(QUARTERS + q) * MAIN : (QUARTERS + q + 1) * MAIN, :] = scaled[here, cols]
        send_refs[k][2 * QUARTERS * MAIN :, :] = tail[here]


def expert_kernel(*refs):
    back_count = len(refs) - 8
    experts = back_count // 2
    recv_refs = refs[:experts]
    gate_ref, up_ref, down_ref = refs[experts : experts + 3]
    back_refs = refs[experts + 3 : 2 * experts + 3]
    x_ref, s_ref, dg_ref, du_ref, hid_ref = refs[2 * experts + 3 :]
    width = recv_refs[0].shape[1]
    main_rows = experts * MAIN
    tail = jnp.concatenate([ref[2 * QUARTERS * MAIN :, :] for ref in recv_refs], axis=0)
    row = iota((4 * experts, main_rows), 0)
    col = iota((4 * experts, main_rows), 1)
    kind = (row >= 2 * experts).astype(jnp.int32)
    chunk = jnp.right_shift(row - kind * 2 * experts, 1)
    base = chunk * MAIN + kind * 8 + jnp.bitwise_and(row, 1) * 4
    for q in range(QUARTERS):
        cols = slice(q * width, (q + 1) * width)
        picked = jnp.dot(mask(col == base + q), tail, preferred_element_type=F32).astype(BF)
        x_ref[main_rows:, cols] = picked[: 2 * experts]
        s_ref[main_rows:, cols] = picked[2 * experts :]
        for i, ref in enumerate(recv_refs):
            here = slice(i * MAIN, (i + 1) * MAIN)
            x_ref[here, cols] = ref[q * MAIN : (q + 1) * MAIN, :]
            s_ref[here, cols] = ref[(QUARTERS + q) * MAIN : (QUARTERS + q + 1) * MAIN, :]
    rows = x_ref[...]
    gate_pre = jnp.dot(rows, gate_ref[...], preferred_element_type=F32)
    up_pre = jnp.dot(rows, up_ref[...], preferred_element_type=F32)
    hidden_grad = jnp.dot(s_ref[...], down_ref[...], preferred_element_type=F32)
    sig = jax.nn.sigmoid(gate_pre)
    activated = gate_pre * sig
    hidden = (activated * up_pre).astype(BF)
    slope = sig * (1.0 + gate_pre * (1.0 - sig))
    gate_delta = (hidden_grad * up_pre * slope).astype(BF)
    up_delta = (hidden_grad * activated).astype(BF)
    hid_ref[...] = hidden
    dg_ref[...] = gate_delta
    du_ref[...] = up_delta
    grad = (
        lax.dot_general(gate_delta, gate_ref[...], CONTRACT_COLS, preferred_element_type=F32)
        + lax.dot_general(up_delta, up_ref[...], CONTRACT_COLS, preferred_element_type=F32)
    ).astype(BF)
    product = hidden.astype(F32) * hidden_grad
    product = jnp.concatenate(
        [product, jnp.zeros((width - product.shape[0], product.shape[1]), F32)], axis=0
    )
    gate_lanes = lax.dot_general(
        jnp.ones((8, product.shape[1]), F32),
        product,
        CONTRACT_COLS,
        preferred_element_type=F32,
        precision=lax.Precision.HIGHEST,
    )
    trow = iota((main_rows, 2 * experts), 0)
    tcol = iota((main_rows, 2 * experts), 1)
    inner = jnp.bitwise_and(trow, MAIN - 1)
    source = jnp.right_shift(trow, 4) * 2 + jnp.right_shift(inner, 2)
    spread = jnp.zeros((main_rows, width), F32)
    for q in range(QUARTERS):
        cols = slice(q * width, (q + 1) * width)
        mine = jnp.logical_and(jnp.bitwise_and(inner, 3) == q, inner < 8)
        place = mask(jnp.logical_and(mine, tcol == source))
        spread += jnp.dot(place, grad[main_rows:, cols], preferred_element_type=F32)
        for i, ref in enumerate(back_refs):
            ref[q * MAIN : (q + 1) * MAIN, :] = grad[i * MAIN : (i + 1) * MAIN, cols]
    for i, ref in enumerate(back_refs):
        ref[QUARTERS * MAIN :, :] = jnp.concatenate(
            [spread[i * MAIN : i * MAIN + 8], gate_lanes], axis=0
        ).astype(BF)


def grads_of(half, x_ref, s_ref, dg_ref, du_ref, hid_ref):
    rows = x_ref.shape[1] // 2
    cols = pl.ds(pl.multiple_of(half * rows, rows), rows)
    x_half = x_ref[:, cols]
    s_half = s_ref[:, cols]
    return (
        lax.dot_general(x_half, dg_ref[...], CONTRACT_ROWS, preferred_element_type=F32),
        lax.dot_general(x_half, du_ref[...], CONTRACT_ROWS, preferred_element_type=F32),
        lax.dot_general(s_half, hid_ref[...], CONTRACT_ROWS, preferred_element_type=F32),
    )


def other_half_kernel(x_ref, s_ref, dg_ref, du_ref, hid_ref, out_ref):
    half = 1 - lax.axis_index("replica")
    parts = grads_of(half, x_ref, s_ref, dg_ref, du_ref, hid_ref)
    rows = parts[0].shape[0]
    for n in range(3):
        out_ref[n * rows : (n + 1) * rows, :] = parts[n].astype(BF)


def own_half_kernel(
    x_ref, s_ref, dg_ref, du_ref, hid_ref, came_ref, gate_ref, up_ref, down_ref
):
    parts = grads_of(lax.axis_index("replica"), x_ref, s_ref, dg_ref, du_ref, hid_ref)
    rows = parts[0].shape[0]
    for n, out_ref in enumerate((gate_ref, up_ref, down_ref)):
        came = came_ref[n * rows : (n + 1) * rows, :].astype(F32)
        out_ref[...] = (parts[n].astype(BF).astype(F32) + came).astype(BF)


def combine_kernel(ids_ref, slot_ref, gates_ref, *refs):
    token_ref, grad_ref = refs[-2:]
    ret_refs = refs[:-2]
    topk, tokens = ids_ref.shape
    experts = len(ret_refs)
    width = ret_refs[0].shape[1]
    ids = ids_ref[...]
    slot = slot_ref[...]
    slot16 = repeat_rows(slot, MAIN)
    inner = jnp.bitwise_and(iota(slot16.shape, 0), MAIN - 1)
    onehot = mask(slot16 == inner)
    wanted = MAIN + jnp.right_shift(inner, 2)
    last = jnp.where(jnp.logical_and(slot16 == wanted, inner < 8), 1.0, 0.0)
    quarter = jnp.bitwise_and(inner, 3)
    tail = jnp.concatenate([ref[QUARTERS * MAIN :, :] for ref in ret_refs], axis=0)
    for q in range(QUARTERS):
        main = jnp.concatenate([ref[q * MAIN : (q + 1) * MAIN, :] for ref in ret_refs], axis=0)
        place = jnp.where(quarter == q, last, 0.0).astype(BF)
        total = lax.dot_general(onehot, main, CONTRACT_ROWS, preferred_element_type=F32)
        total += lax.dot_general(place, tail, CONTRACT_ROWS, preferred_element_type=F32)
        token_ref[:, q * width : (q + 1) * width] = total.astype(BF)
    lane_index = iota((width, tokens), 0)
    found = []
    for k, ref in enumerate(ret_refs):
        mine = slot[k : k + 1]
        lane = jnp.where(mine < MAIN, k * MAIN + mine, experts * MAIN + 2 * k + mine - MAIN)
        lane = jnp.where(mine < 0, -1, lane)
        sums = jnp.dot(
            ref[QUARTERS * MAIN :, :], mask(lane_index == lane), preferred_element_type=F32
        )
        found.append(sums[8:9])
    found = jnp.concatenate(found, axis=0)
    kept = slot >= 0
    grads = jnp.where(kept, found / jnp.where(kept, gates_ref[...], 1.0), 0.0)
    expert_row = partners(experts, tokens)
    by_choice = [
        jnp.sum(jnp.where(expert_row == ids[k : k + 1], grads, 0.0), axis=0, keepdims=True)
        for k in range(topk)
    ]
    grad_ref[...] = jnp.concatenate(by_choice, axis=0).astype(BF)


def local_call(kernel, outs, arrays, name, flops, moved, space=pltpu.VMEM, scratch=(), limit=16):
    vmem = pl.BlockSpec(memory_space=pltpu.VMEM)
    return pl.pallas_call(
        kernel,
        out_shape=[jax.ShapeDtypeStruct(shape, kind) for shape, kind in outs],
        in_specs=[pl.BlockSpec(memory_space=space)] * len(arrays),
        out_specs=[vmem] * len(outs),
        scratch_shapes=list(scratch),
        compiler_params=pltpu.CompilerParams(vmem_limit_bytes=int(limit * MIB)),
        cost_estimate=pl.CostEstimate(flops=flops, bytes_accessed=moved, transcendentals=0),
        name=name,
    )(*arrays)


def exchange(chunks):
    count = len(chunks)
    moved = [
        lax.ppermute(chunk, "expert", [(i, i ^ step) for i in range(count)])
        for chunk, step in zip(chunks[1:], STEPS[1:])
    ]
    return [chunks[0], *moved]


def hold_kernel(*refs):
    *refs, sems = refs
    count = len(refs) // 2
    loads = [
        pltpu.make_async_copy(source, place, sems.at[n])
        for n, (source, place) in enumerate(zip(refs[:count], refs[count:]))
    ]
    for load in loads:
        load.start()
    for load in loads:
        load.wait()


def per_device_moving_rows(
    tokens,
    cotangent,
    expert_ids,
    gate_values,
    replica_pick,
    replica_plan,
    gate_proj,
    up_proj,
    down_proj,
):
    experts = lax.axis_size("expert")
    token_count, model_width = tokens.shape
    topk = expert_ids.shape[1]
    hidden_width = gate_proj.shape[2]
    width = model_width // QUARTERS
    served = experts * (MAIN + 2)
    small = (topk, token_count)
    routed = local_call(
        route_kernel,
        [((SEND_ROWS, width), BF)] * experts
        + [((experts, token_count), jnp.int32), ((experts, token_count), F32)],
        [replica_plan, expert_ids.T, replica_pick.T, gate_values.T, tokens, cotangent],
        "route",
        2 * 2 * served * token_count * model_width,
        2 * 2 * (token_count + served) * model_width,
        space=pltpu.HBM,
        limit=54,
        scratch=[
            pltpu.SMEM((experts,), jnp.int32),
            pltpu.VMEM(small, jnp.int32),
            pltpu.VMEM(small, jnp.int32),
            pltpu.VMEM(small, BF),
            pltpu.VMEM(tokens.shape, BF),
            pltpu.VMEM(tokens.shape, BF),
            pltpu.SemaphoreType.DMA((6,)),
        ],
    )
    slot, gates = routed[experts:]
    recv = exchange(routed[:experts])
    held = [recv[0], gate_proj[0], up_proj[0], down_proj[0]]
    held = local_call(
        hold_kernel,
        [(array.shape, BF) for array in held],
        held,
        "hold",
        0,
        4 * 3 * model_width * hidden_width,
        space=pltpu.HBM,
        limit=51.25,
        scratch=[pltpu.SemaphoreType.DMA((len(held),))],
    )
    matmul = 2 * served * model_width * hidden_width
    outs = local_call(
        expert_kernel,
        [((BACK_ROWS, width), BF)] * experts
        + [((served, model_width), BF)] * 2
        + [((served, hidden_width), BF)] * 3,
        [held[0], *recv[1:], *held[1:]],
        "expert_rows",
        5 * matmul,
        2 * 3 * model_width * hidden_width,
    )
    factors = outs[experts:]
    returned = exchange(outs[:experts])
    half = model_width // 2
    (leaving,) = local_call(
        other_half_kernel,
        [((3 * half, hidden_width), BF)],
        factors,
        "other_half",
        1,
        1,
    )
    came = lax.ppermute(leaving, "replica", [(0, 1), (1, 0)])
    shares = local_call(
        own_half_kernel,
        [((half, hidden_width), BF)] * 3,
        [*factors, came],
        "own_half",
        1,
        1,
    )
    returned, shares = lax.optimization_barrier((returned, shares))
    token_grad, gate_grad = local_call(
        combine_kernel,
        [((token_count, model_width), BF), ((topk, token_count), BF)],
        [expert_ids.T, slot, gates, *returned],
        "combine",
        2 * served * token_count * model_width,
        2 * 2 * token_count * model_width,
    )
    return (token_grad, gate_grad.T, shares[0][None], shares[1][None], shares[2][None])


def per_device(tokens, cotangent, expert_ids, gate_values, replica_pick, replica_plan, *matrices):
    experts = lax.axis_size("expert")
    slots = (copies_of(experts) + 1) * CAP
    row_bytes = 3 * 2 * tokens.shape[1] * experts
    matrix_bytes = 4 * sum(2 * m[0].size for m in matrices)
    fits = slots == MAIN + 2 and experts == 8 and lax.axis_size("replica") == 2
    rows_cheaper = slots * row_bytes < 2 * CAP * row_bytes + matrix_bytes
    plan = per_device_moving_rows if fits and rows_cheaper else per_device_moving_weights
    return plan(
        tokens, cotangent, expert_ids, gate_values, replica_pick, replica_plan, *matrices
    )


def solution(mesh):
    placed = (
        P(("parts", "expert", "replica"), None),
        P(("parts", "expert", "replica"), None),
        P(("parts", "expert", "replica"), None),
        P(("parts", "expert", "replica"), None),
        P(("parts", "expert", "replica"), None),
        P("parts"),
        P("expert", None, None),
        P("expert", None, None),
        P("expert", None, None),
    )
    return jax.shard_map(
        per_device,
        mesh=mesh,
        in_specs=placed,
        out_specs=(
            P(("parts", "expert", "replica"), None),
            P(("parts", "expert", "replica"), None),
            P(("parts", "expert"), "replica", None),
            P(("parts", "expert"), "replica", None),
            P(("parts", "expert"), "replica", None),
        ),
        check_vma=False,
    )
```

```python
import jax
import jax.numpy as jnp
from jax import lax
from jax.experimental import pallas as pl
from jax.experimental.pallas import tpu as pltpu
from jax.sharding import PartitionSpec as P

CAP = 6


def route_assignments(flat_ids, flat_pick, replica_plan, capacity):
    experts = replica_plan.shape[0]
    lane_ids = jnp.arange(experts, dtype=jnp.int32)
    same_plan = replica_plan[:, None] == replica_plan[None, :]
    earlier = lane_ids[None, :] < lane_ids[:, None]
    position = jnp.sum(jnp.logical_and(same_plan, earlier), axis=1)
    hot_mask = jnp.any(replica_plan[None, :] == lane_ids[:, None], axis=1)
    is_hot = jnp.any(
        jnp.logical_and(flat_ids[:, None] == lane_ids[None, :], hot_mask[None, :]), axis=1
    )
    use_copy = jnp.logical_and(is_hot, flat_pick >= 1)
    matches = jnp.logical_and(
        replica_plan[None, :] == flat_ids[:, None], position[None, :] == flat_pick[:, None] - 1
    )
    holder = jnp.sum(jnp.where(matches, lane_ids[None, :], 0), axis=1)
    target = jnp.where(use_copy, holder, flat_ids)
    copy_role = use_copy.astype(jnp.int32)
    bucket = target * 2 + copy_role
    sequence = jnp.arange(bucket.shape[0], dtype=jnp.int32)
    arrival = jnp.sum(
        jnp.logical_and(bucket[None, :] == bucket[:, None], sequence[None, :] < sequence[:, None]),
        axis=1,
    )
    kept_mask = arrival < capacity
    slot_index = target * (2 * capacity) + copy_role * capacity + jnp.minimum(arrival, capacity - 1)
    return (slot_index, kept_mask)


def fill_slots(slot_index, kept_mask, slot_count):
    slot_ids = jnp.arange(slot_count, dtype=jnp.int32)
    matches = jnp.logical_and(slot_index[None, :] == slot_ids[:, None], kept_mask[None, :])
    sequence = jnp.arange(slot_index.shape[0], dtype=jnp.int32)
    source = jnp.sum(jnp.where(matches, sequence[None, :], 0), axis=1)
    filled = jnp.any(matches, axis=1)
    return (source, filled)


def expert_backward(row_block, upstream, weight, gate_w, up_w, down_w):
    contract_cols = (((1,), (1,)), ((), ()))
    contract_rows = (((0,), (0,)), ((), ()))
    gate_pre = jnp.dot(row_block, gate_w, preferred_element_type=jnp.float32)
    up_pre = jnp.dot(row_block, up_w, preferred_element_type=jnp.float32)
    sigmoid_gate = jax.nn.sigmoid(gate_pre)
    activated = gate_pre * sigmoid_gate
    hidden = (activated * up_pre).astype(jnp.bfloat16)
    output_rows = lax.dot_general(hidden, down_w, contract_cols, preferred_element_type=jnp.float32)
    weight_col = weight.astype(jnp.float32)[:, None]
    upstream_f = upstream.astype(jnp.float32)
    gate_rows = jnp.sum(upstream_f * output_rows, axis=1)
    hidden_grad = weight_col * jnp.dot(upstream, down_w, preferred_element_type=jnp.float32)
    slope = sigmoid_gate * (1.0 + gate_pre * (1.0 - sigmoid_gate))
    gate_delta = (hidden_grad * up_pre * slope).astype(jnp.bfloat16)
    up_delta = (hidden_grad * activated).astype(jnp.bfloat16)
    input_grad = (
        lax.dot_general(gate_delta, gate_w, contract_cols, preferred_element_type=jnp.float32)
        + lax.dot_general(up_delta, up_w, contract_cols, preferred_element_type=jnp.float32)
    ).astype(jnp.bfloat16)
    scaled = (weight_col * upstream_f).astype(jnp.bfloat16)
    grad_set = (
        lax.dot_general(row_block, gate_delta, contract_rows, preferred_element_type=jnp.float32),
        lax.dot_general(row_block, up_delta, contract_rows, preferred_element_type=jnp.float32),
        lax.dot_general(scaled, hidden, contract_rows, preferred_element_type=jnp.float32),
    )
    return (input_grad, gate_rows, grad_set)


def per_device_moving_weights(
    tokens,
    cotangent,
    expert_ids,
    gate_values,
    replica_pick,
    replica_plan,
    gate_proj,
    up_proj,
    down_proj,
):
    experts = lax.axis_size("expert")
    capacity = CAP
    slot_total = 2 * capacity
    model_width = tokens.shape[1]
    topk = expert_ids.shape[1]
    token_count = tokens.shape[0]
    slot_index, kept_mask = route_assignments(
        expert_ids.reshape(-1), replica_pick.reshape(-1), replica_plan, capacity
    )
    source, filled = fill_slots(slot_index, kept_mask, experts * slot_total)
    token_of = source // topk
    zero_half = jnp.zeros((), jnp.bfloat16)
    send_rows = jnp.where(filled[:, None], jnp.take(tokens, token_of, axis=0), zero_half).reshape(
        experts, slot_total, model_width
    )
    send_upstream = jnp.where(
        filled[:, None], jnp.take(cotangent, token_of, axis=0), zero_half
    ).reshape(experts, slot_total, model_width)
    send_weight = jnp.where(filled, gate_values.reshape(-1)[source], zero_half).reshape(
        experts, slot_total
    )
    arrived = lax.all_to_all(send_rows, "expert", split_axis=0, concat_axis=0, tiled=True)
    own_gate = gate_proj[0]
    own_up = up_proj[0]
    own_down = down_proj[0]
    hidden_width = own_gate.shape[1]
    spread = (
        lax.all_to_all(
            own_gate.reshape(experts, -1), "expert", split_axis=0, concat_axis=0, tiled=True
        ),
        lax.all_to_all(
            own_up.reshape(experts, -1), "expert", split_axis=0, concat_axis=0, tiled=True
        ),
        lax.all_to_all(
            own_down.reshape(experts, -1), "expert", split_axis=0, concat_axis=0, tiled=True
        ),
    )
    chosen_gate = jnp.take(spread[0], replica_plan, axis=0)
    chosen_up = jnp.take(spread[1], replica_plan, axis=0)
    chosen_down = jnp.take(spread[2], replica_plan, axis=0)
    collected = (
        lax.all_to_all(chosen_gate, "expert", split_axis=0, concat_axis=0, tiled=True),
        lax.all_to_all(chosen_up, "expert", split_axis=0, concat_axis=0, tiled=True),
        lax.all_to_all(chosen_down, "expert", split_axis=0, concat_axis=0, tiled=True),
    )
    copy_gate = collected[0].reshape(model_width, hidden_width)
    copy_up = collected[1].reshape(model_width, hidden_width)
    copy_down = collected[2].reshape(model_width, hidden_width)
    arrived_up, arrived_weight = (
        lax.all_to_all(send_upstream, "expert", split_axis=0, concat_axis=0, tiled=True),
        lax.all_to_all(send_weight, "expert", split_axis=0, concat_axis=0, tiled=True),
    )
    owned_dx, owned_gate_rows, owned_grads = expert_backward(
        arrived[:, :capacity].reshape(-1, model_width),
        arrived_up[:, :capacity].reshape(-1, model_width),
        arrived_weight[:, :capacity].reshape(-1),
        own_gate,
        own_up,
        own_down,
    )
    copied_dx, copied_gate_rows, copied_grads = expert_backward(
        arrived[:, capacity:].reshape(-1, model_width),
        arrived_up[:, capacity:].reshape(-1, model_width),
        arrived_weight[:, capacity:].reshape(-1),
        copy_gate,
        copy_up,
        copy_down,
    )
    back_rows = jnp.concatenate(
        [
            owned_dx.reshape(experts, capacity, model_width),
            copied_dx.reshape(experts, capacity, model_width),
        ],
        axis=1,
    )
    back_gate = jnp.concatenate(
        [owned_gate_rows.reshape(experts, capacity), copied_gate_rows.reshape(experts, capacity)],
        axis=1,
    ).astype(jnp.bfloat16)
    returned, returned_gate = (
        lax.all_to_all(back_rows, "expert", split_axis=0, concat_axis=0, tiled=True),
        lax.all_to_all(back_gate, "expert", split_axis=0, concat_axis=0, tiled=True),
    )
    copy_pieces = (
        copied_grads[0].astype(jnp.bfloat16).reshape(experts, -1),
        copied_grads[1].astype(jnp.bfloat16).reshape(experts, -1),
        copied_grads[2].astype(jnp.bfloat16).reshape(experts, -1),
    )
    grad_spread = (
        lax.all_to_all(copy_pieces[0], "expert", split_axis=0, concat_axis=0, tiled=True),
        lax.all_to_all(copy_pieces[1], "expert", split_axis=0, concat_axis=0, tiled=True),
        lax.all_to_all(copy_pieces[2], "expert", split_axis=0, concat_axis=0, tiled=True),
    )
    lane_ids = jnp.arange(experts, dtype=jnp.int32)
    owner_map = (replica_plan[None, :] == lane_ids[:, None]).astype(jnp.bfloat16)
    summed_gate = jnp.dot(owner_map, grad_spread[0], preferred_element_type=jnp.float32).astype(
        jnp.bfloat16
    )
    summed_up = jnp.dot(owner_map, grad_spread[1], preferred_element_type=jnp.float32).astype(
        jnp.bfloat16
    )
    summed_down = jnp.dot(owner_map, grad_spread[2], preferred_element_type=jnp.float32).astype(
        jnp.bfloat16
    )
    grad_back = (
        lax.all_to_all(summed_gate, "expert", split_axis=0, concat_axis=0, tiled=True),
        lax.all_to_all(summed_up, "expert", split_axis=0, concat_axis=0, tiled=True),
        lax.all_to_all(summed_down, "expert", split_axis=0, concat_axis=0, tiled=True),
    )
    total_gate = owned_grads[0] + grad_back[0].reshape(model_width, hidden_width).astype(
        jnp.float32
    )
    total_up = owned_grads[1] + grad_back[1].reshape(model_width, hidden_width).astype(jnp.float32)
    total_down = owned_grads[2] + grad_back[2].reshape(model_width, hidden_width).astype(
        jnp.float32
    )
    shares = (
        lax.psum_scatter(
            total_gate.astype(jnp.bfloat16), "replica", scatter_dimension=0, tiled=True
        ).astype(jnp.float32),
        lax.psum_scatter(
            total_up.astype(jnp.bfloat16), "replica", scatter_dimension=0, tiled=True
        ).astype(jnp.float32),
        lax.psum_scatter(
            total_down.astype(jnp.bfloat16), "replica", scatter_dimension=0, tiled=True
        ).astype(jnp.float32),
    )
    flat_back = returned.reshape(experts * slot_total, model_width)
    picked_rows = jnp.take(flat_back, slot_index, axis=0)
    picked_rows = jnp.where(kept_mask[:, None], picked_rows, zero_half).astype(jnp.float32)
    token_grad = jnp.sum(picked_rows.reshape(token_count, topk, model_width), axis=1).astype(
        jnp.bfloat16
    )
    gate_grad = jnp.where(kept_mask, returned_gate.reshape(-1)[slot_index], zero_half).reshape(
        token_count, topk
    )
    return (
        token_grad,
        gate_grad,
        shares[0].astype(jnp.bfloat16)[None],
        shares[1].astype(jnp.bfloat16)[None],
        shares[2].astype(jnp.bfloat16)[None],
    )


BF = jnp.bfloat16
F32 = jnp.float32
CONTRACT_ROWS = (((0,), (0,)), ((), ()))
CONTRACT_COLS = (((1,), (1,)), ((), ()))
MIB = 1024 * 1024

BASES = (4, 6, 2)
ORDER = (0, 2, 4, 3, 5, 1, 6, 7)
LONG = 8 * 10**9
MAIN = 16
QUARTERS = 4
SEND_ROWS = 2 * QUARTERS * MAIN + 16
BACK_ROWS = QUARTERS * MAIN + 16


def copies_of(experts):
    return 2 if experts <= 8 else 8


def iota(shape, axis):
    return lax.broadcasted_iota(jnp.int32, shape, axis)


def partners(experts, tokens):
    row = iota((experts, tokens), 0)
    step = jnp.bitwise_xor(jnp.bitwise_and(row, 1), lax.axis_index("replica"))
    for d, base in enumerate(BASES):
        step = jnp.where(jnp.right_shift(row, 1) == d + 1, step + base, step)
    step = jnp.where(row < 2, row, step)
    return jnp.bitwise_xor(step, lax.axis_index("expert"))


def chunk_views(refs, rows):
    return [(refs[0], 0), (refs[1], 0)] + [(ref, part * rows) for ref in refs[2:] for part in (0, 1)]


def mask(condition):
    return condition.astype(F32).astype(BF)


def repeat_rows(table, times):
    width = table.shape[1]
    return jnp.concatenate(
        [jnp.broadcast_to(table[e : e + 1], (times, width)) for e in range(table.shape[0])], axis=0
    )


def route_kernel(plan_hbm, ids_hbm, pick_hbm, gate_hbm, tok_hbm, cot_hbm, *refs):
    sems = refs[-1]
    plan_ref, ids_ref, pick_ref, gate_ref, tok_ref, cot_ref = refs[-7:-1]
    slot_ref, gates_ref = refs[-9:-7]
    send_refs = refs[:-9]
    topk, tokens = ids_ref.shape
    experts = len(send_refs)
    width = tok_ref.shape[1] // QUARTERS
    copies = copies_of(experts)
    loads = [
        pltpu.make_async_copy(source, place, sems.at[n])
        for n, (source, place) in enumerate(
            (
                (plan_hbm, plan_ref),
                (ids_hbm, ids_ref),
                (pick_hbm, pick_ref),
                (gate_hbm, gate_ref),
                (tok_hbm, tok_ref),
                (cot_hbm, cot_ref),
            )
        )
    ]
    for load in loads:
        load.start()
    before = mask(iota((tokens, tokens), 0) < iota((tokens, tokens), 1))
    expert_row = partners(experts, tokens)
    for load in loads[:4]:
        load.wait()
    ids = ids_ref[...]
    pick = pick_ref[...]
    gate = gate_ref[...].astype(F32)
    named = jnp.zeros((experts, tokens), jnp.int32)
    gates = jnp.zeros((experts, tokens), F32)
    for k in range(topk):
        hit = ids[k : k + 1] == expert_row
        named = jnp.where(hit, pick[k : k + 1] + 1, named)
        gates = jnp.where(hit, gate[k : k + 1], gates)
    hot = jnp.zeros((experts, tokens), jnp.int32)
    for j in range(experts):
        hot = jnp.where(expert_row == plan_ref[j], 1, hot)
    chosen = jnp.where(named == 0, -1, jnp.where(hot > 0, named - 1, 0))
    masks = jnp.concatenate([(chosen == c).astype(F32) for c in range(copies + 1)], axis=0)
    rank = jnp.dot(masks.astype(BF), before, preferred_element_type=F32).astype(jnp.int32)
    slot = jnp.full((experts, tokens), -1, jnp.int32)
    for c in range(copies + 1):
        rank_c = rank[c * experts : (c + 1) * experts]
        keep = jnp.logical_and(chosen == c, rank_c < CAP)
        slot = jnp.where(keep, c * CAP + rank_c, slot)
    slot_ref[...] = slot
    gates_ref[...] = gates
    slot16 = repeat_rows(slot, MAIN)
    gate16 = repeat_rows(gates, MAIN)
    inner = jnp.bitwise_and(iota(slot16.shape, 0), MAIN - 1)
    onehot = (slot16 == inner).astype(F32)
    wanted = MAIN + jnp.bitwise_and(jnp.right_shift(inner, 2), 1)
    last = (slot16 == wanted).astype(F32)
    last_rows = jnp.where(inner >= 8, 0.0, last)
    last_scaled = jnp.where(inner >= 8, last * gate16, 0.0)
    quarter = jnp.bitwise_and(inner, 3)
    for load in loads[4:]:
        load.wait()
    rows = jnp.dot(onehot.astype(BF), tok_ref[...], preferred_element_type=F32).astype(BF)
    scaled = jnp.dot(
        (onehot * gate16).astype(BF), cot_ref[...], preferred_element_type=F32
    ).astype(BF)
    tail = jnp.zeros((experts * MAIN, width), F32)
    for q in range(QUARTERS):
        cols = slice(q * width, (q + 1) * width)
        mine = quarter == q
        tail += jnp.dot(
            jnp.where(mine, last_rows, 0.0).astype(BF), tok_ref[:, cols], preferred_element_type=F32
        )
        tail += jnp.dot(
            jnp.where(mine, last_scaled, 0.0).astype(BF),
            cot_ref[:, cols],
            preferred_element_type=F32,
        )
    tail = tail.astype(BF)
    for c, ref in enumerate(send_refs):
        here = slice(c * MAIN, (c + 1) * MAIN)
        for q in range(QUARTERS):
            cols = slice(q * width, (q + 1) * width)
            ref[q * MAIN : (q + 1) * MAIN, :] = rows[here, cols]
            ref[(QUARTERS + q) * MAIN : (QUARTERS + q + 1) * MAIN, :] = scaled[here, cols]
        ref[2 * QUARTERS * MAIN :, :] = tail[here]


def expert_kernel(*refs):
    experts = len(ORDER)
    recv_refs = [refs[ORDER.index(c)] for c in range(experts)]
    gate_ref, up_ref, down_ref = refs[experts : experts + 3]
    back_views = chunk_views(refs[experts + 3 : -5], BACK_ROWS)
    x_ref, s_ref, dg_ref, du_ref, hid_ref = refs[-5:]
    width = refs[0].shape[1]
    main_rows = experts * MAIN
    tail = jnp.concatenate([ref[2 * QUARTERS * MAIN :, :] for ref in recv_refs], axis=0)
    row = iota((4 * experts, main_rows), 0)
    col = iota((4 * experts, main_rows), 1)
    kind = (row >= 2 * experts).astype(jnp.int32)
    chunk = jnp.right_shift(row - kind * 2 * experts, 1)
    base = chunk * MAIN + kind * 8 + jnp.bitwise_and(row, 1) * 4
    for q in range(QUARTERS):
        cols = slice(q * width, (q + 1) * width)
        picked = jnp.dot(mask(col == base + q), tail, preferred_element_type=F32).astype(BF)
        x_ref[main_rows:, cols] = picked[: 2 * experts]
        s_ref[main_rows:, cols] = picked[2 * experts :]
        for i, ref in enumerate(recv_refs):
            here = slice(i * MAIN, (i + 1) * MAIN)
            x_ref[here, cols] = ref[q * MAIN : (q + 1) * MAIN, :]
            s_ref[here, cols] = ref[(QUARTERS + q) * MAIN : (QUARTERS + q + 1) * MAIN, :]
    rows = x_ref[...]
    gate_pre = jnp.dot(rows, gate_ref[...], preferred_element_type=F32)
    up_pre = jnp.dot(rows, up_ref[...], preferred_element_type=F32)
    hidden_grad = jnp.dot(s_ref[...], down_ref[...], preferred_element_type=F32)
    sig = jax.nn.sigmoid(gate_pre)
    activated = gate_pre * sig
    hidden = (activated * up_pre).astype(BF)
    slope = sig * (1.0 + gate_pre * (1.0 - sig))
    gate_delta = (hidden_grad * up_pre * slope).astype(BF)
    up_delta = (hidden_grad * activated).astype(BF)
    hid_ref[...] = hidden
    dg_ref[...] = gate_delta
    du_ref[...] = up_delta
    grad = (
        lax.dot_general(gate_delta, gate_ref[...], CONTRACT_COLS, preferred_element_type=F32)
        + lax.dot_general(up_delta, up_ref[...], CONTRACT_COLS, preferred_element_type=F32)
    ).astype(BF)
    product = hidden.astype(F32) * hidden_grad
    product = jnp.concatenate(
        [product, jnp.zeros((width - product.shape[0], product.shape[1]), F32)], axis=0
    )
    gate_lanes = lax.dot_general(
        jnp.ones((8, product.shape[1]), F32),
        product,
        CONTRACT_COLS,
        preferred_element_type=F32,
        precision=lax.Precision.HIGHEST,
    )
    trow = iota((main_rows, 2 * experts), 0)
    tcol = iota((main_rows, 2 * experts), 1)
    inner = jnp.bitwise_and(trow, MAIN - 1)
    source = jnp.right_shift(trow, 4) * 2 + jnp.right_shift(inner, 2)
    spread = jnp.zeros((main_rows, width), F32)
    for q in range(QUARTERS):
        cols = slice(q * width, (q + 1) * width)
        mine = jnp.logical_and(jnp.bitwise_and(inner, 3) == q, inner < 8)
        place = mask(jnp.logical_and(mine, tcol == source))
        spread += jnp.dot(place, grad[main_rows:, cols], preferred_element_type=F32)
        for i, (ref, first) in enumerate(back_views):
            low = first + q * MAIN
            ref[low : low + MAIN, :] = grad[i * MAIN : (i + 1) * MAIN, cols]
    for i, (ref, first) in enumerate(back_views):
        low = first + QUARTERS * MAIN
        ref[low : low + 16, :] = jnp.concatenate(
            [spread[i * MAIN : i * MAIN + 8], gate_lanes], axis=0
        ).astype(BF)


def grads_of(half, x_ref, s_ref, dg_ref, du_ref, hid_ref):
    rows = x_ref.shape[1] // 2
    cols = pl.ds(pl.multiple_of(half * rows, rows), rows)
    x_half = x_ref[:, cols]
    s_half = s_ref[:, cols]
    return (
        lax.dot_general(x_half, dg_ref[...], CONTRACT_ROWS, preferred_element_type=F32),
        lax.dot_general(x_half, du_ref[...], CONTRACT_ROWS, preferred_element_type=F32),
        lax.dot_general(s_half, hid_ref[...], CONTRACT_ROWS, preferred_element_type=F32),
    )


def other_half_kernel(x_ref, s_ref, dg_ref, du_ref, hid_ref, out_ref):
    half = 1 - lax.axis_index("replica")
    parts = grads_of(half, x_ref, s_ref, dg_ref, du_ref, hid_ref)
    rows = parts[0].shape[0]
    for n in range(3):
        out_ref[n * rows : (n + 1) * rows, :] = parts[n].astype(BF)


def own_half_kernel(
    x_ref, s_ref, dg_ref, du_ref, hid_ref, came_ref, gate_ref, up_ref, down_ref
):
    parts = grads_of(lax.axis_index("replica"), x_ref, s_ref, dg_ref, du_ref, hid_ref)
    rows = parts[0].shape[0]
    for n, out_ref in enumerate((gate_ref, up_ref, down_ref)):
        came = came_ref[n * rows : (n + 1) * rows, :].astype(F32)
        out_ref[...] = (parts[n].astype(BF).astype(F32) + came).astype(BF)


def combine_kernel(ids_ref, slot_ref, gates_ref, *refs):
    token_ref, grad_ref = refs[-2:]
    doubles = 2 + len(BASES)
    ret_views = [(refs[0], 0), (refs[1], 0)]
    for kept_ref, given_ref in zip(refs[2:doubles], refs[doubles:-2]):
        ret_views += [(kept_ref, 0), (given_ref, BACK_ROWS)]
    topk, tokens = ids_ref.shape
    experts = len(ret_views)
    width = refs[0].shape[1]
    ids = ids_ref[...]
    slot = slot_ref[...]
    slot16 = repeat_rows(slot, MAIN)
    inner = jnp.bitwise_and(iota(slot16.shape, 0), MAIN - 1)
    onehot = mask(slot16 == inner)
    wanted = MAIN + jnp.right_shift(inner, 2)
    last = jnp.where(jnp.logical_and(slot16 == wanted, inner < 8), 1.0, 0.0)
    quarter = jnp.bitwise_and(inner, 3)
    tails = [ref[first + BACK_ROWS - 16 : first + BACK_ROWS, :] for ref, first in ret_views]
    tail = jnp.concatenate(tails, axis=0)
    for q in range(QUARTERS):
        main = jnp.concatenate(
            [ref[first + q * MAIN : first + (q + 1) * MAIN, :] for ref, first in ret_views], axis=0
        )
        place = jnp.where(quarter == q, last, 0.0).astype(BF)
        total = lax.dot_general(onehot, main, CONTRACT_ROWS, preferred_element_type=F32)
        total += lax.dot_general(place, tail, CONTRACT_ROWS, preferred_element_type=F32)
        token_ref[:, q * width : (q + 1) * width] = total.astype(BF)
    lane_index = iota((width, tokens), 0)
    found = []
    for c in range(experts):
        mine = slot[c : c + 1]
        lane = jnp.where(mine < MAIN, c * MAIN + mine, experts * MAIN + 2 * c + mine - MAIN)
        lane = jnp.where(mine < 0, -1, lane)
        sums = jnp.dot(tails[c], mask(lane_index == lane), preferred_element_type=F32)
        found.append(sums[8:9])
    found = jnp.concatenate(found, axis=0)
    kept = slot >= 0
    grads = jnp.where(kept, found / jnp.where(kept, gates_ref[...], 1.0), 0.0)
    expert_row = partners(experts, tokens)
    by_choice = [
        jnp.sum(jnp.where(expert_row == ids[k : k + 1], grads, 0.0), axis=0, keepdims=True)
        for k in range(topk)
    ]
    grad_ref[...] = jnp.concatenate(by_choice, axis=0).astype(BF)


def local_call(kernel, outs, arrays, name, flops, moved, space=pltpu.VMEM, scratch=(), limit=16):
    vmem = pl.BlockSpec(memory_space=pltpu.VMEM)
    return pl.pallas_call(
        kernel,
        out_shape=[jax.ShapeDtypeStruct(shape, kind) for shape, kind in outs],
        in_specs=[pl.BlockSpec(memory_space=space)] * len(arrays),
        out_specs=[vmem] * len(outs),
        scratch_shapes=list(scratch),
        compiler_params=pltpu.CompilerParams(vmem_limit_bytes=limit * MIB),
        cost_estimate=pl.CostEstimate(flops=flops, bytes_accessed=moved, transcendentals=0),
        name=name,
    )(*arrays)


def to_step(chunk, base):
    experts = lax.axis_size("expert")
    if base == 1:
        return lax.ppermute(chunk, "expert", [(i, i ^ 1) for i in range(experts)])
    pairs = [(2 * i + r, 2 * (i ^ (base + r)) + r) for i in range(experts) for r in range(2)]
    return lax.ppermute(chunk, ("expert", "replica"), pairs)


def to_twin(chunk):
    return lax.ppermute(chunk, "replica", [(0, 1), (1, 0)])


def per_device_moving_rows(
    tokens,
    cotangent,
    expert_ids,
    gate_values,
    replica_pick,
    replica_plan,
    gate_proj,
    up_proj,
    down_proj,
):
    experts = lax.axis_size("expert")
    token_count, model_width = tokens.shape
    topk = expert_ids.shape[1]
    hidden_width = gate_proj.shape[2]
    width = model_width // QUARTERS
    served = experts * (MAIN + 2)
    small = (topk, token_count)
    count = len(BASES)
    *chunks, slot, gates = local_call(
        route_kernel,
        [((SEND_ROWS, width), BF)] * experts
        + [((experts, token_count), jnp.int32), ((experts, token_count), F32)],
        [replica_plan, expert_ids.T, replica_pick.T, gate_values.T, tokens, cotangent],
        "route",
        LONG,
        2 * 2 * (token_count + served) * model_width,
        space=pltpu.HBM,
        limit=54,
        scratch=[
            pltpu.SMEM((experts,), jnp.int32),
            pltpu.VMEM(small, jnp.int32),
            pltpu.VMEM(small, jnp.int32),
            pltpu.VMEM(small, BF),
            pltpu.VMEM(tokens.shape, BF),
            pltpu.VMEM(tokens.shape, BF),
            pltpu.SemaphoreType.DMA((6,)),
        ],
    )
    recv = list(chunks)
    far = [to_twin(chunks[3]), to_twin(chunks[5])]
    far, near = lax.optimization_barrier((far, [chunks[1], chunks[6]]))
    for d, twin in enumerate([*far, to_twin(chunks[7])]):
        recv[3 + 2 * d] = to_step(twin, BASES[d])
    recv[2] = to_step(chunks[2], 4)
    recv[4] = to_step(chunks[4], 6)
    recv[6] = to_step(near[1], 2)
    recv[1] = to_step(near[0], 1)
    matmul = 2 * served * model_width * hidden_width
    outs = local_call(
        expert_kernel,
        [((BACK_ROWS, width), BF)] * 2
        + [((2 * BACK_ROWS, width), BF)] * count
        + [((served, model_width), BF)] * 2
        + [((served, hidden_width), BF)] * 3,
        [*(recv[c] for c in ORDER), gate_proj[0], up_proj[0], down_proj[0]],
        "expert_rows",
        5 * matmul,
        2 * 3 * model_width * hidden_width,
    )
    backs, factors = outs[: 2 + count], outs[2 + count :]
    kept = list(map(to_step, backs[2:], BASES))
    near = to_step(backs[1], 1)
    half = model_width // 2
    (leaving,) = local_call(
        other_half_kernel,
        [((3 * half, hidden_width), BF)],
        factors,
        "other_half",
        1,
        1,
    )
    shares = local_call(
        own_half_kernel,
        [((half, hidden_width), BF)] * 3,
        [*factors, to_twin(leaving)],
        "own_half",
        1,
        1,
    )
    kept[0], near = lax.optimization_barrier((kept[0], near))
    kept[1], shares = lax.optimization_barrier((kept[1], shares))
    returned = [backs[0], near, *kept, *map(to_twin, kept)]
    token_grad, gate_grad = local_call(
        combine_kernel,
        [((token_count, model_width), BF), ((topk, token_count), BF)],
        [expert_ids.T, slot, gates, *returned],
        "combine",
        2 * served * token_count * model_width,
        2 * 2 * token_count * model_width,
    )
    return (token_grad, gate_grad.T, shares[0][None], shares[1][None], shares[2][None])


def per_device(tokens, cotangent, expert_ids, gate_values, replica_pick, replica_plan, *matrices):
    experts = lax.axis_size("expert")
    slots = (copies_of(experts) + 1) * CAP
    row_bytes = 3 * 2 * tokens.shape[1] * experts
    matrix_bytes = 4 * sum(2 * m[0].size for m in matrices)
    fits = slots == MAIN + 2 and experts == 8 and lax.axis_size("replica") == 2
    rows_cheaper = slots * row_bytes < 2 * CAP * row_bytes + matrix_bytes
    plan = per_device_moving_rows if fits and rows_cheaper else per_device_moving_weights
    return plan(
        tokens, cotangent, expert_ids, gate_values, replica_pick, replica_plan, *matrices
    )


def solution(mesh):
    placed = (
        P(("parts", "expert", "replica"), None),
        P(("parts", "expert", "replica"), None),
        P(("parts", "expert", "replica"), None),
        P(("parts", "expert", "replica"), None),
        P(("parts", "expert", "replica"), None),
        P("parts"),
        P("expert", None, None),
        P("expert", None, None),
        P("expert", None, None),
    )
    return jax.shard_map(
        per_device,
        mesh=mesh,
        in_specs=placed,
        out_specs=(
            P(("parts", "expert", "replica"), None),
            P(("parts", "expert", "replica"), None),
            P(("parts", "expert"), "replica", None),
            P(("parts", "expert"), "replica", None),
            P(("parts", "expert"), "replica", None),
        ),
        check_vma=False,
    )
```

```python
import jax
import jax.numpy as jnp
from jax import lax
from jax.experimental import pallas as pl
from jax.experimental.pallas import tpu as pltpu
from jax.sharding import PartitionSpec as P

CAP = 6


def route_assignments(flat_ids, flat_pick, replica_plan, capacity):
    experts = replica_plan.shape[0]
    lane_ids = jnp.arange(experts, dtype=jnp.int32)
    same_plan = replica_plan[:, None] == replica_plan[None, :]
    earlier = lane_ids[None, :] < lane_ids[:, None]
    position = jnp.sum(jnp.logical_and(same_plan, earlier), axis=1)
    hot_mask = jnp.any(replica_plan[None, :] == lane_ids[:, None], axis=1)
    is_hot = jnp.any(
        jnp.logical_and(flat_ids[:, None] == lane_ids[None, :], hot_mask[None, :]), axis=1
    )
    use_copy = jnp.logical_and(is_hot, flat_pick >= 1)
    matches = jnp.logical_and(
        replica_plan[None, :] == flat_ids[:, None], position[None, :] == flat_pick[:, None] - 1
    )
    holder = jnp.sum(jnp.where(matches, lane_ids[None, :], 0), axis=1)
    target = jnp.where(use_copy, holder, flat_ids)
    copy_role = use_copy.astype(jnp.int32)
    bucket = target * 2 + copy_role
    sequence = jnp.arange(bucket.shape[0], dtype=jnp.int32)
    arrival = jnp.sum(
        jnp.logical_and(bucket[None, :] == bucket[:, None], sequence[None, :] < sequence[:, None]),
        axis=1,
    )
    kept_mask = arrival < capacity
    slot_index = target * (2 * capacity) + copy_role * capacity + jnp.minimum(arrival, capacity - 1)
    return (slot_index, kept_mask)


def fill_slots(slot_index, kept_mask, slot_count):
    slot_ids = jnp.arange(slot_count, dtype=jnp.int32)
    matches = jnp.logical_and(slot_index[None, :] == slot_ids[:, None], kept_mask[None, :])
    sequence = jnp.arange(slot_index.shape[0], dtype=jnp.int32)
    source = jnp.sum(jnp.where(matches, sequence[None, :], 0), axis=1)
    filled = jnp.any(matches, axis=1)
    return (source, filled)


def expert_backward(row_block, upstream, weight, gate_w, up_w, down_w):
    contract_cols = (((1,), (1,)), ((), ()))
    contract_rows = (((0,), (0,)), ((), ()))
    gate_pre = jnp.dot(row_block, gate_w, preferred_element_type=jnp.float32)
    up_pre = jnp.dot(row_block, up_w, preferred_element_type=jnp.float32)
    sigmoid_gate = jax.nn.sigmoid(gate_pre)
    activated = gate_pre * sigmoid_gate
    hidden = (activated * up_pre).astype(jnp.bfloat16)
    output_rows = lax.dot_general(hidden, down_w, contract_cols, preferred_element_type=jnp.float32)
    weight_col = weight.astype(jnp.float32)[:, None]
    upstream_f = upstream.astype(jnp.float32)
    gate_rows = jnp.sum(upstream_f * output_rows, axis=1)
    hidden_grad = weight_col * jnp.dot(upstream, down_w, preferred_element_type=jnp.float32)
    slope = sigmoid_gate * (1.0 + gate_pre * (1.0 - sigmoid_gate))
    gate_delta = (hidden_grad * up_pre * slope).astype(jnp.bfloat16)
    up_delta = (hidden_grad * activated).astype(jnp.bfloat16)
    input_grad = (
        lax.dot_general(gate_delta, gate_w, contract_cols, preferred_element_type=jnp.float32)
        + lax.dot_general(up_delta, up_w, contract_cols, preferred_element_type=jnp.float32)
    ).astype(jnp.bfloat16)
    scaled = (weight_col * upstream_f).astype(jnp.bfloat16)
    grad_set = (
        lax.dot_general(row_block, gate_delta, contract_rows, preferred_element_type=jnp.float32),
        lax.dot_general(row_block, up_delta, contract_rows, preferred_element_type=jnp.float32),
        lax.dot_general(scaled, hidden, contract_rows, preferred_element_type=jnp.float32),
    )
    return (input_grad, gate_rows, grad_set)


def per_device_moving_weights(
    tokens,
    cotangent,
    expert_ids,
    gate_values,
    replica_pick,
    replica_plan,
    gate_proj,
    up_proj,
    down_proj,
):
    experts = lax.axis_size("expert")
    capacity = CAP
    slot_total = 2 * capacity
    model_width = tokens.shape[1]
    topk = expert_ids.shape[1]
    token_count = tokens.shape[0]
    slot_index, kept_mask = route_assignments(
        expert_ids.reshape(-1), replica_pick.reshape(-1), replica_plan, capacity
    )
    source, filled = fill_slots(slot_index, kept_mask, experts * slot_total)
    token_of = source // topk
    zero_half = jnp.zeros((), jnp.bfloat16)
    send_rows = jnp.where(filled[:, None], jnp.take(tokens, token_of, axis=0), zero_half).reshape(
        experts, slot_total, model_width
    )
    send_upstream = jnp.where(
        filled[:, None], jnp.take(cotangent, token_of, axis=0), zero_half
    ).reshape(experts, slot_total, model_width)
    send_weight = jnp.where(filled, gate_values.reshape(-1)[source], zero_half).reshape(
        experts, slot_total
    )
    arrived = lax.all_to_all(send_rows, "expert", split_axis=0, concat_axis=0, tiled=True)
    own_gate = gate_proj[0]
    own_up = up_proj[0]
    own_down = down_proj[0]
    hidden_width = own_gate.shape[1]
    spread = (
        lax.all_to_all(
            own_gate.reshape(experts, -1), "expert", split_axis=0, concat_axis=0, tiled=True
        ),
        lax.all_to_all(
            own_up.reshape(experts, -1), "expert", split_axis=0, concat_axis=0, tiled=True
        ),
        lax.all_to_all(
            own_down.reshape(experts, -1), "expert", split_axis=0, concat_axis=0, tiled=True
        ),
    )
    chosen_gate = jnp.take(spread[0], replica_plan, axis=0)
    chosen_up = jnp.take(spread[1], replica_plan, axis=0)
    chosen_down = jnp.take(spread[2], replica_plan, axis=0)
    collected = (
        lax.all_to_all(chosen_gate, "expert", split_axis=0, concat_axis=0, tiled=True),
        lax.all_to_all(chosen_up, "expert", split_axis=0, concat_axis=0, tiled=True),
        lax.all_to_all(chosen_down, "expert", split_axis=0, concat_axis=0, tiled=True),
    )
    copy_gate = collected[0].reshape(model_width, hidden_width)
    copy_up = collected[1].reshape(model_width, hidden_width)
    copy_down = collected[2].reshape(model_width, hidden_width)
    arrived_up, arrived_weight = (
        lax.all_to_all(send_upstream, "expert", split_axis=0, concat_axis=0, tiled=True),
        lax.all_to_all(send_weight, "expert", split_axis=0, concat_axis=0, tiled=True),
    )
    owned_dx, owned_gate_rows, owned_grads = expert_backward(
        arrived[:, :capacity].reshape(-1, model_width),
        arrived_up[:, :capacity].reshape(-1, model_width),
        arrived_weight[:, :capacity].reshape(-1),
        own_gate,
        own_up,
        own_down,
    )
    copied_dx, copied_gate_rows, copied_grads = expert_backward(
        arrived[:, capacity:].reshape(-1, model_width),
        arrived_up[:, capacity:].reshape(-1, model_width),
        arrived_weight[:, capacity:].reshape(-1),
        copy_gate,
        copy_up,
        copy_down,
    )
    back_rows = jnp.concatenate(
        [
            owned_dx.reshape(experts, capacity, model_width),
            copied_dx.reshape(experts, capacity, model_width),
        ],
        axis=1,
    )
    back_gate = jnp.concatenate(
        [owned_gate_rows.reshape(experts, capacity), copied_gate_rows.reshape(experts, capacity)],
        axis=1,
    ).astype(jnp.bfloat16)
    returned, returned_gate = (
        lax.all_to_all(back_rows, "expert", split_axis=0, concat_axis=0, tiled=True),
        lax.all_to_all(back_gate, "expert", split_axis=0, concat_axis=0, tiled=True),
    )
    copy_pieces = (
        copied_grads[0].astype(jnp.bfloat16).reshape(experts, -1),
        copied_grads[1].astype(jnp.bfloat16).reshape(experts, -1),
        copied_grads[2].astype(jnp.bfloat16).reshape(experts, -1),
    )
    grad_spread = (
        lax.all_to_all(copy_pieces[0], "expert", split_axis=0, concat_axis=0, tiled=True),
        lax.all_to_all(copy_pieces[1], "expert", split_axis=0, concat_axis=0, tiled=True),
        lax.all_to_all(copy_pieces[2], "expert", split_axis=0, concat_axis=0, tiled=True),
    )
    lane_ids = jnp.arange(experts, dtype=jnp.int32)
    owner_map = (replica_plan[None, :] == lane_ids[:, None]).astype(jnp.bfloat16)
    summed_gate = jnp.dot(owner_map, grad_spread[0], preferred_element_type=jnp.float32).astype(
        jnp.bfloat16
    )
    summed_up = jnp.dot(owner_map, grad_spread[1], preferred_element_type=jnp.float32).astype(
        jnp.bfloat16
    )
    summed_down = jnp.dot(owner_map, grad_spread[2], preferred_element_type=jnp.float32).astype(
        jnp.bfloat16
    )
    grad_back = (
        lax.all_to_all(summed_gate, "expert", split_axis=0, concat_axis=0, tiled=True),
        lax.all_to_all(summed_up, "expert", split_axis=0, concat_axis=0, tiled=True),
        lax.all_to_all(summed_down, "expert", split_axis=0, concat_axis=0, tiled=True),
    )
    total_gate = owned_grads[0] + grad_back[0].reshape(model_width, hidden_width).astype(
        jnp.float32
    )
    total_up = owned_grads[1] + grad_back[1].reshape(model_width, hidden_width).astype(jnp.float32)
    total_down = owned_grads[2] + grad_back[2].reshape(model_width, hidden_width).astype(
        jnp.float32
    )
    shares = (
        lax.psum_scatter(
            total_gate.astype(jnp.bfloat16), "replica", scatter_dimension=0, tiled=True
        ).astype(jnp.float32),
        lax.psum_scatter(
            total_up.astype(jnp.bfloat16), "replica", scatter_dimension=0, tiled=True
        ).astype(jnp.float32),
        lax.psum_scatter(
            total_down.astype(jnp.bfloat16), "replica", scatter_dimension=0, tiled=True
        ).astype(jnp.float32),
    )
    flat_back = returned.reshape(experts * slot_total, model_width)
    picked_rows = jnp.take(flat_back, slot_index, axis=0)
    picked_rows = jnp.where(kept_mask[:, None], picked_rows, zero_half).astype(jnp.float32)
    token_grad = jnp.sum(picked_rows.reshape(token_count, topk, model_width), axis=1).astype(
        jnp.bfloat16
    )
    gate_grad = jnp.where(kept_mask, returned_gate.reshape(-1)[slot_index], zero_half).reshape(
        token_count, topk
    )
    return (
        token_grad,
        gate_grad,
        shares[0].astype(jnp.bfloat16)[None],
        shares[1].astype(jnp.bfloat16)[None],
        shares[2].astype(jnp.bfloat16)[None],
    )


BF = jnp.bfloat16
F32 = jnp.float32
CONTRACT_ROWS = (((0,), (0,)), ((), ()))
CONTRACT_COLS = (((1,), (1,)), ((), ()))
MIB = 1024 * 1024

BASES = (4, 6, 2)
ORDER = (0, 1, 2, 4, 6, 3, 5, 7)
LONG = 8 * 10**9
MAIN = 16
QUARTERS = 4
SEND_ROWS = 2 * QUARTERS * MAIN + 16
BACK_ROWS = QUARTERS * MAIN + 16


def copies_of(experts):
    return 2 if experts <= 8 else 8


def iota(shape, axis):
    return lax.broadcasted_iota(jnp.int32, shape, axis)


def partners(experts, tokens):
    row = iota((experts, tokens), 0)
    step = jnp.bitwise_xor(jnp.bitwise_and(row, 1), lax.axis_index("replica"))
    for d, base in enumerate(BASES):
        step = jnp.where(jnp.right_shift(row, 1) == d + 1, step + base, step)
    step = jnp.where(row < 2, row, step)
    return jnp.bitwise_xor(step, lax.axis_index("expert"))


def chunk_views(refs, rows):
    return [(refs[0], 0), (refs[1], 0)] + [(ref, part * rows) for ref in refs[2:] for part in (0, 1)]


def mask(condition):
    return condition.astype(F32).astype(BF)


def repeat_rows(table, times):
    width = table.shape[1]
    return jnp.concatenate(
        [jnp.broadcast_to(table[e : e + 1], (times, width)) for e in range(table.shape[0])], axis=0
    )


def route_kernel(plan_hbm, ids_hbm, pick_hbm, gate_hbm, tok_hbm, cot_hbm, *refs):
    sems = refs[-1]
    plan_ref, ids_ref, pick_ref, gate_ref, tok_ref, cot_ref = refs[-7:-1]
    slot_ref, gates_ref = refs[-9:-7]
    send_refs = refs[:-9]
    topk, tokens = ids_ref.shape
    experts = len(send_refs)
    width = tok_ref.shape[1] // QUARTERS
    copies = copies_of(experts)
    loads = [
        pltpu.make_async_copy(source, place, sems.at[n])
        for n, (source, place) in enumerate(
            (
                (plan_hbm, plan_ref),
                (ids_hbm, ids_ref),
                (pick_hbm, pick_ref),
                (gate_hbm, gate_ref),
                (tok_hbm, tok_ref),
                (cot_hbm, cot_ref),
            )
        )
    ]
    for load in loads:
        load.start()
    before = mask(iota((tokens, tokens), 0) < iota((tokens, tokens), 1))
    expert_row = partners(experts, tokens)
    for load in loads[:4]:
        load.wait()
    ids = ids_ref[...]
    pick = pick_ref[...]
    gate = gate_ref[...].astype(F32)
    named = jnp.zeros((experts, tokens), jnp.int32)
    gates = jnp.zeros((experts, tokens), F32)
    for k in range(topk):
        hit = ids[k : k + 1] == expert_row
        named = jnp.where(hit, pick[k : k + 1] + 1, named)
        gates = jnp.where(hit, gate[k : k + 1], gates)
    hot = jnp.zeros((experts, tokens), jnp.int32)
    for j in range(experts):
        hot = jnp.where(expert_row == plan_ref[j], 1, hot)
    chosen = jnp.where(named == 0, -1, jnp.where(hot > 0, named - 1, 0))
    masks = jnp.concatenate([(chosen == c).astype(F32) for c in range(copies + 1)], axis=0)
    rank = jnp.dot(masks.astype(BF), before, preferred_element_type=F32).astype(jnp.int32)
    slot = jnp.full((experts, tokens), -1, jnp.int32)
    for c in range(copies + 1):
        rank_c = rank[c * experts : (c + 1) * experts]
        keep = jnp.logical_and(chosen == c, rank_c < CAP)
        slot = jnp.where(keep, c * CAP + rank_c, slot)
    slot_ref[...] = slot
    gates_ref[...] = gates
    slot16 = repeat_rows(slot, MAIN)
    gate16 = repeat_rows(gates, MAIN)
    inner = jnp.bitwise_and(iota(slot16.shape, 0), MAIN - 1)
    onehot = (slot16 == inner).astype(F32)
    wanted = MAIN + jnp.bitwise_and(jnp.right_shift(inner, 2), 1)
    last = (slot16 == wanted).astype(F32)
    last_rows = jnp.where(inner >= 8, 0.0, last)
    last_scaled = jnp.where(inner >= 8, last * gate16, 0.0)
    quarter = jnp.bitwise_and(inner, 3)
    for load in loads[4:]:
        load.wait()
    rows = jnp.dot(onehot.astype(BF), tok_ref[...], preferred_element_type=F32).astype(BF)
    scaled = jnp.dot(
        (onehot * gate16).astype(BF), cot_ref[...], preferred_element_type=F32
    ).astype(BF)
    tail = jnp.zeros((experts * MAIN, width), F32)
    for q in range(QUARTERS):
        cols = slice(q * width, (q + 1) * width)
        mine = quarter == q
        tail += jnp.dot(
            jnp.where(mine, last_rows, 0.0).astype(BF), tok_ref[:, cols], preferred_element_type=F32
        )
        tail += jnp.dot(
            jnp.where(mine, last_scaled, 0.0).astype(BF),
            cot_ref[:, cols],
            preferred_element_type=F32,
        )
    tail = tail.astype(BF)
    for c, ref in enumerate(send_refs):
        here = slice(c * MAIN, (c + 1) * MAIN)
        for q in range(QUARTERS):
            cols = slice(q * width, (q + 1) * width)
            ref[q * MAIN : (q + 1) * MAIN, :] = rows[here, cols]
            ref[(QUARTERS + q) * MAIN : (QUARTERS + q + 1) * MAIN, :] = scaled[here, cols]
        ref[2 * QUARTERS * MAIN :, :] = tail[here]


def expert_kernel(*refs):
    experts = len(ORDER)
    recv_refs = [refs[ORDER.index(c)] for c in range(experts)]
    gate_ref, up_ref, down_ref = refs[experts : experts + 3]
    back_views = chunk_views(refs[experts + 3 : -5], BACK_ROWS)
    x_ref, s_ref, dg_ref, du_ref, hid_ref = refs[-5:]
    width = refs[0].shape[1]
    main_rows = experts * MAIN
    tail = jnp.concatenate([ref[2 * QUARTERS * MAIN :, :] for ref in recv_refs], axis=0)
    row = iota((4 * experts, main_rows), 0)
    col = iota((4 * experts, main_rows), 1)
    kind = (row >= 2 * experts).astype(jnp.int32)
    chunk = jnp.right_shift(row - kind * 2 * experts, 1)
    base = chunk * MAIN + kind * 8 + jnp.bitwise_and(row, 1) * 4
    for q in range(QUARTERS):
        cols = slice(q * width, (q + 1) * width)
        picked = jnp.dot(mask(col == base + q), tail, preferred_element_type=F32).astype(BF)
        x_ref[main_rows:, cols] = picked[: 2 * experts]
        s_ref[main_rows:, cols] = picked[2 * experts :]
        for i, ref in enumerate(recv_refs):
            here = slice(i * MAIN, (i + 1) * MAIN)
            x_ref[here, cols] = ref[q * MAIN : (q + 1) * MAIN, :]
            s_ref[here, cols] = ref[(QUARTERS + q) * MAIN : (QUARTERS + q + 1) * MAIN, :]
    rows = x_ref[...]
    gate_pre = jnp.dot(rows, gate_ref[...], preferred_element_type=F32)
    up_pre = jnp.dot(rows, up_ref[...], preferred_element_type=F32)
    hidden_grad = jnp.dot(s_ref[...], down_ref[...], preferred_element_type=F32)
    sig = jax.nn.sigmoid(gate_pre)
    activated = gate_pre * sig
    hidden = (activated * up_pre).astype(BF)
    slope = sig * (1.0 + gate_pre * (1.0 - sig))
    gate_delta = (hidden_grad * up_pre * slope).astype(BF)
    up_delta = (hidden_grad * activated).astype(BF)
    hid_ref[...] = hidden
    dg_ref[...] = gate_delta
    du_ref[...] = up_delta
    grad = (
        lax.dot_general(gate_delta, gate_ref[...], CONTRACT_COLS, preferred_element_type=F32)
        + lax.dot_general(up_delta, up_ref[...], CONTRACT_COLS, preferred_element_type=F32)
    ).astype(BF)
    product = hidden.astype(F32) * hidden_grad
    product = jnp.concatenate(
        [product, jnp.zeros((width - product.shape[0], product.shape[1]), F32)], axis=0
    )
    gate_lanes = lax.dot_general(
        jnp.ones((8, product.shape[1]), F32),
        product,
        CONTRACT_COLS,
        preferred_element_type=F32,
        precision=lax.Precision.HIGHEST,
    )
    trow = iota((main_rows, 2 * experts), 0)
    tcol = iota((main_rows, 2 * experts), 1)
    inner = jnp.bitwise_and(trow, MAIN - 1)
    source = jnp.right_shift(trow, 4) * 2 + jnp.right_shift(inner, 2)
    spread = jnp.zeros((main_rows, width), F32)
    for q in range(QUARTERS):
        cols = slice(q * width, (q + 1) * width)
        mine = jnp.logical_and(jnp.bitwise_and(inner, 3) == q, inner < 8)
        place = mask(jnp.logical_and(mine, tcol == source))
        spread += jnp.dot(place, grad[main_rows:, cols], preferred_element_type=F32)
        for i, (ref, first) in enumerate(back_views):
            low = first + q * MAIN
            ref[low : low + MAIN, :] = grad[i * MAIN : (i + 1) * MAIN, cols]
    for i, (ref, first) in enumerate(back_views):
        low = first + QUARTERS * MAIN
        ref[low : low + 16, :] = jnp.concatenate(
            [spread[i * MAIN : i * MAIN + 8], gate_lanes], axis=0
        ).astype(BF)


def grads_of(half, x_ref, s_ref, dg_ref, du_ref, hid_ref):
    rows = x_ref.shape[1] // 2
    cols = pl.ds(pl.multiple_of(half * rows, rows), rows)
    x_half = x_ref[:, cols]
    s_half = s_ref[:, cols]
    return (
        lax.dot_general(x_half, dg_ref[...], CONTRACT_ROWS, preferred_element_type=F32),
        lax.dot_general(x_half, du_ref[...], CONTRACT_ROWS, preferred_element_type=F32),
        lax.dot_general(s_half, hid_ref[...], CONTRACT_ROWS, preferred_element_type=F32),
    )


def other_half_kernel(x_ref, s_ref, dg_ref, du_ref, hid_ref, out_ref):
    half = 1 - lax.axis_index("replica")
    parts = grads_of(half, x_ref, s_ref, dg_ref, du_ref, hid_ref)
    rows = parts[0].shape[0]
    for n in range(3):
        out_ref[n * rows : (n + 1) * rows, :] = parts[n].astype(BF)


def own_half_kernel(
    x_ref, s_ref, dg_ref, du_ref, hid_ref, came_ref, gate_ref, up_ref, down_ref
):
    parts = grads_of(lax.axis_index("replica"), x_ref, s_ref, dg_ref, du_ref, hid_ref)
    rows = parts[0].shape[0]
    for n, out_ref in enumerate((gate_ref, up_ref, down_ref)):
        came = came_ref[n * rows : (n + 1) * rows, :].astype(F32)
        out_ref[...] = (parts[n].astype(BF).astype(F32) + came).astype(BF)


def combine_kernel(ids_ref, slot_ref, gates_ref, *refs):
    token_ref, grad_ref = refs[-2:]
    doubles = 2 + len(BASES)
    ret_views = [(refs[0], 0), (refs[1], 0)]
    for kept_ref, given_ref in zip(refs[2:doubles], refs[doubles:-2]):
        ret_views += [(kept_ref, 0), (given_ref, BACK_ROWS)]
    topk, tokens = ids_ref.shape
    experts = len(ret_views)
    width = refs[0].shape[1]
    ids = ids_ref[...]
    slot = slot_ref[...]
    slot16 = repeat_rows(slot, MAIN)
    inner = jnp.bitwise_and(iota(slot16.shape, 0), MAIN - 1)
    onehot = mask(slot16 == inner)
    wanted = MAIN + jnp.right_shift(inner, 2)
    last = jnp.where(jnp.logical_and(slot16 == wanted, inner < 8), 1.0, 0.0)
    quarter = jnp.bitwise_and(inner, 3)
    tails = [ref[first + BACK_ROWS - 16 : first + BACK_ROWS, :] for ref, first in ret_views]
    tail = jnp.concatenate(tails, axis=0)
    for q in range(QUARTERS):
        main = jnp.concatenate(
            [ref[first + q * MAIN : first + (q + 1) * MAIN, :] for ref, first in ret_views], axis=0
        )
        place = jnp.where(quarter == q, last, 0.0).astype(BF)
        total = lax.dot_general(onehot, main, CONTRACT_ROWS, preferred_element_type=F32)
        total += lax.dot_general(place, tail, CONTRACT_ROWS, preferred_element_type=F32)
        token_ref[:, q * width : (q + 1) * width] = total.astype(BF)
    lane_index = iota((width, tokens), 0)
    found = []
    for c in range(experts):
        mine = slot[c : c + 1]
        lane = jnp.where(mine < MAIN, c * MAIN + mine, experts * MAIN + 2 * c + mine - MAIN)
        lane = jnp.where(mine < 0, -1, lane)
        sums = jnp.dot(tails[c], mask(lane_index == lane), preferred_element_type=F32)
        found.append(sums[8:9])
    found = jnp.concatenate(found, axis=0)
    kept = slot >= 0
    grads = jnp.where(kept, found / jnp.where(kept, gates_ref[...], 1.0), 0.0)
    expert_row = partners(experts, tokens)
    by_choice = [
        jnp.sum(jnp.where(expert_row == ids[k : k + 1], grads, 0.0), axis=0, keepdims=True)
        for k in range(topk)
    ]
    grad_ref[...] = jnp.concatenate(by_choice, axis=0).astype(BF)


def local_call(kernel, outs, arrays, name, flops, moved, space=pltpu.VMEM, scratch=(), limit=16):
    vmem = pl.BlockSpec(memory_space=pltpu.VMEM)
    return pl.pallas_call(
        kernel,
        out_shape=[jax.ShapeDtypeStruct(shape, kind) for shape, kind in outs],
        in_specs=[pl.BlockSpec(memory_space=space)] * len(arrays),
        out_specs=[vmem] * len(outs),
        scratch_shapes=list(scratch),
        compiler_params=pltpu.CompilerParams(vmem_limit_bytes=limit * MIB),
        cost_estimate=pl.CostEstimate(flops=flops, bytes_accessed=moved, transcendentals=0),
        name=name,
    )(*arrays)


def to_step(chunk, base):
    experts = lax.axis_size("expert")
    if base == 1:
        return lax.ppermute(chunk, "expert", [(i, i ^ 1) for i in range(experts)])
    pairs = [(2 * i + r, 2 * (i ^ (base + r)) + r) for i in range(experts) for r in range(2)]
    return lax.ppermute(chunk, ("expert", "replica"), pairs)


def to_twin(chunk):
    return lax.ppermute(chunk, "replica", [(0, 1), (1, 0)])


def per_device_moving_rows(
    tokens,
    cotangent,
    expert_ids,
    gate_values,
    replica_pick,
    replica_plan,
    gate_proj,
    up_proj,
    down_proj,
):
    experts = lax.axis_size("expert")
    token_count, model_width = tokens.shape
    topk = expert_ids.shape[1]
    hidden_width = gate_proj.shape[2]
    width = model_width // QUARTERS
    served = experts * (MAIN + 2)
    small = (topk, token_count)
    count = len(BASES)
    *chunks, slot, gates = local_call(
        route_kernel,
        [((SEND_ROWS, width), BF)] * experts
        + [((experts, token_count), jnp.int32), ((experts, token_count), F32)],
        [replica_plan, expert_ids.T, replica_pick.T, gate_values.T, tokens, cotangent],
        "route",
        LONG,
        2 * 2 * (token_count + served) * model_width,
        space=pltpu.HBM,
        limit=54,
        scratch=[
            pltpu.SMEM((experts,), jnp.int32),
            pltpu.VMEM(small, jnp.int32),
            pltpu.VMEM(small, jnp.int32),
            pltpu.VMEM(small, BF),
            pltpu.VMEM(tokens.shape, BF),
            pltpu.VMEM(tokens.shape, BF),
            pltpu.SemaphoreType.DMA((6,)),
        ],
    )
    recv = list(chunks)
    far = [to_twin(chunks[3]), to_twin(chunks[5])]
    far, near = lax.optimization_barrier((far, [chunks[6], chunks[7]]))
    for d, twin in enumerate([*far, to_twin(near[1])]):
        recv[3 + 2 * d] = to_step(twin, BASES[d])
    recv[2] = to_step(chunks[2], 4)
    recv[4] = to_step(chunks[4], 6)
    recv[6] = to_step(near[0], 2)
    recv[1] = to_step(chunks[1], 1)
    matmul = 2 * served * model_width * hidden_width
    outs = local_call(
        expert_kernel,
        [((BACK_ROWS, width), BF)] * 2
        + [((2 * BACK_ROWS, width), BF)] * count
        + [((served, model_width), BF)] * 2
        + [((served, hidden_width), BF)] * 3,
        [*(recv[c] for c in ORDER), gate_proj[0], up_proj[0], down_proj[0]],
        "expert_rows",
        5 * matmul,
        2 * 3 * model_width * hidden_width,
    )
    backs, factors = outs[: 2 + count], outs[2 + count :]
    kept = list(map(to_step, backs[2:], BASES))
    near = to_step(backs[1], 1)
    half = model_width // 2
    (leaving,) = local_call(
        other_half_kernel,
        [((3 * half, hidden_width), BF)],
        factors,
        "other_half",
        1,
        1,
    )
    shares = local_call(
        own_half_kernel,
        [((half, hidden_width), BF)] * 3,
        [*factors, to_twin(leaving)],
        "own_half",
        1,
        1,
    )
    kept[0], near, shares = lax.optimization_barrier((kept[0], near, shares))
    returned = [backs[0], near, *kept, *map(to_twin, kept)]
    token_grad, gate_grad = local_call(
        combine_kernel,
        [((token_count, model_width), BF), ((topk, token_count), BF)],
        [expert_ids.T, slot, gates, *returned],
        "combine",
        2 * served * token_count * model_width,
        2 * 2 * token_count * model_width,
    )
    return (token_grad, gate_grad.T, shares[0][None], shares[1][None], shares[2][None])


def per_device(tokens, cotangent, expert_ids, gate_values, replica_pick, replica_plan, *matrices):
    experts = lax.axis_size("expert")
    slots = (copies_of(experts) + 1) * CAP
    row_bytes = 3 * 2 * tokens.shape[1] * experts
    matrix_bytes = 4 * sum(2 * m[0].size for m in matrices)
    fits = slots == MAIN + 2 and experts == 8 and lax.axis_size("replica") == 2
    rows_cheaper = slots * row_bytes < 2 * CAP * row_bytes + matrix_bytes
    plan = per_device_moving_rows if fits and rows_cheaper else per_device_moving_weights
    return plan(
        tokens, cotangent, expert_ids, gate_values, replica_pick, replica_plan, *matrices
    )


def solution(mesh):
    placed = (
        P(("parts", "expert", "replica"), None),
        P(("parts", "expert", "replica"), None),
        P(("parts", "expert", "replica"), None),
        P(("parts", "expert", "replica"), None),
        P(("parts", "expert", "replica"), None),
        P("parts"),
        P("expert", None, None),
        P("expert", None, None),
        P("expert", None, None),
    )
    return jax.shard_map(
        per_device,
        mesh=mesh,
        in_specs=placed,
        out_specs=(
            P(("parts", "expert", "replica"), None),
            P(("parts", "expert", "replica"), None),
            P(("parts", "expert"), "replica", None),
            P(("parts", "expert"), "replica", None),
            P(("parts", "expert"), "replica", None),
        ),
        check_vma=False,
    )
```

```python
import jax
import jax.numpy as jnp
from jax import lax
from jax.experimental import pallas as pl
from jax.experimental.pallas import tpu as pltpu
from jax.sharding import PartitionSpec as P

CAP = 6


def route_assignments(flat_ids, flat_pick, replica_plan, capacity):
    experts = replica_plan.shape[0]
    lane_ids = jnp.arange(experts, dtype=jnp.int32)
    same_plan = replica_plan[:, None] == replica_plan[None, :]
    earlier = lane_ids[None, :] < lane_ids[:, None]
    position = jnp.sum(jnp.logical_and(same_plan, earlier), axis=1)
    hot_mask = jnp.any(replica_plan[None, :] == lane_ids[:, None], axis=1)
    is_hot = jnp.any(
        jnp.logical_and(flat_ids[:, None] == lane_ids[None, :], hot_mask[None, :]), axis=1
    )
    use_copy = jnp.logical_and(is_hot, flat_pick >= 1)
    matches = jnp.logical_and(
        replica_plan[None, :] == flat_ids[:, None], position[None, :] == flat_pick[:, None] - 1
    )
    holder = jnp.sum(jnp.where(matches, lane_ids[None, :], 0), axis=1)
    target = jnp.where(use_copy, holder, flat_ids)
    copy_role = use_copy.astype(jnp.int32)
    bucket = target * 2 + copy_role
    sequence = jnp.arange(bucket.shape[0], dtype=jnp.int32)
    arrival = jnp.sum(
        jnp.logical_and(bucket[None, :] == bucket[:, None], sequence[None, :] < sequence[:, None]),
        axis=1,
    )
    kept_mask = arrival < capacity
    slot_index = target * (2 * capacity) + copy_role * capacity + jnp.minimum(arrival, capacity - 1)
    return (slot_index, kept_mask)


def fill_slots(slot_index, kept_mask, slot_count):
    slot_ids = jnp.arange(slot_count, dtype=jnp.int32)
    matches = jnp.logical_and(slot_index[None, :] == slot_ids[:, None], kept_mask[None, :])
    sequence = jnp.arange(slot_index.shape[0], dtype=jnp.int32)
    source = jnp.sum(jnp.where(matches, sequence[None, :], 0), axis=1)
    filled = jnp.any(matches, axis=1)
    return (source, filled)


def expert_backward(row_block, upstream, weight, gate_w, up_w, down_w):
    contract_cols = (((1,), (1,)), ((), ()))
    contract_rows = (((0,), (0,)), ((), ()))
    gate_pre = jnp.dot(row_block, gate_w, preferred_element_type=jnp.float32)
    up_pre = jnp.dot(row_block, up_w, preferred_element_type=jnp.float32)
    sigmoid_gate = jax.nn.sigmoid(gate_pre)
    activated = gate_pre * sigmoid_gate
    hidden = (activated * up_pre).astype(jnp.bfloat16)
    output_rows = lax.dot_general(hidden, down_w, contract_cols, preferred_element_type=jnp.float32)
    weight_col = weight.astype(jnp.float32)[:, None]
    upstream_f = upstream.astype(jnp.float32)
    gate_rows = jnp.sum(upstream_f * output_rows, axis=1)
    hidden_grad = weight_col * jnp.dot(upstream, down_w, preferred_element_type=jnp.float32)
    slope = sigmoid_gate * (1.0 + gate_pre * (1.0 - sigmoid_gate))
    gate_delta = (hidden_grad * up_pre * slope).astype(jnp.bfloat16)
    up_delta = (hidden_grad * activated).astype(jnp.bfloat16)
    input_grad = (
        lax.dot_general(gate_delta, gate_w, contract_cols, preferred_element_type=jnp.float32)
        + lax.dot_general(up_delta, up_w, contract_cols, preferred_element_type=jnp.float32)
    ).astype(jnp.bfloat16)
    scaled = (weight_col * upstream_f).astype(jnp.bfloat16)
    grad_set = (
        lax.dot_general(row_block, gate_delta, contract_rows, preferred_element_type=jnp.float32),
        lax.dot_general(row_block, up_delta, contract_rows, preferred_element_type=jnp.float32),
        lax.dot_general(scaled, hidden, contract_rows, preferred_element_type=jnp.float32),
    )
    return (input_grad, gate_rows, grad_set)


def per_device_moving_weights(
    tokens,
    cotangent,
    expert_ids,
    gate_values,
    replica_pick,
    replica_plan,
    gate_proj,
    up_proj,
    down_proj,
):
    experts = lax.axis_size("expert")
    capacity = CAP
    slot_total = 2 * capacity
    model_width = tokens.shape[1]
    topk = expert_ids.shape[1]
    token_count = tokens.shape[0]
    slot_index, kept_mask = route_assignments(
        expert_ids.reshape(-1), replica_pick.reshape(-1), replica_plan, capacity
    )
    source, filled = fill_slots(slot_index, kept_mask, experts * slot_total)
    token_of = source // topk
    zero_half = jnp.zeros((), jnp.bfloat16)
    send_rows = jnp.where(filled[:, None], jnp.take(tokens, token_of, axis=0), zero_half).reshape(
        experts, slot_total, model_width
    )
    send_upstream = jnp.where(
        filled[:, None], jnp.take(cotangent, token_of, axis=0), zero_half
    ).reshape(experts, slot_total, model_width)
    send_weight = jnp.where(filled, gate_values.reshape(-1)[source], zero_half).reshape(
        experts, slot_total
    )
    arrived = lax.all_to_all(send_rows, "expert", split_axis=0, concat_axis=0, tiled=True)
    own_gate = gate_proj[0]
    own_up = up_proj[0]
    own_down = down_proj[0]
    hidden_width = own_gate.shape[1]
    spread = (
        lax.all_to_all(
            own_gate.reshape(experts, -1), "expert", split_axis=0, concat_axis=0, tiled=True
        ),
        lax.all_to_all(
            own_up.reshape(experts, -1), "expert", split_axis=0, concat_axis=0, tiled=True
        ),
        lax.all_to_all(
            own_down.reshape(experts, -1), "expert", split_axis=0, concat_axis=0, tiled=True
        ),
    )
    chosen_gate = jnp.take(spread[0], replica_plan, axis=0)
    chosen_up = jnp.take(spread[1], replica_plan, axis=0)
    chosen_down = jnp.take(spread[2], replica_plan, axis=0)
    collected = (
        lax.all_to_all(chosen_gate, "expert", split_axis=0, concat_axis=0, tiled=True),
        lax.all_to_all(chosen_up, "expert", split_axis=0, concat_axis=0, tiled=True),
        lax.all_to_all(chosen_down, "expert", split_axis=0, concat_axis=0, tiled=True),
    )
    copy_gate = collected[0].reshape(model_width, hidden_width)
    copy_up = collected[1].reshape(model_width, hidden_width)
    copy_down = collected[2].reshape(model_width, hidden_width)
    arrived_up, arrived_weight = (
        lax.all_to_all(send_upstream, "expert", split_axis=0, concat_axis=0, tiled=True),
        lax.all_to_all(send_weight, "expert", split_axis=0, concat_axis=0, tiled=True),
    )
    owned_dx, owned_gate_rows, owned_grads = expert_backward(
        arrived[:, :capacity].reshape(-1, model_width),
        arrived_up[:, :capacity].reshape(-1, model_width),
        arrived_weight[:, :capacity].reshape(-1),
        own_gate,
        own_up,
        own_down,
    )
    copied_dx, copied_gate_rows, copied_grads = expert_backward(
        arrived[:, capacity:].reshape(-1, model_width),
        arrived_up[:, capacity:].reshape(-1, model_width),
        arrived_weight[:, capacity:].reshape(-1),
        copy_gate,
        copy_up,
        copy_down,
    )
    back_rows = jnp.concatenate(
        [
            owned_dx.reshape(experts, capacity, model_width),
            copied_dx.reshape(experts, capacity, model_width),
        ],
        axis=1,
    )
    back_gate = jnp.concatenate(
        [owned_gate_rows.reshape(experts, capacity), copied_gate_rows.reshape(experts, capacity)],
        axis=1,
    ).astype(jnp.bfloat16)
    returned, returned_gate = (
        lax.all_to_all(back_rows, "expert", split_axis=0, concat_axis=0, tiled=True),
        lax.all_to_all(back_gate, "expert", split_axis=0, concat_axis=0, tiled=True),
    )
    copy_pieces = (
        copied_grads[0].astype(jnp.bfloat16).reshape(experts, -1),
        copied_grads[1].astype(jnp.bfloat16).reshape(experts, -1),
        copied_grads[2].astype(jnp.bfloat16).reshape(experts, -1),
    )
    grad_spread = (
        lax.all_to_all(copy_pieces[0], "expert", split_axis=0, concat_axis=0, tiled=True),
        lax.all_to_all(copy_pieces[1], "expert", split_axis=0, concat_axis=0, tiled=True),
        lax.all_to_all(copy_pieces[2], "expert", split_axis=0, concat_axis=0, tiled=True),
    )
    lane_ids = jnp.arange(experts, dtype=jnp.int32)
    owner_map = (replica_plan[None, :] == lane_ids[:, None]).astype(jnp.bfloat16)
    summed_gate = jnp.dot(owner_map, grad_spread[0], preferred_element_type=jnp.float32).astype(
        jnp.bfloat16
    )
    summed_up = jnp.dot(owner_map, grad_spread[1], preferred_element_type=jnp.float32).astype(
        jnp.bfloat16
    )
    summed_down = jnp.dot(owner_map, grad_spread[2], preferred_element_type=jnp.float32).astype(
        jnp.bfloat16
    )
    grad_back = (
        lax.all_to_all(summed_gate, "expert", split_axis=0, concat_axis=0, tiled=True),
        lax.all_to_all(summed_up, "expert", split_axis=0, concat_axis=0, tiled=True),
        lax.all_to_all(summed_down, "expert", split_axis=0, concat_axis=0, tiled=True),
    )
    total_gate = owned_grads[0] + grad_back[0].reshape(model_width, hidden_width).astype(
        jnp.float32
    )
    total_up = owned_grads[1] + grad_back[1].reshape(model_width, hidden_width).astype(jnp.float32)
    total_down = owned_grads[2] + grad_back[2].reshape(model_width, hidden_width).astype(
        jnp.float32
    )
    shares = (
        lax.psum_scatter(
            total_gate.astype(jnp.bfloat16), "replica", scatter_dimension=0, tiled=True
        ).astype(jnp.float32),
        lax.psum_scatter(
            total_up.astype(jnp.bfloat16), "replica", scatter_dimension=0, tiled=True
        ).astype(jnp.float32),
        lax.psum_scatter(
            total_down.astype(jnp.bfloat16), "replica", scatter_dimension=0, tiled=True
        ).astype(jnp.float32),
    )
    flat_back = returned.reshape(experts * slot_total, model_width)
    picked_rows = jnp.take(flat_back, slot_index, axis=0)
    picked_rows = jnp.where(kept_mask[:, None], picked_rows, zero_half).astype(jnp.float32)
    token_grad = jnp.sum(picked_rows.reshape(token_count, topk, model_width), axis=1).astype(
        jnp.bfloat16
    )
    gate_grad = jnp.where(kept_mask, returned_gate.reshape(-1)[slot_index], zero_half).reshape(
        token_count, topk
    )
    return (
        token_grad,
        gate_grad,
        shares[0].astype(jnp.bfloat16)[None],
        shares[1].astype(jnp.bfloat16)[None],
        shares[2].astype(jnp.bfloat16)[None],
    )


BF = jnp.bfloat16
F32 = jnp.float32
CONTRACT_ROWS = (((0,), (0,)), ((), ()))
CONTRACT_COLS = (((1,), (1,)), ((), ()))
MIB = 1024 * 1024

BASES = (4, 6, 2)
ORDER = (0, 1, 2, 4, 6, 3, 7, 5)
LONG = 8 * 10**9
MAIN = 16
QUARTERS = 4
SEND_ROWS = 2 * QUARTERS * MAIN + 16
BACK_ROWS = QUARTERS * MAIN + 16


def copies_of(experts):
    return 2 if experts <= 8 else 8


def iota(shape, axis):
    return lax.broadcasted_iota(jnp.int32, shape, axis)


def partners(experts, tokens):
    row = iota((experts, tokens), 0)
    step = jnp.bitwise_xor(jnp.bitwise_and(row, 1), lax.axis_index("replica"))
    for d, base in enumerate(BASES):
        step = jnp.where(jnp.right_shift(row, 1) == d + 1, step + base, step)
    step = jnp.where(row < 2, row, step)
    return jnp.bitwise_xor(step, lax.axis_index("expert"))


def chunk_views(refs, rows):
    return [(refs[0], 0), (refs[1], 0)] + [(ref, part * rows) for ref in refs[2:] for part in (0, 1)]


def mask(condition):
    return condition.astype(F32).astype(BF)


def repeat_rows(table, times):
    width = table.shape[1]
    return jnp.concatenate(
        [jnp.broadcast_to(table[e : e + 1], (times, width)) for e in range(table.shape[0])], axis=0
    )


def route_kernel(plan_hbm, ids_hbm, pick_hbm, gate_hbm, tok_hbm, cot_hbm, *refs):
    sems = refs[-1]
    plan_ref, ids_ref, pick_ref, gate_ref, tok_ref, cot_ref = refs[-7:-1]
    slot_ref, gates_ref = refs[-9:-7]
    send_refs = refs[:-9]
    topk, tokens = ids_ref.shape
    experts = len(send_refs)
    width = tok_ref.shape[1] // QUARTERS
    copies = copies_of(experts)
    loads = [
        pltpu.make_async_copy(source, place, sems.at[n])
        for n, (source, place) in enumerate(
            (
                (plan_hbm, plan_ref),
                (ids_hbm, ids_ref),
                (pick_hbm, pick_ref),
                (gate_hbm, gate_ref),
                (tok_hbm, tok_ref),
                (cot_hbm, cot_ref),
            )
        )
    ]
    for load in loads:
        load.start()
    before = mask(iota((tokens, tokens), 0) < iota((tokens, tokens), 1))
    expert_row = partners(experts, tokens)
    for load in loads[:4]:
        load.wait()
    ids = ids_ref[...]
    pick = pick_ref[...]
    gate = gate_ref[...].astype(F32)
    named = jnp.zeros((experts, tokens), jnp.int32)
    gates = jnp.zeros((experts, tokens), F32)
    for k in range(topk):
        hit = ids[k : k + 1] == expert_row
        named = jnp.where(hit, pick[k : k + 1] + 1, named)
        gates = jnp.where(hit, gate[k : k + 1], gates)
    hot = jnp.zeros((experts, tokens), jnp.int32)
    for j in range(experts):
        hot = jnp.where(expert_row == plan_ref[j], 1, hot)
    chosen = jnp.where(named == 0, -1, jnp.where(hot > 0, named - 1, 0))
    masks = jnp.concatenate([(chosen == c).astype(F32) for c in range(copies + 1)], axis=0)
    rank = jnp.dot(masks.astype(BF), before, preferred_element_type=F32).astype(jnp.int32)
    slot = jnp.full((experts, tokens), -1, jnp.int32)
    for c in range(copies + 1):
        rank_c = rank[c * experts : (c + 1) * experts]
        keep = jnp.logical_and(chosen == c, rank_c < CAP)
        slot = jnp.where(keep, c * CAP + rank_c, slot)
    slot_ref[...] = slot
    gates_ref[...] = gates
    slot16 = repeat_rows(slot, MAIN)
    gate16 = repeat_rows(gates, MAIN)
    inner = jnp.bitwise_and(iota(slot16.shape, 0), MAIN - 1)
    onehot = (slot16 == inner).astype(F32)
    wanted = MAIN + jnp.bitwise_and(jnp.right_shift(inner, 2), 1)
    last = (slot16 == wanted).astype(F32)
    last_rows = jnp.where(inner >= 8, 0.0, last)
    last_scaled = jnp.where(inner >= 8, last * gate16, 0.0)
    quarter = jnp.bitwise_and(inner, 3)
    for load in loads[4:]:
        load.wait()
    rows = jnp.dot(onehot.astype(BF), tok_ref[...], preferred_element_type=F32).astype(BF)
    scaled = jnp.dot(
        (onehot * gate16).astype(BF), cot_ref[...], preferred_element_type=F32
    ).astype(BF)
    tail = jnp.zeros((experts * MAIN, width), F32)
    for q in range(QUARTERS):
        cols = slice(q * width, (q + 1) * width)
        mine = quarter == q
        tail += jnp.dot(
            jnp.where(mine, last_rows, 0.0).astype(BF), tok_ref[:, cols], preferred_element_type=F32
        )
        tail += jnp.dot(
            jnp.where(mine, last_scaled, 0.0).astype(BF),
            cot_ref[:, cols],
            preferred_element_type=F32,
        )
    tail = tail.astype(BF)
    for c, ref in enumerate(send_refs):
        here = slice(c * MAIN, (c + 1) * MAIN)
        for q in range(QUARTERS):
            cols = slice(q * width, (q + 1) * width)
            ref[q * MAIN : (q + 1) * MAIN, :] = rows[here, cols]
            ref[(QUARTERS + q) * MAIN : (QUARTERS + q + 1) * MAIN, :] = scaled[here, cols]
        ref[2 * QUARTERS * MAIN :, :] = tail[here]


def expert_kernel(*refs):
    experts = len(ORDER)
    recv_refs = [refs[ORDER.index(c)] for c in range(experts)]
    gate_ref, up_ref, down_ref = refs[experts : experts + 3]
    back_views = chunk_views(refs[experts + 3 : -5], BACK_ROWS)
    x_ref, s_ref, dg_ref, du_ref, hid_ref = refs[-5:]
    width = refs[0].shape[1]
    main_rows = experts * MAIN
    tail = jnp.concatenate([ref[2 * QUARTERS * MAIN :, :] for ref in recv_refs], axis=0)
    row = iota((4 * experts, main_rows), 0)
    col = iota((4 * experts, main_rows), 1)
    kind = (row >= 2 * experts).astype(jnp.int32)
    chunk = jnp.right_shift(row - kind * 2 * experts, 1)
    base = chunk * MAIN + kind * 8 + jnp.bitwise_and(row, 1) * 4
    for q in range(QUARTERS):
        cols = slice(q * width, (q + 1) * width)
        picked = jnp.dot(mask(col == base + q), tail, preferred_element_type=F32).astype(BF)
        x_ref[main_rows:, cols] = picked[: 2 * experts]
        s_ref[main_rows:, cols] = picked[2 * experts :]
        for i, ref in enumerate(recv_refs):
            here = slice(i * MAIN, (i + 1) * MAIN)
            x_ref[here, cols] = ref[q * MAIN : (q + 1) * MAIN, :]
            s_ref[here, cols] = ref[(QUARTERS + q) * MAIN : (QUARTERS + q + 1) * MAIN, :]
    rows = x_ref[...]
    gate_pre = jnp.dot(rows, gate_ref[...], preferred_element_type=F32)
    up_pre = jnp.dot(rows, up_ref[...], preferred_element_type=F32)
    hidden_grad = jnp.dot(s_ref[...], down_ref[...], preferred_element_type=F32)
    sig = jax.nn.sigmoid(gate_pre)
    activated = gate_pre * sig
    hidden = (activated * up_pre).astype(BF)
    slope = sig * (1.0 + gate_pre * (1.0 - sig))
    gate_delta = (hidden_grad * up_pre * slope).astype(BF)
    up_delta = (hidden_grad * activated).astype(BF)
    hid_ref[...] = hidden
    dg_ref[...] = gate_delta
    du_ref[...] = up_delta
    grad = (
        lax.dot_general(gate_delta, gate_ref[...], CONTRACT_COLS, preferred_element_type=F32)
        + lax.dot_general(up_delta, up_ref[...], CONTRACT_COLS, preferred_element_type=F32)
    ).astype(BF)
    product = hidden.astype(F32) * hidden_grad
    product = jnp.concatenate(
        [product, jnp.zeros((width - product.shape[0], product.shape[1]), F32)], axis=0
    )
    gate_lanes = lax.dot_general(
        jnp.ones((8, product.shape[1]), F32),
        product,
        CONTRACT_COLS,
        preferred_element_type=F32,
        precision=lax.Precision.HIGHEST,
    )
    trow = iota((main_rows, 2 * experts), 0)
    tcol = iota((main_rows, 2 * experts), 1)
    inner = jnp.bitwise_and(trow, MAIN - 1)
    source = jnp.right_shift(trow, 4) * 2 + jnp.right_shift(inner, 2)
    spread = jnp.zeros((main_rows, width), F32)
    for q in range(QUARTERS):
        cols = slice(q * width, (q + 1) * width)
        mine = jnp.logical_and(jnp.bitwise_and(inner, 3) == q, inner < 8)
        place = mask(jnp.logical_and(mine, tcol == source))
        spread += jnp.dot(place, grad[main_rows:, cols], preferred_element_type=F32)
        for i, (ref, first) in enumerate(back_views):
            low = first + q * MAIN
            ref[low : low + MAIN, :] = grad[i * MAIN : (i + 1) * MAIN, cols]
    for i, (ref, first) in enumerate(back_views):
        low = first + QUARTERS * MAIN
        ref[low : low + 16, :] = jnp.concatenate(
            [spread[i * MAIN : i * MAIN + 8], gate_lanes], axis=0
        ).astype(BF)


def grads_of(half, x_ref, s_ref, dg_ref, du_ref, hid_ref):
    rows = x_ref.shape[1] // 2
    cols = pl.ds(pl.multiple_of(half * rows, rows), rows)
    x_half = x_ref[:, cols]
    s_half = s_ref[:, cols]
    return (
        lax.dot_general(x_half, dg_ref[...], CONTRACT_ROWS, preferred_element_type=F32),
        lax.dot_general(x_half, du_ref[...], CONTRACT_ROWS, preferred_element_type=F32),
        lax.dot_general(s_half, hid_ref[...], CONTRACT_ROWS, preferred_element_type=F32),
    )


def other_half_kernel(x_ref, s_ref, dg_ref, du_ref, hid_ref, out_ref):
    half = 1 - lax.axis_index("replica")
    parts = grads_of(half, x_ref, s_ref, dg_ref, du_ref, hid_ref)
    rows = parts[0].shape[0]
    for n in range(3):
        out_ref[n * rows : (n + 1) * rows, :] = parts[n].astype(BF)


def own_half_kernel(
    x_ref, s_ref, dg_ref, du_ref, hid_ref, came_ref, gate_ref, up_ref, down_ref
):
    parts = grads_of(lax.axis_index("replica"), x_ref, s_ref, dg_ref, du_ref, hid_ref)
    rows = parts[0].shape[0]
    for n, out_ref in enumerate((gate_ref, up_ref, down_ref)):
        came = came_ref[n * rows : (n + 1) * rows, :].astype(F32)
        out_ref[...] = (parts[n].astype(BF).astype(F32) + came).astype(BF)


def combine_kernel(ids_ref, slot_ref, gates_ref, *refs):
    token_ref, grad_ref = refs[-2:]
    doubles = 2 + len(BASES)
    ret_views = [(refs[0], 0), (refs[1], 0)]
    for kept_ref, given_ref in zip(refs[2:doubles], refs[doubles:-2]):
        ret_views += [(kept_ref, 0), (given_ref, BACK_ROWS)]
    topk, tokens = ids_ref.shape
    experts = len(ret_views)
    width = refs[0].shape[1]
    ids = ids_ref[...]
    slot = slot_ref[...]
    slot16 = repeat_rows(slot, MAIN)
    inner = jnp.bitwise_and(iota(slot16.shape, 0), MAIN - 1)
    onehot = mask(slot16 == inner)
    wanted = MAIN + jnp.right_shift(inner, 2)
    last = jnp.where(jnp.logical_and(slot16 == wanted, inner < 8), 1.0, 0.0)
    quarter = jnp.bitwise_and(inner, 3)
    tails = [ref[first + BACK_ROWS - 16 : first + BACK_ROWS, :] for ref, first in ret_views]
    tail = jnp.concatenate(tails, axis=0)
    for q in range(QUARTERS):
        main = jnp.concatenate(
            [ref[first + q * MAIN : first + (q + 1) * MAIN, :] for ref, first in ret_views], axis=0
        )
        place = jnp.where(quarter == q, last, 0.0).astype(BF)
        total = lax.dot_general(onehot, main, CONTRACT_ROWS, preferred_element_type=F32)
        total += lax.dot_general(place, tail, CONTRACT_ROWS, preferred_element_type=F32)
        token_ref[:, q * width : (q + 1) * width] = total.astype(BF)
    lane_index = iota((width, tokens), 0)
    found = []
    for c in range(experts):
        mine = slot[c : c + 1]
        lane = jnp.where(mine < MAIN, c * MAIN + mine, experts * MAIN + 2 * c + mine - MAIN)
        lane = jnp.where(mine < 0, -1, lane)
        sums = jnp.dot(tails[c], mask(lane_index == lane), preferred_element_type=F32)
        found.append(sums[8:9])
    found = jnp.concatenate(found, axis=0)
    kept = slot >= 0
    grads = jnp.where(kept, found / jnp.where(kept, gates_ref[...], 1.0), 0.0)
    expert_row = partners(experts, tokens)
    by_choice = [
        jnp.sum(jnp.where(expert_row == ids[k : k + 1], grads, 0.0), axis=0, keepdims=True)
        for k in range(topk)
    ]
    grad_ref[...] = jnp.concatenate(by_choice, axis=0).astype(BF)


def local_call(kernel, outs, arrays, name, flops, moved, space=pltpu.VMEM, scratch=(), limit=16):
    vmem = pl.BlockSpec(memory_space=pltpu.VMEM)
    return pl.pallas_call(
        kernel,
        out_shape=[jax.ShapeDtypeStruct(shape, kind) for shape, kind in outs],
        in_specs=[pl.BlockSpec(memory_space=space)] * len(arrays),
        out_specs=[vmem] * len(outs),
        scratch_shapes=list(scratch),
        compiler_params=pltpu.CompilerParams(vmem_limit_bytes=limit * MIB),
        cost_estimate=pl.CostEstimate(flops=flops, bytes_accessed=moved, transcendentals=0),
        name=name,
    )(*arrays)


def to_step(chunk, base):
    experts = lax.axis_size("expert")
    if base == 1:
        return lax.ppermute(chunk, "expert", [(i, i ^ 1) for i in range(experts)])
    pairs = [(2 * i + r, 2 * (i ^ (base + r)) + r) for i in range(experts) for r in range(2)]
    return lax.ppermute(chunk, ("expert", "replica"), pairs)


def to_twin(chunk):
    return lax.ppermute(chunk, "replica", [(0, 1), (1, 0)])


def hold_kernel(source_ref, place_ref):
    place_ref[...] = source_ref[...]


def per_device_moving_rows(
    tokens,
    cotangent,
    expert_ids,
    gate_values,
    replica_pick,
    replica_plan,
    gate_proj,
    up_proj,
    down_proj,
):
    experts = lax.axis_size("expert")
    token_count, model_width = tokens.shape
    topk = expert_ids.shape[1]
    hidden_width = gate_proj.shape[2]
    width = model_width // QUARTERS
    served = experts * (MAIN + 2)
    small = (topk, token_count)
    count = len(BASES)
    *chunks, slot, gates = local_call(
        route_kernel,
        [((SEND_ROWS, width), BF)] * experts
        + [((experts, token_count), jnp.int32), ((experts, token_count), F32)],
        [replica_plan, expert_ids.T, replica_pick.T, gate_values.T, tokens, cotangent],
        "route",
        LONG,
        2 * 2 * (token_count + served) * model_width,
        space=pltpu.HBM,
        limit=54,
        scratch=[
            pltpu.SMEM((experts,), jnp.int32),
            pltpu.VMEM(small, jnp.int32),
            pltpu.VMEM(small, jnp.int32),
            pltpu.VMEM(small, BF),
            pltpu.VMEM(tokens.shape, BF),
            pltpu.VMEM(tokens.shape, BF),
            pltpu.SemaphoreType.DMA((6,)),
        ],
    )
    recv = list(chunks)
    recv[1] = to_step(chunks[1], 1)
    twin = [to_twin(chunks[c]) for c in (3, 5, 7)]
    twin, mine = lax.optimization_barrier((twin, chunks[4]))
    for d, base in enumerate(BASES):
        recv[2 + 2 * d] = to_step(mine if base == 6 else chunks[2 + 2 * d], base)
        recv[3 + 2 * d] = to_step(twin[d], base)
    (held,) = local_call(hold_kernel, [(recv[0].shape, BF)], [recv[0]], "hold", 1, 1)
    matmul = 2 * served * model_width * hidden_width
    outs = local_call(
        expert_kernel,
        [((BACK_ROWS, width), BF)] * 2
        + [((2 * BACK_ROWS, width), BF)] * count
        + [((served, model_width), BF)] * 2
        + [((served, hidden_width), BF)] * 3,
        [held, *(recv[c] for c in ORDER[1:]), gate_proj[0], up_proj[0], down_proj[0]],
        "expert_rows",
        5 * matmul,
        2 * 3 * model_width * hidden_width,
    )
    backs, factors = outs[: 2 + count], outs[2 + count :]
    kept = list(map(to_step, backs[2:], BASES))
    near = to_step(backs[1], 1)
    half = model_width // 2
    (leaving,) = local_call(
        other_half_kernel,
        [((3 * half, hidden_width), BF)],
        factors,
        "other_half",
        1,
        1,
    )
    shares = local_call(
        own_half_kernel,
        [((half, hidden_width), BF)] * 3,
        [*factors, to_twin(leaving)],
        "own_half",
        1,
        1,
    )
    kept[0], near, shares = lax.optimization_barrier((kept[0], near, shares))
    returned = [backs[0], near, *kept, *map(to_twin, kept)]
    token_grad, gate_grad = local_call(
        combine_kernel,
        [((token_count, model_width), BF), ((topk, token_count), BF)],
        [expert_ids.T, slot, gates, *returned],
        "combine",
        2 * served * token_count * model_width,
        2 * 2 * token_count * model_width,
    )
    return (token_grad, gate_grad.T, shares[0][None], shares[1][None], shares[2][None])


def per_device(tokens, cotangent, expert_ids, gate_values, replica_pick, replica_plan, *matrices):
    experts = lax.axis_size("expert")
    slots = (copies_of(experts) + 1) * CAP
    row_bytes = 3 * 2 * tokens.shape[1] * experts
    matrix_bytes = 4 * sum(2 * m[0].size for m in matrices)
    fits = slots == MAIN + 2 and experts == 8 and lax.axis_size("replica") == 2
    rows_cheaper = slots * row_bytes < 2 * CAP * row_bytes + matrix_bytes
    plan = per_device_moving_rows if fits and rows_cheaper else per_device_moving_weights
    return plan(
        tokens, cotangent, expert_ids, gate_values, replica_pick, replica_plan, *matrices
    )


def solution(mesh):
    placed = (
        P(("parts", "expert", "replica"), None),
        P(("parts", "expert", "replica"), None),
        P(("parts", "expert", "replica"), None),
        P(("parts", "expert", "replica"), None),
        P(("parts", "expert", "replica"), None),
        P("parts"),
        P("expert", None, None),
        P("expert", None, None),
        P("expert", None, None),
    )
    return jax.shard_map(
        per_device,
        mesh=mesh,
        in_specs=placed,
        out_specs=(
            P(("parts", "expert", "replica"), None),
            P(("parts", "expert", "replica"), None),
            P(("parts", "expert"), "replica", None),
            P(("parts", "expert"), "replica", None),
            P(("parts", "expert"), "replica", None),
        ),
        check_vma=False,
    )
```

```python
import jax
import jax.numpy as jnp
from jax import lax
from jax.experimental import pallas as pl
from jax.experimental.pallas import tpu as pltpu
from jax.sharding import PartitionSpec as P

CAP = 6


def route_assignments(flat_ids, flat_pick, replica_plan, capacity):
    experts = replica_plan.shape[0]
    lane_ids = jnp.arange(experts, dtype=jnp.int32)
    same_plan = replica_plan[:, None] == replica_plan[None, :]
    earlier = lane_ids[None, :] < lane_ids[:, None]
    position = jnp.sum(jnp.logical_and(same_plan, earlier), axis=1)
    hot_mask = jnp.any(replica_plan[None, :] == lane_ids[:, None], axis=1)
    is_hot = jnp.any(
        jnp.logical_and(flat_ids[:, None] == lane_ids[None, :], hot_mask[None, :]), axis=1
    )
    use_copy = jnp.logical_and(is_hot, flat_pick >= 1)
    matches = jnp.logical_and(
        replica_plan[None, :] == flat_ids[:, None], position[None, :] == flat_pick[:, None] - 1
    )
    holder = jnp.sum(jnp.where(matches, lane_ids[None, :], 0), axis=1)
    target = jnp.where(use_copy, holder, flat_ids)
    copy_role = use_copy.astype(jnp.int32)
    bucket = target * 2 + copy_role
    sequence = jnp.arange(bucket.shape[0], dtype=jnp.int32)
    arrival = jnp.sum(
        jnp.logical_and(bucket[None, :] == bucket[:, None], sequence[None, :] < sequence[:, None]),
        axis=1,
    )
    kept_mask = arrival < capacity
    slot_index = target * (2 * capacity) + copy_role * capacity + jnp.minimum(arrival, capacity - 1)
    return (slot_index, kept_mask)


def fill_slots(slot_index, kept_mask, slot_count):
    slot_ids = jnp.arange(slot_count, dtype=jnp.int32)
    matches = jnp.logical_and(slot_index[None, :] == slot_ids[:, None], kept_mask[None, :])
    sequence = jnp.arange(slot_index.shape[0], dtype=jnp.int32)
    source = jnp.sum(jnp.where(matches, sequence[None, :], 0), axis=1)
    filled = jnp.any(matches, axis=1)
    return (source, filled)


def expert_backward(row_block, upstream, weight, gate_w, up_w, down_w):
    contract_cols = (((1,), (1,)), ((), ()))
    contract_rows = (((0,), (0,)), ((), ()))
    gate_pre = jnp.dot(row_block, gate_w, preferred_element_type=jnp.float32)
    up_pre = jnp.dot(row_block, up_w, preferred_element_type=jnp.float32)
    sigmoid_gate = jax.nn.sigmoid(gate_pre)
    activated = gate_pre * sigmoid_gate
    hidden = (activated * up_pre).astype(jnp.bfloat16)
    output_rows = lax.dot_general(hidden, down_w, contract_cols, preferred_element_type=jnp.float32)
    weight_col = weight.astype(jnp.float32)[:, None]
    upstream_f = upstream.astype(jnp.float32)
    gate_rows = jnp.sum(upstream_f * output_rows, axis=1)
    hidden_grad = weight_col * jnp.dot(upstream, down_w, preferred_element_type=jnp.float32)
    slope = sigmoid_gate * (1.0 + gate_pre * (1.0 - sigmoid_gate))
    gate_delta = (hidden_grad * up_pre * slope).astype(jnp.bfloat16)
    up_delta = (hidden_grad * activated).astype(jnp.bfloat16)
    input_grad = (
        lax.dot_general(gate_delta, gate_w, contract_cols, preferred_element_type=jnp.float32)
        + lax.dot_general(up_delta, up_w, contract_cols, preferred_element_type=jnp.float32)
    ).astype(jnp.bfloat16)
    scaled = (weight_col * upstream_f).astype(jnp.bfloat16)
    grad_set = (
        lax.dot_general(row_block, gate_delta, contract_rows, preferred_element_type=jnp.float32),
        lax.dot_general(row_block, up_delta, contract_rows, preferred_element_type=jnp.float32),
        lax.dot_general(scaled, hidden, contract_rows, preferred_element_type=jnp.float32),
    )
    return (input_grad, gate_rows, grad_set)


def per_device_moving_weights(
    tokens,
    cotangent,
    expert_ids,
    gate_values,
    replica_pick,
    replica_plan,
    gate_proj,
    up_proj,
    down_proj,
):
    experts = lax.axis_size("expert")
    capacity = CAP
    slot_total = 2 * capacity
    model_width = tokens.shape[1]
    topk = expert_ids.shape[1]
    token_count = tokens.shape[0]
    slot_index, kept_mask = route_assignments(
        expert_ids.reshape(-1), replica_pick.reshape(-1), replica_plan, capacity
    )
    source, filled = fill_slots(slot_index, kept_mask, experts * slot_total)
    token_of = source // topk
    zero_half = jnp.zeros((), jnp.bfloat16)
    send_rows = jnp.where(filled[:, None], jnp.take(tokens, token_of, axis=0), zero_half).reshape(
        experts, slot_total, model_width
    )
    send_upstream = jnp.where(
        filled[:, None], jnp.take(cotangent, token_of, axis=0), zero_half
    ).reshape(experts, slot_total, model_width)
    send_weight = jnp.where(filled, gate_values.reshape(-1)[source], zero_half).reshape(
        experts, slot_total
    )
    arrived = lax.all_to_all(send_rows, "expert", split_axis=0, concat_axis=0, tiled=True)
    own_gate = gate_proj[0]
    own_up = up_proj[0]
    own_down = down_proj[0]
    hidden_width = own_gate.shape[1]
    spread = (
        lax.all_to_all(
            own_gate.reshape(experts, -1), "expert", split_axis=0, concat_axis=0, tiled=True
        ),
        lax.all_to_all(
            own_up.reshape(experts, -1), "expert", split_axis=0, concat_axis=0, tiled=True
        ),
        lax.all_to_all(
            own_down.reshape(experts, -1), "expert", split_axis=0, concat_axis=0, tiled=True
        ),
    )
    chosen_gate = jnp.take(spread[0], replica_plan, axis=0)
    chosen_up = jnp.take(spread[1], replica_plan, axis=0)
    chosen_down = jnp.take(spread[2], replica_plan, axis=0)
    collected = (
        lax.all_to_all(chosen_gate, "expert", split_axis=0, concat_axis=0, tiled=True),
        lax.all_to_all(chosen_up, "expert", split_axis=0, concat_axis=0, tiled=True),
        lax.all_to_all(chosen_down, "expert", split_axis=0, concat_axis=0, tiled=True),
    )
    copy_gate = collected[0].reshape(model_width, hidden_width)
    copy_up = collected[1].reshape(model_width, hidden_width)
    copy_down = collected[2].reshape(model_width, hidden_width)
    arrived_up, arrived_weight = (
        lax.all_to_all(send_upstream, "expert", split_axis=0, concat_axis=0, tiled=True),
        lax.all_to_all(send_weight, "expert", split_axis=0, concat_axis=0, tiled=True),
    )
    owned_dx, owned_gate_rows, owned_grads = expert_backward(
        arrived[:, :capacity].reshape(-1, model_width),
        arrived_up[:, :capacity].reshape(-1, model_width),
        arrived_weight[:, :capacity].reshape(-1),
        own_gate,
        own_up,
        own_down,
    )
    copied_dx, copied_gate_rows, copied_grads = expert_backward(
        arrived[:, capacity:].reshape(-1, model_width),
        arrived_up[:, capacity:].reshape(-1, model_width),
        arrived_weight[:, capacity:].reshape(-1),
        copy_gate,
        copy_up,
        copy_down,
    )
    back_rows = jnp.concatenate(
        [
            owned_dx.reshape(experts, capacity, model_width),
            copied_dx.reshape(experts, capacity, model_width),
        ],
        axis=1,
    )
    back_gate = jnp.concatenate(
        [owned_gate_rows.reshape(experts, capacity), copied_gate_rows.reshape(experts, capacity)],
        axis=1,
    ).astype(jnp.bfloat16)
    returned, returned_gate = (
        lax.all_to_all(back_rows, "expert", split_axis=0, concat_axis=0, tiled=True),
        lax.all_to_all(back_gate, "expert", split_axis=0, concat_axis=0, tiled=True),
    )
    copy_pieces = (
        copied_grads[0].astype(jnp.bfloat16).reshape(experts, -1),
        copied_grads[1].astype(jnp.bfloat16).reshape(experts, -1),
        copied_grads[2].astype(jnp.bfloat16).reshape(experts, -1),
    )
    grad_spread = (
        lax.all_to_all(copy_pieces[0], "expert", split_axis=0, concat_axis=0, tiled=True),
        lax.all_to_all(copy_pieces[1], "expert", split_axis=0, concat_axis=0, tiled=True),
        lax.all_to_all(copy_pieces[2], "expert", split_axis=0, concat_axis=0, tiled=True),
    )
    lane_ids = jnp.arange(experts, dtype=jnp.int32)
    owner_map = (replica_plan[None, :] == lane_ids[:, None]).astype(jnp.bfloat16)
    summed_gate = jnp.dot(owner_map, grad_spread[0], preferred_element_type=jnp.float32).astype(
        jnp.bfloat16
    )
    summed_up = jnp.dot(owner_map, grad_spread[1], preferred_element_type=jnp.float32).astype(
        jnp.bfloat16
    )
    summed_down = jnp.dot(owner_map, grad_spread[2], preferred_element_type=jnp.float32).astype(
        jnp.bfloat16
    )
    grad_back = (
        lax.all_to_all(summed_gate, "expert", split_axis=0, concat_axis=0, tiled=True),
        lax.all_to_all(summed_up, "expert", split_axis=0, concat_axis=0, tiled=True),
        lax.all_to_all(summed_down, "expert", split_axis=0, concat_axis=0, tiled=True),
    )
    total_gate = owned_grads[0] + grad_back[0].reshape(model_width, hidden_width).astype(
        jnp.float32
    )
    total_up = owned_grads[1] + grad_back[1].reshape(model_width, hidden_width).astype(jnp.float32)
    total_down = owned_grads[2] + grad_back[2].reshape(model_width, hidden_width).astype(
        jnp.float32
    )
    shares = (
        lax.psum_scatter(
            total_gate.astype(jnp.bfloat16), "replica", scatter_dimension=0, tiled=True
        ).astype(jnp.float32),
        lax.psum_scatter(
            total_up.astype(jnp.bfloat16), "replica", scatter_dimension=0, tiled=True
        ).astype(jnp.float32),
        lax.psum_scatter(
            total_down.astype(jnp.bfloat16), "replica", scatter_dimension=0, tiled=True
        ).astype(jnp.float32),
    )
    flat_back = returned.reshape(experts * slot_total, model_width)
    picked_rows = jnp.take(flat_back, slot_index, axis=0)
    picked_rows = jnp.where(kept_mask[:, None], picked_rows, zero_half).astype(jnp.float32)
    token_grad = jnp.sum(picked_rows.reshape(token_count, topk, model_width), axis=1).astype(
        jnp.bfloat16
    )
    gate_grad = jnp.where(kept_mask, returned_gate.reshape(-1)[slot_index], zero_half).reshape(
        token_count, topk
    )
    return (
        token_grad,
        gate_grad,
        shares[0].astype(jnp.bfloat16)[None],
        shares[1].astype(jnp.bfloat16)[None],
        shares[2].astype(jnp.bfloat16)[None],
    )


BF = jnp.bfloat16
F32 = jnp.float32
CONTRACT_ROWS = (((0,), (0,)), ((), ()))
CONTRACT_COLS = (((1,), (1,)), ((), ()))
MIB = 1024 * 1024

BASES = (4, 6, 2)
ORDER = (0, 1, 2, 4, 6, 3, 7, 5)
LONG = 8 * 10**9
MAIN = 16
QUARTERS = 4
SEND_ROWS = 2 * QUARTERS * MAIN + 16
BACK_ROWS = QUARTERS * MAIN + 16


def copies_of(experts):
    return 2 if experts <= 8 else 8


def iota(shape, axis):
    return lax.broadcasted_iota(jnp.int32, shape, axis)


def partners(experts, tokens):
    row = iota((experts, tokens), 0)
    step = jnp.bitwise_xor(jnp.bitwise_and(row, 1), lax.axis_index("replica"))
    for d, base in enumerate(BASES):
        step = jnp.where(jnp.right_shift(row, 1) == d + 1, step + base, step)
    step = jnp.where(row < 2, row, step)
    return jnp.bitwise_xor(step, lax.axis_index("expert"))


def chunk_views(refs, rows):
    return [(refs[0], 0), (refs[1], 0)] + [(ref, part * rows) for ref in refs[2:] for part in (0, 1)]


def mask(condition):
    return condition.astype(F32).astype(BF)


def repeat_rows(table, times):
    width = table.shape[1]
    return jnp.concatenate(
        [jnp.broadcast_to(table[e : e + 1], (times, width)) for e in range(table.shape[0])], axis=0
    )


def route_kernel(plan_hbm, ids_hbm, pick_hbm, gate_hbm, tok_hbm, cot_hbm, *refs):
    sems = refs[-1]
    plan_ref, ids_ref, pick_ref, gate_ref, tok_ref, cot_ref = refs[-7:-1]
    slot_ref, gates_ref = refs[-9:-7]
    send_refs = refs[:-9]
    topk, tokens = ids_ref.shape
    experts = len(send_refs)
    width = tok_ref.shape[1] // QUARTERS
    copies = copies_of(experts)
    loads = [
        pltpu.make_async_copy(source, place, sems.at[n])
        for n, (source, place) in enumerate(
            (
                (plan_hbm, plan_ref),
                (ids_hbm, ids_ref),
                (pick_hbm, pick_ref),
                (gate_hbm, gate_ref),
                (tok_hbm, tok_ref),
                (cot_hbm, cot_ref),
            )
        )
    ]
    for load in loads:
        load.start()
    before = mask(iota((tokens, tokens), 0) < iota((tokens, tokens), 1))
    expert_row = partners(experts, tokens)
    for load in loads[:4]:
        load.wait()
    ids = ids_ref[...]
    pick = pick_ref[...]
    gate = gate_ref[...].astype(F32)
    named = jnp.zeros((experts, tokens), jnp.int32)
    gates = jnp.zeros((experts, tokens), F32)
    for k in range(topk):
        hit = ids[k : k + 1] == expert_row
        named = jnp.where(hit, pick[k : k + 1] + 1, named)
        gates = jnp.where(hit, gate[k : k + 1], gates)
    hot = jnp.zeros((experts, tokens), jnp.int32)
    for j in range(experts):
        hot = jnp.where(expert_row == plan_ref[j], 1, hot)
    chosen = jnp.where(named == 0, -1, jnp.where(hot > 0, named - 1, 0))
    masks = jnp.concatenate([(chosen == c).astype(F32) for c in range(copies + 1)], axis=0)
    rank = jnp.dot(masks.astype(BF), before, preferred_element_type=F32).astype(jnp.int32)
    slot = jnp.full((experts, tokens), -1, jnp.int32)
    for c in range(copies + 1):
        rank_c = rank[c * experts : (c + 1) * experts]
        keep = jnp.logical_and(chosen == c, rank_c < CAP)
        slot = jnp.where(keep, c * CAP + rank_c, slot)
    slot_ref[...] = slot
    gates_ref[...] = gates
    slot16 = repeat_rows(slot, MAIN)
    gate16 = repeat_rows(gates, MAIN)
    inner = jnp.bitwise_and(iota(slot16.shape, 0), MAIN - 1)
    onehot = (slot16 == inner).astype(F32)
    wanted = MAIN + jnp.bitwise_and(jnp.right_shift(inner, 2), 1)
    last = (slot16 == wanted).astype(F32)
    last_rows = jnp.where(inner >= 8, 0.0, last)
    last_scaled = jnp.where(inner >= 8, last * gate16, 0.0)
    quarter = jnp.bitwise_and(inner, 3)
    for load in loads[4:]:
        load.wait()
    rows = jnp.dot(onehot.astype(BF), tok_ref[...], preferred_element_type=F32).astype(BF)
    scaled = jnp.dot(
        (onehot * gate16).astype(BF), cot_ref[...], preferred_element_type=F32
    ).astype(BF)
    tail = jnp.zeros((experts * MAIN, width), F32)
    for q in range(QUARTERS):
        cols = slice(q * width, (q + 1) * width)
        mine = quarter == q
        tail += jnp.dot(
            jnp.where(mine, last_rows, 0.0).astype(BF), tok_ref[:, cols], preferred_element_type=F32
        )
        tail += jnp.dot(
            jnp.where(mine, last_scaled, 0.0).astype(BF),
            cot_ref[:, cols],
            preferred_element_type=F32,
        )
    tail = tail.astype(BF)
    for c, ref in enumerate(send_refs):
        here = slice(c * MAIN, (c + 1) * MAIN)
        for q in range(QUARTERS):
            cols = slice(q * width, (q + 1) * width)
            ref[q * MAIN : (q + 1) * MAIN, :] = rows[here, cols]
            ref[(QUARTERS + q) * MAIN : (QUARTERS + q + 1) * MAIN, :] = scaled[here, cols]
        ref[2 * QUARTERS * MAIN :, :] = tail[here]


def expert_kernel(*refs):
    experts = len(ORDER)
    recv_refs = [refs[ORDER.index(c)] for c in range(experts)]
    gate_ref, up_ref, down_ref = refs[experts : experts + 3]
    back_views = chunk_views(refs[experts + 3 : -5], BACK_ROWS)
    x_ref, s_ref, dg_ref, du_ref, hid_ref = refs[-5:]
    width = refs[0].shape[1]
    main_rows = experts * MAIN
    tail = jnp.concatenate([ref[2 * QUARTERS * MAIN :, :] for ref in recv_refs], axis=0)
    row = iota((4 * experts, main_rows), 0)
    col = iota((4 * experts, main_rows), 1)
    kind = (row >= 2 * experts).astype(jnp.int32)
    chunk = jnp.right_shift(row - kind * 2 * experts, 1)
    base = chunk * MAIN + kind * 8 + jnp.bitwise_and(row, 1) * 4
    for q in range(QUARTERS):
        cols = slice(q * width, (q + 1) * width)
        picked = jnp.dot(mask(col == base + q), tail, preferred_element_type=F32).astype(BF)
        x_ref[main_rows:, cols] = picked[: 2 * experts]
        s_ref[main_rows:, cols] = picked[2 * experts :]
        for i, ref in enumerate(recv_refs):
            here = slice(i * MAIN, (i + 1) * MAIN)
            x_ref[here, cols] = ref[q * MAIN : (q + 1) * MAIN, :]
            s_ref[here, cols] = ref[(QUARTERS + q) * MAIN : (QUARTERS + q + 1) * MAIN, :]
    rows = x_ref[...]
    gate_pre = jnp.dot(rows, gate_ref[...], preferred_element_type=F32)
    up_pre = jnp.dot(rows, up_ref[...], preferred_element_type=F32)
    hidden_grad = jnp.dot(s_ref[...], down_ref[...], preferred_element_type=F32)
    sig = jax.nn.sigmoid(gate_pre)
    activated = gate_pre * sig
    hidden = (activated * up_pre).astype(BF)
    slope = sig * (1.0 + gate_pre * (1.0 - sig))
    gate_delta = (hidden_grad * up_pre * slope).astype(BF)
    up_delta = (hidden_grad * activated).astype(BF)
    hid_ref[...] = hidden
    dg_ref[...] = gate_delta
    du_ref[...] = up_delta
    grad = (
        lax.dot_general(gate_delta, gate_ref[...], CONTRACT_COLS, preferred_element_type=F32)
        + lax.dot_general(up_delta, up_ref[...], CONTRACT_COLS, preferred_element_type=F32)
    ).astype(BF)
    product = hidden.astype(F32) * hidden_grad
    product = jnp.concatenate(
        [product, jnp.zeros((width - product.shape[0], product.shape[1]), F32)], axis=0
    )
    gate_lanes = lax.dot_general(
        jnp.ones((8, product.shape[1]), F32),
        product,
        CONTRACT_COLS,
        preferred_element_type=F32,
        precision=lax.Precision.HIGHEST,
    )
    trow = iota((main_rows, 2 * experts), 0)
    tcol = iota((main_rows, 2 * experts), 1)
    inner = jnp.bitwise_and(trow, MAIN - 1)
    source = jnp.right_shift(trow, 4) * 2 + jnp.right_shift(inner, 2)
    spread = jnp.zeros((main_rows, width), F32)
    for q in range(QUARTERS):
        cols = slice(q * width, (q + 1) * width)
        mine = jnp.logical_and(jnp.bitwise_and(inner, 3) == q, inner < 8)
        place = mask(jnp.logical_and(mine, tcol == source))
        spread += jnp.dot(place, grad[main_rows:, cols], preferred_element_type=F32)
        for i, (ref, first) in enumerate(back_views):
            low = first + q * MAIN
            ref[low : low + MAIN, :] = grad[i * MAIN : (i + 1) * MAIN, cols]
    for i, (ref, first) in enumerate(back_views):
        low = first + QUARTERS * MAIN
        ref[low : low + 16, :] = jnp.concatenate(
            [spread[i * MAIN : i * MAIN + 8], gate_lanes], axis=0
        ).astype(BF)


def grads_of(half, x_ref, s_ref, dg_ref, du_ref, hid_ref):
    rows = x_ref.shape[1] // 2
    cols = pl.ds(pl.multiple_of(half * rows, rows), rows)
    x_half = x_ref[:, cols]
    s_half = s_ref[:, cols]
    return (
        lax.dot_general(x_half, dg_ref[...], CONTRACT_ROWS, preferred_element_type=F32),
        lax.dot_general(x_half, du_ref[...], CONTRACT_ROWS, preferred_element_type=F32),
        lax.dot_general(s_half, hid_ref[...], CONTRACT_ROWS, preferred_element_type=F32),
    )


def other_half_kernel(x_ref, s_ref, dg_ref, du_ref, hid_ref, out_ref):
    half = 1 - lax.axis_index("replica")
    parts = grads_of(half, x_ref, s_ref, dg_ref, du_ref, hid_ref)
    rows = parts[0].shape[0]
    for n in range(3):
        out_ref[n * rows : (n + 1) * rows, :] = parts[n].astype(BF)


def own_half_kernel(
    x_ref, s_ref, dg_ref, du_ref, hid_ref, came_ref, gate_ref, up_ref, down_ref
):
    parts = grads_of(lax.axis_index("replica"), x_ref, s_ref, dg_ref, du_ref, hid_ref)
    rows = parts[0].shape[0]
    for n, out_ref in enumerate((gate_ref, up_ref, down_ref)):
        came = came_ref[n * rows : (n + 1) * rows, :].astype(F32)
        out_ref[...] = (parts[n].astype(BF).astype(F32) + came).astype(BF)


def combine_kernel(ids_ref, slot_ref, gates_ref, *refs):
    token_ref, grad_ref = refs[-2:]
    doubles = 2 + len(BASES)
    ret_views = [(refs[0], 0), (refs[1], 0)]
    for kept_ref, given_ref in zip(refs[2:doubles], refs[doubles:-2]):
        ret_views += [(kept_ref, 0), (given_ref, BACK_ROWS)]
    topk, tokens = ids_ref.shape
    experts = len(ret_views)
    width = refs[0].shape[1]
    ids = ids_ref[...]
    slot = slot_ref[...]
    slot16 = repeat_rows(slot, MAIN)
    inner = jnp.bitwise_and(iota(slot16.shape, 0), MAIN - 1)
    onehot = mask(slot16 == inner)
    wanted = MAIN + jnp.right_shift(inner, 2)
    last = jnp.where(jnp.logical_and(slot16 == wanted, inner < 8), 1.0, 0.0)
    quarter = jnp.bitwise_and(inner, 3)
    tails = [ref[first + BACK_ROWS - 16 : first + BACK_ROWS, :] for ref, first in ret_views]
    tail = jnp.concatenate(tails, axis=0)
    for q in range(QUARTERS):
        main = jnp.concatenate(
            [ref[first + q * MAIN : first + (q + 1) * MAIN, :] for ref, first in ret_views], axis=0
        )
        place = jnp.where(quarter == q, last, 0.0).astype(BF)
        total = lax.dot_general(onehot, main, CONTRACT_ROWS, preferred_element_type=F32)
        total += lax.dot_general(place, tail, CONTRACT_ROWS, preferred_element_type=F32)
        token_ref[:, q * width : (q + 1) * width] = total.astype(BF)
    lane_index = iota((width, tokens), 0)
    found = []
    for c in range(experts):
        mine = slot[c : c + 1]
        lane = jnp.where(mine < MAIN, c * MAIN + mine, experts * MAIN + 2 * c + mine - MAIN)
        lane = jnp.where(mine < 0, -1, lane)
        sums = jnp.dot(tails[c], mask(lane_index == lane), preferred_element_type=F32)
        found.append(sums[8:9])
    found = jnp.concatenate(found, axis=0)
    kept = slot >= 0
    grads = jnp.where(kept, found / jnp.where(kept, gates_ref[...], 1.0), 0.0)
    expert_row = partners(experts, tokens)
    by_choice = [
        jnp.sum(jnp.where(expert_row == ids[k : k + 1], grads, 0.0), axis=0, keepdims=True)
        for k in range(topk)
    ]
    grad_ref[...] = jnp.concatenate(by_choice, axis=0).astype(BF)


def local_call(kernel, outs, arrays, name, flops, moved, space=pltpu.VMEM, scratch=(), limit=16):
    vmem = pl.BlockSpec(memory_space=pltpu.VMEM)
    return pl.pallas_call(
        kernel,
        out_shape=[jax.ShapeDtypeStruct(shape, kind) for shape, kind in outs],
        in_specs=[pl.BlockSpec(memory_space=space)] * len(arrays),
        out_specs=[vmem] * len(outs),
        scratch_shapes=list(scratch),
        compiler_params=pltpu.CompilerParams(vmem_limit_bytes=limit * MIB),
        cost_estimate=pl.CostEstimate(flops=flops, bytes_accessed=moved, transcendentals=0),
        name=name,
    )(*arrays)


def to_step(chunk, base):
    experts = lax.axis_size("expert")
    if base == 1:
        return lax.ppermute(chunk, "expert", [(i, i ^ 1) for i in range(experts)])
    pairs = [(2 * i + r, 2 * (i ^ (base + r)) + r) for i in range(experts) for r in range(2)]
    return lax.ppermute(chunk, ("expert", "replica"), pairs)


def to_twin(chunk):
    return lax.ppermute(chunk, "replica", [(0, 1), (1, 0)])


def hold_kernel(source_ref, place_ref):
    place_ref[...] = source_ref[...]


def per_device_moving_rows(
    tokens,
    cotangent,
    expert_ids,
    gate_values,
    replica_pick,
    replica_plan,
    gate_proj,
    up_proj,
    down_proj,
):
    experts = lax.axis_size("expert")
    token_count, model_width = tokens.shape
    topk = expert_ids.shape[1]
    hidden_width = gate_proj.shape[2]
    width = model_width // QUARTERS
    served = experts * (MAIN + 2)
    small = (topk, token_count)
    count = len(BASES)
    *chunks, slot, gates = local_call(
        route_kernel,
        [((SEND_ROWS, width), BF)] * experts
        + [((experts, token_count), jnp.int32), ((experts, token_count), F32)],
        [replica_plan, expert_ids.T, replica_pick.T, gate_values.T, tokens, cotangent],
        "route",
        LONG,
        2 * 2 * (token_count + served) * model_width,
        space=pltpu.HBM,
        limit=54,
        scratch=[
            pltpu.SMEM((experts,), jnp.int32),
            pltpu.VMEM(small, jnp.int32),
            pltpu.VMEM(small, jnp.int32),
            pltpu.VMEM(small, BF),
            pltpu.VMEM(tokens.shape, BF),
            pltpu.VMEM(tokens.shape, BF),
            pltpu.SemaphoreType.DMA((6,)),
        ],
    )
    recv = list(chunks)
    recv[1] = to_step(chunks[1], 1)
    twin = [to_twin(chunks[c]) for c in (3, 5, 7)]
    twin, mine = lax.optimization_barrier((twin, [chunks[4], chunks[6]]))
    for d, base in enumerate(BASES):
        recv[2 + 2 * d] = to_step(mine[d - 1] if d else chunks[2], base)
        recv[3 + 2 * d] = to_step(twin[d], base)
    (held,) = local_call(hold_kernel, [(recv[0].shape, BF)], [recv[0]], "hold", 1, 1)
    matmul = 2 * served * model_width * hidden_width
    outs = local_call(
        expert_kernel,
        [((BACK_ROWS, width), BF)] * 2
        + [((2 * BACK_ROWS, width), BF)] * count
        + [((served, model_width), BF)] * 2
        + [((served, hidden_width), BF)] * 3,
        [held, *(recv[c] for c in ORDER[1:]), gate_proj[0], up_proj[0], down_proj[0]],
        "expert_rows",
        5 * matmul,
        2 * 3 * model_width * hidden_width,
    )
    backs, factors = outs[: 2 + count], outs[2 + count :]
    kept = list(map(to_step, backs[2:], BASES))
    near = to_step(backs[1], 1)
    half = model_width // 2
    (leaving,) = local_call(
        other_half_kernel,
        [((3 * half, hidden_width), BF)],
        factors,
        "other_half",
        1,
        1,
    )
    shares = local_call(
        own_half_kernel,
        [((half, hidden_width), BF)] * 3,
        [*factors, to_twin(leaving)],
        "own_half",
        1,
        1,
    )
    kept[1], near, shares = lax.optimization_barrier((kept[1], near, shares))
    kept[2], near = lax.optimization_barrier((kept[2], near))
    returned = [backs[0], near, *kept, *map(to_twin, kept)]
    token_grad, gate_grad = local_call(
        combine_kernel,
        [((token_count, model_width), BF), ((topk, token_count), BF)],
        [expert_ids.T, slot, gates, *returned],
        "combine",
        2 * served * token_count * model_width,
        2 * 2 * token_count * model_width,
    )
    return (token_grad, gate_grad.T, shares[0][None], shares[1][None], shares[2][None])


def per_device(tokens, cotangent, expert_ids, gate_values, replica_pick, replica_plan, *matrices):
    experts = lax.axis_size("expert")
    slots = (copies_of(experts) + 1) * CAP
    row_bytes = 3 * 2 * tokens.shape[1] * experts
    matrix_bytes = 4 * sum(2 * m[0].size for m in matrices)
    fits = slots == MAIN + 2 and experts == 8 and lax.axis_size("replica") == 2
    rows_cheaper = slots * row_bytes < 2 * CAP * row_bytes + matrix_bytes
    plan = per_device_moving_rows if fits and rows_cheaper else per_device_moving_weights
    return plan(
        tokens, cotangent, expert_ids, gate_values, replica_pick, replica_plan, *matrices
    )


def solution(mesh):
    placed = (
        P(("parts", "expert", "replica"), None),
        P(("parts", "expert", "replica"), None),
        P(("parts", "expert", "replica"), None),
        P(("parts", "expert", "replica"), None),
        P(("parts", "expert", "replica"), None),
        P("parts"),
        P("expert", None, None),
        P("expert", None, None),
        P("expert", None, None),
    )
    return jax.shard_map(
        per_device,
        mesh=mesh,
        in_specs=placed,
        out_specs=(
            P(("parts", "expert", "replica"), None),
            P(("parts", "expert", "replica"), None),
            P(("parts", "expert"), "replica", None),
            P(("parts", "expert"), "replica", None),
            P(("parts", "expert"), "replica", None),
        ),
        check_vma=False,
    )
```

```python
import jax
import jax.numpy as jnp
from jax import lax
from jax.experimental import pallas as pl
from jax.experimental.pallas import tpu as pltpu
from jax.sharding import PartitionSpec as P

CAP = 6


def route_assignments(flat_ids, flat_pick, replica_plan, capacity):
    experts = replica_plan.shape[0]
    lane_ids = jnp.arange(experts, dtype=jnp.int32)
    same_plan = replica_plan[:, None] == replica_plan[None, :]
    earlier = lane_ids[None, :] < lane_ids[:, None]
    position = jnp.sum(jnp.logical_and(same_plan, earlier), axis=1)
    hot_mask = jnp.any(replica_plan[None, :] == lane_ids[:, None], axis=1)
    is_hot = jnp.any(
        jnp.logical_and(flat_ids[:, None] == lane_ids[None, :], hot_mask[None, :]), axis=1
    )
    use_copy = jnp.logical_and(is_hot, flat_pick >= 1)
    matches = jnp.logical_and(
        replica_plan[None, :] == flat_ids[:, None], position[None, :] == flat_pick[:, None] - 1
    )
    holder = jnp.sum(jnp.where(matches, lane_ids[None, :], 0), axis=1)
    target = jnp.where(use_copy, holder, flat_ids)
    copy_role = use_copy.astype(jnp.int32)
    bucket = target * 2 + copy_role
    sequence = jnp.arange(bucket.shape[0], dtype=jnp.int32)
    arrival = jnp.sum(
        jnp.logical_and(bucket[None, :] == bucket[:, None], sequence[None, :] < sequence[:, None]),
        axis=1,
    )
    kept_mask = arrival < capacity
    slot_index = target * (2 * capacity) + copy_role * capacity + jnp.minimum(arrival, capacity - 1)
    return (slot_index, kept_mask)


def fill_slots(slot_index, kept_mask, slot_count):
    slot_ids = jnp.arange(slot_count, dtype=jnp.int32)
    matches = jnp.logical_and(slot_index[None, :] == slot_ids[:, None], kept_mask[None, :])
    sequence = jnp.arange(slot_index.shape[0], dtype=jnp.int32)
    source = jnp.sum(jnp.where(matches, sequence[None, :], 0), axis=1)
    filled = jnp.any(matches, axis=1)
    return (source, filled)


def expert_backward(row_block, upstream, weight, gate_w, up_w, down_w):
    contract_cols = (((1,), (1,)), ((), ()))
    contract_rows = (((0,), (0,)), ((), ()))
    gate_pre = jnp.dot(row_block, gate_w, preferred_element_type=jnp.float32)
    up_pre = jnp.dot(row_block, up_w, preferred_element_type=jnp.float32)
    sigmoid_gate = jax.nn.sigmoid(gate_pre)
    activated = gate_pre * sigmoid_gate
    hidden = (activated * up_pre).astype(jnp.bfloat16)
    output_rows = lax.dot_general(hidden, down_w, contract_cols, preferred_element_type=jnp.float32)
    weight_col = weight.astype(jnp.float32)[:, None]
    upstream_f = upstream.astype(jnp.float32)
    gate_rows = jnp.sum(upstream_f * output_rows, axis=1)
    hidden_grad = weight_col * jnp.dot(upstream, down_w, preferred_element_type=jnp.float32)
    slope = sigmoid_gate * (1.0 + gate_pre * (1.0 - sigmoid_gate))
    gate_delta = (hidden_grad * up_pre * slope).astype(jnp.bfloat16)
    up_delta = (hidden_grad * activated).astype(jnp.bfloat16)
    input_grad = (
        lax.dot_general(gate_delta, gate_w, contract_cols, preferred_element_type=jnp.float32)
        + lax.dot_general(up_delta, up_w, contract_cols, preferred_element_type=jnp.float32)
    ).astype(jnp.bfloat16)
    scaled = (weight_col * upstream_f).astype(jnp.bfloat16)
    grad_set = (
        lax.dot_general(row_block, gate_delta, contract_rows, preferred_element_type=jnp.float32),
        lax.dot_general(row_block, up_delta, contract_rows, preferred_element_type=jnp.float32),
        lax.dot_general(scaled, hidden, contract_rows, preferred_element_type=jnp.float32),
    )
    return (input_grad, gate_rows, grad_set)


def per_device_moving_weights(
    tokens,
    cotangent,
    expert_ids,
    gate_values,
    replica_pick,
    replica_plan,
    gate_proj,
    up_proj,
    down_proj,
):
    experts = lax.axis_size("expert")
    capacity = CAP
    slot_total = 2 * capacity
    model_width = tokens.shape[1]
    topk = expert_ids.shape[1]
    token_count = tokens.shape[0]
    slot_index, kept_mask = route_assignments(
        expert_ids.reshape(-1), replica_pick.reshape(-1), replica_plan, capacity
    )
    source, filled = fill_slots(slot_index, kept_mask, experts * slot_total)
    token_of = source // topk
    zero_half = jnp.zeros((), jnp.bfloat16)
    send_rows = jnp.where(filled[:, None], jnp.take(tokens, token_of, axis=0), zero_half).reshape(
        experts, slot_total, model_width
    )
    send_upstream = jnp.where(
        filled[:, None], jnp.take(cotangent, token_of, axis=0), zero_half
    ).reshape(experts, slot_total, model_width)
    send_weight = jnp.where(filled, gate_values.reshape(-1)[source], zero_half).reshape(
        experts, slot_total
    )
    arrived = lax.all_to_all(send_rows, "expert", split_axis=0, concat_axis=0, tiled=True)
    own_gate = gate_proj[0]
    own_up = up_proj[0]
    own_down = down_proj[0]
    hidden_width = own_gate.shape[1]
    spread = (
        lax.all_to_all(
            own_gate.reshape(experts, -1), "expert", split_axis=0, concat_axis=0, tiled=True
        ),
        lax.all_to_all(
            own_up.reshape(experts, -1), "expert", split_axis=0, concat_axis=0, tiled=True
        ),
        lax.all_to_all(
            own_down.reshape(experts, -1), "expert", split_axis=0, concat_axis=0, tiled=True
        ),
    )
    chosen_gate = jnp.take(spread[0], replica_plan, axis=0)
    chosen_up = jnp.take(spread[1], replica_plan, axis=0)
    chosen_down = jnp.take(spread[2], replica_plan, axis=0)
    collected = (
        lax.all_to_all(chosen_gate, "expert", split_axis=0, concat_axis=0, tiled=True),
        lax.all_to_all(chosen_up, "expert", split_axis=0, concat_axis=0, tiled=True),
        lax.all_to_all(chosen_down, "expert", split_axis=0, concat_axis=0, tiled=True),
    )
    copy_gate = collected[0].reshape(model_width, hidden_width)
    copy_up = collected[1].reshape(model_width, hidden_width)
    copy_down = collected[2].reshape(model_width, hidden_width)
    arrived_up, arrived_weight = (
        lax.all_to_all(send_upstream, "expert", split_axis=0, concat_axis=0, tiled=True),
        lax.all_to_all(send_weight, "expert", split_axis=0, concat_axis=0, tiled=True),
    )
    owned_dx, owned_gate_rows, owned_grads = expert_backward(
        arrived[:, :capacity].reshape(-1, model_width),
        arrived_up[:, :capacity].reshape(-1, model_width),
        arrived_weight[:, :capacity].reshape(-1),
        own_gate,
        own_up,
        own_down,
    )
    copied_dx, copied_gate_rows, copied_grads = expert_backward(
        arrived[:, capacity:].reshape(-1, model_width),
        arrived_up[:, capacity:].reshape(-1, model_width),
        arrived_weight[:, capacity:].reshape(-1),
        copy_gate,
        copy_up,
        copy_down,
    )
    back_rows = jnp.concatenate(
        [
            owned_dx.reshape(experts, capacity, model_width),
            copied_dx.reshape(experts, capacity, model_width),
        ],
        axis=1,
    )
    back_gate = jnp.concatenate(
        [owned_gate_rows.reshape(experts, capacity), copied_gate_rows.reshape(experts, capacity)],
        axis=1,
    ).astype(jnp.bfloat16)
    returned, returned_gate = (
        lax.all_to_all(back_rows, "expert", split_axis=0, concat_axis=0, tiled=True),
        lax.all_to_all(back_gate, "expert", split_axis=0, concat_axis=0, tiled=True),
    )
    copy_pieces = (
        copied_grads[0].astype(jnp.bfloat16).reshape(experts, -1),
        copied_grads[1].astype(jnp.bfloat16).reshape(experts, -1),
        copied_grads[2].astype(jnp.bfloat16).reshape(experts, -1),
    )
    grad_spread = (
        lax.all_to_all(copy_pieces[0], "expert", split_axis=0, concat_axis=0, tiled=True),
        lax.all_to_all(copy_pieces[1], "expert", split_axis=0, concat_axis=0, tiled=True),
        lax.all_to_all(copy_pieces[2], "expert", split_axis=0, concat_axis=0, tiled=True),
    )
    lane_ids = jnp.arange(experts, dtype=jnp.int32)
    owner_map = (replica_plan[None, :] == lane_ids[:, None]).astype(jnp.bfloat16)
    summed_gate = jnp.dot(owner_map, grad_spread[0], preferred_element_type=jnp.float32).astype(
        jnp.bfloat16
    )
    summed_up = jnp.dot(owner_map, grad_spread[1], preferred_element_type=jnp.float32).astype(
        jnp.bfloat16
    )
    summed_down = jnp.dot(owner_map, grad_spread[2], preferred_element_type=jnp.float32).astype(
        jnp.bfloat16
    )
    grad_back = (
        lax.all_to_all(summed_gate, "expert", split_axis=0, concat_axis=0, tiled=True),
        lax.all_to_all(summed_up, "expert", split_axis=0, concat_axis=0, tiled=True),
        lax.all_to_all(summed_down, "expert", split_axis=0, concat_axis=0, tiled=True),
    )
    total_gate = owned_grads[0] + grad_back[0].reshape(model_width, hidden_width).astype(
        jnp.float32
    )
    total_up = owned_grads[1] + grad_back[1].reshape(model_width, hidden_width).astype(jnp.float32)
    total_down = owned_grads[2] + grad_back[2].reshape(model_width, hidden_width).astype(
        jnp.float32
    )
    shares = (
        lax.psum_scatter(
            total_gate.astype(jnp.bfloat16), "replica", scatter_dimension=0, tiled=True
        ).astype(jnp.float32),
        lax.psum_scatter(
            total_up.astype(jnp.bfloat16), "replica", scatter_dimension=0, tiled=True
        ).astype(jnp.float32),
        lax.psum_scatter(
            total_down.astype(jnp.bfloat16), "replica", scatter_dimension=0, tiled=True
        ).astype(jnp.float32),
    )
    flat_back = returned.reshape(experts * slot_total, model_width)
    picked_rows = jnp.take(flat_back, slot_index, axis=0)
    picked_rows = jnp.where(kept_mask[:, None], picked_rows, zero_half).astype(jnp.float32)
    token_grad = jnp.sum(picked_rows.reshape(token_count, topk, model_width), axis=1).astype(
        jnp.bfloat16
    )
    gate_grad = jnp.where(kept_mask, returned_gate.reshape(-1)[slot_index], zero_half).reshape(
        token_count, topk
    )
    return (
        token_grad,
        gate_grad,
        shares[0].astype(jnp.bfloat16)[None],
        shares[1].astype(jnp.bfloat16)[None],
        shares[2].astype(jnp.bfloat16)[None],
    )


BF = jnp.bfloat16
F32 = jnp.float32
CONTRACT_ROWS = (((0,), (0,)), ((), ()))
CONTRACT_COLS = (((1,), (1,)), ((), ()))
MIB = 1024 * 1024

SINGLES = 4
BASES = (4, 6)
ORDER = (0, 1, 4, 6, 2, 5, 7, 3)
LONG = 8 * 10**9
MAIN = 16
QUARTERS = 4
SEND_ROWS = 2 * QUARTERS * MAIN + 16
BACK_ROWS = QUARTERS * MAIN + 16


def copies_of(experts):
    return 2 if experts <= 8 else 8


def iota(shape, axis):
    return lax.broadcasted_iota(jnp.int32, shape, axis)


def partners(experts, tokens):
    row = iota((experts, tokens), 0)
    step = jnp.bitwise_xor(jnp.bitwise_and(row, 1), lax.axis_index("replica"))
    for d, base in enumerate(BASES):
        step = jnp.where(jnp.right_shift(row - SINGLES, 1) == d, step + base, step)
    step = jnp.where(row < SINGLES, row, step)
    return jnp.bitwise_xor(step, lax.axis_index("expert"))


def chunk_views(refs, rows):
    singles, doubles = refs[:SINGLES], refs[SINGLES:]
    return [(ref, 0) for ref in singles] + [(ref, part * rows) for ref in doubles for part in (0, 1)]


def mask(condition):
    return condition.astype(F32).astype(BF)


def repeat_rows(table, times):
    width = table.shape[1]
    return jnp.concatenate(
        [jnp.broadcast_to(table[e : e + 1], (times, width)) for e in range(table.shape[0])], axis=0
    )


def route_kernel(plan_hbm, ids_hbm, pick_hbm, gate_hbm, tok_hbm, cot_hbm, *refs):
    sems = refs[-1]
    plan_ref, ids_ref, pick_ref, gate_ref, tok_ref, cot_ref = refs[-7:-1]
    slot_ref, gates_ref = refs[-9:-7]
    send_refs = refs[:-9]
    topk, tokens = ids_ref.shape
    experts = len(send_refs)
    width = tok_ref.shape[1] // QUARTERS
    copies = copies_of(experts)
    loads = [
        pltpu.make_async_copy(source, place, sems.at[n])
        for n, (source, place) in enumerate(
            (
                (plan_hbm, plan_ref),
                (ids_hbm, ids_ref),
                (pick_hbm, pick_ref),
                (gate_hbm, gate_ref),
                (tok_hbm, tok_ref),
                (cot_hbm, cot_ref),
            )
        )
    ]
    for load in loads:
        load.start()
    before = mask(iota((tokens, tokens), 0) < iota((tokens, tokens), 1))
    expert_row = partners(experts, tokens)
    for load in loads[:4]:
        load.wait()
    ids = ids_ref[...]
    pick = pick_ref[...]
    gate = gate_ref[...].astype(F32)
    named = jnp.zeros((experts, tokens), jnp.int32)
    gates = jnp.zeros((experts, tokens), F32)
    for k in range(topk):
        hit = ids[k : k + 1] == expert_row
        named = jnp.where(hit, pick[k : k + 1] + 1, named)
        gates = jnp.where(hit, gate[k : k + 1], gates)
    hot = jnp.zeros((experts, tokens), jnp.int32)
    for j in range(experts):
        hot = jnp.where(expert_row == plan_ref[j], 1, hot)
    chosen = jnp.where(named == 0, -1, jnp.where(hot > 0, named - 1, 0))
    masks = jnp.concatenate([(chosen == c).astype(F32) for c in range(copies + 1)], axis=0)
    rank = jnp.dot(masks.astype(BF), before, preferred_element_type=F32).astype(jnp.int32)
    slot = jnp.full((experts, tokens), -1, jnp.int32)
    for c in range(copies + 1):
        rank_c = rank[c * experts : (c + 1) * experts]
        keep = jnp.logical_and(chosen == c, rank_c < CAP)
        slot = jnp.where(keep, c * CAP + rank_c, slot)
    slot_ref[...] = slot
    gates_ref[...] = gates
    slot16 = repeat_rows(slot, MAIN)
    gate16 = repeat_rows(gates, MAIN)
    inner = jnp.bitwise_and(iota(slot16.shape, 0), MAIN - 1)
    onehot = (slot16 == inner).astype(F32)
    wanted = MAIN + jnp.bitwise_and(jnp.right_shift(inner, 2), 1)
    last = (slot16 == wanted).astype(F32)
    last_rows = jnp.where(inner >= 8, 0.0, last)
    last_scaled = jnp.where(inner >= 8, last * gate16, 0.0)
    quarter = jnp.bitwise_and(inner, 3)
    for load in loads[4:]:
        load.wait()
    rows = jnp.dot(onehot.astype(BF), tok_ref[...], preferred_element_type=F32).astype(BF)
    scaled = jnp.dot(
        (onehot * gate16).astype(BF), cot_ref[...], preferred_element_type=F32
    ).astype(BF)
    tail = jnp.zeros((experts * MAIN, width), F32)
    for q in range(QUARTERS):
        cols = slice(q * width, (q + 1) * width)
        mine = quarter == q
        tail += jnp.dot(
            jnp.where(mine, last_rows, 0.0).astype(BF), tok_ref[:, cols], preferred_element_type=F32
        )
        tail += jnp.dot(
            jnp.where(mine, last_scaled, 0.0).astype(BF),
            cot_ref[:, cols],
            preferred_element_type=F32,
        )
    tail = tail.astype(BF)
    for c, ref in enumerate(send_refs):
        here = slice(c * MAIN, (c + 1) * MAIN)
        for q in range(QUARTERS):
            cols = slice(q * width, (q + 1) * width)
            ref[q * MAIN : (q + 1) * MAIN, :] = rows[here, cols]
            ref[(QUARTERS + q) * MAIN : (QUARTERS + q + 1) * MAIN, :] = scaled[here, cols]
        ref[2 * QUARTERS * MAIN :, :] = tail[here]


def expert_kernel(*refs):
    experts = len(ORDER)
    recv_refs = [refs[ORDER.index(c)] for c in range(experts)]
    gate_ref, up_ref, down_ref = refs[experts : experts + 3]
    back_views = chunk_views(refs[experts + 3 : -5], BACK_ROWS)
    x_ref, s_ref, dg_ref, du_ref, hid_ref = refs[-5:]
    width = refs[0].shape[1]
    main_rows = experts * MAIN
    tail = jnp.concatenate([ref[2 * QUARTERS * MAIN :, :] for ref in recv_refs], axis=0)
    row = iota((4 * experts, main_rows), 0)
    col = iota((4 * experts, main_rows), 1)
    kind = (row >= 2 * experts).astype(jnp.int32)
    chunk = jnp.right_shift(row - kind * 2 * experts, 1)
    base = chunk * MAIN + kind * 8 + jnp.bitwise_and(row, 1) * 4
    for q in range(QUARTERS):
        cols = slice(q * width, (q + 1) * width)
        picked = jnp.dot(mask(col == base + q), tail, preferred_element_type=F32).astype(BF)
        x_ref[main_rows:, cols] = picked[: 2 * experts]
        s_ref[main_rows:, cols] = picked[2 * experts :]
        for i, ref in enumerate(recv_refs):
            here = slice(i * MAIN, (i + 1) * MAIN)
            x_ref[here, cols] = ref[q * MAIN : (q + 1) * MAIN, :]
            s_ref[here, cols] = ref[(QUARTERS + q) * MAIN : (QUARTERS + q + 1) * MAIN, :]
    rows = x_ref[...]
    gate_pre = jnp.dot(rows, gate_ref[...], preferred_element_type=F32)
    up_pre = jnp.dot(rows, up_ref[...], preferred_element_type=F32)
    hidden_grad = jnp.dot(s_ref[...], down_ref[...], preferred_element_type=F32)
    sig = jax.nn.sigmoid(gate_pre)
    activated = gate_pre * sig
    hidden = (activated * up_pre).astype(BF)
    slope = sig * (1.0 + gate_pre * (1.0 - sig))
    gate_delta = (hidden_grad * up_pre * slope).astype(BF)
    up_delta = (hidden_grad * activated).astype(BF)
    hid_ref[...] = hidden
    dg_ref[...] = gate_delta
    du_ref[...] = up_delta
    grad = (
        lax.dot_general(gate_delta, gate_ref[...], CONTRACT_COLS, preferred_element_type=F32)
        + lax.dot_general(up_delta, up_ref[...], CONTRACT_COLS, preferred_element_type=F32)
    ).astype(BF)
    product = hidden.astype(F32) * hidden_grad
    product = jnp.concatenate(
        [product, jnp.zeros((width - product.shape[0], product.shape[1]), F32)], axis=0
    )
    gate_lanes = lax.dot_general(
        jnp.ones((8, product.shape[1]), F32),
        product,
        CONTRACT_COLS,
        preferred_element_type=F32,
        precision=lax.Precision.HIGHEST,
    )
    trow = iota((main_rows, 2 * experts), 0)
    tcol = iota((main_rows, 2 * experts), 1)
    inner = jnp.bitwise_and(trow, MAIN - 1)
    source = jnp.right_shift(trow, 4) * 2 + jnp.right_shift(inner, 2)
    spread = jnp.zeros((main_rows, width), F32)
    for q in range(QUARTERS):
        cols = slice(q * width, (q + 1) * width)
        mine = jnp.logical_and(jnp.bitwise_and(inner, 3) == q, inner < 8)
        place = mask(jnp.logical_and(mine, tcol == source))
        spread += jnp.dot(place, grad[main_rows:, cols], preferred_element_type=F32)
        for i, (ref, first) in enumerate(back_views):
            low = first + q * MAIN
            ref[low : low + MAIN, :] = grad[i * MAIN : (i + 1) * MAIN, cols]
    for i, (ref, first) in enumerate(back_views):
        low = first + QUARTERS * MAIN
        ref[low : low + 16, :] = jnp.concatenate(
            [spread[i * MAIN : i * MAIN + 8], gate_lanes], axis=0
        ).astype(BF)


def grads_of(half, x_ref, s_ref, dg_ref, du_ref, hid_ref):
    rows = x_ref.shape[1] // 2
    cols = pl.ds(pl.multiple_of(half * rows, rows), rows)
    x_half = x_ref[:, cols]
    s_half = s_ref[:, cols]
    return (
        lax.dot_general(x_half, dg_ref[...], CONTRACT_ROWS, preferred_element_type=F32),
        lax.dot_general(x_half, du_ref[...], CONTRACT_ROWS, preferred_element_type=F32),
        lax.dot_general(s_half, hid_ref[...], CONTRACT_ROWS, preferred_element_type=F32),
    )


def other_half_kernel(x_ref, s_ref, dg_ref, du_ref, hid_ref, out_ref):
    half = 1 - lax.axis_index("replica")
    parts = grads_of(half, x_ref, s_ref, dg_ref, du_ref, hid_ref)
    rows = parts[0].shape[0]
    for n in range(3):
        out_ref[n * rows : (n + 1) * rows, :] = parts[n].astype(BF)


def own_half_kernel(
    x_ref, s_ref, dg_ref, du_ref, hid_ref, came_ref, gate_ref, up_ref, down_ref
):
    parts = grads_of(lax.axis_index("replica"), x_ref, s_ref, dg_ref, du_ref, hid_ref)
    rows = parts[0].shape[0]
    for n, out_ref in enumerate((gate_ref, up_ref, down_ref)):
        came = came_ref[n * rows : (n + 1) * rows, :].astype(F32)
        out_ref[...] = (parts[n].astype(BF).astype(F32) + came).astype(BF)


def combine_kernel(ids_ref, slot_ref, gates_ref, *refs):
    token_ref, grad_ref = refs[-2:]
    doubles = SINGLES + len(BASES)
    ret_views = [(ref, 0) for ref in refs[:SINGLES]]
    for kept_ref, given_ref in zip(refs[SINGLES:doubles], refs[doubles:-2]):
        ret_views += [(kept_ref, 0), (given_ref, BACK_ROWS)]
    topk, tokens = ids_ref.shape
    experts = len(ret_views)
    width = refs[0].shape[1]
    ids = ids_ref[...]
    slot = slot_ref[...]
    slot16 = repeat_rows(slot, MAIN)
    inner = jnp.bitwise_and(iota(slot16.shape, 0), MAIN - 1)
    onehot = mask(slot16 == inner)
    wanted = MAIN + jnp.right_shift(inner, 2)
    last = jnp.where(jnp.logical_and(slot16 == wanted, inner < 8), 1.0, 0.0)
    quarter = jnp.bitwise_and(inner, 3)
    tails = [ref[first + BACK_ROWS - 16 : first + BACK_ROWS, :] for ref, first in ret_views]
    tail = jnp.concatenate(tails, axis=0)
    for q in range(QUARTERS):
        main = jnp.concatenate(
            [ref[first + q * MAIN : first + (q + 1) * MAIN, :] for ref, first in ret_views], axis=0
        )
        place = jnp.where(quarter == q, last, 0.0).astype(BF)
        total = lax.dot_general(onehot, main, CONTRACT_ROWS, preferred_element_type=F32)
        total += lax.dot_general(place, tail, CONTRACT_ROWS, preferred_element_type=F32)
        token_ref[:, q * width : (q + 1) * width] = total.astype(BF)
    lane_index = iota((width, tokens), 0)
    found = []
    for c in range(experts):
        mine = slot[c : c + 1]
        lane = jnp.where(mine < MAIN, c * MAIN + mine, experts * MAIN + 2 * c + mine - MAIN)
        lane = jnp.where(mine < 0, -1, lane)
        sums = jnp.dot(tails[c], mask(lane_index == lane), preferred_element_type=F32)
        found.append(sums[8:9])
    found = jnp.concatenate(found, axis=0)
    kept = slot >= 0
    grads = jnp.where(kept, found / jnp.where(kept, gates_ref[...], 1.0), 0.0)
    expert_row = partners(experts, tokens)
    by_choice = [
        jnp.sum(jnp.where(expert_row == ids[k : k + 1], grads, 0.0), axis=0, keepdims=True)
        for k in range(topk)
    ]
    grad_ref[...] = jnp.concatenate(by_choice, axis=0).astype(BF)


def local_call(kernel, outs, arrays, name, flops, moved, space=pltpu.VMEM, scratch=(), limit=16):
    vmem = pl.BlockSpec(memory_space=pltpu.VMEM)
    return pl.pallas_call(
        kernel,
        out_shape=[jax.ShapeDtypeStruct(shape, kind) for shape, kind in outs],
        in_specs=[pl.BlockSpec(memory_space=space)] * len(arrays),
        out_specs=[vmem] * len(outs),
        scratch_shapes=list(scratch),
        compiler_params=pltpu.CompilerParams(vmem_limit_bytes=limit * MIB),
        cost_estimate=pl.CostEstimate(flops=flops, bytes_accessed=moved, transcendentals=0),
        name=name,
    )(*arrays)


def to_step(chunk, step):
    experts = lax.axis_size("expert")
    if step < SINGLES:
        return lax.ppermute(chunk, "expert", [(i, i ^ step) for i in range(experts)])
    pairs = [(2 * i + r, 2 * (i ^ (step + r)) + r) for i in range(experts) for r in range(2)]
    return lax.ppermute(chunk, ("expert", "replica"), pairs)


def to_twin(chunk):
    return lax.ppermute(chunk, "replica", [(0, 1), (1, 0)])


def hold_kernel(source_ref, place_ref):
    place_ref[...] = source_ref[...]


def per_device_moving_rows(
    tokens,
    cotangent,
    expert_ids,
    gate_values,
    replica_pick,
    replica_plan,
    gate_proj,
    up_proj,
    down_proj,
):
    experts = lax.axis_size("expert")
    token_count, model_width = tokens.shape
    topk = expert_ids.shape[1]
    hidden_width = gate_proj.shape[2]
    width = model_width // QUARTERS
    served = experts * (MAIN + 2)
    small = (topk, token_count)
    *chunks, slot, gates = local_call(
        route_kernel,
        [((SEND_ROWS, width), BF)] * experts
        + [((experts, token_count), jnp.int32), ((experts, token_count), F32)],
        [replica_plan, expert_ids.T, replica_pick.T, gate_values.T, tokens, cotangent],
        "route",
        LONG,
        2 * 2 * (token_count + served) * model_width,
        space=pltpu.HBM,
        limit=54,
        scratch=[
            pltpu.SMEM((experts,), jnp.int32),
            pltpu.VMEM(small, jnp.int32),
            pltpu.VMEM(small, jnp.int32),
            pltpu.VMEM(small, BF),
            pltpu.VMEM(tokens.shape, BF),
            pltpu.VMEM(tokens.shape, BF),
            pltpu.SemaphoreType.DMA((6,)),
        ],
    )
    recv = list(chunks)
    twin = [to_twin(chunks[c]) for c in (5, 7)]
    twin, far, near = lax.optimization_barrier((twin, chunks[6], chunks[2:4]))
    recv[1] = to_step(chunks[1], 1)
    recv[2] = to_step(near[0], 2)
    recv[3] = to_step(near[1], 3)
    recv[4] = to_step(chunks[4], 4)
    recv[5] = to_step(twin[0], 4)
    recv[6] = to_step(far, 6)
    recv[7] = to_step(twin[1], 6)
    (held,) = local_call(hold_kernel, [(recv[0].shape, BF)], [recv[0]], "hold", 1, 1)
    matmul = 2 * served * model_width * hidden_width
    outs = local_call(
        expert_kernel,
        [((BACK_ROWS, width), BF)] * SINGLES
        + [((2 * BACK_ROWS, width), BF)] * len(BASES)
        + [((served, model_width), BF)] * 2
        + [((served, hidden_width), BF)] * 3,
        [held, *(recv[c] for c in ORDER[1:]), gate_proj[0], up_proj[0], down_proj[0]],
        "expert_rows",
        5 * matmul,
        2 * 3 * model_width * hidden_width,
    )
    backs, factors = outs[:-5], outs[-5:]
    kept = list(map(to_step, backs[SINGLES:], BASES))
    near = [to_step(backs[c], c) for c in range(1, SINGLES)]
    half = model_width // 2
    (leaving,) = local_call(
        other_half_kernel,
        [((3 * half, hidden_width), BF)],
        factors,
        "other_half",
        1,
        1,
    )
    shares = local_call(
        own_half_kernel,
        [((half, hidden_width), BF)] * 3,
        [*factors, to_twin(leaving)],
        "own_half",
        1,
        1,
    )
    kept, near, shares = lax.optimization_barrier((kept, near, shares))
    first = to_twin(kept[0])
    kept[1], first = lax.optimization_barrier((kept[1], first))
    returned = [backs[0], *near, *kept, first, to_twin(kept[1])]
    token_grad, gate_grad = local_call(
        combine_kernel,
        [((token_count, model_width), BF), ((topk, token_count), BF)],
        [expert_ids.T, slot, gates, *returned],
        "combine",
        2 * served * token_count * model_width,
        2 * 2 * token_count * model_width,
    )
    return (token_grad, gate_grad.T, shares[0][None], shares[1][None], shares[2][None])


def per_device(tokens, cotangent, expert_ids, gate_values, replica_pick, replica_plan, *matrices):
    experts = lax.axis_size("expert")
    slots = (copies_of(experts) + 1) * CAP
    row_bytes = 3 * 2 * tokens.shape[1] * experts
    matrix_bytes = 4 * sum(2 * m[0].size for m in matrices)
    fits = slots == MAIN + 2 and experts == 8 and lax.axis_size("replica") == 2
    rows_cheaper = slots * row_bytes < 2 * CAP * row_bytes + matrix_bytes
    plan = per_device_moving_rows if fits and rows_cheaper else per_device_moving_weights
    return plan(
        tokens, cotangent, expert_ids, gate_values, replica_pick, replica_plan, *matrices
    )


def solution(mesh):
    placed = (
        P(("parts", "expert", "replica"), None),
        P(("parts", "expert", "replica"), None),
        P(("parts", "expert", "replica"), None),
        P(("parts", "expert", "replica"), None),
        P(("parts", "expert", "replica"), None),
        P("parts"),
        P("expert", None, None),
        P("expert", None, None),
        P("expert", None, None),
    )
    return jax.shard_map(
        per_device,
        mesh=mesh,
        in_specs=placed,
        out_specs=(
            P(("parts", "expert", "replica"), None),
            P(("parts", "expert", "replica"), None),
            P(("parts", "expert"), "replica", None),
            P(("parts", "expert"), "replica", None),
            P(("parts", "expert"), "replica", None),
        ),
        check_vma=False,
    )
```

```python
import jax
import jax.numpy as jnp
from jax import lax
from jax.experimental import pallas as pl
from jax.experimental.pallas import tpu as pltpu
from jax.sharding import PartitionSpec as P

CAP = 6


def route_assignments(flat_ids, flat_pick, replica_plan, capacity):
    experts = replica_plan.shape[0]
    lane_ids = jnp.arange(experts, dtype=jnp.int32)
    same_plan = replica_plan[:, None] == replica_plan[None, :]
    earlier = lane_ids[None, :] < lane_ids[:, None]
    position = jnp.sum(jnp.logical_and(same_plan, earlier), axis=1)
    hot_mask = jnp.any(replica_plan[None, :] == lane_ids[:, None], axis=1)
    is_hot = jnp.any(
        jnp.logical_and(flat_ids[:, None] == lane_ids[None, :], hot_mask[None, :]), axis=1
    )
    use_copy = jnp.logical_and(is_hot, flat_pick >= 1)
    matches = jnp.logical_and(
        replica_plan[None, :] == flat_ids[:, None], position[None, :] == flat_pick[:, None] - 1
    )
    holder = jnp.sum(jnp.where(matches, lane_ids[None, :], 0), axis=1)
    target = jnp.where(use_copy, holder, flat_ids)
    copy_role = use_copy.astype(jnp.int32)
    bucket = target * 2 + copy_role
    sequence = jnp.arange(bucket.shape[0], dtype=jnp.int32)
    arrival = jnp.sum(
        jnp.logical_and(bucket[None, :] == bucket[:, None], sequence[None, :] < sequence[:, None]),
        axis=1,
    )
    kept_mask = arrival < capacity
    slot_index = target * (2 * capacity) + copy_role * capacity + jnp.minimum(arrival, capacity - 1)
    return (slot_index, kept_mask)


def fill_slots(slot_index, kept_mask, slot_count):
    slot_ids = jnp.arange(slot_count, dtype=jnp.int32)
    matches = jnp.logical_and(slot_index[None, :] == slot_ids[:, None], kept_mask[None, :])
    sequence = jnp.arange(slot_index.shape[0], dtype=jnp.int32)
    source = jnp.sum(jnp.where(matches, sequence[None, :], 0), axis=1)
    filled = jnp.any(matches, axis=1)
    return (source, filled)


def expert_backward(row_block, upstream, weight, gate_w, up_w, down_w):
    contract_cols = (((1,), (1,)), ((), ()))
    contract_rows = (((0,), (0,)), ((), ()))
    gate_pre = jnp.dot(row_block, gate_w, preferred_element_type=jnp.float32)
    up_pre = jnp.dot(row_block, up_w, preferred_element_type=jnp.float32)
    sigmoid_gate = jax.nn.sigmoid(gate_pre)
    activated = gate_pre * sigmoid_gate
    hidden = (activated * up_pre).astype(jnp.bfloat16)
    output_rows = lax.dot_general(hidden, down_w, contract_cols, preferred_element_type=jnp.float32)
    weight_col = weight.astype(jnp.float32)[:, None]
    upstream_f = upstream.astype(jnp.float32)
    gate_rows = jnp.sum(upstream_f * output_rows, axis=1)
    hidden_grad = weight_col * jnp.dot(upstream, down_w, preferred_element_type=jnp.float32)
    slope = sigmoid_gate * (1.0 + gate_pre * (1.0 - sigmoid_gate))
    gate_delta = (hidden_grad * up_pre * slope).astype(jnp.bfloat16)
    up_delta = (hidden_grad * activated).astype(jnp.bfloat16)
    input_grad = (
        lax.dot_general(gate_delta, gate_w, contract_cols, preferred_element_type=jnp.float32)
        + lax.dot_general(up_delta, up_w, contract_cols, preferred_element_type=jnp.float32)
    ).astype(jnp.bfloat16)
    scaled = (weight_col * upstream_f).astype(jnp.bfloat16)
    grad_set = (
        lax.dot_general(row_block, gate_delta, contract_rows, preferred_element_type=jnp.float32),
        lax.dot_general(row_block, up_delta, contract_rows, preferred_element_type=jnp.float32),
        lax.dot_general(scaled, hidden, contract_rows, preferred_element_type=jnp.float32),
    )
    return (input_grad, gate_rows, grad_set)


def per_device_moving_weights(
    tokens,
    cotangent,
    expert_ids,
    gate_values,
    replica_pick,
    replica_plan,
    gate_proj,
    up_proj,
    down_proj,
):
    experts = lax.axis_size("expert")
    capacity = CAP
    slot_total = 2 * capacity
    model_width = tokens.shape[1]
    topk = expert_ids.shape[1]
    token_count = tokens.shape[0]
    slot_index, kept_mask = route_assignments(
        expert_ids.reshape(-1), replica_pick.reshape(-1), replica_plan, capacity
    )
    source, filled = fill_slots(slot_index, kept_mask, experts * slot_total)
    token_of = source // topk
    zero_half = jnp.zeros((), jnp.bfloat16)
    send_rows = jnp.where(filled[:, None], jnp.take(tokens, token_of, axis=0), zero_half).reshape(
        experts, slot_total, model_width
    )
    send_upstream = jnp.where(
        filled[:, None], jnp.take(cotangent, token_of, axis=0), zero_half
    ).reshape(experts, slot_total, model_width)
    send_weight = jnp.where(filled, gate_values.reshape(-1)[source], zero_half).reshape(
        experts, slot_total
    )
    arrived = lax.all_to_all(send_rows, "expert", split_axis=0, concat_axis=0, tiled=True)
    own_gate = gate_proj[0]
    own_up = up_proj[0]
    own_down = down_proj[0]
    hidden_width = own_gate.shape[1]
    spread = (
        lax.all_to_all(
            own_gate.reshape(experts, -1), "expert", split_axis=0, concat_axis=0, tiled=True
        ),
        lax.all_to_all(
            own_up.reshape(experts, -1), "expert", split_axis=0, concat_axis=0, tiled=True
        ),
        lax.all_to_all(
            own_down.reshape(experts, -1), "expert", split_axis=0, concat_axis=0, tiled=True
        ),
    )
    chosen_gate = jnp.take(spread[0], replica_plan, axis=0)
    chosen_up = jnp.take(spread[1], replica_plan, axis=0)
    chosen_down = jnp.take(spread[2], replica_plan, axis=0)
    collected = (
        lax.all_to_all(chosen_gate, "expert", split_axis=0, concat_axis=0, tiled=True),
        lax.all_to_all(chosen_up, "expert", split_axis=0, concat_axis=0, tiled=True),
        lax.all_to_all(chosen_down, "expert", split_axis=0, concat_axis=0, tiled=True),
    )
    copy_gate = collected[0].reshape(model_width, hidden_width)
    copy_up = collected[1].reshape(model_width, hidden_width)
    copy_down = collected[2].reshape(model_width, hidden_width)
    arrived_up, arrived_weight = (
        lax.all_to_all(send_upstream, "expert", split_axis=0, concat_axis=0, tiled=True),
        lax.all_to_all(send_weight, "expert", split_axis=0, concat_axis=0, tiled=True),
    )
    owned_dx, owned_gate_rows, owned_grads = expert_backward(
        arrived[:, :capacity].reshape(-1, model_width),
        arrived_up[:, :capacity].reshape(-1, model_width),
        arrived_weight[:, :capacity].reshape(-1),
        own_gate,
        own_up,
        own_down,
    )
    copied_dx, copied_gate_rows, copied_grads = expert_backward(
        arrived[:, capacity:].reshape(-1, model_width),
        arrived_up[:, capacity:].reshape(-1, model_width),
        arrived_weight[:, capacity:].reshape(-1),
        copy_gate,
        copy_up,
        copy_down,
    )
    back_rows = jnp.concatenate(
        [
            owned_dx.reshape(experts, capacity, model_width),
            copied_dx.reshape(experts, capacity, model_width),
        ],
        axis=1,
    )
    back_gate = jnp.concatenate(
        [owned_gate_rows.reshape(experts, capacity), copied_gate_rows.reshape(experts, capacity)],
        axis=1,
    ).astype(jnp.bfloat16)
    returned, returned_gate = (
        lax.all_to_all(back_rows, "expert", split_axis=0, concat_axis=0, tiled=True),
        lax.all_to_all(back_gate, "expert", split_axis=0, concat_axis=0, tiled=True),
    )
    copy_pieces = (
        copied_grads[0].astype(jnp.bfloat16).reshape(experts, -1),
        copied_grads[1].astype(jnp.bfloat16).reshape(experts, -1),
        copied_grads[2].astype(jnp.bfloat16).reshape(experts, -1),
    )
    grad_spread = (
        lax.all_to_all(copy_pieces[0], "expert", split_axis=0, concat_axis=0, tiled=True),
        lax.all_to_all(copy_pieces[1], "expert", split_axis=0, concat_axis=0, tiled=True),
        lax.all_to_all(copy_pieces[2], "expert", split_axis=0, concat_axis=0, tiled=True),
    )
    lane_ids = jnp.arange(experts, dtype=jnp.int32)
    owner_map = (replica_plan[None, :] == lane_ids[:, None]).astype(jnp.bfloat16)
    summed_gate = jnp.dot(owner_map, grad_spread[0], preferred_element_type=jnp.float32).astype(
        jnp.bfloat16
    )
    summed_up = jnp.dot(owner_map, grad_spread[1], preferred_element_type=jnp.float32).astype(
        jnp.bfloat16
    )
    summed_down = jnp.dot(owner_map, grad_spread[2], preferred_element_type=jnp.float32).astype(
        jnp.bfloat16
    )
    grad_back = (
        lax.all_to_all(summed_gate, "expert", split_axis=0, concat_axis=0, tiled=True),
        lax.all_to_all(summed_up, "expert", split_axis=0, concat_axis=0, tiled=True),
        lax.all_to_all(summed_down, "expert", split_axis=0, concat_axis=0, tiled=True),
    )
    total_gate = owned_grads[0] + grad_back[0].reshape(model_width, hidden_width).astype(
        jnp.float32
    )
    total_up = owned_grads[1] + grad_back[1].reshape(model_width, hidden_width).astype(jnp.float32)
    total_down = owned_grads[2] + grad_back[2].reshape(model_width, hidden_width).astype(
        jnp.float32
    )
    shares = (
        lax.psum_scatter(
            total_gate.astype(jnp.bfloat16), "replica", scatter_dimension=0, tiled=True
        ).astype(jnp.float32),
        lax.psum_scatter(
            total_up.astype(jnp.bfloat16), "replica", scatter_dimension=0, tiled=True
        ).astype(jnp.float32),
        lax.psum_scatter(
            total_down.astype(jnp.bfloat16), "replica", scatter_dimension=0, tiled=True
        ).astype(jnp.float32),
    )
    flat_back = returned.reshape(experts * slot_total, model_width)
    picked_rows = jnp.take(flat_back, slot_index, axis=0)
    picked_rows = jnp.where(kept_mask[:, None], picked_rows, zero_half).astype(jnp.float32)
    token_grad = jnp.sum(picked_rows.reshape(token_count, topk, model_width), axis=1).astype(
        jnp.bfloat16
    )
    gate_grad = jnp.where(kept_mask, returned_gate.reshape(-1)[slot_index], zero_half).reshape(
        token_count, topk
    )
    return (
        token_grad,
        gate_grad,
        shares[0].astype(jnp.bfloat16)[None],
        shares[1].astype(jnp.bfloat16)[None],
        shares[2].astype(jnp.bfloat16)[None],
    )


BF = jnp.bfloat16
F32 = jnp.float32
CONTRACT_ROWS = (((0,), (0,)), ((), ()))
CONTRACT_COLS = (((1,), (1,)), ((), ()))
MIB = 1024 * 1024

BASES = (4, 6, 2)
ORDER = (0, 1, 2, 4, 6, 3, 7, 5)
LONG = 8 * 10**9
MAIN = 16
QUARTERS = 4
SEND_ROWS = 2 * QUARTERS * MAIN + 16
BACK_ROWS = QUARTERS * MAIN + 16


def copies_of(experts):
    return 2 if experts <= 8 else 8


def iota(shape, axis):
    return lax.broadcasted_iota(jnp.int32, shape, axis)


def partners(experts, tokens):
    row = iota((experts, tokens), 0)
    step = jnp.bitwise_xor(jnp.bitwise_and(row, 1), lax.axis_index("replica"))
    for d, base in enumerate(BASES):
        step = jnp.where(jnp.right_shift(row, 1) == d + 1, step + base, step)
    step = jnp.where(row < 2, row, step)
    return jnp.bitwise_xor(step, lax.axis_index("expert"))


def chunk_views(refs, rows):
    return [(refs[0], 0), (refs[1], 0)] + [(ref, part * rows) for ref in refs[2:] for part in (0, 1)]


def mask(condition):
    return condition.astype(F32).astype(BF)


def repeat_rows(table, times):
    width = table.shape[1]
    return jnp.concatenate(
        [jnp.broadcast_to(table[e : e + 1], (times, width)) for e in range(table.shape[0])], axis=0
    )


def route_kernel(plan_hbm, ids_hbm, pick_hbm, gate_hbm, tok_hbm, cot_hbm, *refs):
    sems = refs[-1]
    plan_ref, ids_ref, pick_ref, gate_ref, tok_ref, cot_ref = refs[-7:-1]
    slot_ref, gates_ref = refs[-9:-7]
    send_refs = refs[:-9]
    topk, tokens = ids_ref.shape
    experts = len(send_refs)
    width = tok_ref.shape[1] // QUARTERS
    copies = copies_of(experts)
    loads = [
        pltpu.make_async_copy(source, place, sems.at[n])
        for n, (source, place) in enumerate(
            (
                (plan_hbm, plan_ref),
                (ids_hbm, ids_ref),
                (pick_hbm, pick_ref),
                (gate_hbm, gate_ref),
                (tok_hbm, tok_ref),
                (cot_hbm, cot_ref),
            )
        )
    ]
    for load in loads:
        load.start()
    before = mask(iota((tokens, tokens), 0) < iota((tokens, tokens), 1))
    expert_row = partners(experts, tokens)
    for load in loads[:4]:
        load.wait()
    ids = ids_ref[...]
    pick = pick_ref[...]
    gate = gate_ref[...].astype(F32)
    named = jnp.zeros((experts, tokens), jnp.int32)
    gates = jnp.zeros((experts, tokens), F32)
    for k in range(topk):
        hit = ids[k : k + 1] == expert_row
        named = jnp.where(hit, pick[k : k + 1] + 1, named)
        gates = jnp.where(hit, gate[k : k + 1], gates)
    hot = jnp.zeros((experts, tokens), jnp.int32)
    for j in range(experts):
        hot = jnp.where(expert_row == plan_ref[j], 1, hot)
    chosen = jnp.where(named == 0, -1, jnp.where(hot > 0, named - 1, 0))
    masks = jnp.concatenate([(chosen == c).astype(F32) for c in range(copies + 1)], axis=0)
    rank = jnp.dot(masks.astype(BF), before, preferred_element_type=F32).astype(jnp.int32)
    slot = jnp.full((experts, tokens), -1, jnp.int32)
    for c in range(copies + 1):
        rank_c = rank[c * experts : (c + 1) * experts]
        keep = jnp.logical_and(chosen == c, rank_c < CAP)
        slot = jnp.where(keep, c * CAP + rank_c, slot)
    slot_ref[...] = slot
    gates_ref[...] = gates
    slot16 = repeat_rows(slot, MAIN)
    gate16 = repeat_rows(gates, MAIN)
    inner = jnp.bitwise_and(iota(slot16.shape, 0), MAIN - 1)
    onehot = (slot16 == inner).astype(F32)
    wanted = MAIN + jnp.bitwise_and(jnp.right_shift(inner, 2), 1)
    last = (slot16 == wanted).astype(F32)
    last_rows = jnp.where(inner >= 8, 0.0, last)
    last_scaled = jnp.where(inner >= 8, last * gate16, 0.0)
    quarter = jnp.bitwise_and(inner, 3)
    for load in loads[4:]:
        load.wait()
    rows = jnp.dot(onehot.astype(BF), tok_ref[...], preferred_element_type=F32).astype(BF)
    scaled = jnp.dot(
        (onehot * gate16).astype(BF), cot_ref[...], preferred_element_type=F32
    ).astype(BF)
    tail = jnp.zeros((experts * MAIN, width), F32)
    for q in range(QUARTERS):
        cols = slice(q * width, (q + 1) * width)
        mine = quarter == q
        tail += jnp.dot(
            jnp.where(mine, last_rows, 0.0).astype(BF), tok_ref[:, cols], preferred_element_type=F32
        )
        tail += jnp.dot(
            jnp.where(mine, last_scaled, 0.0).astype(BF),
            cot_ref[:, cols],
            preferred_element_type=F32,
        )
    tail = tail.astype(BF)
    for c, ref in enumerate(send_refs):
        here = slice(c * MAIN, (c + 1) * MAIN)
        for q in range(QUARTERS):
            cols = slice(q * width, (q + 1) * width)
            ref[q * MAIN : (q + 1) * MAIN, :] = rows[here, cols]
            ref[(QUARTERS + q) * MAIN : (QUARTERS + q + 1) * MAIN, :] = scaled[here, cols]
        ref[2 * QUARTERS * MAIN :, :] = tail[here]


def expert_kernel(*refs):
    experts = len(ORDER)
    recv_refs = [refs[ORDER.index(c)] for c in range(experts)]
    gate_ref, up_ref, down_ref = refs[experts : experts + 3]
    back_views = chunk_views(refs[experts + 3 : -5], BACK_ROWS)
    x_ref, s_ref, dg_ref, du_ref, hid_ref = refs[-5:]
    width = refs[0].shape[1]
    main_rows = experts * MAIN
    tail = jnp.concatenate([ref[2 * QUARTERS * MAIN :, :] for ref in recv_refs], axis=0)
    row = iota((4 * experts, main_rows), 0)
    col = iota((4 * experts, main_rows), 1)
    kind = (row >= 2 * experts).astype(jnp.int32)
    chunk = jnp.right_shift(row - kind * 2 * experts, 1)
    base = chunk * MAIN + kind * 8 + jnp.bitwise_and(row, 1) * 4
    for q in range(QUARTERS):
        cols = slice(q * width, (q + 1) * width)
        picked = jnp.dot(mask(col == base + q), tail, preferred_element_type=F32).astype(BF)
        x_ref[main_rows:, cols] = picked[: 2 * experts]
        s_ref[main_rows:, cols] = picked[2 * experts :]
        for i, ref in enumerate(recv_refs):
            here = slice(i * MAIN, (i + 1) * MAIN)
            x_ref[here, cols] = ref[q * MAIN : (q + 1) * MAIN, :]
            s_ref[here, cols] = ref[(QUARTERS + q) * MAIN : (QUARTERS + q + 1) * MAIN, :]
    rows = x_ref[...]
    gate_pre = jnp.dot(rows, gate_ref[...], preferred_element_type=F32)
    up_pre = jnp.dot(rows, up_ref[...], preferred_element_type=F32)
    hidden_grad = jnp.dot(s_ref[...], down_ref[...], preferred_element_type=F32)
    sig = jax.nn.sigmoid(gate_pre)
    activated = gate_pre * sig
    hidden = (activated * up_pre).astype(BF)
    slope = sig * (1.0 + gate_pre * (1.0 - sig))
    gate_delta = (hidden_grad * up_pre * slope).astype(BF)
    up_delta = (hidden_grad * activated).astype(BF)
    hid_ref[...] = hidden
    dg_ref[...] = gate_delta
    du_ref[...] = up_delta
    grad = (
        lax.dot_general(gate_delta, gate_ref[...], CONTRACT_COLS, preferred_element_type=F32)
        + lax.dot_general(up_delta, up_ref[...], CONTRACT_COLS, preferred_element_type=F32)
    ).astype(BF)
    product = hidden.astype(F32) * hidden_grad
    product = jnp.concatenate(
        [product, jnp.zeros((width - product.shape[0], product.shape[1]), F32)], axis=0
    )
    high = product.astype(BF)
    low = (product - high.astype(F32)).astype(BF)
    ones = jnp.ones((8, product.shape[1]), BF)
    gate_lanes = lax.dot_general(
        ones, high, CONTRACT_COLS, preferred_element_type=F32
    ) + lax.dot_general(ones, low, CONTRACT_COLS, preferred_element_type=F32)
    trow = iota((main_rows, 2 * experts), 0)
    tcol = iota((main_rows, 2 * experts), 1)
    inner = jnp.bitwise_and(trow, MAIN - 1)
    source = jnp.right_shift(trow, 4) * 2 + jnp.right_shift(inner, 2)
    spread = jnp.zeros((main_rows, width), F32)
    for q in range(QUARTERS):
        cols = slice(q * width, (q + 1) * width)
        mine = jnp.logical_and(jnp.bitwise_and(inner, 3) == q, inner < 8)
        place = mask(jnp.logical_and(mine, tcol == source))
        spread += jnp.dot(place, grad[main_rows:, cols], preferred_element_type=F32)
        for i, (ref, first) in enumerate(back_views):
            low = first + q * MAIN
            ref[low : low + MAIN, :] = grad[i * MAIN : (i + 1) * MAIN, cols]
    for i, (ref, first) in enumerate(back_views):
        low = first + QUARTERS * MAIN
        ref[low : low + 16, :] = jnp.concatenate(
            [spread[i * MAIN : i * MAIN + 8], gate_lanes], axis=0
        ).astype(BF)


def grads_of(half, x_ref, s_ref, dg_ref, du_ref, hid_ref):
    rows = x_ref.shape[1] // 2
    cols = pl.ds(pl.multiple_of(half * rows, rows), rows)
    x_half = x_ref[:, cols]
    s_half = s_ref[:, cols]
    return (
        lax.dot_general(x_half, dg_ref[...], CONTRACT_ROWS, preferred_element_type=F32),
        lax.dot_general(x_half, du_ref[...], CONTRACT_ROWS, preferred_element_type=F32),
        lax.dot_general(s_half, hid_ref[...], CONTRACT_ROWS, preferred_element_type=F32),
    )


def other_half_kernel(x_ref, s_ref, dg_ref, du_ref, hid_ref, out_ref):
    half = 1 - lax.axis_index("replica")
    parts = grads_of(half, x_ref, s_ref, dg_ref, du_ref, hid_ref)
    rows = parts[0].shape[0]
    for n in range(3):
        out_ref[n * rows : (n + 1) * rows, :] = parts[n].astype(BF)


def own_half_kernel(
    x_ref, s_ref, dg_ref, du_ref, hid_ref, came_ref, gate_ref, up_ref, down_ref
):
    parts = grads_of(lax.axis_index("replica"), x_ref, s_ref, dg_ref, du_ref, hid_ref)
    rows = parts[0].shape[0]
    for n, out_ref in enumerate((gate_ref, up_ref, down_ref)):
        came = came_ref[n * rows : (n + 1) * rows, :].astype(F32)
        out_ref[...] = (parts[n].astype(BF).astype(F32) + came).astype(BF)


def combine_chunks(chunks, views, ids_ref, slot_ref, gates_ref):
    topk, tokens = ids_ref.shape
    experts = slot_ref.shape[0]
    width = views[0][0].shape[1]
    slot = jnp.concatenate([slot_ref[c : c + 1] for c in chunks], axis=0)
    slot16 = repeat_rows(slot, MAIN)
    inner = jnp.bitwise_and(iota(slot16.shape, 0), MAIN - 1)
    onehot = mask(slot16 == inner)
    wanted = MAIN + jnp.right_shift(inner, 2)
    last = jnp.where(jnp.logical_and(slot16 == wanted, inner < 8), 1.0, 0.0)
    quarter = jnp.bitwise_and(inner, 3)
    tails = [ref[first + BACK_ROWS - 16 : first + BACK_ROWS, :] for ref, first in views]
    tail = jnp.concatenate(tails, axis=0)
    totals = []
    for q in range(QUARTERS):
        main = jnp.concatenate(
            [ref[first + q * MAIN : first + (q + 1) * MAIN, :] for ref, first in views], axis=0
        )
        place = jnp.where(quarter == q, last, 0.0).astype(BF)
        total = lax.dot_general(onehot, main, CONTRACT_ROWS, preferred_element_type=F32)
        total += lax.dot_general(place, tail, CONTRACT_ROWS, preferred_element_type=F32)
        totals.append(total)
    lane_index = iota((width, tokens), 0)
    expert_row = partners(experts, tokens)
    by_choice = jnp.zeros((topk, tokens), F32)
    for place, c in enumerate(chunks):
        mine = slot[place : place + 1]
        lane = jnp.where(mine < MAIN, c * MAIN + mine, experts * MAIN + 2 * c + mine - MAIN)
        lane = jnp.where(mine < 0, -1, lane)
        sums = jnp.dot(tails[place], mask(lane_index == lane), preferred_element_type=F32)
        kept = mine >= 0
        grad = jnp.where(kept, sums[8:9] / jnp.where(kept, gates_ref[c : c + 1], 1.0), 0.0)
        by_choice += jnp.where(ids_ref[...] == expert_row[c : c + 1], grad, 0.0)
    return totals, by_choice


LAST = 3


def combine_kernel(ids_ref, slot_ref, gates_ref, *refs):
    token_ref, grad_ref = refs[-2:]
    singles = [(refs[0], 0), (refs[1], 0)]
    kept_refs = refs[2 : 2 + len(BASES)]
    given_refs = refs[2 + len(BASES) : -2]
    views = dict(enumerate(singles))
    for d, ref in enumerate(kept_refs):
        views[2 + 2 * d] = (ref, 0)
    for d, ref in enumerate(given_refs):
        views[LAST + 2 + 2 * d] = (ref, BACK_ROWS)
    chunks = sorted(views)
    totals, by_choice = combine_chunks(
        chunks, [views[c] for c in chunks], ids_ref, slot_ref, gates_ref
    )
    width = totals[0].shape[1]
    for q, total in enumerate(totals):
        token_ref[:, q * width : (q + 1) * width] = total
    grad_ref[...] = by_choice


def combine_last_kernel(
    ids_ref, slot_ref, gates_ref, given_ref, token_sum_ref, grad_sum_ref, token_ref, grad_ref
):
    totals, by_choice = combine_chunks(
        [LAST], [(given_ref, BACK_ROWS)], ids_ref, slot_ref, gates_ref
    )
    width = totals[0].shape[1]
    for q, total in enumerate(totals):
        cols = slice(q * width, (q + 1) * width)
        token_ref[:, cols] = (token_sum_ref[:, cols] + total).astype(BF)
    grad_ref[...] = (grad_sum_ref[...] + by_choice).astype(BF)


def local_call(kernel, outs, arrays, name, flops, moved, space=pltpu.VMEM, scratch=(), limit=16):
    vmem = pl.BlockSpec(memory_space=pltpu.VMEM)
    return pl.pallas_call(
        kernel,
        out_shape=[jax.ShapeDtypeStruct(shape, kind) for shape, kind in outs],
        in_specs=[pl.BlockSpec(memory_space=space)] * len(arrays),
        out_specs=[vmem] * len(outs),
        scratch_shapes=list(scratch),
        compiler_params=pltpu.CompilerParams(vmem_limit_bytes=limit * MIB),
        cost_estimate=pl.CostEstimate(flops=flops, bytes_accessed=moved, transcendentals=0),
        name=name,
    )(*arrays)


def to_step(chunk, base):
    experts = lax.axis_size("expert")
    if base == 1:
        return lax.ppermute(chunk, "expert", [(i, i ^ 1) for i in range(experts)])
    pairs = [(2 * i + r, 2 * (i ^ (base + r)) + r) for i in range(experts) for r in range(2)]
    return lax.ppermute(chunk, ("expert", "replica"), pairs)


def to_twin(chunk):
    return lax.ppermute(chunk, "replica", [(0, 1), (1, 0)])


def hold_kernel(source_ref, place_ref):
    place_ref[...] = source_ref[...]


def per_device_moving_rows(
    tokens,
    cotangent,
    expert_ids,
    gate_values,
    replica_pick,
    replica_plan,
    gate_proj,
    up_proj,
    down_proj,
):
    experts = lax.axis_size("expert")
    token_count, model_width = tokens.shape
    topk = expert_ids.shape[1]
    hidden_width = gate_proj.shape[2]
    width = model_width // QUARTERS
    served = experts * (MAIN + 2)
    small = (topk, token_count)
    count = len(BASES)
    *chunks, slot, gates = local_call(
        route_kernel,
        [((SEND_ROWS, width), BF)] * experts
        + [((experts, token_count), jnp.int32), ((experts, token_count), F32)],
        [replica_plan, expert_ids.T, replica_pick.T, gate_values.T, tokens, cotangent],
        "route",
        LONG,
        2 * 2 * (token_count + served) * model_width,
        space=pltpu.HBM,
        limit=54,
        scratch=[
            pltpu.SMEM((experts,), jnp.int32),
            pltpu.VMEM(small, jnp.int32),
            pltpu.VMEM(small, jnp.int32),
            pltpu.VMEM(small, BF),
            pltpu.VMEM(tokens.shape, BF),
            pltpu.VMEM(tokens.shape, BF),
            pltpu.SemaphoreType.DMA((6,)),
        ],
    )
    recv = list(chunks)
    recv[1] = to_step(chunks[1], 1)
    twin = [to_twin(chunks[c]) for c in (3, 5, 7)]
    twin, mine = lax.optimization_barrier((twin, chunks[4]))
    for d, base in enumerate(BASES):
        recv[2 + 2 * d] = to_step(mine if base == 6 else chunks[2 + 2 * d], base)
        recv[3 + 2 * d] = to_step(twin[d], base)
    (held,) = local_call(hold_kernel, [(recv[0].shape, BF)], [recv[0]], "hold", 1, 1)
    matmul = 2 * served * model_width * hidden_width
    outs = local_call(
        expert_kernel,
        [((BACK_ROWS, width), BF)] * 2
        + [((2 * BACK_ROWS, width), BF)] * count
        + [((served, model_width), BF)] * 2
        + [((served, hidden_width), BF)] * 3,
        [held, *(recv[c] for c in ORDER[1:]), gate_proj[0], up_proj[0], down_proj[0]],
        "expert_rows",
        5 * matmul,
        2 * 3 * model_width * hidden_width,
    )
    backs, factors = outs[: 2 + count], outs[2 + count :]
    kept = list(map(to_step, backs[2:], BASES))
    near = to_step(backs[1], 1)
    half = model_width // 2
    (leaving,) = local_call(
        other_half_kernel,
        [((3 * half, hidden_width), BF)],
        factors,
        "other_half",
        1,
        1,
    )
    shares = local_call(
        own_half_kernel,
        [((half, hidden_width), BF)] * 3,
        [*factors, to_twin(leaving)],
        "own_half",
        1,
        1,
    )
    kept[0], near, shares = lax.optimization_barrier((kept[0], near, shares))
    routes = [expert_ids.T, slot, gates]
    sums = local_call(
        combine_kernel,
        [((token_count, model_width), F32), ((topk, token_count), F32)],
        [*routes, backs[0], near, *kept, *map(to_twin, kept[1:])],
        "combine",
        1,
        1,
    )
    token_grad, gate_grad = local_call(
        combine_last_kernel,
        [((token_count, model_width), BF), ((topk, token_count), BF)],
        [*routes, to_twin(kept[0]), *sums],
        "combine_last",
        1,
        1,
    )
    return (token_grad, gate_grad.T, shares[0][None], shares[1][None], shares[2][None])


def per_device(tokens, cotangent, expert_ids, gate_values, replica_pick, replica_plan, *matrices):
    experts = lax.axis_size("expert")
    slots = (copies_of(experts) + 1) * CAP
    row_bytes = 3 * 2 * tokens.shape[1] * experts
    matrix_bytes = 4 * sum(2 * m[0].size for m in matrices)
    fits = slots == MAIN + 2 and experts == 8 and lax.axis_size("replica") == 2
    rows_cheaper = slots * row_bytes < 2 * CAP * row_bytes + matrix_bytes
    plan = per_device_moving_rows if fits and rows_cheaper else per_device_moving_weights
    return plan(
        tokens, cotangent, expert_ids, gate_values, replica_pick, replica_plan, *matrices
    )


def solution(mesh):
    placed = (
        P(("parts", "expert", "replica"), None),
        P(("parts", "expert", "replica"), None),
        P(("parts", "expert", "replica"), None),
        P(("parts", "expert", "replica"), None),
        P(("parts", "expert", "replica"), None),
        P("parts"),
        P("expert", None, None),
        P("expert", None, None),
        P("expert", None, None),
    )
    return jax.shard_map(
        per_device,
        mesh=mesh,
        in_specs=placed,
        out_specs=(
            P(("parts", "expert", "replica"), None),
            P(("parts", "expert", "replica"), None),
            P(("parts", "expert"), "replica", None),
            P(("parts", "expert"), "replica", None),
            P(("parts", "expert"), "replica", None),
        ),
        check_vma=False,
    )
```

```python
import jax
import jax.numpy as jnp
from jax import lax
from jax.experimental import pallas as pl
from jax.experimental.pallas import tpu as pltpu
from jax.sharding import PartitionSpec as P

CAP = 6


def route_assignments(flat_ids, flat_pick, replica_plan, capacity):
    experts = replica_plan.shape[0]
    lane_ids = jnp.arange(experts, dtype=jnp.int32)
    same_plan = replica_plan[:, None] == replica_plan[None, :]
    earlier = lane_ids[None, :] < lane_ids[:, None]
    position = jnp.sum(jnp.logical_and(same_plan, earlier), axis=1)
    hot_mask = jnp.any(replica_plan[None, :] == lane_ids[:, None], axis=1)
    is_hot = jnp.any(
        jnp.logical_and(flat_ids[:, None] == lane_ids[None, :], hot_mask[None, :]), axis=1
    )
    use_copy = jnp.logical_and(is_hot, flat_pick >= 1)
    matches = jnp.logical_and(
        replica_plan[None, :] == flat_ids[:, None], position[None, :] == flat_pick[:, None] - 1
    )
    holder = jnp.sum(jnp.where(matches, lane_ids[None, :], 0), axis=1)
    target = jnp.where(use_copy, holder, flat_ids)
    copy_role = use_copy.astype(jnp.int32)
    bucket = target * 2 + copy_role
    sequence = jnp.arange(bucket.shape[0], dtype=jnp.int32)
    arrival = jnp.sum(
        jnp.logical_and(bucket[None, :] == bucket[:, None], sequence[None, :] < sequence[:, None]),
        axis=1,
    )
    kept_mask = arrival < capacity
    slot_index = target * (2 * capacity) + copy_role * capacity + jnp.minimum(arrival, capacity - 1)
    return (slot_index, kept_mask)


def fill_slots(slot_index, kept_mask, slot_count):
    slot_ids = jnp.arange(slot_count, dtype=jnp.int32)
    matches = jnp.logical_and(slot_index[None, :] == slot_ids[:, None], kept_mask[None, :])
    sequence = jnp.arange(slot_index.shape[0], dtype=jnp.int32)
    source = jnp.sum(jnp.where(matches, sequence[None, :], 0), axis=1)
    filled = jnp.any(matches, axis=1)
    return (source, filled)


def expert_backward(row_block, upstream, weight, gate_w, up_w, down_w):
    contract_cols = (((1,), (1,)), ((), ()))
    contract_rows = (((0,), (0,)), ((), ()))
    gate_pre = jnp.dot(row_block, gate_w, preferred_element_type=jnp.float32)
    up_pre = jnp.dot(row_block, up_w, preferred_element_type=jnp.float32)
    sigmoid_gate = jax.nn.sigmoid(gate_pre)
    activated = gate_pre * sigmoid_gate
    hidden = (activated * up_pre).astype(jnp.bfloat16)
    output_rows = lax.dot_general(hidden, down_w, contract_cols, preferred_element_type=jnp.float32)
    weight_col = weight.astype(jnp.float32)[:, None]
    upstream_f = upstream.astype(jnp.float32)
    gate_rows = jnp.sum(upstream_f * output_rows, axis=1)
    hidden_grad = weight_col * jnp.dot(upstream, down_w, preferred_element_type=jnp.float32)
    slope = sigmoid_gate * (1.0 + gate_pre * (1.0 - sigmoid_gate))
    gate_delta = (hidden_grad * up_pre * slope).astype(jnp.bfloat16)
    up_delta = (hidden_grad * activated).astype(jnp.bfloat16)
    input_grad = (
        lax.dot_general(gate_delta, gate_w, contract_cols, preferred_element_type=jnp.float32)
        + lax.dot_general(up_delta, up_w, contract_cols, preferred_element_type=jnp.float32)
    ).astype(jnp.bfloat16)
    scaled = (weight_col * upstream_f).astype(jnp.bfloat16)
    grad_set = (
        lax.dot_general(row_block, gate_delta, contract_rows, preferred_element_type=jnp.float32),
        lax.dot_general(row_block, up_delta, contract_rows, preferred_element_type=jnp.float32),
        lax.dot_general(scaled, hidden, contract_rows, preferred_element_type=jnp.float32),
    )
    return (input_grad, gate_rows, grad_set)


def per_device_moving_weights(
    tokens,
    cotangent,
    expert_ids,
    gate_values,
    replica_pick,
    replica_plan,
    gate_proj,
    up_proj,
    down_proj,
):
    experts = lax.axis_size("expert")
    capacity = CAP
    slot_total = 2 * capacity
    model_width = tokens.shape[1]
    topk = expert_ids.shape[1]
    token_count = tokens.shape[0]
    slot_index, kept_mask = route_assignments(
        expert_ids.reshape(-1), replica_pick.reshape(-1), replica_plan, capacity
    )
    source, filled = fill_slots(slot_index, kept_mask, experts * slot_total)
    token_of = source // topk
    zero_half = jnp.zeros((), jnp.bfloat16)
    send_rows = jnp.where(filled[:, None], jnp.take(tokens, token_of, axis=0), zero_half).reshape(
        experts, slot_total, model_width
    )
    send_upstream = jnp.where(
        filled[:, None], jnp.take(cotangent, token_of, axis=0), zero_half
    ).reshape(experts, slot_total, model_width)
    send_weight = jnp.where(filled, gate_values.reshape(-1)[source], zero_half).reshape(
        experts, slot_total
    )
    arrived = lax.all_to_all(send_rows, "expert", split_axis=0, concat_axis=0, tiled=True)
    own_gate = gate_proj[0]
    own_up = up_proj[0]
    own_down = down_proj[0]
    hidden_width = own_gate.shape[1]
    spread = (
        lax.all_to_all(
            own_gate.reshape(experts, -1), "expert", split_axis=0, concat_axis=0, tiled=True
        ),
        lax.all_to_all(
            own_up.reshape(experts, -1), "expert", split_axis=0, concat_axis=0, tiled=True
        ),
        lax.all_to_all(
            own_down.reshape(experts, -1), "expert", split_axis=0, concat_axis=0, tiled=True
        ),
    )
    chosen_gate = jnp.take(spread[0], replica_plan, axis=0)
    chosen_up = jnp.take(spread[1], replica_plan, axis=0)
    chosen_down = jnp.take(spread[2], replica_plan, axis=0)
    collected = (
        lax.all_to_all(chosen_gate, "expert", split_axis=0, concat_axis=0, tiled=True),
        lax.all_to_all(chosen_up, "expert", split_axis=0, concat_axis=0, tiled=True),
        lax.all_to_all(chosen_down, "expert", split_axis=0, concat_axis=0, tiled=True),
    )
    copy_gate = collected[0].reshape(model_width, hidden_width)
    copy_up = collected[1].reshape(model_width, hidden_width)
    copy_down = collected[2].reshape(model_width, hidden_width)
    arrived_up, arrived_weight = (
        lax.all_to_all(send_upstream, "expert", split_axis=0, concat_axis=0, tiled=True),
        lax.all_to_all(send_weight, "expert", split_axis=0, concat_axis=0, tiled=True),
    )
    owned_dx, owned_gate_rows, owned_grads = expert_backward(
        arrived[:, :capacity].reshape(-1, model_width),
        arrived_up[:, :capacity].reshape(-1, model_width),
        arrived_weight[:, :capacity].reshape(-1),
        own_gate,
        own_up,
        own_down,
    )
    copied_dx, copied_gate_rows, copied_grads = expert_backward(
        arrived[:, capacity:].reshape(-1, model_width),
        arrived_up[:, capacity:].reshape(-1, model_width),
        arrived_weight[:, capacity:].reshape(-1),
        copy_gate,
        copy_up,
        copy_down,
    )
    back_rows = jnp.concatenate(
        [
            owned_dx.reshape(experts, capacity, model_width),
            copied_dx.reshape(experts, capacity, model_width),
        ],
        axis=1,
    )
    back_gate = jnp.concatenate(
        [owned_gate_rows.reshape(experts, capacity), copied_gate_rows.reshape(experts, capacity)],
        axis=1,
    ).astype(jnp.bfloat16)
    returned, returned_gate = (
        lax.all_to_all(back_rows, "expert", split_axis=0, concat_axis=0, tiled=True),
        lax.all_to_all(back_gate, "expert", split_axis=0, concat_axis=0, tiled=True),
    )
    copy_pieces = (
        copied_grads[0].astype(jnp.bfloat16).reshape(experts, -1),
        copied_grads[1].astype(jnp.bfloat16).reshape(experts, -1),
        copied_grads[2].astype(jnp.bfloat16).reshape(experts, -1),
    )
    grad_spread = (
        lax.all_to_all(copy_pieces[0], "expert", split_axis=0, concat_axis=0, tiled=True),
        lax.all_to_all(copy_pieces[1], "expert", split_axis=0, concat_axis=0, tiled=True),
        lax.all_to_all(copy_pieces[2], "expert", split_axis=0, concat_axis=0, tiled=True),
    )
    lane_ids = jnp.arange(experts, dtype=jnp.int32)
    owner_map = (replica_plan[None, :] == lane_ids[:, None]).astype(jnp.bfloat16)
    summed_gate = jnp.dot(owner_map, grad_spread[0], preferred_element_type=jnp.float32).astype(
        jnp.bfloat16
    )
    summed_up = jnp.dot(owner_map, grad_spread[1], preferred_element_type=jnp.float32).astype(
        jnp.bfloat16
    )
    summed_down = jnp.dot(owner_map, grad_spread[2], preferred_element_type=jnp.float32).astype(
        jnp.bfloat16
    )
    grad_back = (
        lax.all_to_all(summed_gate, "expert", split_axis=0, concat_axis=0, tiled=True),
        lax.all_to_all(summed_up, "expert", split_axis=0, concat_axis=0, tiled=True),
        lax.all_to_all(summed_down, "expert", split_axis=0, concat_axis=0, tiled=True),
    )
    total_gate = owned_grads[0] + grad_back[0].reshape(model_width, hidden_width).astype(
        jnp.float32
    )
    total_up = owned_grads[1] + grad_back[1].reshape(model_width, hidden_width).astype(jnp.float32)
    total_down = owned_grads[2] + grad_back[2].reshape(model_width, hidden_width).astype(
        jnp.float32
    )
    shares = (
        lax.psum_scatter(
            total_gate.astype(jnp.bfloat16), "replica", scatter_dimension=0, tiled=True
        ).astype(jnp.float32),
        lax.psum_scatter(
            total_up.astype(jnp.bfloat16), "replica", scatter_dimension=0, tiled=True
        ).astype(jnp.float32),
        lax.psum_scatter(
            total_down.astype(jnp.bfloat16), "replica", scatter_dimension=0, tiled=True
        ).astype(jnp.float32),
    )
    flat_back = returned.reshape(experts * slot_total, model_width)
    picked_rows = jnp.take(flat_back, slot_index, axis=0)
    picked_rows = jnp.where(kept_mask[:, None], picked_rows, zero_half).astype(jnp.float32)
    token_grad = jnp.sum(picked_rows.reshape(token_count, topk, model_width), axis=1).astype(
        jnp.bfloat16
    )
    gate_grad = jnp.where(kept_mask, returned_gate.reshape(-1)[slot_index], zero_half).reshape(
        token_count, topk
    )
    return (
        token_grad,
        gate_grad,
        shares[0].astype(jnp.bfloat16)[None],
        shares[1].astype(jnp.bfloat16)[None],
        shares[2].astype(jnp.bfloat16)[None],
    )


BF = jnp.bfloat16
F32 = jnp.float32
CONTRACT_ROWS = (((0,), (0,)), ((), ()))
CONTRACT_COLS = (((1,), (1,)), ((), ()))
MIB = 1024 * 1024

BASES = (4, 6, 2)
ORDER = (0, 2, 1, 4, 3, 6, 5, 7)
LONG = 8 * 10**9
MAIN = 16
QUARTERS = 4
SEND_ROWS = 2 * QUARTERS * MAIN + 16
BACK_ROWS = QUARTERS * MAIN + 16


def copies_of(experts):
    return 2 if experts <= 8 else 8


def iota(shape, axis):
    return lax.broadcasted_iota(jnp.int32, shape, axis)


def partners(experts, tokens):
    row = iota((experts, tokens), 0)
    step = jnp.bitwise_xor(jnp.bitwise_and(row, 1), lax.axis_index("replica"))
    for d, base in enumerate(BASES):
        step = jnp.where(jnp.right_shift(row, 1) == d + 1, step + base, step)
    step = jnp.where(row < 2, row, step)
    return jnp.bitwise_xor(step, lax.axis_index("expert"))


def chunk_views(refs, rows):
    return [(refs[0], 0), (refs[1], 0)] + [(ref, part * rows) for ref in refs[2:] for part in (0, 1)]


def mask(condition):
    return condition.astype(F32).astype(BF)


def repeat_rows(table, times):
    width = table.shape[1]
    return jnp.concatenate(
        [jnp.broadcast_to(table[e : e + 1], (times, width)) for e in range(table.shape[0])], axis=0
    )


def route_kernel(plan_hbm, ids_hbm, pick_hbm, gate_hbm, tok_hbm, cot_hbm, *refs):
    sems = refs[-1]
    plan_ref, ids_ref, pick_ref, gate_ref, tok_ref, cot_ref = refs[-7:-1]
    slot_ref, gates_ref = refs[-9:-7]
    send_refs = refs[:-9]
    topk, tokens = ids_ref.shape
    experts = len(send_refs)
    width = tok_ref.shape[1] // QUARTERS
    copies = copies_of(experts)
    loads = [
        pltpu.make_async_copy(source, place, sems.at[n])
        for n, (source, place) in enumerate(
            (
                (plan_hbm, plan_ref),
                (ids_hbm, ids_ref),
                (pick_hbm, pick_ref),
                (gate_hbm, gate_ref),
                (tok_hbm, tok_ref),
                (cot_hbm, cot_ref),
            )
        )
    ]
    for load in loads:
        load.start()
    before = mask(iota((tokens, tokens), 0) < iota((tokens, tokens), 1))
    expert_row = partners(experts, tokens)
    for load in loads[:4]:
        load.wait()
    ids = ids_ref[...]
    pick = pick_ref[...]
    gate = gate_ref[...].astype(F32)
    named = jnp.zeros((experts, tokens), jnp.int32)
    gates = jnp.zeros((experts, tokens), F32)
    for k in range(topk):
        hit = ids[k : k + 1] == expert_row
        named = jnp.where(hit, pick[k : k + 1] + 1, named)
        gates = jnp.where(hit, gate[k : k + 1], gates)
    hot = jnp.zeros((experts, tokens), jnp.int32)
    for j in range(experts):
        hot = jnp.where(expert_row == plan_ref[j], 1, hot)
    chosen = jnp.where(named == 0, -1, jnp.where(hot > 0, named - 1, 0))
    masks = jnp.concatenate([(chosen == c).astype(F32) for c in range(copies + 1)], axis=0)
    rank = jnp.dot(masks.astype(BF), before, preferred_element_type=F32).astype(jnp.int32)
    slot = jnp.full((experts, tokens), -1, jnp.int32)
    for c in range(copies + 1):
        rank_c = rank[c * experts : (c + 1) * experts]
        keep = jnp.logical_and(chosen == c, rank_c < CAP)
        slot = jnp.where(keep, c * CAP + rank_c, slot)
    slot_ref[...] = slot
    gates_ref[...] = gates
    slot16 = repeat_rows(slot, MAIN)
    gate16 = repeat_rows(gates, MAIN)
    inner = jnp.bitwise_and(iota(slot16.shape, 0), MAIN - 1)
    onehot = (slot16 == inner).astype(F32)
    wanted = MAIN + jnp.bitwise_and(jnp.right_shift(inner, 2), 1)
    last = (slot16 == wanted).astype(F32)
    last_rows = jnp.where(inner >= 8, 0.0, last)
    last_scaled = jnp.where(inner >= 8, last * gate16, 0.0)
    quarter = jnp.bitwise_and(inner, 3)
    for load in loads[4:]:
        load.wait()
    rows = jnp.dot(onehot.astype(BF), tok_ref[...], preferred_element_type=F32).astype(BF)
    scaled = jnp.dot(
        (onehot * gate16).astype(BF), cot_ref[...], preferred_element_type=F32
    ).astype(BF)
    tail = jnp.zeros((experts * MAIN, width), F32)
    for q in range(QUARTERS):
        cols = slice(q * width, (q + 1) * width)
        mine = quarter == q
        tail += jnp.dot(
            jnp.where(mine, last_rows, 0.0).astype(BF), tok_ref[:, cols], preferred_element_type=F32
        )
        tail += jnp.dot(
            jnp.where(mine, last_scaled, 0.0).astype(BF),
            cot_ref[:, cols],
            preferred_element_type=F32,
        )
    tail = tail.astype(BF)
    for c, ref in enumerate(send_refs):
        here = slice(c * MAIN, (c + 1) * MAIN)
        for q in range(QUARTERS):
            cols = slice(q * width, (q + 1) * width)
            ref[q * MAIN : (q + 1) * MAIN, :] = rows[here, cols]
            ref[(QUARTERS + q) * MAIN : (QUARTERS + q + 1) * MAIN, :] = scaled[here, cols]
        ref[2 * QUARTERS * MAIN :, :] = tail[here]


def expert_kernel(*refs):
    experts = len(ORDER)
    recv_refs = [refs[ORDER.index(c)] for c in range(experts)]
    gate_ref, up_ref, down_ref = refs[experts : experts + 3]
    back_views = chunk_views(refs[experts + 3 : -5], BACK_ROWS)
    x_ref, s_ref, dg_ref, du_ref, hid_ref = refs[-5:]
    width = refs[0].shape[1]
    main_rows = experts * MAIN
    tail = jnp.concatenate([ref[2 * QUARTERS * MAIN :, :] for ref in recv_refs], axis=0)
    row = iota((4 * experts, main_rows), 0)
    col = iota((4 * experts, main_rows), 1)
    kind = (row >= 2 * experts).astype(jnp.int32)
    chunk = jnp.right_shift(row - kind * 2 * experts, 1)
    base = chunk * MAIN + kind * 8 + jnp.bitwise_and(row, 1) * 4
    for q in range(QUARTERS):
        cols = slice(q * width, (q + 1) * width)
        picked = jnp.dot(mask(col == base + q), tail, preferred_element_type=F32).astype(BF)
        x_ref[main_rows:, cols] = picked[: 2 * experts]
        s_ref[main_rows:, cols] = picked[2 * experts :]
        for i, ref in enumerate(recv_refs):
            here = slice(i * MAIN, (i + 1) * MAIN)
            x_ref[here, cols] = ref[q * MAIN : (q + 1) * MAIN, :]
            s_ref[here, cols] = ref[(QUARTERS + q) * MAIN : (QUARTERS + q + 1) * MAIN, :]
    rows = x_ref[...]
    gate_pre = jnp.dot(rows, gate_ref[...], preferred_element_type=F32)
    up_pre = jnp.dot(rows, up_ref[...], preferred_element_type=F32)
    hidden_grad = jnp.dot(s_ref[...], down_ref[...], preferred_element_type=F32)
    sig = jax.nn.sigmoid(gate_pre)
    activated = gate_pre * sig
    hidden = (activated * up_pre).astype(BF)
    slope = sig * (1.0 + gate_pre * (1.0 - sig))
    gate_delta = (hidden_grad * up_pre * slope).astype(BF)
    up_delta = (hidden_grad * activated).astype(BF)
    hid_ref[...] = hidden
    dg_ref[...] = gate_delta
    du_ref[...] = up_delta
    grad = (
        lax.dot_general(gate_delta, gate_ref[...], CONTRACT_COLS, preferred_element_type=F32)
        + lax.dot_general(up_delta, up_ref[...], CONTRACT_COLS, preferred_element_type=F32)
    ).astype(BF)
    product = hidden.astype(F32) * hidden_grad
    product = jnp.concatenate(
        [product, jnp.zeros((width - product.shape[0], product.shape[1]), F32)], axis=0
    )
    high = product.astype(BF)
    low = (product - high.astype(F32)).astype(BF)
    ones = jnp.ones((8, product.shape[1]), BF)
    gate_lanes = lax.dot_general(
        ones, high, CONTRACT_COLS, preferred_element_type=F32
    ) + lax.dot_general(ones, low, CONTRACT_COLS, preferred_element_type=F32)
    trow = iota((main_rows, 2 * experts), 0)
    tcol = iota((main_rows, 2 * experts), 1)
    inner = jnp.bitwise_and(trow, MAIN - 1)
    source = jnp.right_shift(trow, 4) * 2 + jnp.right_shift(inner, 2)
    spread = jnp.zeros((main_rows, width), F32)
    for q in range(QUARTERS):
        cols = slice(q * width, (q + 1) * width)
        mine = jnp.logical_and(jnp.bitwise_and(inner, 3) == q, inner < 8)
        place = mask(jnp.logical_and(mine, tcol == source))
        spread += jnp.dot(place, grad[main_rows:, cols], preferred_element_type=F32)
        for i, (ref, first) in enumerate(back_views):
            low = first + q * MAIN
            ref[low : low + MAIN, :] = grad[i * MAIN : (i + 1) * MAIN, cols]
    for i, (ref, first) in enumerate(back_views):
        low = first + QUARTERS * MAIN
        ref[low : low + 16, :] = jnp.concatenate(
            [spread[i * MAIN : i * MAIN + 8], gate_lanes], axis=0
        ).astype(BF)


def grads_of(half, x_ref, s_ref, dg_ref, du_ref, hid_ref):
    rows = x_ref.shape[1] // 2
    cols = pl.ds(pl.multiple_of(half * rows, rows), rows)
    x_half = x_ref[:, cols]
    s_half = s_ref[:, cols]
    return (
        lax.dot_general(x_half, dg_ref[...], CONTRACT_ROWS, preferred_element_type=F32),
        lax.dot_general(x_half, du_ref[...], CONTRACT_ROWS, preferred_element_type=F32),
        lax.dot_general(s_half, hid_ref[...], CONTRACT_ROWS, preferred_element_type=F32),
    )


def other_half_kernel(x_ref, s_ref, dg_ref, du_ref, hid_ref, out_ref):
    half = 1 - lax.axis_index("replica")
    parts = grads_of(half, x_ref, s_ref, dg_ref, du_ref, hid_ref)
    rows = parts[0].shape[0]
    for n in range(3):
        out_ref[n * rows : (n + 1) * rows, :] = parts[n].astype(BF)


def own_half_kernel(
    x_ref, s_ref, dg_ref, du_ref, hid_ref, came_ref, gate_ref, up_ref, down_ref
):
    parts = grads_of(lax.axis_index("replica"), x_ref, s_ref, dg_ref, du_ref, hid_ref)
    rows = parts[0].shape[0]
    for n, out_ref in enumerate((gate_ref, up_ref, down_ref)):
        came = came_ref[n * rows : (n + 1) * rows, :].astype(F32)
        out_ref[...] = (parts[n].astype(BF).astype(F32) + came).astype(BF)


def combine_chunks(chunks, views, ids_ref, slot_ref, gates_ref):
    topk, tokens = ids_ref.shape
    experts = slot_ref.shape[0]
    width = views[0][0].shape[1]
    slot = jnp.concatenate([slot_ref[c : c + 1] for c in chunks], axis=0)
    slot16 = repeat_rows(slot, MAIN)
    inner = jnp.bitwise_and(iota(slot16.shape, 0), MAIN - 1)
    onehot = mask(slot16 == inner)
    wanted = MAIN + jnp.right_shift(inner, 2)
    last = jnp.where(jnp.logical_and(slot16 == wanted, inner < 8), 1.0, 0.0)
    quarter = jnp.bitwise_and(inner, 3)
    tails = [ref[first + BACK_ROWS - 16 : first + BACK_ROWS, :] for ref, first in views]
    tail = jnp.concatenate(tails, axis=0)
    totals = []
    for q in range(QUARTERS):
        main = jnp.concatenate(
            [ref[first + q * MAIN : first + (q + 1) * MAIN, :] for ref, first in views], axis=0
        )
        place = jnp.where(quarter == q, last, 0.0).astype(BF)
        total = lax.dot_general(onehot, main, CONTRACT_ROWS, preferred_element_type=F32)
        total += lax.dot_general(place, tail, CONTRACT_ROWS, preferred_element_type=F32)
        totals.append(total)
    lane_index = iota((width, tokens), 0)
    expert_row = partners(experts, tokens)
    by_choice = jnp.zeros((topk, tokens), F32)
    for place, c in enumerate(chunks):
        mine = slot[place : place + 1]
        lane = jnp.where(mine < MAIN, c * MAIN + mine, experts * MAIN + 2 * c + mine - MAIN)
        lane = jnp.where(mine < 0, -1, lane)
        sums = jnp.dot(tails[place], mask(lane_index == lane), preferred_element_type=F32)
        kept = mine >= 0
        grad = jnp.where(kept, sums[8:9] / jnp.where(kept, gates_ref[c : c + 1], 1.0), 0.0)
        by_choice += jnp.where(ids_ref[...] == expert_row[c : c + 1], grad, 0.0)
    return totals, by_choice


LAST = 3


def combine_kernel(ids_ref, slot_ref, gates_ref, *refs):
    token_ref, grad_ref = refs[-2:]
    singles = [(refs[0], 0), (refs[1], 0)]
    kept_refs = refs[2 : 2 + len(BASES)]
    given_refs = refs[2 + len(BASES) : -2]
    views = dict(enumerate(singles))
    for d, ref in enumerate(kept_refs):
        views[2 + 2 * d] = (ref, 0)
    for d, ref in enumerate(given_refs):
        views[LAST + 2 + 2 * d] = (ref, BACK_ROWS)
    chunks = sorted(views)
    totals, by_choice = combine_chunks(
        chunks, [views[c] for c in chunks], ids_ref, slot_ref, gates_ref
    )
    width = totals[0].shape[1]
    for q, total in enumerate(totals):
        token_ref[:, q * width : (q + 1) * width] = total
    grad_ref[...] = by_choice


def combine_last_kernel(
    ids_ref, slot_ref, gates_ref, given_ref, token_sum_ref, grad_sum_ref, token_ref, grad_ref
):
    totals, by_choice = combine_chunks(
        [LAST], [(given_ref, BACK_ROWS)], ids_ref, slot_ref, gates_ref
    )
    width = totals[0].shape[1]
    for q, total in enumerate(totals):
        cols = slice(q * width, (q + 1) * width)
        token_ref[:, cols] = (token_sum_ref[:, cols] + total).astype(BF)
    grad_ref[...] = (grad_sum_ref[...] + by_choice).astype(BF)


def local_call(kernel, outs, arrays, name, flops, moved, space=pltpu.VMEM, scratch=(), limit=16):
    vmem = pl.BlockSpec(memory_space=pltpu.VMEM)
    return pl.pallas_call(
        kernel,
        out_shape=[jax.ShapeDtypeStruct(shape, kind) for shape, kind in outs],
        in_specs=[pl.BlockSpec(memory_space=space)] * len(arrays),
        out_specs=[vmem] * len(outs),
        scratch_shapes=list(scratch),
        compiler_params=pltpu.CompilerParams(vmem_limit_bytes=limit * MIB),
        cost_estimate=pl.CostEstimate(flops=flops, bytes_accessed=moved, transcendentals=0),
        name=name,
    )(*arrays)


def to_step(chunk, base):
    experts = lax.axis_size("expert")
    if base == 1:
        return lax.ppermute(chunk, "expert", [(i, i ^ 1) for i in range(experts)])
    pairs = [(2 * i + r, 2 * (i ^ (base + r)) + r) for i in range(experts) for r in range(2)]
    return lax.ppermute(chunk, ("expert", "replica"), pairs)


def to_twin(chunk):
    return lax.ppermute(chunk, "replica", [(0, 1), (1, 0)])


def hold_kernel(source_ref, place_ref):
    place_ref[...] = source_ref[...]


def per_device_moving_rows(
    tokens,
    cotangent,
    expert_ids,
    gate_values,
    replica_pick,
    replica_plan,
    gate_proj,
    up_proj,
    down_proj,
):
    experts = lax.axis_size("expert")
    token_count, model_width = tokens.shape
    topk = expert_ids.shape[1]
    hidden_width = gate_proj.shape[2]
    width = model_width // QUARTERS
    served = experts * (MAIN + 2)
    small = (topk, token_count)
    count = len(BASES)
    *chunks, slot, gates = local_call(
        route_kernel,
        [((SEND_ROWS, width), BF)] * experts
        + [((experts, token_count), jnp.int32), ((experts, token_count), F32)],
        [replica_plan, expert_ids.T, replica_pick.T, gate_values.T, tokens, cotangent],
        "route",
        LONG,
        2 * 2 * (token_count + served) * model_width,
        space=pltpu.HBM,
        limit=54,
        scratch=[
            pltpu.SMEM((experts,), jnp.int32),
            pltpu.VMEM(small, jnp.int32),
            pltpu.VMEM(small, jnp.int32),
            pltpu.VMEM(small, BF),
            pltpu.VMEM(tokens.shape, BF),
            pltpu.VMEM(tokens.shape, BF),
            pltpu.SemaphoreType.DMA((6,)),
        ],
    )
    recv = list(chunks)
    recv[1] = to_step(chunks[1], 1)
    recv[2] = to_step(chunks[2], 4)
    twin = [to_twin(chunks[c]) for c in (3, 5, 7)]
    recv[1], twin, mine = lax.optimization_barrier((recv[1], twin, chunks[6]))
    recv[4] = to_step(chunks[4], 6)
    recv[6] = to_step(mine, 2)
    recv[3] = to_step(twin[0], 4)
    recv[5] = to_step(twin[1], 6)
    recv[7] = to_step(twin[2], 2)
    (held,) = local_call(hold_kernel, [(recv[0].shape, BF)], [recv[0]], "hold", 1, 1)
    matmul = 2 * served * model_width * hidden_width
    outs = local_call(
        expert_kernel,
        [((BACK_ROWS, width), BF)] * 2
        + [((2 * BACK_ROWS, width), BF)] * count
        + [((served, model_width), BF)] * 2
        + [((served, hidden_width), BF)] * 3,
        [held, *(recv[c] for c in ORDER[1:]), gate_proj[0], up_proj[0], down_proj[0]],
        "expert_rows",
        5 * matmul,
        2 * 3 * model_width * hidden_width,
    )
    backs, factors = outs[: 2 + count], outs[2 + count :]
    kept = list(map(to_step, backs[2:], BASES))
    near = to_step(backs[1], 1)
    half = model_width // 2
    (leaving,) = local_call(
        other_half_kernel,
        [((3 * half, hidden_width), BF)],
        factors,
        "other_half",
        1,
        1,
    )
    shares = local_call(
        own_half_kernel,
        [((half, hidden_width), BF)] * 3,
        [*factors, to_twin(leaving)],
        "own_half",
        1,
        1,
    )
    kept[0], near, shares = lax.optimization_barrier((kept[0], near, shares))
    routes = [expert_ids.T, slot, gates]
    sums = local_call(
        combine_kernel,
        [((token_count, model_width), F32), ((topk, token_count), F32)],
        [*routes, backs[0], near, *kept, *map(to_twin, kept[1:])],
        "combine",
        1,
        1,
    )
    token_grad, gate_grad = local_call(
        combine_last_kernel,
        [((token_count, model_width), BF), ((topk, token_count), BF)],
        [*routes, to_twin(kept[0]), *sums],
        "combine_last",
        1,
        1,
    )
    return (token_grad, gate_grad.T, shares[0][None], shares[1][None], shares[2][None])


def per_device(tokens, cotangent, expert_ids, gate_values, replica_pick, replica_plan, *matrices):
    experts = lax.axis_size("expert")
    slots = (copies_of(experts) + 1) * CAP
    row_bytes = 3 * 2 * tokens.shape[1] * experts
    matrix_bytes = 4 * sum(2 * m[0].size for m in matrices)
    fits = slots == MAIN + 2 and experts == 8 and lax.axis_size("replica") == 2
    rows_cheaper = slots * row_bytes < 2 * CAP * row_bytes + matrix_bytes
    plan = per_device_moving_rows if fits and rows_cheaper else per_device_moving_weights
    return plan(
        tokens, cotangent, expert_ids, gate_values, replica_pick, replica_plan, *matrices
    )


def solution(mesh):
    placed = (
        P(("parts", "expert", "replica"), None),
        P(("parts", "expert", "replica"), None),
        P(("parts", "expert", "replica"), None),
        P(("parts", "expert", "replica"), None),
        P(("parts", "expert", "replica"), None),
        P("parts"),
        P("expert", None, None),
        P("expert", None, None),
        P("expert", None, None),
    )
    return jax.shard_map(
        per_device,
        mesh=mesh,
        in_specs=placed,
        out_specs=(
            P(("parts", "expert", "replica"), None),
            P(("parts", "expert", "replica"), None),
            P(("parts", "expert"), "replica", None),
            P(("parts", "expert"), "replica", None),
            P(("parts", "expert"), "replica", None),
        ),
        check_vma=False,
    )
```

```python
import jax
import jax.numpy as jnp
from jax import lax
from jax.experimental import pallas as pl
from jax.experimental.pallas import tpu as pltpu
from jax.sharding import PartitionSpec as P

CAP = 6


def route_assignments(flat_ids, flat_pick, replica_plan, capacity):
    experts = replica_plan.shape[0]
    lane_ids = jnp.arange(experts, dtype=jnp.int32)
    same_plan = replica_plan[:, None] == replica_plan[None, :]
    earlier = lane_ids[None, :] < lane_ids[:, None]
    position = jnp.sum(jnp.logical_and(same_plan, earlier), axis=1)
    hot_mask = jnp.any(replica_plan[None, :] == lane_ids[:, None], axis=1)
    is_hot = jnp.any(
        jnp.logical_and(flat_ids[:, None] == lane_ids[None, :], hot_mask[None, :]), axis=1
    )
    use_copy = jnp.logical_and(is_hot, flat_pick >= 1)
    matches = jnp.logical_and(
        replica_plan[None, :] == flat_ids[:, None], position[None, :] == flat_pick[:, None] - 1
    )
    holder = jnp.sum(jnp.where(matches, lane_ids[None, :], 0), axis=1)
    target = jnp.where(use_copy, holder, flat_ids)
    copy_role = use_copy.astype(jnp.int32)
    bucket = target * 2 + copy_role
    sequence = jnp.arange(bucket.shape[0], dtype=jnp.int32)
    arrival = jnp.sum(
        jnp.logical_and(bucket[None, :] == bucket[:, None], sequence[None, :] < sequence[:, None]),
        axis=1,
    )
    kept_mask = arrival < capacity
    slot_index = target * (2 * capacity) + copy_role * capacity + jnp.minimum(arrival, capacity - 1)
    return (slot_index, kept_mask)


def fill_slots(slot_index, kept_mask, slot_count):
    slot_ids = jnp.arange(slot_count, dtype=jnp.int32)
    matches = jnp.logical_and(slot_index[None, :] == slot_ids[:, None], kept_mask[None, :])
    sequence = jnp.arange(slot_index.shape[0], dtype=jnp.int32)
    source = jnp.sum(jnp.where(matches, sequence[None, :], 0), axis=1)
    filled = jnp.any(matches, axis=1)
    return (source, filled)


def expert_backward(row_block, upstream, weight, gate_w, up_w, down_w):
    contract_cols = (((1,), (1,)), ((), ()))
    contract_rows = (((0,), (0,)), ((), ()))
    gate_pre = jnp.dot(row_block, gate_w, preferred_element_type=jnp.float32)
    up_pre = jnp.dot(row_block, up_w, preferred_element_type=jnp.float32)
    sigmoid_gate = jax.nn.sigmoid(gate_pre)
    activated = gate_pre * sigmoid_gate
    hidden = (activated * up_pre).astype(jnp.bfloat16)
    output_rows = lax.dot_general(hidden, down_w, contract_cols, preferred_element_type=jnp.float32)
    weight_col = weight.astype(jnp.float32)[:, None]
    upstream_f = upstream.astype(jnp.float32)
    gate_rows = jnp.sum(upstream_f * output_rows, axis=1)
    hidden_grad = weight_col * jnp.dot(upstream, down_w, preferred_element_type=jnp.float32)
    slope = sigmoid_gate * (1.0 + gate_pre * (1.0 - sigmoid_gate))
    gate_delta = (hidden_grad * up_pre * slope).astype(jnp.bfloat16)
    up_delta = (hidden_grad * activated).astype(jnp.bfloat16)
    input_grad = (
        lax.dot_general(gate_delta, gate_w, contract_cols, preferred_element_type=jnp.float32)
        + lax.dot_general(up_delta, up_w, contract_cols, preferred_element_type=jnp.float32)
    ).astype(jnp.bfloat16)
    scaled = (weight_col * upstream_f).astype(jnp.bfloat16)
    grad_set = (
        lax.dot_general(row_block, gate_delta, contract_rows, preferred_element_type=jnp.float32),
        lax.dot_general(row_block, up_delta, contract_rows, preferred_element_type=jnp.float32),
        lax.dot_general(scaled, hidden, contract_rows, preferred_element_type=jnp.float32),
    )
    return (input_grad, gate_rows, grad_set)


def per_device_moving_weights(
    tokens,
    cotangent,
    expert_ids,
    gate_values,
    replica_pick,
    replica_plan,
    gate_proj,
    up_proj,
    down_proj,
):
    experts = lax.axis_size("expert")
    capacity = CAP
    slot_total = 2 * capacity
    model_width = tokens.shape[1]
    topk = expert_ids.shape[1]
    token_count = tokens.shape[0]
    slot_index, kept_mask = route_assignments(
        expert_ids.reshape(-1), replica_pick.reshape(-1), replica_plan, capacity
    )
    source, filled = fill_slots(slot_index, kept_mask, experts * slot_total)
    token_of = source // topk
    zero_half = jnp.zeros((), jnp.bfloat16)
    send_rows = jnp.where(filled[:, None], jnp.take(tokens, token_of, axis=0), zero_half).reshape(
        experts, slot_total, model_width
    )
    send_upstream = jnp.where(
        filled[:, None], jnp.take(cotangent, token_of, axis=0), zero_half
    ).reshape(experts, slot_total, model_width)
    send_weight = jnp.where(filled, gate_values.reshape(-1)[source], zero_half).reshape(
        experts, slot_total
    )
    arrived = lax.all_to_all(send_rows, "expert", split_axis=0, concat_axis=0, tiled=True)
    own_gate = gate_proj[0]
    own_up = up_proj[0]
    own_down = down_proj[0]
    hidden_width = own_gate.shape[1]
    spread = (
        lax.all_to_all(
            own_gate.reshape(experts, -1), "expert", split_axis=0, concat_axis=0, tiled=True
        ),
        lax.all_to_all(
            own_up.reshape(experts, -1), "expert", split_axis=0, concat_axis=0, tiled=True
        ),
        lax.all_to_all(
            own_down.reshape(experts, -1), "expert", split_axis=0, concat_axis=0, tiled=True
        ),
    )
    chosen_gate = jnp.take(spread[0], replica_plan, axis=0)
    chosen_up = jnp.take(spread[1], replica_plan, axis=0)
    chosen_down = jnp.take(spread[2], replica_plan, axis=0)
    collected = (
        lax.all_to_all(chosen_gate, "expert", split_axis=0, concat_axis=0, tiled=True),
        lax.all_to_all(chosen_up, "expert", split_axis=0, concat_axis=0, tiled=True),
        lax.all_to_all(chosen_down, "expert", split_axis=0, concat_axis=0, tiled=True),
    )
    copy_gate = collected[0].reshape(model_width, hidden_width)
    copy_up = collected[1].reshape(model_width, hidden_width)
    copy_down = collected[2].reshape(model_width, hidden_width)
    arrived_up, arrived_weight = (
        lax.all_to_all(send_upstream, "expert", split_axis=0, concat_axis=0, tiled=True),
        lax.all_to_all(send_weight, "expert", split_axis=0, concat_axis=0, tiled=True),
    )
    owned_dx, owned_gate_rows, owned_grads = expert_backward(
        arrived[:, :capacity].reshape(-1, model_width),
        arrived_up[:, :capacity].reshape(-1, model_width),
        arrived_weight[:, :capacity].reshape(-1),
        own_gate,
        own_up,
        own_down,
    )
    copied_dx, copied_gate_rows, copied_grads = expert_backward(
        arrived[:, capacity:].reshape(-1, model_width),
        arrived_up[:, capacity:].reshape(-1, model_width),
        arrived_weight[:, capacity:].reshape(-1),
        copy_gate,
        copy_up,
        copy_down,
    )
    back_rows = jnp.concatenate(
        [
            owned_dx.reshape(experts, capacity, model_width),
            copied_dx.reshape(experts, capacity, model_width),
        ],
        axis=1,
    )
    back_gate = jnp.concatenate(
        [owned_gate_rows.reshape(experts, capacity), copied_gate_rows.reshape(experts, capacity)],
        axis=1,
    ).astype(jnp.bfloat16)
    returned, returned_gate = (
        lax.all_to_all(back_rows, "expert", split_axis=0, concat_axis=0, tiled=True),
        lax.all_to_all(back_gate, "expert", split_axis=0, concat_axis=0, tiled=True),
    )
    copy_pieces = (
        copied_grads[0].astype(jnp.bfloat16).reshape(experts, -1),
        copied_grads[1].astype(jnp.bfloat16).reshape(experts, -1),
        copied_grads[2].astype(jnp.bfloat16).reshape(experts, -1),
    )
    grad_spread = (
        lax.all_to_all(copy_pieces[0], "expert", split_axis=0, concat_axis=0, tiled=True),
        lax.all_to_all(copy_pieces[1], "expert", split_axis=0, concat_axis=0, tiled=True),
        lax.all_to_all(copy_pieces[2], "expert", split_axis=0, concat_axis=0, tiled=True),
    )
    lane_ids = jnp.arange(experts, dtype=jnp.int32)
    owner_map = (replica_plan[None, :] == lane_ids[:, None]).astype(jnp.bfloat16)
    summed_gate = jnp.dot(owner_map, grad_spread[0], preferred_element_type=jnp.float32).astype(
        jnp.bfloat16
    )
    summed_up = jnp.dot(owner_map, grad_spread[1], preferred_element_type=jnp.float32).astype(
        jnp.bfloat16
    )
    summed_down = jnp.dot(owner_map, grad_spread[2], preferred_element_type=jnp.float32).astype(
        jnp.bfloat16
    )
    grad_back = (
        lax.all_to_all(summed_gate, "expert", split_axis=0, concat_axis=0, tiled=True),
        lax.all_to_all(summed_up, "expert", split_axis=0, concat_axis=0, tiled=True),
        lax.all_to_all(summed_down, "expert", split_axis=0, concat_axis=0, tiled=True),
    )
    total_gate = owned_grads[0] + grad_back[0].reshape(model_width, hidden_width).astype(
        jnp.float32
    )
    total_up = owned_grads[1] + grad_back[1].reshape(model_width, hidden_width).astype(jnp.float32)
    total_down = owned_grads[2] + grad_back[2].reshape(model_width, hidden_width).astype(
        jnp.float32
    )
    shares = (
        lax.psum_scatter(
            total_gate.astype(jnp.bfloat16), "replica", scatter_dimension=0, tiled=True
        ).astype(jnp.float32),
        lax.psum_scatter(
            total_up.astype(jnp.bfloat16), "replica", scatter_dimension=0, tiled=True
        ).astype(jnp.float32),
        lax.psum_scatter(
            total_down.astype(jnp.bfloat16), "replica", scatter_dimension=0, tiled=True
        ).astype(jnp.float32),
    )
    flat_back = returned.reshape(experts * slot_total, model_width)
    picked_rows = jnp.take(flat_back, slot_index, axis=0)
    picked_rows = jnp.where(kept_mask[:, None], picked_rows, zero_half).astype(jnp.float32)
    token_grad = jnp.sum(picked_rows.reshape(token_count, topk, model_width), axis=1).astype(
        jnp.bfloat16
    )
    gate_grad = jnp.where(kept_mask, returned_gate.reshape(-1)[slot_index], zero_half).reshape(
        token_count, topk
    )
    return (
        token_grad,
        gate_grad,
        shares[0].astype(jnp.bfloat16)[None],
        shares[1].astype(jnp.bfloat16)[None],
        shares[2].astype(jnp.bfloat16)[None],
    )


BF = jnp.bfloat16
F32 = jnp.float32
CONTRACT_ROWS = (((0,), (0,)), ((), ()))
CONTRACT_COLS = (((1,), (1,)), ((), ()))
MIB = 1024 * 1024

BASES = (4, 6, 2)
ORDER = (0, 1, 2, 4, 6, 3, 7, 5)
LONG = 8 * 10**9
MAIN = 16
QUARTERS = 4
SEND_ROWS = 2 * QUARTERS * MAIN + 16
MAIN_ROWS = QUARTERS * MAIN
BACK_ROWS = MAIN_ROWS + 16
DOUBLE_ROWS = 2 * MAIN_ROWS + 24


def copies_of(experts):
    return 2 if experts <= 8 else 8


def iota(shape, axis):
    return lax.broadcasted_iota(jnp.int32, shape, axis)


def partners(experts, tokens):
    row = iota((experts, tokens), 0)
    step = jnp.bitwise_xor(jnp.bitwise_and(row, 1), lax.axis_index("replica"))
    for d, base in enumerate(BASES):
        step = jnp.where(jnp.right_shift(row, 1) == d + 1, step + base, step)
    step = jnp.where(row < 2, row, step)
    return jnp.bitwise_xor(step, lax.axis_index("expert"))


def mask(condition):
    return condition.astype(F32).astype(BF)


def repeat_rows(table, times):
    width = table.shape[1]
    return jnp.concatenate(
        [jnp.broadcast_to(table[e : e + 1], (times, width)) for e in range(table.shape[0])], axis=0
    )


def route_kernel(plan_hbm, ids_hbm, pick_hbm, gate_hbm, tok_hbm, cot_hbm, *refs):
    sems = refs[-1]
    plan_ref, ids_ref, pick_ref, gate_ref, tok_ref, cot_ref = refs[-7:-1]
    slot_ref, gates_ref = refs[-9:-7]
    send_refs = refs[:-9]
    topk, tokens = ids_ref.shape
    experts = len(send_refs)
    width = tok_ref.shape[1] // QUARTERS
    copies = copies_of(experts)
    loads = [
        pltpu.make_async_copy(source, place, sems.at[n])
        for n, (source, place) in enumerate(
            (
                (plan_hbm, plan_ref),
                (ids_hbm, ids_ref),
                (pick_hbm, pick_ref),
                (gate_hbm, gate_ref),
                (tok_hbm, tok_ref),
                (cot_hbm, cot_ref),
            )
        )
    ]
    for load in loads:
        load.start()
    before = mask(iota((tokens, tokens), 0) < iota((tokens, tokens), 1))
    expert_row = partners(experts, tokens)
    for load in loads[:4]:
        load.wait()
    ids = ids_ref[...]
    pick = pick_ref[...]
    gate = gate_ref[...].astype(F32)
    named = jnp.zeros((experts, tokens), jnp.int32)
    gates = jnp.zeros((experts, tokens), F32)
    for k in range(topk):
        hit = ids[k : k + 1] == expert_row
        named = jnp.where(hit, pick[k : k + 1] + 1, named)
        gates = jnp.where(hit, gate[k : k + 1], gates)
    hot = jnp.zeros((experts, tokens), jnp.int32)
    for j in range(experts):
        hot = jnp.where(expert_row == plan_ref[j], 1, hot)
    chosen = jnp.where(named == 0, -1, jnp.where(hot > 0, named - 1, 0))
    masks = jnp.concatenate([(chosen == c).astype(F32) for c in range(copies + 1)], axis=0)
    rank = jnp.dot(masks.astype(BF), before, preferred_element_type=F32).astype(jnp.int32)
    slot = jnp.full((experts, tokens), -1, jnp.int32)
    for c in range(copies + 1):
        rank_c = rank[c * experts : (c + 1) * experts]
        keep = jnp.logical_and(chosen == c, rank_c < CAP)
        slot = jnp.where(keep, c * CAP + rank_c, slot)
    slot_ref[...] = slot
    gates_ref[...] = gates
    slot16 = repeat_rows(slot, MAIN)
    gate16 = repeat_rows(gates, MAIN)
    inner = jnp.bitwise_and(iota(slot16.shape, 0), MAIN - 1)
    onehot = (slot16 == inner).astype(F32)
    wanted = MAIN + jnp.bitwise_and(jnp.right_shift(inner, 2), 1)
    last = (slot16 == wanted).astype(F32)
    last_rows = jnp.where(inner >= 8, 0.0, last)
    last_scaled = jnp.where(inner >= 8, last * gate16, 0.0)
    quarter = jnp.bitwise_and(inner, 3)
    for load in loads[4:]:
        load.wait()
    rows = jnp.dot(onehot.astype(BF), tok_ref[...], preferred_element_type=F32).astype(BF)
    scaled = jnp.dot(
        (onehot * gate16).astype(BF), cot_ref[...], preferred_element_type=F32
    ).astype(BF)
    tail = jnp.zeros((experts * MAIN, width), F32)
    for q in range(QUARTERS):
        cols = slice(q * width, (q + 1) * width)
        mine = quarter == q
        tail += jnp.dot(
            jnp.where(mine, last_rows, 0.0).astype(BF), tok_ref[:, cols], preferred_element_type=F32
        )
        tail += jnp.dot(
            jnp.where(mine, last_scaled, 0.0).astype(BF),
            cot_ref[:, cols],
            preferred_element_type=F32,
        )
    tail = tail.astype(BF)
    for c, ref in enumerate(send_refs):
        here = slice(c * MAIN, (c + 1) * MAIN)
        for q in range(QUARTERS):
            cols = slice(q * width, (q + 1) * width)
            ref[q * MAIN : (q + 1) * MAIN, :] = rows[here, cols]
            ref[(QUARTERS + q) * MAIN : (QUARTERS + q + 1) * MAIN, :] = scaled[here, cols]
        ref[2 * QUARTERS * MAIN :, :] = tail[here]


def expert_kernel(*refs):
    experts = len(ORDER)
    recv_refs = [refs[ORDER.index(c)] for c in range(experts)]
    gate_ref, up_ref, down_ref = refs[experts : experts + 3]
    back_refs = refs[experts + 3 : -5]
    x_ref, s_ref, dg_ref, du_ref, hid_ref = refs[-5:]
    width = refs[0].shape[1]
    main_rows = experts * MAIN
    tail = jnp.concatenate([ref[2 * QUARTERS * MAIN :, :] for ref in recv_refs], axis=0)
    row = iota((4 * experts, main_rows), 0)
    col = iota((4 * experts, main_rows), 1)
    kind = (row >= 2 * experts).astype(jnp.int32)
    chunk = jnp.right_shift(row - kind * 2 * experts, 1)
    base = chunk * MAIN + kind * 8 + jnp.bitwise_and(row, 1) * 4
    for q in range(QUARTERS):
        cols = slice(q * width, (q + 1) * width)
        picked = jnp.dot(mask(col == base + q), tail, preferred_element_type=F32).astype(BF)
        x_ref[main_rows:, cols] = picked[: 2 * experts]
        s_ref[main_rows:, cols] = picked[2 * experts :]
        for i, ref in enumerate(recv_refs):
            here = slice(i * MAIN, (i + 1) * MAIN)
            x_ref[here, cols] = ref[q * MAIN : (q + 1) * MAIN, :]
            s_ref[here, cols] = ref[(QUARTERS + q) * MAIN : (QUARTERS + q + 1) * MAIN, :]
    rows = x_ref[...]
    gate_pre = jnp.dot(rows, gate_ref[...], preferred_element_type=F32)
    up_pre = jnp.dot(rows, up_ref[...], preferred_element_type=F32)
    hidden_grad = jnp.dot(s_ref[...], down_ref[...], preferred_element_type=F32)
    sig = jax.nn.sigmoid(gate_pre)
    activated = gate_pre * sig
    hidden = (activated * up_pre).astype(BF)
    slope = sig * (1.0 + gate_pre * (1.0 - sig))
    gate_delta = (hidden_grad * up_pre * slope).astype(BF)
    up_delta = (hidden_grad * activated).astype(BF)
    hid_ref[...] = hidden
    dg_ref[...] = gate_delta
    du_ref[...] = up_delta
    grad = (
        lax.dot_general(gate_delta, gate_ref[...], CONTRACT_COLS, preferred_element_type=F32)
        + lax.dot_general(up_delta, up_ref[...], CONTRACT_COLS, preferred_element_type=F32)
    ).astype(BF)
    product = hidden.astype(F32) * hidden_grad
    product = jnp.concatenate(
        [product, jnp.zeros((width - product.shape[0], product.shape[1]), F32)], axis=0
    )
    high = product.astype(BF)
    low = (product - high.astype(F32)).astype(BF)
    ones = jnp.ones((8, product.shape[1]), BF)
    gate_lanes = lax.dot_general(
        ones, high, CONTRACT_COLS, preferred_element_type=F32
    ) + lax.dot_general(ones, low, CONTRACT_COLS, preferred_element_type=F32)
    trow = iota((main_rows, 2 * experts), 0)
    tcol = iota((main_rows, 2 * experts), 1)
    inner = jnp.bitwise_and(trow, MAIN - 1)
    source = jnp.right_shift(trow, 4) * 2 + jnp.right_shift(inner, 2)
    spread = jnp.zeros((main_rows, width), F32)
    for q in range(QUARTERS):
        cols = slice(q * width, (q + 1) * width)
        mine = jnp.logical_and(jnp.bitwise_and(inner, 3) == q, inner < 8)
        place = mask(jnp.logical_and(mine, tcol == source))
        spread += jnp.dot(place, grad[main_rows:, cols], preferred_element_type=F32)
        for i in range(experts):
            single = i < 2
            low = q * MAIN + (0 if single else (i % 2) * MAIN_ROWS)
            ref = back_refs[i if single else 1 + i // 2]
            ref[low : low + MAIN, :] = grad[i * MAIN : (i + 1) * MAIN, cols]
    for n, ref in enumerate(back_refs):
        if n < 2:
            ref[MAIN_ROWS:, :] = jnp.concatenate(
                [spread[n * MAIN : n * MAIN + 8], gate_lanes], axis=0
            ).astype(BF)
        else:
            i = 2 * n - 2
            both = [spread[c * MAIN : c * MAIN + 8] for c in (i, i + 1)]
            ref[2 * MAIN_ROWS : 2 * MAIN_ROWS + 16, :] = jnp.concatenate(both, axis=0).astype(BF)
            ref[2 * MAIN_ROWS + 16 :, :] = gate_lanes.astype(BF)


def grads_of(half, x_ref, s_ref, dg_ref, du_ref, hid_ref):
    rows = x_ref.shape[1] // 2
    cols = pl.ds(pl.multiple_of(half * rows, rows), rows)
    x_half = x_ref[:, cols]
    s_half = s_ref[:, cols]
    return (
        lax.dot_general(x_half, dg_ref[...], CONTRACT_ROWS, preferred_element_type=F32),
        lax.dot_general(x_half, du_ref[...], CONTRACT_ROWS, preferred_element_type=F32),
        lax.dot_general(s_half, hid_ref[...], CONTRACT_ROWS, preferred_element_type=F32),
    )


def other_half_kernel(x_ref, s_ref, dg_ref, du_ref, hid_ref, out_ref):
    half = 1 - lax.axis_index("replica")
    parts = grads_of(half, x_ref, s_ref, dg_ref, du_ref, hid_ref)
    rows = parts[0].shape[0]
    for n in range(3):
        out_ref[n * rows : (n + 1) * rows, :] = parts[n].astype(BF)


def own_half_kernel(
    x_ref, s_ref, dg_ref, du_ref, hid_ref, came_ref, gate_ref, up_ref, down_ref
):
    parts = grads_of(lax.axis_index("replica"), x_ref, s_ref, dg_ref, du_ref, hid_ref)
    rows = parts[0].shape[0]
    for n, out_ref in enumerate((gate_ref, up_ref, down_ref)):
        came = came_ref[n * rows : (n + 1) * rows, :].astype(F32)
        out_ref[...] = (parts[n].astype(BF).astype(F32) + came).astype(BF)


def tail_of(ref, part):
    if part is None:
        return ref[MAIN_ROWS:, :]
    both = ref[2 * MAIN_ROWS : 2 * MAIN_ROWS + 16, :].astype(F32)
    sums = ref[2 * MAIN_ROWS + 16 :, :].astype(F32)
    return jnp.concatenate([both[8 * part : 8 * part + 8], sums], axis=0).astype(BF)


def combine_chunks(chunks, views, ids_ref, slot_ref, gates_ref):
    topk, tokens = ids_ref.shape
    experts = slot_ref.shape[0]
    width = views[0][0].shape[1]
    slot = jnp.concatenate([slot_ref[c : c + 1] for c in chunks], axis=0)
    slot16 = repeat_rows(slot, MAIN)
    inner = jnp.bitwise_and(iota(slot16.shape, 0), MAIN - 1)
    onehot = mask(slot16 == inner)
    wanted = MAIN + jnp.right_shift(inner, 2)
    last = jnp.where(jnp.logical_and(slot16 == wanted, inner < 8), 1.0, 0.0)
    quarter = jnp.bitwise_and(inner, 3)
    tails = [tail_of(*view) for view in views]
    starts = [(ref, MAIN_ROWS if part else 0) for ref, part in views]
    tail = jnp.concatenate(tails, axis=0)
    totals = []
    for q in range(QUARTERS):
        main = jnp.concatenate(
            [ref[first + q * MAIN : first + (q + 1) * MAIN, :] for ref, first in starts], axis=0
        )
        place = jnp.where(quarter == q, last, 0.0).astype(BF)
        total = lax.dot_general(onehot, main, CONTRACT_ROWS, preferred_element_type=F32)
        total += lax.dot_general(place, tail, CONTRACT_ROWS, preferred_element_type=F32)
        totals.append(total)
    lane_index = iota((width, tokens), 0)
    expert_row = partners(experts, tokens)
    by_choice = jnp.zeros((topk, tokens), F32)
    for place, c in enumerate(chunks):
        mine = slot[place : place + 1]
        lane = jnp.where(mine < MAIN, c * MAIN + mine, experts * MAIN + 2 * c + mine - MAIN)
        lane = jnp.where(mine < 0, -1, lane)
        sums = jnp.dot(tails[place], mask(lane_index == lane), preferred_element_type=F32)
        kept = mine >= 0
        grad = jnp.where(kept, sums[8:9] / jnp.where(kept, gates_ref[c : c + 1], 1.0), 0.0)
        by_choice += jnp.where(ids_ref[...] == expert_row[c : c + 1], grad, 0.0)
    return totals, by_choice


LAST = 3


def combine_kernel(ids_ref, slot_ref, gates_ref, *refs):
    token_ref, grad_ref = refs[-2:]
    singles = [(refs[0], None), (refs[1], None)]
    kept_refs = refs[2 : 2 + len(BASES)]
    given_refs = refs[2 + len(BASES) : -2]
    views = dict(enumerate(singles))
    for d, ref in enumerate(kept_refs):
        views[2 + 2 * d] = (ref, 0)
    for d, ref in enumerate(given_refs):
        views[LAST + 2 + 2 * d] = (ref, 1)
    chunks = sorted(views)
    totals, by_choice = combine_chunks(
        chunks, [views[c] for c in chunks], ids_ref, slot_ref, gates_ref
    )
    width = totals[0].shape[1]
    for q, total in enumerate(totals):
        token_ref[:, q * width : (q + 1) * width] = total
    grad_ref[...] = by_choice


def combine_last_kernel(
    ids_ref,
    slot_ref,
    gates_ref,
    given_ref,
    token_sum_ref,
    grad_sum_ref,
    token_hbm,
    grad_ref,
    token_ref,
    sems,
):
    totals, by_choice = combine_chunks([LAST], [(given_ref, 1)], ids_ref, slot_ref, gates_ref)
    width = totals[0].shape[1]
    stores = []
    for q, total in enumerate(totals):
        cols = slice(q * width, (q + 1) * width)
        token_ref[:, cols] = (token_sum_ref[:, cols] + total).astype(BF)
        stores.append(
            pltpu.make_async_copy(token_ref.at[:, cols], token_hbm.at[:, cols], sems.at[q])
        )
        stores[q].start()
    grad_ref[...] = (grad_sum_ref[...] + by_choice).astype(BF)
    for store in stores:
        store.wait()


def local_call(kernel, outs, arrays, name, flops, moved, space=pltpu.VMEM, scratch=(), limit=16, first=None):
    vmem = pl.BlockSpec(memory_space=pltpu.VMEM)
    return pl.pallas_call(
        kernel,
        out_shape=[jax.ShapeDtypeStruct(shape, kind) for shape, kind in outs],
        in_specs=[pl.BlockSpec(memory_space=space)] * len(arrays),
        out_specs=[pl.BlockSpec(memory_space=first or pltpu.VMEM)] + [vmem] * (len(outs) - 1),
        scratch_shapes=list(scratch),
        compiler_params=pltpu.CompilerParams(vmem_limit_bytes=limit * MIB),
        cost_estimate=pl.CostEstimate(flops=flops, bytes_accessed=moved, transcendentals=0),
        name=name,
    )(*arrays)


def to_step(chunk, base):
    experts = lax.axis_size("expert")
    if base == 1:
        return lax.ppermute(chunk, "expert", [(i, i ^ 1) for i in range(experts)])
    pairs = [(2 * i + r, 2 * (i ^ (base + r)) + r) for i in range(experts) for r in range(2)]
    return lax.ppermute(chunk, ("expert", "replica"), pairs)


def to_twin(chunk):
    return lax.ppermute(chunk, "replica", [(0, 1), (1, 0)])


def hold_kernel(source_ref, place_ref):
    place_ref[...] = source_ref[...]


def per_device_moving_rows(
    tokens,
    cotangent,
    expert_ids,
    gate_values,
    replica_pick,
    replica_plan,
    gate_proj,
    up_proj,
    down_proj,
):
    experts = lax.axis_size("expert")
    token_count, model_width = tokens.shape
    topk = expert_ids.shape[1]
    hidden_width = gate_proj.shape[2]
    width = model_width // QUARTERS
    served = experts * (MAIN + 2)
    small = (topk, token_count)
    count = len(BASES)
    *chunks, slot, gates = local_call(
        route_kernel,
        [((SEND_ROWS, width), BF)] * experts
        + [((experts, token_count), jnp.int32), ((experts, token_count), F32)],
        [replica_plan, expert_ids.T, replica_pick.T, gate_values.T, tokens, cotangent],
        "route",
        LONG,
        2 * 2 * (token_count + served) * model_width,
        space=pltpu.HBM,
        limit=54,
        scratch=[
            pltpu.SMEM((experts,), jnp.int32),
            pltpu.VMEM(small, jnp.int32),
            pltpu.VMEM(small, jnp.int32),
            pltpu.VMEM(small, BF),
            pltpu.VMEM(tokens.shape, BF),
            pltpu.VMEM(tokens.shape, BF),
            pltpu.SemaphoreType.DMA((6,)),
        ],
    )
    recv = list(chunks)
    recv[1] = to_step(chunks[1], 1)
    twin = [to_twin(chunks[c]) for c in (3, 5, 7)]
    twin, mine = lax.optimization_barrier((twin, chunks[4]))
    for d, base in enumerate(BASES):
        recv[2 + 2 * d] = to_step(mine if base == 6 else chunks[2 + 2 * d], base)
        recv[3 + 2 * d] = to_step(twin[d], base)
    (held,) = local_call(hold_kernel, [(recv[0].shape, BF)], [recv[0]], "hold", 1, 1)
    matmul = 2 * served * model_width * hidden_width
    outs = local_call(
        expert_kernel,
        [((BACK_ROWS, width), BF)] * 2
        + [((DOUBLE_ROWS, width), BF)] * count
        + [((served, model_width), BF)] * 2
        + [((served, hidden_width), BF)] * 3,
        [held, *(recv[c] for c in ORDER[1:]), gate_proj[0], up_proj[0], down_proj[0]],
        "expert_rows",
        5 * matmul,
        2 * 3 * model_width * hidden_width,
    )
    backs, factors = outs[: 2 + count], outs[2 + count :]
    kept = list(map(to_step, backs[2:], BASES))
    near = to_step(backs[1], 1)
    half = model_width // 2
    (leaving,) = local_call(
        other_half_kernel,
        [((3 * half, hidden_width), BF)],
        factors,
        "other_half",
        1,
        1,
    )
    shares = local_call(
        own_half_kernel,
        [((half, hidden_width), BF)] * 3,
        [*factors, to_twin(leaving)],
        "own_half",
        1,
        1,
    )
    kept[0], near, shares = lax.optimization_barrier((kept[0], near, shares))
    routes = [expert_ids.T, slot, gates]
    sums = local_call(
        combine_kernel,
        [((token_count, model_width), F32), ((topk, token_count), F32)],
        [*routes, backs[0], near, *kept, *map(to_twin, kept[1:])],
        "combine",
        1,
        1,
    )
    token_grad, gate_grad = local_call(
        combine_last_kernel,
        [((token_count, model_width), BF), ((topk, token_count), BF)],
        [*routes, to_twin(kept[0]), *sums],
        "combine_last",
        1,
        1,
        scratch=[pltpu.VMEM((token_count, model_width), BF), pltpu.SemaphoreType.DMA((QUARTERS,))],
        first=pltpu.HBM,
    )
    return (token_grad, gate_grad.T, shares[0][None], shares[1][None], shares[2][None])


def per_device(tokens, cotangent, expert_ids, gate_values, replica_pick, replica_plan, *matrices):
    experts = lax.axis_size("expert")
    slots = (copies_of(experts) + 1) * CAP
    row_bytes = 3 * 2 * tokens.shape[1] * experts
    matrix_bytes = 4 * sum(2 * m[0].size for m in matrices)
    fits = slots == MAIN + 2 and experts == 8 and lax.axis_size("replica") == 2
    rows_cheaper = slots * row_bytes < 2 * CAP * row_bytes + matrix_bytes
    plan = per_device_moving_rows if fits and rows_cheaper else per_device_moving_weights
    return plan(
        tokens, cotangent, expert_ids, gate_values, replica_pick, replica_plan, *matrices
    )


def solution(mesh):
    placed = (
        P(("parts", "expert", "replica"), None),
        P(("parts", "expert", "replica"), None),
        P(("parts", "expert", "replica"), None),
        P(("parts", "expert", "replica"), None),
        P(("parts", "expert", "replica"), None),
        P("parts"),
        P("expert", None, None),
        P("expert", None, None),
        P("expert", None, None),
    )
    return jax.shard_map(
        per_device,
        mesh=mesh,
        in_specs=placed,
        out_specs=(
            P(("parts", "expert", "replica"), None),
            P(("parts", "expert", "replica"), None),
            P(("parts", "expert"), "replica", None),
            P(("parts", "expert"), "replica", None),
            P(("parts", "expert"), "replica", None),
        ),
        check_vma=False,
    )
```

```python
import jax
import jax.numpy as jnp
from jax import lax
from jax.experimental import pallas as pl
from jax.experimental.pallas import tpu as pltpu
from jax.sharding import PartitionSpec as P

CAP = 6


def route_assignments(flat_ids, flat_pick, replica_plan, capacity):
    experts = replica_plan.shape[0]
    lane_ids = jnp.arange(experts, dtype=jnp.int32)
    same_plan = replica_plan[:, None] == replica_plan[None, :]
    earlier = lane_ids[None, :] < lane_ids[:, None]
    position = jnp.sum(jnp.logical_and(same_plan, earlier), axis=1)
    hot_mask = jnp.any(replica_plan[None, :] == lane_ids[:, None], axis=1)
    is_hot = jnp.any(
        jnp.logical_and(flat_ids[:, None] == lane_ids[None, :], hot_mask[None, :]), axis=1
    )
    use_copy = jnp.logical_and(is_hot, flat_pick >= 1)
    matches = jnp.logical_and(
        replica_plan[None, :] == flat_ids[:, None], position[None, :] == flat_pick[:, None] - 1
    )
    holder = jnp.sum(jnp.where(matches, lane_ids[None, :], 0), axis=1)
    target = jnp.where(use_copy, holder, flat_ids)
    copy_role = use_copy.astype(jnp.int32)
    bucket = target * 2 + copy_role
    sequence = jnp.arange(bucket.shape[0], dtype=jnp.int32)
    arrival = jnp.sum(
        jnp.logical_and(bucket[None, :] == bucket[:, None], sequence[None, :] < sequence[:, None]),
        axis=1,
    )
    kept_mask = arrival < capacity
    slot_index = target * (2 * capacity) + copy_role * capacity + jnp.minimum(arrival, capacity - 1)
    return (slot_index, kept_mask)


def fill_slots(slot_index, kept_mask, slot_count):
    slot_ids = jnp.arange(slot_count, dtype=jnp.int32)
    matches = jnp.logical_and(slot_index[None, :] == slot_ids[:, None], kept_mask[None, :])
    sequence = jnp.arange(slot_index.shape[0], dtype=jnp.int32)
    source = jnp.sum(jnp.where(matches, sequence[None, :], 0), axis=1)
    filled = jnp.any(matches, axis=1)
    return (source, filled)


def expert_backward(row_block, upstream, weight, gate_w, up_w, down_w):
    contract_cols = (((1,), (1,)), ((), ()))
    contract_rows = (((0,), (0,)), ((), ()))
    gate_pre = jnp.dot(row_block, gate_w, preferred_element_type=jnp.float32)
    up_pre = jnp.dot(row_block, up_w, preferred_element_type=jnp.float32)
    sigmoid_gate = jax.nn.sigmoid(gate_pre)
    activated = gate_pre * sigmoid_gate
    hidden = (activated * up_pre).astype(jnp.bfloat16)
    output_rows = lax.dot_general(hidden, down_w, contract_cols, preferred_element_type=jnp.float32)
    weight_col = weight.astype(jnp.float32)[:, None]
    upstream_f = upstream.astype(jnp.float32)
    gate_rows = jnp.sum(upstream_f * output_rows, axis=1)
    hidden_grad = weight_col * jnp.dot(upstream, down_w, preferred_element_type=jnp.float32)
    slope = sigmoid_gate * (1.0 + gate_pre * (1.0 - sigmoid_gate))
    gate_delta = (hidden_grad * up_pre * slope).astype(jnp.bfloat16)
    up_delta = (hidden_grad * activated).astype(jnp.bfloat16)
    input_grad = (
        lax.dot_general(gate_delta, gate_w, contract_cols, preferred_element_type=jnp.float32)
        + lax.dot_general(up_delta, up_w, contract_cols, preferred_element_type=jnp.float32)
    ).astype(jnp.bfloat16)
    scaled = (weight_col * upstream_f).astype(jnp.bfloat16)
    grad_set = (
        lax.dot_general(row_block, gate_delta, contract_rows, preferred_element_type=jnp.float32),
        lax.dot_general(row_block, up_delta, contract_rows, preferred_element_type=jnp.float32),
        lax.dot_general(scaled, hidden, contract_rows, preferred_element_type=jnp.float32),
    )
    return (input_grad, gate_rows, grad_set)


def per_device_moving_weights(
    tokens,
    cotangent,
    expert_ids,
    gate_values,
    replica_pick,
    replica_plan,
    gate_proj,
    up_proj,
    down_proj,
):
    experts = lax.axis_size("expert")
    capacity = CAP
    slot_total = 2 * capacity
    model_width = tokens.shape[1]
    topk = expert_ids.shape[1]
    token_count = tokens.shape[0]
    slot_index, kept_mask = route_assignments(
        expert_ids.reshape(-1), replica_pick.reshape(-1), replica_plan, capacity
    )
    source, filled = fill_slots(slot_index, kept_mask, experts * slot_total)
    token_of = source // topk
    zero_half = jnp.zeros((), jnp.bfloat16)
    send_rows = jnp.where(filled[:, None], jnp.take(tokens, token_of, axis=0), zero_half).reshape(
        experts, slot_total, model_width
    )
    send_upstream = jnp.where(
        filled[:, None], jnp.take(cotangent, token_of, axis=0), zero_half
    ).reshape(experts, slot_total, model_width)
    send_weight = jnp.where(filled, gate_values.reshape(-1)[source], zero_half).reshape(
        experts, slot_total
    )
    arrived = lax.all_to_all(send_rows, "expert", split_axis=0, concat_axis=0, tiled=True)
    own_gate = gate_proj[0]
    own_up = up_proj[0]
    own_down = down_proj[0]
    hidden_width = own_gate.shape[1]
    spread = (
        lax.all_to_all(
            own_gate.reshape(experts, -1), "expert", split_axis=0, concat_axis=0, tiled=True
        ),
        lax.all_to_all(
            own_up.reshape(experts, -1), "expert", split_axis=0, concat_axis=0, tiled=True
        ),
        lax.all_to_all(
            own_down.reshape(experts, -1), "expert", split_axis=0, concat_axis=0, tiled=True
        ),
    )
    chosen_gate = jnp.take(spread[0], replica_plan, axis=0)
    chosen_up = jnp.take(spread[1], replica_plan, axis=0)
    chosen_down = jnp.take(spread[2], replica_plan, axis=0)
    collected = (
        lax.all_to_all(chosen_gate, "expert", split_axis=0, concat_axis=0, tiled=True),
        lax.all_to_all(chosen_up, "expert", split_axis=0, concat_axis=0, tiled=True),
        lax.all_to_all(chosen_down, "expert", split_axis=0, concat_axis=0, tiled=True),
    )
    copy_gate = collected[0].reshape(model_width, hidden_width)
    copy_up = collected[1].reshape(model_width, hidden_width)
    copy_down = collected[2].reshape(model_width, hidden_width)
    arrived_up, arrived_weight = (
        lax.all_to_all(send_upstream, "expert", split_axis=0, concat_axis=0, tiled=True),
        lax.all_to_all(send_weight, "expert", split_axis=0, concat_axis=0, tiled=True),
    )
    owned_dx, owned_gate_rows, owned_grads = expert_backward(
        arrived[:, :capacity].reshape(-1, model_width),
        arrived_up[:, :capacity].reshape(-1, model_width),
        arrived_weight[:, :capacity].reshape(-1),
        own_gate,
        own_up,
        own_down,
    )
    copied_dx, copied_gate_rows, copied_grads = expert_backward(
        arrived[:, capacity:].reshape(-1, model_width),
        arrived_up[:, capacity:].reshape(-1, model_width),
        arrived_weight[:, capacity:].reshape(-1),
        copy_gate,
        copy_up,
        copy_down,
    )
    back_rows = jnp.concatenate(
        [
            owned_dx.reshape(experts, capacity, model_width),
            copied_dx.reshape(experts, capacity, model_width),
        ],
        axis=1,
    )
    back_gate = jnp.concatenate(
        [owned_gate_rows.reshape(experts, capacity), copied_gate_rows.reshape(experts, capacity)],
        axis=1,
    ).astype(jnp.bfloat16)
    returned, returned_gate = (
        lax.all_to_all(back_rows, "expert", split_axis=0, concat_axis=0, tiled=True),
        lax.all_to_all(back_gate, "expert", split_axis=0, concat_axis=0, tiled=True),
    )
    copy_pieces = (
        copied_grads[0].astype(jnp.bfloat16).reshape(experts, -1),
        copied_grads[1].astype(jnp.bfloat16).reshape(experts, -1),
        copied_grads[2].astype(jnp.bfloat16).reshape(experts, -1),
    )
    grad_spread = (
        lax.all_to_all(copy_pieces[0], "expert", split_axis=0, concat_axis=0, tiled=True),
        lax.all_to_all(copy_pieces[1], "expert", split_axis=0, concat_axis=0, tiled=True),
        lax.all_to_all(copy_pieces[2], "expert", split_axis=0, concat_axis=0, tiled=True),
    )
    lane_ids = jnp.arange(experts, dtype=jnp.int32)
    owner_map = (replica_plan[None, :] == lane_ids[:, None]).astype(jnp.bfloat16)
    summed_gate = jnp.dot(owner_map, grad_spread[0], preferred_element_type=jnp.float32).astype(
        jnp.bfloat16
    )
    summed_up = jnp.dot(owner_map, grad_spread[1], preferred_element_type=jnp.float32).astype(
        jnp.bfloat16
    )
    summed_down = jnp.dot(owner_map, grad_spread[2], preferred_element_type=jnp.float32).astype(
        jnp.bfloat16
    )
    grad_back = (
        lax.all_to_all(summed_gate, "expert", split_axis=0, concat_axis=0, tiled=True),
        lax.all_to_all(summed_up, "expert", split_axis=0, concat_axis=0, tiled=True),
        lax.all_to_all(summed_down, "expert", split_axis=0, concat_axis=0, tiled=True),
    )
    total_gate = owned_grads[0] + grad_back[0].reshape(model_width, hidden_width).astype(
        jnp.float32
    )
    total_up = owned_grads[1] + grad_back[1].reshape(model_width, hidden_width).astype(jnp.float32)
    total_down = owned_grads[2] + grad_back[2].reshape(model_width, hidden_width).astype(
        jnp.float32
    )
    shares = (
        lax.psum_scatter(
            total_gate.astype(jnp.bfloat16), "replica", scatter_dimension=0, tiled=True
        ).astype(jnp.float32),
        lax.psum_scatter(
            total_up.astype(jnp.bfloat16), "replica", scatter_dimension=0, tiled=True
        ).astype(jnp.float32),
        lax.psum_scatter(
            total_down.astype(jnp.bfloat16), "replica", scatter_dimension=0, tiled=True
        ).astype(jnp.float32),
    )
    flat_back = returned.reshape(experts * slot_total, model_width)
    picked_rows = jnp.take(flat_back, slot_index, axis=0)
    picked_rows = jnp.where(kept_mask[:, None], picked_rows, zero_half).astype(jnp.float32)
    token_grad = jnp.sum(picked_rows.reshape(token_count, topk, model_width), axis=1).astype(
        jnp.bfloat16
    )
    gate_grad = jnp.where(kept_mask, returned_gate.reshape(-1)[slot_index], zero_half).reshape(
        token_count, topk
    )
    return (
        token_grad,
        gate_grad,
        shares[0].astype(jnp.bfloat16)[None],
        shares[1].astype(jnp.bfloat16)[None],
        shares[2].astype(jnp.bfloat16)[None],
    )


BF = jnp.bfloat16
F32 = jnp.float32
CONTRACT_ROWS = (((0,), (0,)), ((), ()))
CONTRACT_COLS = (((1,), (1,)), ((), ()))
MIB = 1024 * 1024

BASES = (4, 6, 2)
ORDER = (0, 1, 2, 4, 6, 3, 7, 5)
LONG = 8 * 10**9
MAIN = 16
QUARTERS = 4
SEND_ROWS = 2 * QUARTERS * MAIN + 16
MAIN_ROWS = QUARTERS * MAIN
BACK_ROWS = MAIN_ROWS + 16
DOUBLE_ROWS = 2 * MAIN_ROWS + 24


def copies_of(experts):
    return 2 if experts <= 8 else 8


def iota(shape, axis):
    return lax.broadcasted_iota(jnp.int32, shape, axis)


def partners(experts, tokens):
    row = iota((experts, tokens), 0)
    step = jnp.bitwise_xor(jnp.bitwise_and(row, 1), lax.axis_index("replica"))
    for d, base in enumerate(BASES):
        step = jnp.where(jnp.right_shift(row, 1) == d + 1, step + base, step)
    step = jnp.where(row < 2, row, step)
    return jnp.bitwise_xor(step, lax.axis_index("expert"))


def mask(condition):
    return condition.astype(F32).astype(BF)


def repeat_rows(table, times):
    width = table.shape[1]
    return jnp.concatenate(
        [jnp.broadcast_to(table[e : e + 1], (times, width)) for e in range(table.shape[0])], axis=0
    )


def route_kernel(plan_hbm, ids_hbm, pick_hbm, gate_hbm, tok_hbm, cot_hbm, *refs):
    sems = refs[-1]
    plan_ref, ids_ref, pick_ref, gate_ref, tok_ref, cot_ref = refs[-7:-1]
    slot_ref, gates_ref = refs[-9:-7]
    send_refs = refs[:-9]
    topk, tokens = ids_ref.shape
    experts = len(send_refs)
    width = tok_ref.shape[1] // QUARTERS
    copies = copies_of(experts)
    loads = [
        pltpu.make_async_copy(source, place, sems.at[n])
        for n, (source, place) in enumerate(
            (
                (plan_hbm, plan_ref),
                (ids_hbm, ids_ref),
                (pick_hbm, pick_ref),
                (gate_hbm, gate_ref),
                (tok_hbm, tok_ref),
                (cot_hbm, cot_ref),
            )
        )
    ]
    for load in loads:
        load.start()
    before = mask(iota((tokens, tokens), 0) < iota((tokens, tokens), 1))
    expert_row = partners(experts, tokens)
    for load in loads[:4]:
        load.wait()
    ids = ids_ref[...]
    pick = pick_ref[...]
    gate = gate_ref[...].astype(F32)
    named = jnp.zeros((experts, tokens), jnp.int32)
    gates = jnp.zeros((experts, tokens), F32)
    for k in range(topk):
        hit = ids[k : k + 1] == expert_row
        named = jnp.where(hit, pick[k : k + 1] + 1, named)
        gates = jnp.where(hit, gate[k : k + 1], gates)
    hot = jnp.zeros((experts, tokens), jnp.int32)
    for j in range(experts):
        hot = jnp.where(expert_row == plan_ref[j], 1, hot)
    chosen = jnp.where(named == 0, -1, jnp.where(hot > 0, named - 1, 0))
    masks = jnp.concatenate([(chosen == c).astype(F32) for c in range(copies + 1)], axis=0)
    rank = jnp.dot(masks.astype(BF), before, preferred_element_type=F32).astype(jnp.int32)
    slot = jnp.full((experts, tokens), -1, jnp.int32)
    for c in range(copies + 1):
        rank_c = rank[c * experts : (c + 1) * experts]
        keep = jnp.logical_and(chosen == c, rank_c < CAP)
        slot = jnp.where(keep, c * CAP + rank_c, slot)
    slot_ref[...] = slot
    gates_ref[...] = gates
    slot16 = repeat_rows(slot, MAIN)
    gate16 = repeat_rows(gates, MAIN)
    inner = jnp.bitwise_and(iota(slot16.shape, 0), MAIN - 1)
    onehot = (slot16 == inner).astype(F32)
    wanted = MAIN + jnp.bitwise_and(jnp.right_shift(inner, 2), 1)
    last = (slot16 == wanted).astype(F32)
    last_rows = jnp.where(inner >= 8, 0.0, last)
    last_scaled = jnp.where(inner >= 8, last * gate16, 0.0)
    quarter = jnp.bitwise_and(inner, 3)
    for load in loads[4:]:
        load.wait()
    rows = jnp.dot(onehot.astype(BF), tok_ref[...], preferred_element_type=F32).astype(BF)
    scaled = jnp.dot(
        (onehot * gate16).astype(BF), cot_ref[...], preferred_element_type=F32
    ).astype(BF)
    tail = jnp.zeros((experts * MAIN, width), F32)
    for q in range(QUARTERS):
        cols = slice(q * width, (q + 1) * width)
        mine = quarter == q
        tail += jnp.dot(
            jnp.where(mine, last_rows, 0.0).astype(BF), tok_ref[:, cols], preferred_element_type=F32
        )
        tail += jnp.dot(
            jnp.where(mine, last_scaled, 0.0).astype(BF),
            cot_ref[:, cols],
            preferred_element_type=F32,
        )
    tail = tail.astype(BF)
    for c, ref in enumerate(send_refs):
        here = slice(c * MAIN, (c + 1) * MAIN)
        for q in range(QUARTERS):
            cols = slice(q * width, (q + 1) * width)
            ref[q * MAIN : (q + 1) * MAIN, :] = rows[here, cols]
            ref[(QUARTERS + q) * MAIN : (QUARTERS + q + 1) * MAIN, :] = scaled[here, cols]
        ref[2 * QUARTERS * MAIN :, :] = tail[here]


def expert_kernel(*refs):
    experts = len(ORDER)
    recv_refs = [refs[ORDER.index(c)] for c in range(experts)]
    gate_ref, up_ref, down_ref = refs[experts : experts + 3]
    back_refs = refs[experts + 3 : -5]
    x_ref, s_ref, dg_ref, du_ref, hid_ref = refs[-5:]
    width = refs[0].shape[1]
    main_rows = experts * MAIN
    tail = jnp.concatenate([ref[2 * QUARTERS * MAIN :, :] for ref in recv_refs], axis=0)
    row = iota((4 * experts, main_rows), 0)
    col = iota((4 * experts, main_rows), 1)
    kind = (row >= 2 * experts).astype(jnp.int32)
    chunk = jnp.right_shift(row - kind * 2 * experts, 1)
    base = chunk * MAIN + kind * 8 + jnp.bitwise_and(row, 1) * 4
    for q in range(QUARTERS):
        cols = slice(q * width, (q + 1) * width)
        picked = jnp.dot(mask(col == base + q), tail, preferred_element_type=F32).astype(BF)
        x_ref[main_rows:, cols] = picked[: 2 * experts]
        s_ref[main_rows:, cols] = picked[2 * experts :]
        for i, ref in enumerate(recv_refs):
            here = slice(i * MAIN, (i + 1) * MAIN)
            x_ref[here, cols] = ref[q * MAIN : (q + 1) * MAIN, :]
            s_ref[here, cols] = ref[(QUARTERS + q) * MAIN : (QUARTERS + q + 1) * MAIN, :]
    rows = x_ref[...]
    gate_pre = jnp.dot(rows, gate_ref[...], preferred_element_type=F32)
    up_pre = jnp.dot(rows, up_ref[...], preferred_element_type=F32)
    hidden_grad = jnp.dot(s_ref[...], down_ref[...], preferred_element_type=F32)
    sig = jax.nn.sigmoid(gate_pre)
    activated = gate_pre * sig
    hidden = (activated * up_pre).astype(BF)
    slope = sig * (1.0 + gate_pre * (1.0 - sig))
    gate_delta = (hidden_grad * up_pre * slope).astype(BF)
    up_delta = (hidden_grad * activated).astype(BF)
    hid_ref[...] = hidden
    dg_ref[...] = gate_delta
    du_ref[...] = up_delta
    grad = (
        lax.dot_general(gate_delta, gate_ref[...], CONTRACT_COLS, preferred_element_type=F32)
        + lax.dot_general(up_delta, up_ref[...], CONTRACT_COLS, preferred_element_type=F32)
    ).astype(BF)
    product = hidden.astype(F32) * hidden_grad
    product = jnp.concatenate(
        [product, jnp.zeros((width - product.shape[0], product.shape[1]), F32)], axis=0
    )
    high = product.astype(BF)
    low = (product - high.astype(F32)).astype(BF)
    ones = jnp.ones((8, product.shape[1]), BF)
    gate_lanes = lax.dot_general(
        ones, high, CONTRACT_COLS, preferred_element_type=F32
    ) + lax.dot_general(ones, low, CONTRACT_COLS, preferred_element_type=F32)
    trow = iota((main_rows, 2 * experts), 0)
    tcol = iota((main_rows, 2 * experts), 1)
    inner = jnp.bitwise_and(trow, MAIN - 1)
    source = jnp.right_shift(trow, 4) * 2 + jnp.right_shift(inner, 2)
    spread = jnp.zeros((main_rows, width), F32)
    for q in range(QUARTERS):
        cols = slice(q * width, (q + 1) * width)
        mine = jnp.logical_and(jnp.bitwise_and(inner, 3) == q, inner < 8)
        place = mask(jnp.logical_and(mine, tcol == source))
        spread += jnp.dot(place, grad[main_rows:, cols], preferred_element_type=F32)
        for i in range(experts):
            single = i < 2
            low = q * MAIN + (0 if single else (i % 2) * MAIN_ROWS)
            ref = back_refs[i if single else 1 + i // 2]
            ref[low : low + MAIN, :] = grad[i * MAIN : (i + 1) * MAIN, cols]
    for n, ref in enumerate(back_refs):
        if n < 2:
            ref[MAIN_ROWS:, :] = jnp.concatenate(
                [spread[n * MAIN : n * MAIN + 8], gate_lanes], axis=0
            ).astype(BF)
        else:
            i = 2 * n - 2
            both = [spread[c * MAIN : c * MAIN + 8] for c in (i, i + 1)]
            ref[2 * MAIN_ROWS : 2 * MAIN_ROWS + 16, :] = jnp.concatenate(both, axis=0).astype(BF)
            ref[2 * MAIN_ROWS + 16 :, :] = gate_lanes.astype(BF)


def grads_of(half, x_ref, s_ref, dg_ref, du_ref, hid_ref):
    rows = x_ref.shape[1] // 2
    cols = pl.ds(pl.multiple_of(half * rows, rows), rows)
    x_half = x_ref[:, cols]
    s_half = s_ref[:, cols]
    return (
        lax.dot_general(x_half, dg_ref[...], CONTRACT_ROWS, preferred_element_type=F32),
        lax.dot_general(x_half, du_ref[...], CONTRACT_ROWS, preferred_element_type=F32),
        lax.dot_general(s_half, hid_ref[...], CONTRACT_ROWS, preferred_element_type=F32),
    )


def other_half_kernel(x_ref, s_ref, dg_ref, du_ref, hid_ref, out_ref):
    half = 1 - lax.axis_index("replica")
    parts = grads_of(half, x_ref, s_ref, dg_ref, du_ref, hid_ref)
    rows = parts[0].shape[0]
    for n in range(3):
        out_ref[n * rows : (n + 1) * rows, :] = parts[n].astype(BF)


def own_half_kernel(
    x_ref, s_ref, dg_ref, du_ref, hid_ref, came_ref, gate_ref, up_ref, down_ref
):
    parts = grads_of(lax.axis_index("replica"), x_ref, s_ref, dg_ref, du_ref, hid_ref)
    rows = parts[0].shape[0]
    for n, out_ref in enumerate((gate_ref, up_ref, down_ref)):
        came = came_ref[n * rows : (n + 1) * rows, :].astype(F32)
        out_ref[...] = (parts[n].astype(BF).astype(F32) + came).astype(BF)


def tail_of(ref, part):
    if part is None:
        return ref[MAIN_ROWS:, :]
    both = ref[2 * MAIN_ROWS : 2 * MAIN_ROWS + 16, :].astype(F32)
    sums = ref[2 * MAIN_ROWS + 16 :, :].astype(F32)
    return jnp.concatenate([both[8 * part : 8 * part + 8], sums], axis=0).astype(BF)


def combine_chunks(chunks, views, ids_ref, slot_ref, gates_ref):
    topk, tokens = ids_ref.shape
    experts = slot_ref.shape[0]
    width = views[0][0].shape[1]
    slot = jnp.concatenate([slot_ref[c : c + 1] for c in chunks], axis=0)
    slot16 = repeat_rows(slot, MAIN)
    inner = jnp.bitwise_and(iota(slot16.shape, 0), MAIN - 1)
    onehot = mask(slot16 == inner)
    wanted = MAIN + jnp.right_shift(inner, 2)
    last = jnp.where(jnp.logical_and(slot16 == wanted, inner < 8), 1.0, 0.0)
    quarter = jnp.bitwise_and(inner, 3)
    tails = [tail_of(*view) for view in views]
    starts = [(ref, MAIN_ROWS if part else 0) for ref, part in views]
    tail = jnp.concatenate(tails, axis=0)
    totals = []
    for q in range(QUARTERS):
        main = jnp.concatenate(
            [ref[first + q * MAIN : first + (q + 1) * MAIN, :] for ref, first in starts], axis=0
        )
        place = jnp.where(quarter == q, last, 0.0).astype(BF)
        total = lax.dot_general(onehot, main, CONTRACT_ROWS, preferred_element_type=F32)
        total += lax.dot_general(place, tail, CONTRACT_ROWS, preferred_element_type=F32)
        totals.append(total)
    lane_index = iota((width, tokens), 0)
    expert_row = partners(experts, tokens)
    by_choice = jnp.zeros((topk, tokens), F32)
    for place, c in enumerate(chunks):
        mine = slot[place : place + 1]
        lane = jnp.where(mine < MAIN, c * MAIN + mine, experts * MAIN + 2 * c + mine - MAIN)
        lane = jnp.where(mine < 0, -1, lane)
        sums = jnp.dot(tails[place], mask(lane_index == lane), preferred_element_type=F32)
        kept = mine >= 0
        grad = jnp.where(kept, sums[8:9] / jnp.where(kept, gates_ref[c : c + 1], 1.0), 0.0)
        by_choice += jnp.where(ids_ref[...] == expert_row[c : c + 1], grad, 0.0)
    return totals, by_choice


LAST = 3


def combine_kernel(ids_ref, slot_ref, gates_ref, *refs):
    token_ref, grad_ref = refs[-2:]
    singles = [(refs[0], None), (refs[1], None)]
    kept_refs = refs[2 : 2 + len(BASES)]
    given_refs = refs[2 + len(BASES) : -2]
    views = dict(enumerate(singles))
    for d, ref in enumerate(kept_refs):
        views[2 + 2 * d] = (ref, 0)
    for d, ref in enumerate(given_refs):
        views[LAST + 2 + 2 * d] = (ref, 1)
    chunks = sorted(views)
    totals, by_choice = combine_chunks(
        chunks, [views[c] for c in chunks], ids_ref, slot_ref, gates_ref
    )
    width = totals[0].shape[1]
    for q, total in enumerate(totals):
        token_ref[:, q * width : (q + 1) * width] = total
    grad_ref[...] = by_choice


def combine_last_kernel(
    ids_ref, slot_ref, gates_ref, given_ref, token_sum_ref, grad_sum_ref, token_ref, grad_ref
):
    totals, by_choice = combine_chunks([LAST], [(given_ref, 1)], ids_ref, slot_ref, gates_ref)
    width = totals[0].shape[1]
    for q, total in enumerate(totals):
        cols = slice(q * width, (q + 1) * width)
        token_ref[:, cols] = (token_sum_ref[:, cols] + total).astype(BF)
    grad_ref[...] = (grad_sum_ref[...] + by_choice).astype(BF)


def local_call(kernel, outs, arrays, name, flops, moved, space=pltpu.VMEM, scratch=(), limit=16):
    vmem = pl.BlockSpec(memory_space=pltpu.VMEM)
    return pl.pallas_call(
        kernel,
        out_shape=[jax.ShapeDtypeStruct(shape, kind) for shape, kind in outs],
        in_specs=[pl.BlockSpec(memory_space=space)] * len(arrays),
        out_specs=[vmem] * len(outs),
        scratch_shapes=list(scratch),
        compiler_params=pltpu.CompilerParams(vmem_limit_bytes=limit * MIB),
        cost_estimate=pl.CostEstimate(flops=flops, bytes_accessed=moved, transcendentals=0),
        name=name,
    )(*arrays)


def to_step(chunk, base):
    experts = lax.axis_size("expert")
    if base == 1:
        return lax.ppermute(chunk, "expert", [(i, i ^ 1) for i in range(experts)])
    pairs = [(2 * i + r, 2 * (i ^ (base + r)) + r) for i in range(experts) for r in range(2)]
    return lax.ppermute(chunk, ("expert", "replica"), pairs)


def to_twin(chunk):
    return lax.ppermute(chunk, "replica", [(0, 1), (1, 0)])


def hold_kernel(source_ref, place_ref):
    place_ref[...] = source_ref[...]


def per_device_moving_rows(
    tokens,
    cotangent,
    expert_ids,
    gate_values,
    replica_pick,
    replica_plan,
    gate_proj,
    up_proj,
    down_proj,
):
    experts = lax.axis_size("expert")
    token_count, model_width = tokens.shape
    topk = expert_ids.shape[1]
    hidden_width = gate_proj.shape[2]
    width = model_width // QUARTERS
    served = experts * (MAIN + 2)
    small = (topk, token_count)
    count = len(BASES)
    *chunks, slot, gates = local_call(
        route_kernel,
        [((SEND_ROWS, width), BF)] * experts
        + [((experts, token_count), jnp.int32), ((experts, token_count), F32)],
        [replica_plan, expert_ids.T, replica_pick.T, gate_values.T, tokens, cotangent],
        "route",
        LONG,
        2 * 2 * (token_count + served) * model_width,
        space=pltpu.HBM,
        limit=54,
        scratch=[
            pltpu.SMEM((experts,), jnp.int32),
            pltpu.VMEM(small, jnp.int32),
            pltpu.VMEM(small, jnp.int32),
            pltpu.VMEM(small, BF),
            pltpu.VMEM(tokens.shape, BF),
            pltpu.VMEM(tokens.shape, BF),
            pltpu.SemaphoreType.DMA((6,)),
        ],
    )
    recv = list(chunks)
    recv[1] = to_step(chunks[1], 1)
    twin = [to_twin(chunks[c]) for c in (3, 5, 7)]
    twin, mine = lax.optimization_barrier((twin, chunks[4]))
    for d, base in enumerate(BASES):
        recv[2 + 2 * d] = to_step(mine if base == 6 else chunks[2 + 2 * d], base)
        recv[3 + 2 * d] = to_step(twin[d], base)
    (held,) = local_call(hold_kernel, [(recv[0].shape, BF)], [recv[0]], "hold", 1, 1)
    matmul = 2 * served * model_width * hidden_width
    outs = local_call(
        expert_kernel,
        [((BACK_ROWS, width), BF)] * 2
        + [((DOUBLE_ROWS, width), BF)] * count
        + [((served, model_width), BF)] * 2
        + [((served, hidden_width), BF)] * 3,
        [held, *(recv[c] for c in ORDER[1:]), gate_proj[0], up_proj[0], down_proj[0]],
        "expert_rows",
        5 * matmul,
        2 * 3 * model_width * hidden_width,
    )
    backs, factors = outs[: 2 + count], outs[2 + count :]
    kept = list(map(to_step, backs[2:], BASES))
    near = to_step(backs[1], 1)
    half = model_width // 2
    (leaving,) = local_call(
        other_half_kernel,
        [((3 * half, hidden_width), BF)],
        factors,
        "other_half",
        1,
        1,
    )
    shares = local_call(
        own_half_kernel,
        [((half, hidden_width), BF)] * 3,
        [*factors, to_twin(leaving)],
        "own_half",
        1,
        1,
    )
    kept[0], near, shares = lax.optimization_barrier((kept[0], near, shares))
    routes = [expert_ids.T, slot, gates]
    sums = local_call(
        combine_kernel,
        [((token_count, model_width), F32), ((topk, token_count), F32)],
        [*routes, backs[0], near, *kept, *map(to_twin, kept[1:])],
        "combine",
        1,
        1,
    )
    token_grad, gate_grad = local_call(
        combine_last_kernel,
        [((token_count, model_width), BF), ((topk, token_count), BF)],
        [*routes, to_twin(kept[0]), *sums],
        "combine_last",
        1,
        1,
    )
    return (token_grad, gate_grad.T, shares[0][None], shares[1][None], shares[2][None])


def per_device(tokens, cotangent, expert_ids, gate_values, replica_pick, replica_plan, *matrices):
    experts = lax.axis_size("expert")
    slots = (copies_of(experts) + 1) * CAP
    row_bytes = 3 * 2 * tokens.shape[1] * experts
    matrix_bytes = 4 * sum(2 * m[0].size for m in matrices)
    fits = slots == MAIN + 2 and experts == 8 and lax.axis_size("replica") == 2
    rows_cheaper = slots * row_bytes < 2 * CAP * row_bytes + matrix_bytes
    plan = per_device_moving_rows if fits and rows_cheaper else per_device_moving_weights
    return plan(
        tokens, cotangent, expert_ids, gate_values, replica_pick, replica_plan, *matrices
    )


def solution(mesh):
    placed = (
        P(("parts", "expert", "replica"), None),
        P(("parts", "expert", "replica"), None),
        P(("parts", "expert", "replica"), None),
        P(("parts", "expert", "replica"), None),
        P(("parts", "expert", "replica"), None),
        P("parts"),
        P("expert", None, None),
        P("expert", None, None),
        P("expert", None, None),
    )
    return jax.shard_map(
        per_device,
        mesh=mesh,
        in_specs=placed,
        out_specs=(
            P(("parts", "expert", "replica"), None),
            P(("parts", "expert", "replica"), None),
            P(("parts", "expert"), "replica", None),
            P(("parts", "expert"), "replica", None),
            P(("parts", "expert"), "replica", None),
        ),
        check_vma=False,
    )
```

```python
import jax
import jax.numpy as jnp
from jax import lax
from jax.experimental import pallas as pl
from jax.experimental.pallas import tpu as pltpu
from jax.sharding import PartitionSpec as P

CAP = 6


def route_assignments(flat_ids, flat_pick, replica_plan, capacity):
    experts = replica_plan.shape[0]
    lane_ids = jnp.arange(experts, dtype=jnp.int32)
    same_plan = replica_plan[:, None] == replica_plan[None, :]
    earlier = lane_ids[None, :] < lane_ids[:, None]
    position = jnp.sum(jnp.logical_and(same_plan, earlier), axis=1)
    hot_mask = jnp.any(replica_plan[None, :] == lane_ids[:, None], axis=1)
    is_hot = jnp.any(
        jnp.logical_and(flat_ids[:, None] == lane_ids[None, :], hot_mask[None, :]), axis=1
    )
    use_copy = jnp.logical_and(is_hot, flat_pick >= 1)
    matches = jnp.logical_and(
        replica_plan[None, :] == flat_ids[:, None], position[None, :] == flat_pick[:, None] - 1
    )
    holder = jnp.sum(jnp.where(matches, lane_ids[None, :], 0), axis=1)
    target = jnp.where(use_copy, holder, flat_ids)
    copy_role = use_copy.astype(jnp.int32)
    bucket = target * 2 + copy_role
    sequence = jnp.arange(bucket.shape[0], dtype=jnp.int32)
    arrival = jnp.sum(
        jnp.logical_and(bucket[None, :] == bucket[:, None], sequence[None, :] < sequence[:, None]),
        axis=1,
    )
    kept_mask = arrival < capacity
    slot_index = target * (2 * capacity) + copy_role * capacity + jnp.minimum(arrival, capacity - 1)
    return (slot_index, kept_mask)


def fill_slots(slot_index, kept_mask, slot_count):
    slot_ids = jnp.arange(slot_count, dtype=jnp.int32)
    matches = jnp.logical_and(slot_index[None, :] == slot_ids[:, None], kept_mask[None, :])
    sequence = jnp.arange(slot_index.shape[0], dtype=jnp.int32)
    source = jnp.sum(jnp.where(matches, sequence[None, :], 0), axis=1)
    filled = jnp.any(matches, axis=1)
    return (source, filled)


def expert_backward(row_block, upstream, weight, gate_w, up_w, down_w):
    contract_cols = (((1,), (1,)), ((), ()))
    contract_rows = (((0,), (0,)), ((), ()))
    gate_pre = jnp.dot(row_block, gate_w, preferred_element_type=jnp.float32)
    up_pre = jnp.dot(row_block, up_w, preferred_element_type=jnp.float32)
    sigmoid_gate = jax.nn.sigmoid(gate_pre)
    activated = gate_pre * sigmoid_gate
    hidden = (activated * up_pre).astype(jnp.bfloat16)
    output_rows = lax.dot_general(hidden, down_w, contract_cols, preferred_element_type=jnp.float32)
    weight_col = weight.astype(jnp.float32)[:, None]
    upstream_f = upstream.astype(jnp.float32)
    gate_rows = jnp.sum(upstream_f * output_rows, axis=1)
    hidden_grad = weight_col * jnp.dot(upstream, down_w, preferred_element_type=jnp.float32)
    slope = sigmoid_gate * (1.0 + gate_pre * (1.0 - sigmoid_gate))
    gate_delta = (hidden_grad * up_pre * slope).astype(jnp.bfloat16)
    up_delta = (hidden_grad * activated).astype(jnp.bfloat16)
    input_grad = (
        lax.dot_general(gate_delta, gate_w, contract_cols, preferred_element_type=jnp.float32)
        + lax.dot_general(up_delta, up_w, contract_cols, preferred_element_type=jnp.float32)
    ).astype(jnp.bfloat16)
    scaled = (weight_col * upstream_f).astype(jnp.bfloat16)
    grad_set = (
        lax.dot_general(row_block, gate_delta, contract_rows, preferred_element_type=jnp.float32),
        lax.dot_general(row_block, up_delta, contract_rows, preferred_element_type=jnp.float32),
        lax.dot_general(scaled, hidden, contract_rows, preferred_element_type=jnp.float32),
    )
    return (input_grad, gate_rows, grad_set)


def per_device_moving_weights(
    tokens,
    cotangent,
    expert_ids,
    gate_values,
    replica_pick,
    replica_plan,
    gate_proj,
    up_proj,
    down_proj,
):
    experts = lax.axis_size("expert")
    capacity = CAP
    slot_total = 2 * capacity
    model_width = tokens.shape[1]
    topk = expert_ids.shape[1]
    token_count = tokens.shape[0]
    slot_index, kept_mask = route_assignments(
        expert_ids.reshape(-1), replica_pick.reshape(-1), replica_plan, capacity
    )
    source, filled = fill_slots(slot_index, kept_mask, experts * slot_total)
    token_of = source // topk
    zero_half = jnp.zeros((), jnp.bfloat16)
    send_rows = jnp.where(filled[:, None], jnp.take(tokens, token_of, axis=0), zero_half).reshape(
        experts, slot_total, model_width
    )
    send_upstream = jnp.where(
        filled[:, None], jnp.take(cotangent, token_of, axis=0), zero_half
    ).reshape(experts, slot_total, model_width)
    send_weight = jnp.where(filled, gate_values.reshape(-1)[source], zero_half).reshape(
        experts, slot_total
    )
    arrived = lax.all_to_all(send_rows, "expert", split_axis=0, concat_axis=0, tiled=True)
    own_gate = gate_proj[0]
    own_up = up_proj[0]
    own_down = down_proj[0]
    hidden_width = own_gate.shape[1]
    spread = (
        lax.all_to_all(
            own_gate.reshape(experts, -1), "expert", split_axis=0, concat_axis=0, tiled=True
        ),
        lax.all_to_all(
            own_up.reshape(experts, -1), "expert", split_axis=0, concat_axis=0, tiled=True
        ),
        lax.all_to_all(
            own_down.reshape(experts, -1), "expert", split_axis=0, concat_axis=0, tiled=True
        ),
    )
    chosen_gate = jnp.take(spread[0], replica_plan, axis=0)
    chosen_up = jnp.take(spread[1], replica_plan, axis=0)
    chosen_down = jnp.take(spread[2], replica_plan, axis=0)
    collected = (
        lax.all_to_all(chosen_gate, "expert", split_axis=0, concat_axis=0, tiled=True),
        lax.all_to_all(chosen_up, "expert", split_axis=0, concat_axis=0, tiled=True),
        lax.all_to_all(chosen_down, "expert", split_axis=0, concat_axis=0, tiled=True),
    )
    copy_gate = collected[0].reshape(model_width, hidden_width)
    copy_up = collected[1].reshape(model_width, hidden_width)
    copy_down = collected[2].reshape(model_width, hidden_width)
    arrived_up, arrived_weight = (
        lax.all_to_all(send_upstream, "expert", split_axis=0, concat_axis=0, tiled=True),
        lax.all_to_all(send_weight, "expert", split_axis=0, concat_axis=0, tiled=True),
    )
    owned_dx, owned_gate_rows, owned_grads = expert_backward(
        arrived[:, :capacity].reshape(-1, model_width),
        arrived_up[:, :capacity].reshape(-1, model_width),
        arrived_weight[:, :capacity].reshape(-1),
        own_gate,
        own_up,
        own_down,
    )
    copied_dx, copied_gate_rows, copied_grads = expert_backward(
        arrived[:, capacity:].reshape(-1, model_width),
        arrived_up[:, capacity:].reshape(-1, model_width),
        arrived_weight[:, capacity:].reshape(-1),
        copy_gate,
        copy_up,
        copy_down,
    )
    back_rows = jnp.concatenate(
        [
            owned_dx.reshape(experts, capacity, model_width),
            copied_dx.reshape(experts, capacity, model_width),
        ],
        axis=1,
    )
    back_gate = jnp.concatenate(
        [owned_gate_rows.reshape(experts, capacity), copied_gate_rows.reshape(experts, capacity)],
        axis=1,
    ).astype(jnp.bfloat16)
    returned, returned_gate = (
        lax.all_to_all(back_rows, "expert", split_axis=0, concat_axis=0, tiled=True),
        lax.all_to_all(back_gate, "expert", split_axis=0, concat_axis=0, tiled=True),
    )
    copy_pieces = (
        copied_grads[0].astype(jnp.bfloat16).reshape(experts, -1),
        copied_grads[1].astype(jnp.bfloat16).reshape(experts, -1),
        copied_grads[2].astype(jnp.bfloat16).reshape(experts, -1),
    )
    grad_spread = (
        lax.all_to_all(copy_pieces[0], "expert", split_axis=0, concat_axis=0, tiled=True),
        lax.all_to_all(copy_pieces[1], "expert", split_axis=0, concat_axis=0, tiled=True),
        lax.all_to_all(copy_pieces[2], "expert", split_axis=0, concat_axis=0, tiled=True),
    )
    lane_ids = jnp.arange(experts, dtype=jnp.int32)
    owner_map = (replica_plan[None, :] == lane_ids[:, None]).astype(jnp.bfloat16)
    summed_gate = jnp.dot(owner_map, grad_spread[0], preferred_element_type=jnp.float32).astype(
        jnp.bfloat16
    )
    summed_up = jnp.dot(owner_map, grad_spread[1], preferred_element_type=jnp.float32).astype(
        jnp.bfloat16
    )
    summed_down = jnp.dot(owner_map, grad_spread[2], preferred_element_type=jnp.float32).astype(
        jnp.bfloat16
    )
    grad_back = (
        lax.all_to_all(summed_gate, "expert", split_axis=0, concat_axis=0, tiled=True),
        lax.all_to_all(summed_up, "expert", split_axis=0, concat_axis=0, tiled=True),
        lax.all_to_all(summed_down, "expert", split_axis=0, concat_axis=0, tiled=True),
    )
    total_gate = owned_grads[0] + grad_back[0].reshape(model_width, hidden_width).astype(
        jnp.float32
    )
    total_up = owned_grads[1] + grad_back[1].reshape(model_width, hidden_width).astype(jnp.float32)
    total_down = owned_grads[2] + grad_back[2].reshape(model_width, hidden_width).astype(
        jnp.float32
    )
    shares = (
        lax.psum_scatter(
            total_gate.astype(jnp.bfloat16), "replica", scatter_dimension=0, tiled=True
        ).astype(jnp.float32),
        lax.psum_scatter(
            total_up.astype(jnp.bfloat16), "replica", scatter_dimension=0, tiled=True
        ).astype(jnp.float32),
        lax.psum_scatter(
            total_down.astype(jnp.bfloat16), "replica", scatter_dimension=0, tiled=True
        ).astype(jnp.float32),
    )
    flat_back = returned.reshape(experts * slot_total, model_width)
    picked_rows = jnp.take(flat_back, slot_index, axis=0)
    picked_rows = jnp.where(kept_mask[:, None], picked_rows, zero_half).astype(jnp.float32)
    token_grad = jnp.sum(picked_rows.reshape(token_count, topk, model_width), axis=1).astype(
        jnp.bfloat16
    )
    gate_grad = jnp.where(kept_mask, returned_gate.reshape(-1)[slot_index], zero_half).reshape(
        token_count, topk
    )
    return (
        token_grad,
        gate_grad,
        shares[0].astype(jnp.bfloat16)[None],
        shares[1].astype(jnp.bfloat16)[None],
        shares[2].astype(jnp.bfloat16)[None],
    )


BF = jnp.bfloat16
F32 = jnp.float32
CONTRACT_ROWS = (((0,), (0,)), ((), ()))
CONTRACT_COLS = (((1,), (1,)), ((), ()))
MIB = 1024 * 1024

BASES = (4, 6, 2)
ORDER = (0, 1, 2, 4, 3, 6, 7, 5)
LONG = 8 * 10**9
MAIN = 16
QUARTERS = 4
SEND_ROWS = 2 * QUARTERS * MAIN + 16
MAIN_ROWS = QUARTERS * MAIN
BACK_ROWS = MAIN_ROWS + 16
DOUBLE_ROWS = 2 * MAIN_ROWS + 24


def copies_of(experts):
    return 2 if experts <= 8 else 8


def iota(shape, axis):
    return lax.broadcasted_iota(jnp.int32, shape, axis)


def partners(experts, tokens):
    row = iota((experts, tokens), 0)
    step = jnp.bitwise_xor(jnp.bitwise_and(row, 1), lax.axis_index("replica"))
    for d, base in enumerate(BASES):
        step = jnp.where(jnp.right_shift(row, 1) == d + 1, step + base, step)
    step = jnp.where(row < 2, row, step)
    return jnp.bitwise_xor(step, lax.axis_index("expert"))


def mask(condition):
    return condition.astype(F32).astype(BF)


def repeat_rows(table, times):
    width = table.shape[1]
    return jnp.concatenate(
        [jnp.broadcast_to(table[e : e + 1], (times, width)) for e in range(table.shape[0])], axis=0
    )


def route_kernel(plan_hbm, ids_hbm, pick_hbm, gate_hbm, tok_hbm, cot_hbm, *refs):
    sems = refs[-1]
    plan_ref, ids_ref, pick_ref, gate_ref, tok_ref, cot_ref = refs[-7:-1]
    slot_ref, gates_ref = refs[-9:-7]
    send_refs = refs[:-9]
    topk, tokens = ids_ref.shape
    experts = len(send_refs)
    width = tok_ref.shape[1] // QUARTERS
    copies = copies_of(experts)
    loads = [
        pltpu.make_async_copy(source, place, sems.at[n])
        for n, (source, place) in enumerate(
            (
                (plan_hbm, plan_ref),
                (ids_hbm, ids_ref),
                (pick_hbm, pick_ref),
                (gate_hbm, gate_ref),
                (tok_hbm, tok_ref),
                (cot_hbm, cot_ref),
            )
        )
    ]
    for load in loads:
        load.start()
    before = mask(iota((tokens, tokens), 0) < iota((tokens, tokens), 1))
    expert_row = partners(experts, tokens)
    for load in loads[:4]:
        load.wait()
    ids = ids_ref[...]
    pick = pick_ref[...]
    gate = gate_ref[...].astype(F32)
    named = jnp.zeros((experts, tokens), jnp.int32)
    gates = jnp.zeros((experts, tokens), F32)
    for k in range(topk):
        hit = ids[k : k + 1] == expert_row
        named = jnp.where(hit, pick[k : k + 1] + 1, named)
        gates = jnp.where(hit, gate[k : k + 1], gates)
    hot = jnp.zeros((experts, tokens), jnp.int32)
    for j in range(experts):
        hot = jnp.where(expert_row == plan_ref[j], 1, hot)
    chosen = jnp.where(named == 0, -1, jnp.where(hot > 0, named - 1, 0))
    masks = jnp.concatenate([(chosen == c).astype(F32) for c in range(copies + 1)], axis=0)
    rank = jnp.dot(masks.astype(BF), before, preferred_element_type=F32).astype(jnp.int32)
    slot = jnp.full((experts, tokens), -1, jnp.int32)
    for c in range(copies + 1):
        rank_c = rank[c * experts : (c + 1) * experts]
        keep = jnp.logical_and(chosen == c, rank_c < CAP)
        slot = jnp.where(keep, c * CAP + rank_c, slot)
    slot_ref[...] = slot
    gates_ref[...] = gates
    slot16 = repeat_rows(slot, MAIN)
    gate16 = repeat_rows(gates, MAIN)
    inner = jnp.bitwise_and(iota(slot16.shape, 0), MAIN - 1)
    onehot = (slot16 == inner).astype(F32)
    wanted = MAIN + jnp.bitwise_and(jnp.right_shift(inner, 2), 1)
    last = (slot16 == wanted).astype(F32)
    last_rows = jnp.where(inner >= 8, 0.0, last)
    last_scaled = jnp.where(inner >= 8, last * gate16, 0.0)
    quarter = jnp.bitwise_and(inner, 3)
    for load in loads[4:]:
        load.wait()
    rows = jnp.dot(onehot.astype(BF), tok_ref[...], preferred_element_type=F32).astype(BF)
    scaled = jnp.dot(
        (onehot * gate16).astype(BF), cot_ref[...], preferred_element_type=F32
    ).astype(BF)
    tail = jnp.zeros((experts * MAIN, width), F32)
    for q in range(QUARTERS):
        cols = slice(q * width, (q + 1) * width)
        mine = quarter == q
        tail += jnp.dot(
            jnp.where(mine, last_rows, 0.0).astype(BF), tok_ref[:, cols], preferred_element_type=F32
        )
        tail += jnp.dot(
            jnp.where(mine, last_scaled, 0.0).astype(BF),
            cot_ref[:, cols],
            preferred_element_type=F32,
        )
    tail = tail.astype(BF)
    for c, ref in enumerate(send_refs):
        here = slice(c * MAIN, (c + 1) * MAIN)
        for q in range(QUARTERS):
            cols = slice(q * width, (q + 1) * width)
            ref[q * MAIN : (q + 1) * MAIN, :] = rows[here, cols]
            ref[(QUARTERS + q) * MAIN : (QUARTERS + q + 1) * MAIN, :] = scaled[here, cols]
        ref[2 * QUARTERS * MAIN :, :] = tail[here]


def expert_kernel(*refs):
    experts = len(ORDER)
    recv_refs = [refs[ORDER.index(c)] for c in range(experts)]
    gate_ref, up_ref, down_ref = refs[experts : experts + 3]
    back_refs = refs[experts + 3 : -5]
    x_ref, s_ref, dg_ref, du_ref, hid_ref = refs[-5:]
    width = refs[0].shape[1]
    main_rows = experts * MAIN
    tail = jnp.concatenate([ref[2 * QUARTERS * MAIN :, :] for ref in recv_refs], axis=0)
    row = iota((4 * experts, main_rows), 0)
    col = iota((4 * experts, main_rows), 1)
    kind = (row >= 2 * experts).astype(jnp.int32)
    chunk = jnp.right_shift(row - kind * 2 * experts, 1)
    base = chunk * MAIN + kind * 8 + jnp.bitwise_and(row, 1) * 4
    for q in range(QUARTERS):
        cols = slice(q * width, (q + 1) * width)
        picked = jnp.dot(mask(col == base + q), tail, preferred_element_type=F32).astype(BF)
        x_ref[main_rows:, cols] = picked[: 2 * experts]
        s_ref[main_rows:, cols] = picked[2 * experts :]
        for i, ref in enumerate(recv_refs):
            here = slice(i * MAIN, (i + 1) * MAIN)
            x_ref[here, cols] = ref[q * MAIN : (q + 1) * MAIN, :]
            s_ref[here, cols] = ref[(QUARTERS + q) * MAIN : (QUARTERS + q + 1) * MAIN, :]
    rows = x_ref[...]
    gate_pre = jnp.dot(rows, gate_ref[...], preferred_element_type=F32)
    up_pre = jnp.dot(rows, up_ref[...], preferred_element_type=F32)
    hidden_grad = jnp.dot(s_ref[...], down_ref[...], preferred_element_type=F32)
    sig = jax.nn.sigmoid(gate_pre)
    activated = gate_pre * sig
    hidden = (activated * up_pre).astype(BF)
    slope = sig * (1.0 + gate_pre * (1.0 - sig))
    gate_delta = (hidden_grad * up_pre * slope).astype(BF)
    up_delta = (hidden_grad * activated).astype(BF)
    hid_ref[...] = hidden
    dg_ref[...] = gate_delta
    du_ref[...] = up_delta
    grad = (
        lax.dot_general(gate_delta, gate_ref[...], CONTRACT_COLS, preferred_element_type=F32)
        + lax.dot_general(up_delta, up_ref[...], CONTRACT_COLS, preferred_element_type=F32)
    ).astype(BF)
    product = hidden.astype(F32) * hidden_grad
    product = jnp.concatenate(
        [product, jnp.zeros((width - product.shape[0], product.shape[1]), F32)], axis=0
    )
    high = product.astype(BF)
    low = (product - high.astype(F32)).astype(BF)
    ones = jnp.ones((8, product.shape[1]), BF)
    gate_lanes = lax.dot_general(
        ones, high, CONTRACT_COLS, preferred_element_type=F32
    ) + lax.dot_general(ones, low, CONTRACT_COLS, preferred_element_type=F32)
    trow = iota((main_rows, 2 * experts), 0)
    tcol = iota((main_rows, 2 * experts), 1)
    inner = jnp.bitwise_and(trow, MAIN - 1)
    source = jnp.right_shift(trow, 4) * 2 + jnp.right_shift(inner, 2)
    spread = jnp.zeros((main_rows, width), F32)
    for q in range(QUARTERS):
        cols = slice(q * width, (q + 1) * width)
        mine = jnp.logical_and(jnp.bitwise_and(inner, 3) == q, inner < 8)
        place = mask(jnp.logical_and(mine, tcol == source))
        spread += jnp.dot(place, grad[main_rows:, cols], preferred_element_type=F32)
        for i in range(experts):
            single = i < 2
            low = q * MAIN + (0 if single else (i % 2) * MAIN_ROWS)
            ref = back_refs[i if single else 1 + i // 2]
            ref[low : low + MAIN, :] = grad[i * MAIN : (i + 1) * MAIN, cols]
    for n, ref in enumerate(back_refs):
        if n < 2:
            ref[MAIN_ROWS:, :] = jnp.concatenate(
                [spread[n * MAIN : n * MAIN + 8], gate_lanes], axis=0
            ).astype(BF)
        else:
            i = 2 * n - 2
            both = [spread[c * MAIN : c * MAIN + 8] for c in (i, i + 1)]
            ref[2 * MAIN_ROWS : 2 * MAIN_ROWS + 16, :] = jnp.concatenate(both, axis=0).astype(BF)
            ref[2 * MAIN_ROWS + 16 :, :] = gate_lanes.astype(BF)


def grads_of(half, x_ref, s_ref, dg_ref, du_ref, hid_ref):
    rows = x_ref.shape[1] // 2
    cols = pl.ds(pl.multiple_of(half * rows, rows), rows)
    x_half = x_ref[:, cols]
    s_half = s_ref[:, cols]
    return (
        lax.dot_general(x_half, dg_ref[...], CONTRACT_ROWS, preferred_element_type=F32),
        lax.dot_general(x_half, du_ref[...], CONTRACT_ROWS, preferred_element_type=F32),
        lax.dot_general(s_half, hid_ref[...], CONTRACT_ROWS, preferred_element_type=F32),
    )


def other_half_kernel(x_ref, s_ref, dg_ref, du_ref, hid_ref, out_ref):
    half = 1 - lax.axis_index("replica")
    parts = grads_of(half, x_ref, s_ref, dg_ref, du_ref, hid_ref)
    rows = parts[0].shape[0]
    for n in range(3):
        out_ref[n * rows : (n + 1) * rows, :] = parts[n].astype(BF)


def own_half_kernel(
    x_ref, s_ref, dg_ref, du_ref, hid_ref, came_ref, gate_ref, up_ref, down_ref
):
    parts = grads_of(lax.axis_index("replica"), x_ref, s_ref, dg_ref, du_ref, hid_ref)
    rows = parts[0].shape[0]
    for n, out_ref in enumerate((gate_ref, up_ref, down_ref)):
        came = came_ref[n * rows : (n + 1) * rows, :].astype(F32)
        out_ref[...] = (parts[n].astype(BF).astype(F32) + came).astype(BF)


def tail_of(ref, part):
    if part is None:
        return ref[MAIN_ROWS:, :]
    both = ref[2 * MAIN_ROWS : 2 * MAIN_ROWS + 16, :].astype(F32)
    sums = ref[2 * MAIN_ROWS + 16 :, :].astype(F32)
    return jnp.concatenate([both[8 * part : 8 * part + 8], sums], axis=0).astype(BF)


def combine_chunks(chunks, views, ids_ref, slot_ref, gates_ref):
    topk, tokens = ids_ref.shape
    experts = slot_ref.shape[0]
    width = views[0][0].shape[1]
    slot = jnp.concatenate([slot_ref[c : c + 1] for c in chunks], axis=0)
    slot16 = repeat_rows(slot, MAIN)
    inner = jnp.bitwise_and(iota(slot16.shape, 0), MAIN - 1)
    onehot = mask(slot16 == inner)
    wanted = MAIN + jnp.right_shift(inner, 2)
    last = jnp.where(jnp.logical_and(slot16 == wanted, inner < 8), 1.0, 0.0)
    quarter = jnp.bitwise_and(inner, 3)
    tails = [tail_of(*view) for view in views]
    starts = [(ref, MAIN_ROWS if part else 0) for ref, part in views]
    tail = jnp.concatenate(tails, axis=0)
    totals = []
    for q in range(QUARTERS):
        main = jnp.concatenate(
            [ref[first + q * MAIN : first + (q + 1) * MAIN, :] for ref, first in starts], axis=0
        )
        place = jnp.where(quarter == q, last, 0.0).astype(BF)
        total = lax.dot_general(onehot, main, CONTRACT_ROWS, preferred_element_type=F32)
        total += lax.dot_general(place, tail, CONTRACT_ROWS, preferred_element_type=F32)
        totals.append(total)
    lane_index = iota((width, tokens), 0)
    expert_row = partners(experts, tokens)
    by_choice = jnp.zeros((topk, tokens), F32)
    for place, c in enumerate(chunks):
        mine = slot[place : place + 1]
        lane = jnp.where(mine < MAIN, c * MAIN + mine, experts * MAIN + 2 * c + mine - MAIN)
        lane = jnp.where(mine < 0, -1, lane)
        sums = jnp.dot(tails[place], mask(lane_index == lane), preferred_element_type=F32)
        kept = mine >= 0
        grad = jnp.where(kept, sums[8:9] / jnp.where(kept, gates_ref[c : c + 1], 1.0), 0.0)
        by_choice += jnp.where(ids_ref[...] == expert_row[c : c + 1], grad, 0.0)
    return totals, by_choice


LAST = 3


def combine_kernel(ids_ref, slot_ref, gates_ref, *refs):
    token_ref, grad_ref = refs[-2:]
    singles = [(refs[0], None), (refs[1], None)]
    kept_refs = refs[2 : 2 + len(BASES)]
    given_refs = refs[2 + len(BASES) : -2]
    views = dict(enumerate(singles))
    for d, ref in enumerate(kept_refs):
        views[2 + 2 * d] = (ref, 0)
    for d, ref in enumerate(given_refs):
        views[LAST + 2 + 2 * d] = (ref, 1)
    chunks = sorted(views)
    totals, by_choice = combine_chunks(
        chunks, [views[c] for c in chunks], ids_ref, slot_ref, gates_ref
    )
    width = totals[0].shape[1]
    for q, total in enumerate(totals):
        token_ref[:, q * width : (q + 1) * width] = total
    grad_ref[...] = by_choice


def combine_last_kernel(
    ids_ref, slot_ref, gates_ref, given_ref, token_sum_ref, grad_sum_ref, token_ref, grad_ref
):
    totals, by_choice = combine_chunks([LAST], [(given_ref, 1)], ids_ref, slot_ref, gates_ref)
    width = totals[0].shape[1]
    for q, total in enumerate(totals):
        cols = slice(q * width, (q + 1) * width)
        token_ref[:, cols] = (token_sum_ref[:, cols] + total).astype(BF)
    grad_ref[...] = (grad_sum_ref[...] + by_choice).astype(BF)


def local_call(kernel, outs, arrays, name, flops, moved, space=pltpu.VMEM, scratch=(), limit=16):
    vmem = pl.BlockSpec(memory_space=pltpu.VMEM)
    return pl.pallas_call(
        kernel,
        out_shape=[jax.ShapeDtypeStruct(shape, kind) for shape, kind in outs],
        in_specs=[pl.BlockSpec(memory_space=space)] * len(arrays),
        out_specs=[vmem] * len(outs),
        scratch_shapes=list(scratch),
        compiler_params=pltpu.CompilerParams(vmem_limit_bytes=limit * MIB),
        cost_estimate=pl.CostEstimate(flops=flops, bytes_accessed=moved, transcendentals=0),
        name=name,
    )(*arrays)


def to_step(chunk, base):
    experts = lax.axis_size("expert")
    if base == 1:
        return lax.ppermute(chunk, "expert", [(i, i ^ 1) for i in range(experts)])
    pairs = [(2 * i + r, 2 * (i ^ (base + r)) + r) for i in range(experts) for r in range(2)]
    return lax.ppermute(chunk, ("expert", "replica"), pairs)


def to_twin(chunk):
    return lax.ppermute(chunk, "replica", [(0, 1), (1, 0)])


def hold_kernel(source_ref, place_ref):
    place_ref[...] = source_ref[...]


def per_device_moving_rows(
    tokens,
    cotangent,
    expert_ids,
    gate_values,
    replica_pick,
    replica_plan,
    gate_proj,
    up_proj,
    down_proj,
):
    experts = lax.axis_size("expert")
    token_count, model_width = tokens.shape
    topk = expert_ids.shape[1]
    hidden_width = gate_proj.shape[2]
    width = model_width // QUARTERS
    served = experts * (MAIN + 2)
    small = (topk, token_count)
    count = len(BASES)
    *chunks, slot, gates = local_call(
        route_kernel,
        [((SEND_ROWS, width), BF)] * experts
        + [((experts, token_count), jnp.int32), ((experts, token_count), F32)],
        [replica_plan, expert_ids.T, replica_pick.T, gate_values.T, tokens, cotangent],
        "route",
        LONG,
        2 * 2 * (token_count + served) * model_width,
        space=pltpu.HBM,
        limit=54,
        scratch=[
            pltpu.SMEM((experts,), jnp.int32),
            pltpu.VMEM(small, jnp.int32),
            pltpu.VMEM(small, jnp.int32),
            pltpu.VMEM(small, BF),
            pltpu.VMEM(tokens.shape, BF),
            pltpu.VMEM(tokens.shape, BF),
            pltpu.SemaphoreType.DMA((6,)),
        ],
    )
    recv = list(chunks)
    recv[1] = to_step(chunks[1], 1)
    recv[2] = to_step(chunks[2], 4)
    twin = [to_twin(chunks[c]) for c in (3, 5, 7)]
    twin, near = lax.optimization_barrier((twin, chunks[6]))
    recv[4] = to_step(chunks[4], 6)
    recv[6] = to_step(near, 2)
    recv[3] = to_step(twin[0], 4)
    recv[5] = to_step(twin[1], 6)
    recv[7] = to_step(twin[2], 2)
    (held,) = local_call(hold_kernel, [(recv[0].shape, BF)], [recv[0]], "hold", 1, 1)
    matmul = 2 * served * model_width * hidden_width
    outs = local_call(
        expert_kernel,
        [((BACK_ROWS, width), BF)] * 2
        + [((DOUBLE_ROWS, width), BF)] * count
        + [((served, model_width), BF)] * 2
        + [((served, hidden_width), BF)] * 3,
        [held, *(recv[c] for c in ORDER[1:]), gate_proj[0], up_proj[0], down_proj[0]],
        "expert_rows",
        5 * matmul,
        2 * 3 * model_width * hidden_width,
    )
    backs, factors = outs[: 2 + count], outs[2 + count :]
    kept = list(map(to_step, backs[2:], BASES))
    near = to_step(backs[1], 1)
    half = model_width // 2
    (leaving,) = local_call(
        other_half_kernel,
        [((3 * half, hidden_width), BF)],
        factors,
        "other_half",
        1,
        1,
    )
    shares = local_call(
        own_half_kernel,
        [((half, hidden_width), BF)] * 3,
        [*factors, to_twin(leaving)],
        "own_half",
        1,
        1,
    )
    kept[0], near, shares = lax.optimization_barrier((kept[0], near, shares))
    routes = [expert_ids.T, slot, gates]
    sums = local_call(
        combine_kernel,
        [((token_count, model_width), F32), ((topk, token_count), F32)],
        [*routes, backs[0], near, *kept, *map(to_twin, kept[1:])],
        "combine",
        1,
        1,
    )
    token_grad, gate_grad = local_call(
        combine_last_kernel,
        [((token_count, model_width), BF), ((topk, token_count), BF)],
        [*routes, to_twin(kept[0]), *sums],
        "combine_last",
        1,
        1,
    )
    return (token_grad, gate_grad.T, shares[0][None], shares[1][None], shares[2][None])


def per_device(tokens, cotangent, expert_ids, gate_values, replica_pick, replica_plan, *matrices):
    experts = lax.axis_size("expert")
    slots = (copies_of(experts) + 1) * CAP
    row_bytes = 3 * 2 * tokens.shape[1] * experts
    matrix_bytes = 4 * sum(2 * m[0].size for m in matrices)
    fits = slots == MAIN + 2 and experts == 8 and lax.axis_size("replica") == 2
    rows_cheaper = slots * row_bytes < 2 * CAP * row_bytes + matrix_bytes
    plan = per_device_moving_rows if fits and rows_cheaper else per_device_moving_weights
    return plan(
        tokens, cotangent, expert_ids, gate_values, replica_pick, replica_plan, *matrices
    )


def solution(mesh):
    placed = (
        P(("parts", "expert", "replica"), None),
        P(("parts", "expert", "replica"), None),
        P(("parts", "expert", "replica"), None),
        P(("parts", "expert", "replica"), None),
        P(("parts", "expert", "replica"), None),
        P("parts"),
        P("expert", None, None),
        P("expert", None, None),
        P("expert", None, None),
    )
    return jax.shard_map(
        per_device,
        mesh=mesh,
        in_specs=placed,
        out_specs=(
            P(("parts", "expert", "replica"), None),
            P(("parts", "expert", "replica"), None),
            P(("parts", "expert"), "replica", None),
            P(("parts", "expert"), "replica", None),
            P(("parts", "expert"), "replica", None),
        ),
        check_vma=False,
    )
```
